32 devices in a mesh: dp: 16 (over z, y, x), mp: 2 (over core).
Axes of the slice: x: 2, y: 2, z: 4, core: 2. Of those that a mesh axis runs over, the one named last changes fastest.
Arguments:
- frames: bfloat16 [36864, 512], P('dp'), may hold values from -6 to 6
- lengths: int32 [32, 2], P('dp'), may hold values from 100 to 1024, as said below
- cotangent: bfloat16 [36864, 512], P('dp'), may hold values from -6 to 6
- ffn1_gain: float32 [512], replicated, may hold values from 0.5 to 1.5
- ffn1_in: bfloat16 [512, 2048], P(None, 'mp'), may hold values from -0.25 to 0.25
- ffn1_out: bfloat16 [2048, 512], P('mp'), may hold values from -0.25 to 0.25
- attn_gain: float32 [512], replicated, may hold values from 0.5 to 1.5
- query_weight: bfloat16 [512, 512], P(None, 'mp'), may hold values from -0.25 to 0.25
- key_weight: bfloat16 [512, 512], P(None, 'mp'), may hold values from -0.25 to 0.25
- value_weight: bfloat16 [512, 512], P(None, 'mp'), may hold values from -0.25 to 0.25
- out_weight: bfloat16 [512, 512], P('mp'), may hold values from -1.5 to 1.5
- rel_table: bfloat16 [129, 512], P(None, 'mp'), may hold values from -6 to 6
- conv_gain: bfloat16 [512], P(('dp', 'mp')), may hold values from 0.5 to 1.5
- pointwise_in: bfloat16 [512, 1024], P(('dp', 'mp')), may hold values from -0.25 to 0.25
- conv_kernel: bfloat16 [512, 32], P(('dp', 'mp')), may hold values from -1 to 1
- bn_gain: bfloat16 [512], P(('dp', 'mp')), may hold values from 0.5 to 1.5
- bn_bias: bfloat16 [512], P(('dp', 'mp')), may hold values from -3 to 3
- pointwise_out: bfloat16 [512, 512], P(('dp', 'mp')), may hold values from -0.5 to 0.5
- ffn2_gain: float32 [512], replicated, may hold values from 0.5 to 1.5
- ffn2_in: bfloat16 [512, 2048], P(None, 'mp'), may hold values from -0.25 to 0.25
- ffn2_out: bfloat16 [2048, 512], P('mp'), may hold values from -0.25 to 0.25
- final_gain: float32 [512], replicated, may hold values from 0.5 to 1.5
Outputs:
- block_output: bfloat16 [36864, 512], P('dp')
- frames_grad: float32 [36864, 512], P('dp')
- ffn1_gain_grad: float32 [512], replicated
- ffn1_in_grad: float32 [512, 2048], P('dp', 'mp')
- ffn1_out_grad: float32 [2048, 512], P('mp', 'dp')
- attn_gain_grad: float32 [512], replicated
- query_grad: float32 [512, 512], P('dp', 'mp')
- key_grad: float32 [512, 512], P('dp', 'mp')
- value_grad: float32 [512, 512], P('dp', 'mp')
- out_weight_grad: float32 [512, 512], P('mp', 'dp')
- rel_table_grad: float32 [129, 512], P(None, 'mp')
- conv_gain_grad: float32 [512], P(('dp', 'mp'))
- pointwise_in_grad: float32 [512, 1024], P(('dp', 'mp'))
- conv_kernel_grad: float32 [512, 32], P(('dp', 'mp'))
- bn_gain_grad: float32 [512], P(('dp', 'mp'))
- bn_bias_grad: float32 [512], P(('dp', 'mp'))
- pointwise_out_grad: float32 [512, 512], P(('dp', 'mp'))
- ffn2_gain_grad: float32 [512], replicated
- ffn2_in_grad: float32 [512, 2048], P('dp', 'mp')
- ffn2_out_grad: float32 [2048, 512], P('mp', 'dp')
- final_gain_grad: float32 [512], replicated
The draws below stay inside these ranges and needn't reach their ends.
Inputs may be any that keep to these rules, and one draw needn't show every extreme that they name: Row r gives the lengths of the 2 utterances that fill slab r from its first frame, in order; their sum is at most 1152, and the slab's remaining frames are padding.
All inputs are finite; a program needn't handle non-finite values.
Results may differ from the reference program's by a relative error of at most 0.035.
Values may be sent and summed in bfloat16 or wider, within the bound.
A program may use at most 384 MiB of HBM per device.

```python
import jax
import jax.numpy as jnp
import numpy as np
from jax import lax

D = 512
HEADS = 8
DH = 64
FF = 2048
K = 32
RW = 64
MB = 2
SLAB = 1152
UPS = 2
QB = 576
MAXLEN = 1024
MINLEN = 100
SLABS = 32
FRAMES = 36864
N_DP = 16
N_MP = 2


def draw_lengths(key, part):
    key = jax.random.fold_in(key, 7)
    first_key, second_key, third_key = jax.random.split(key, 3)
    extent = MAXLEN - MINLEN + 1
    first = MINLEN + jnp.minimum(jax.random.randint(first_key, (SLABS,), 0, extent), jax.random.randint(second_key, (SLABS,), 0, extent))
    places = jnp.arange(SLABS)
    first = jnp.where(places == 0, MAXLEN, first)
    room = jnp.minimum(MAXLEN, SLAB - first)
    second = MINLEN + jax.random.randint(third_key, (SLABS,), 0, 1 << 20) % (room - MINLEN + 1)
    second = jnp.where(places == SLABS - 1, MINLEN, second)
    return jnp.stack([first, second], -1).astype(jnp.int32)


def block_levels(key, shape, shards, least, top_value):
    level = 1.0
    for dim, shards_of in shards:
        draws = jax.random.uniform(jax.random.fold_in(jax.random.fold_in(key, 6), dim), (shards_of,), jnp.float32, least / len(shards), top_value / len(shards))
        level = level * jnp.repeat(jnp.exp(draws), shape[dim] // shards_of).reshape((-1,) + (1,) * (len(shape) - 1 - dim))
    return level


def scatter_about(key, shape, scale, most, cuts=(), kind=jnp.bfloat16):
    drawn = jax.random.normal(key, shape, jnp.float32) * scale
    if len(cuts) > 0:
        drawn = block_levels(key, shape, cuts, -0.22, 0.18) * drawn
    return jnp.clip(drawn, min=-most, max=most).astype(kind)


def setup_inputs(seed: int = 0) -> dict:
    splits = jax.random.split(jax.random.key(seed), 23)
    return {
        "frames": scatter_about(splits[0], (FRAMES, D), 1.0, 6.0, ((0, 16),)),
        "lengths": draw_lengths(jax.random.fold_in(splits[22], 71), 0),
        "cotangent": scatter_about(splits[2], (FRAMES, D), 1.0, 6.0, ((0, 16),)),
        "ffn1_gain": jnp.clip(jax.random.uniform(splits[3], (D,), jnp.float32, 0.5, 1.5), 0.5, 1.5),
        "ffn1_in": scatter_about(splits[4], (D, FF), D ** -0.5, 0.25, ((1, 2),)),
        "ffn1_out": scatter_about(splits[5], (FF, D), (FF // 4) ** -0.5, 0.25, ((0, 2),)),
        "attn_gain": jnp.clip(jax.random.uniform(splits[6], (D,), jnp.float32, 0.5, 1.5), 0.5, 1.5),
        "query_weight": scatter_about(splits[7], (D, D), D ** -0.5, 0.25, ((1, 2),)),
        "key_weight": scatter_about(splits[8], (D, D), D ** -0.5, 0.25, ((1, 2),)),
        "value_weight": scatter_about(splits[9], (D, D), D ** -0.5, 0.25, ((1, 2),)),
        "out_weight": scatter_about(splits[10], (D, D), (D // 32) ** -0.5, 1.5, ((0, 2),)),
        "rel_table": scatter_about(splits[11], (2 * RW + 1, D), 1.0, 6.0, ((1, 2),)),
        "conv_gain": jnp.clip(0.5 + 1.0 * jax.random.uniform(splits[12], (D,), jnp.float32) ** block_levels(splits[12], (D,), ((0, 32),), -0.2, 0.2), 0.5, 1.5).astype(jnp.bfloat16),
        "pointwise_in": scatter_about(splits[13], (D, 2 * D), D ** -0.5, 0.25, ((0, 32),)),
        "conv_kernel": scatter_about(splits[14], (D, K), K ** -0.5, 1.0, ((0, 32),)),
        "bn_gain": jnp.clip(0.5 + 1.0 * jax.random.uniform(splits[15], (D,), jnp.float32) ** block_levels(splits[15], (D,), ((0, 32),), -0.2, 0.2), 0.5, 1.5).astype(jnp.bfloat16),
        "bn_bias": scatter_about(splits[16], (D,), 0.5, 3.0, ((0, 32),)),
        "pointwise_out": scatter_about(splits[17], (D, D), (D // 4) ** -0.5, 0.5, ((0, 32),)),
        "ffn2_gain": jnp.clip(jax.random.uniform(splits[18], (D,), jnp.float32, 0.5, 1.5), 0.5, 1.5),
        "ffn2_in": scatter_about(splits[19], (D, FF), D ** -0.5, 0.25, ((1, 2),)),
        "ffn2_out": scatter_about(splits[20], (FF, D), (FF // 4) ** -0.5, 0.25, ((0, 2),)),
        "final_gain": jnp.clip(jax.random.uniform(splits[21], (D,), jnp.float32, 0.5, 1.5), 0.5, 1.5),
    }


NORM_EPS = 1e-05
BATCH_EPS = 1e-05
MASKED = -1e+30

@jax.custom_vjp
def low(v):
    return lax.optimization_barrier(v.astype(jnp.bfloat16)).astype(jnp.float32)

@jax.custom_vjp
def low_back(v):
    return v

def low_keep(v):
    return (low(v), None)

def low_pass(kept, grad):
    return (grad,)

def back_keep(v):
    return (v, None)

def back_low(kept, grad):
    return (low(grad),)
low.defvjp(low_keep, low_pass)
low_back.defvjp(back_keep, back_low)

def matmul(left, right):
    return jnp.dot(left, right, precision=lax.Precision.HIGHEST, preferred_element_type=jnp.float32)

def layer_norm(values, gain):
    centred = values - lax.optimization_barrier(jnp.mean(values, -1, keepdims=True))
    return centred * lax.rsqrt(lax.optimization_barrier(jnp.mean(centred * centred, -1, keepdims=True)) + NORM_EPS) * gain

def segments(slab_lengths):
    bounds = jnp.cumsum(slab_lengths).astype(jnp.int32)
    places = jnp.arange(SLAB, dtype=jnp.int32)
    return lax.optimization_barrier(jnp.sum((places[:, None] >= bounds[None, :]).astype(jnp.int32), axis=1)).astype(jnp.int32)

def feed_forward(values, gain, w_in, w_out):
    normed = low(layer_norm(values, gain))
    share = FF // N_MP
    summed = jnp.zeros_like(values)
    for group in range(N_MP):
        hidden = low_back(matmul(normed, w_in[:, group * share:(group + 1) * share]))
        active = low(jax.nn.silu(hidden))
        summed = summed + low(matmul(active, w_out[group * share:(group + 1) * share]))
    return low_back(summed)

def relative_scores(query_block_rows, position_table_heads, start):
    width = SLAB + QB - 1
    columns = np.clip(np.arange(width) - (QB - 1) - start, -RW, RW) + RW
    nearby_scores = jnp.einsum('pur,lur->upl', query_block_rows, position_table_heads, precision=lax.Precision.HIGHEST)
    spread = jnp.take(nearby_scores, jnp.asarray(columns, jnp.int32), axis=2)
    flat = spread.reshape(HEADS, QB * width)
    return flat[:, QB - 1:QB - 1 + QB * (width - 1)].reshape(HEADS, QB, width - 1)[:, :, :SLAB]

def attention(values, labels, gain, w_query, w_key, w_value, w_out, table):
    normed = low(layer_norm(values, gain))
    query_rows = low(low_back(matmul(normed, w_query))).reshape(SLAB, HEADS, DH)
    keys = low(low_back(matmul(normed, w_key))).reshape(SLAB, HEADS, DH)
    contents = low(low_back(matmul(normed, w_value))).reshape(SLAB, HEADS, DH)
    position_table_heads = table.reshape(2 * RW + 1, HEADS, DH)
    blocks = []
    for start in range(0, SLAB, QB):
        query_block_rows = query_rows[start:start + QB]
        content = jnp.einsum('qhd,khd->hqk', query_block_rows, keys, precision=lax.Precision.HIGHEST)
        scores = low_back((content + relative_scores(query_block_rows, position_table_heads, start)) * DH ** (-0.5))
        allowed = labels[start:start + QB, None] == labels[None, :]
        scores = jnp.where(allowed[None], scores, MASKED)
        weights = low(jax.nn.softmax(scores, axis=-1))
        blocks.append(jnp.einsum('hqk,khd->qhd', weights, contents, precision=lax.Precision.HIGHEST))
    mixed = low(low_back(jnp.concatenate(blocks, 0).reshape(SLAB, D)))
    share = D // N_MP
    summed = jnp.zeros_like(values)
    for group in range(N_MP):
        summed = summed + low(matmul(mixed[:, group * share:(group + 1) * share], w_out[group * share:(group + 1) * share]))
    return low_back(summed)

def depthwise(values, labels, kernel):
    before = K // 2
    after = K - before - 1
    padded = jnp.pad(values, ((before, after), (0, 0)))
    padded_labels = jnp.pad(labels, (before, after), constant_values=-1)
    result = jnp.zeros_like(values)
    for tap in range(K):
        same = (padded_labels[tap:tap + SLAB] == labels).astype(values.dtype)
        result = result + padded[tap:tap + SLAB] * same[:, None] * kernel[:, tap]
    return result

def micro_block(frames, slab_lengths, weights):
    ffn1_gain, ffn1_in, ffn1_out, attn_gain, w_query, w_key, w_value, w_out, table, conv_gain, point_in, kernel, bn_gain, bn_bias, point_out, ffn2_gain, ffn2_in, ffn2_out, final_gain = weights
    labels = jax.vmap(segments)(slab_lengths)

    def front(pair):
        values, marks = pair
        after_ffn = values + 0.5 * feed_forward(values, ffn1_gain, ffn1_in, ffn1_out)
        after_attn = after_ffn + attention(after_ffn, marks, attn_gain, w_query, w_key, w_value, w_out, table)
        normed = low(layer_norm(after_attn, conv_gain))
        expanded = low_back(matmul(normed, point_in))
        gated = expanded[:, :D] * jax.nn.sigmoid(expanded[:, D:])
        return (after_attn, depthwise(gated, marks, kernel))
    after_attn, mixed = lax.map(jax.checkpoint(front), (frames, labels))
    valid = (labels < UPS).astype(frames.dtype)[..., None]
    count = jnp.sum(valid)
    centre = lax.optimization_barrier(jnp.sum(valid * mixed, (0, 1))) / count
    spread = lax.optimization_barrier(jnp.sum(valid * mixed * mixed, (0, 1))) / count - centre * centre
    inverse = lax.rsqrt(spread + BATCH_EPS)

    def back(triple):
        residual, conv_in, keep = triple
        normal = (conv_in - centre) * inverse * bn_gain + bn_bias
        active = low(jax.nn.silu(normal))
        after_conv = residual + low_back(matmul(active, point_out))
        after_ffn = after_conv + 0.5 * feed_forward(after_conv, ffn2_gain, ffn2_in, ffn2_out)
        return keep * layer_norm(after_ffn, final_gain)
    return lax.map(jax.checkpoint(back), (after_attn, mixed, valid))

def reference(frames, lengths, cotangent, ffn1_gain, ffn1_in, ffn1_out, attn_gain, query_weight, key_weight, value_weight, out_weight, rel_table, conv_gain, pointwise_in, conv_kernel, bn_gain, bn_bias, pointwise_out, ffn2_gain, ffn2_in, ffn2_out, final_gain):
    weights = tuple((item.astype(jnp.float32) for item in (ffn1_gain, ffn1_in, ffn1_out, attn_gain, query_weight, key_weight, value_weight, out_weight, rel_table, conv_gain, pointwise_in, conv_kernel, bn_gain, bn_bias, pointwise_out, ffn2_gain, ffn2_in, ffn2_out, final_gain)))
    slabs = frames.astype(jnp.float32).reshape(N_DP, MB, SLAB, D).transpose(1, 0, 2, 3)
    upstreams = cotangent.astype(jnp.float32).reshape(N_DP, MB, SLAB, D).transpose(1, 0, 2, 3)
    slab_lengths = lengths.reshape(N_DP, MB, UPS).transpose(1, 0, 2)

    def accumulate(totals, inputs):
        values, marks, upstream = inputs

        def forward(slab_values, parameters):
            return micro_block(slab_values, marks, parameters)
        output, pullback = jax.vjp(forward, values, weights)
        grad_values, grad_weights = pullback(upstream)
        return (jax.tree.map(jnp.add, totals, grad_weights), (output, grad_values))
    totals, (outputs, grads) = lax.scan(accumulate, jax.tree.map(jnp.zeros_like, weights), (slabs, slab_lengths, upstreams))
    block_output = outputs.transpose(1, 0, 2, 3).reshape(FRAMES, D).astype(jnp.bfloat16)
    frames_grad = grads.transpose(1, 0, 2, 3).reshape(FRAMES, D)
    grad_ffn1_gain, grad_ffn1_in, grad_ffn1_out, grad_attn_gain, grad_query, grad_key, grad_value, grad_out, grad_table, grad_conv_gain, grad_point_in, grad_kernel, grad_bn_gain, grad_bn_bias, gradient_pointwise_output, grad_ffn2_gain, grad_ffn2_in, grad_ffn2_out, grad_final_gain = totals
    return (block_output, frames_grad, grad_ffn1_gain, grad_ffn1_in, grad_ffn1_out, grad_attn_gain, grad_query, grad_key, grad_value, grad_out, grad_table, grad_conv_gain, grad_point_in, grad_kernel, grad_bn_gain, grad_bn_bias, gradient_pointwise_output, grad_ffn2_gain, grad_ffn2_in, grad_ffn2_out, grad_final_gain)
```

```python
import jax
import jax.numpy as jnp
from jax import lax
from jax.experimental import pallas as pl
from jax.experimental.pallas import tpu as pltpu
from jax.sharding import PartitionSpec as P

D = 512
DH = 64
RW = 64
SLAB = 1152
TAPS = 32
NORM_EPS = 1e-05
BATCH_EPS = 1e-05
MASKED = -1e30

RB = 288
SUB = 64
GAP = 16
TOP = 32
PADDED = 1216
CH = 64
LT = D // 128

f32 = jnp.float32
bf16 = jnp.bfloat16


def params(mib=60):
    return pltpu.CompilerParams(
        dimension_semantics=("arbitrary",), vmem_limit_bytes=mib << 20
    )


def dot(a, b):
    return jnp.dot(a, b, preferred_element_type=f32)


def dot_nt(a, b):
    return lax.dot_general(a, b, (((1,), (1,)), ((), ())), preferred_element_type=f32)


def dot_tn(a, b):
    return lax.dot_general(a, b, (((0,), (0,)), ((), ())), preferred_element_type=f32)


def norm_parts(v):
    c = v - jnp.mean(v, -1, keepdims=True)
    inv = lax.rsqrt(jnp.mean(c * c, -1, keepdims=True) + NORM_EPS)
    return c * inv, inv


def norm_back(gy, gain, xhat, inv):
    e = gy * gain
    inner = jnp.mean(e * xhat, -1, keepdims=True)
    return inv * (e - jnp.mean(e, -1, keepdims=True) - xhat * inner)


def rows_sum(v):
    return jnp.sum(v.reshape(v.shape[0] // 8, 8, v.shape[1]), 0)


def accumulate(ref, step, value):
    @pl.when(step == 0)
    def _():
        ref[...] = value

    @pl.when(step > 0)
    def _():
        ref[...] += value


def row(shape_cols, rows=RB):
    return pl.BlockSpec((rows, shape_cols), lambda i, *m: (i, 0))


def own_row(cols, rows=RB):
    blocks = SLAB // rows
    return pl.BlockSpec((rows, cols), lambda i, m: (m[0] * blocks + i, 0))


def fixed(*shape):
    zeros = (0,) * len(shape)
    return pl.BlockSpec(shape, lambda i, *m: zeros)


def planes(count, cols, rows=RB):
    return pl.BlockSpec((count, rows, cols), lambda i, *m: (0, i, 0))


SMEM = pl.BlockSpec(memory_space=pltpu.SMEM)
VMEM = pl.BlockSpec(memory_space=pltpu.VMEM)


def shape(dims, dtype):
    return jax.ShapeDtypeStruct(dims, dtype)


MESH = pl.DeviceIdType.MESH


def split_axis(n):
    low = 4 if n % 4 == 0 else 1
    return n // low, low


class Place:
    def __init__(self):
        self.n = lax.axis_size("dp")
        self.high, self.low = split_axis(self.n)
        self.me = lax.axis_index("dp")
        self.core = lax.axis_index("mp")
        self.hi = self.me // self.low
        self.lo = self.me % self.low

    def size(self, kind):
        return {"all": self.n, "low": self.low, "high": self.high}[kind]

    def mine(self, kind):
        return {"all": self.me, "low": self.lo, "high": self.hi}[kind]

    def peer(self, kind, j):
        at = (self.mine(kind) + j) % self.size(kind)
        if kind == "low":
            return at, {"dp": self.hi * self.low + at}
        if kind == "high":
            return at, {"dp": at * self.low + self.lo}
        return at, {"dp": at}

    def each(self, kind, do):
        size = self.size(kind)
        if size <= 4:
            for j in range(1, size):
                do(j)
        else:

            def body(j, carry):
                do(j)
                return carry

            lax.fori_loop(1, size, body, 0)

    def greet(self, kinds, core=True):
        barrier = pltpu.get_barrier_semaphore()
        for kind in kinds:
            self.each(
                kind,
                lambda j: pl.semaphore_signal(
                    barrier, inc=1, device_id=self.peer(kind, j)[1], device_id_type=MESH
                ),
            )
        if core:
            pl.semaphore_signal(barrier, inc=1, device_id={"mp": 1 - self.core}, device_id_type=MESH)

    def greeted(self, kinds, core=True):
        count = sum(self.size(kind) - 1 for kind in kinds) + (1 if core else 0)
        if count:
            pl.semaphore_wait(pltpu.get_barrier_semaphore(), count)


class Hop:
    def __init__(self, place, kind, piece, slots, send, recv):
        self.place, self.kind, self.piece = place, kind, piece
        self.slots, self.send, self.recv = slots, send, recv

    def copy(self, j, slot):
        at, device = self.place.peer(self.kind, j)
        return pltpu.make_async_remote_copy(
            src_ref=self.piece(at), dst_ref=self.slots.at[slot], send_sem=self.send.at[j],
            recv_sem=self.recv.at[slot], device_id=device, device_id_type=MESH,
        )

    def start(self):
        mine = self.place.mine(self.kind)
        self.place.each(self.kind, lambda j: self.copy(j, mine).start())

    def wait(self):
        self.place.each(self.kind, lambda j: self.copy(j, self.place.peer(self.kind, j)[0]).wait())

    def total(self):
        total = self.piece(self.place.mine(self.kind))[...].astype(f32)
        size = self.place.size(self.kind)
        if size <= 4:
            for j in range(1, size):
                total = total + self.slots[self.place.peer(self.kind, j)[0]].astype(f32)
            return total
        return lax.fori_loop(
            1, size, lambda j, t: t + self.slots[self.place.peer(self.kind, j)[0]].astype(f32), total
        )


def core_copy(place, src, dst, sems):
    return pltpu.make_async_remote_copy(
        src_ref=src, dst_ref=dst, send_sem=sems.at[0], recv_sem=sems.at[1],
        device_id={"mp": 1 - place.core}, device_id_type=MESH,
    )


def slots_of(size, dims, dtype=bf16):
    return [
        pltpu.VMEM((size, *dims), dtype),
        pltpu.SemaphoreType.DMA((size,)),
        pltpu.SemaphoreType.DMA((size,)),
    ]


class View:
    def __init__(self, index, start, stop, order):
        self.index, self.start, self.stop, self.order = index, start, stop, order
        self.width = stop - start

    def kinds(self):
        return ("low", "high") if self.order == "low" else ("high", "low")

    def mid(self, n, rows):
        high, low = split_axis(n)
        return (high if self.order == "low" else low, rows, self.width)

    def first_scratch(self, n, rows):
        high, low = split_axis(n)
        return slots_of(low if self.order == "low" else high, self.mid(n, rows))

    def second_scratch(self, n, rows):
        size, *dims = self.mid(n, rows)
        return slots_of(size, dims)

    def first(self, place, acc, refs):
        cols = slice(self.start, self.stop)
        if self.index is not None:
            acc = acc.at[self.index]
        if self.order == "low":
            piece = lambda p: acc.at[:, p, :, cols]
        else:
            piece = lambda p: acc.at[p, :, :, cols]
        return Hop(place, self.kinds()[0], piece, *refs)

    def second(self, place, mid, refs):
        return Hop(place, self.kinds()[1], lambda p: mid.at[p], *refs)


PAIR_VIEWS = (View(0, 0, 1024, "low"), View(1, 0, 384, "low"), View(1, 384, 1024, "high"))
FLAT_VIEWS = (View(None, 0, 640, "low"), View(None, 640, 1024, "high"))
CONV_C = 2 * D + D + 128
CONV_VIEWS = (View(None, 0, 1024, "low"), View(None, 1024, CONV_C, "high"))


def firsts(views, n, rows):
    return [ref for v in views for ref in v.first_scratch(n, rows)]


def seconds(views, n, rows):
    return [ref for v in views for ref in v.second_scratch(n, rows)]


def threes(refs):
    return [refs[i : i + 3] for i in range(0, len(refs), 3)]


def remote(collective_id, mib=60):
    return pltpu.CompilerParams(
        dimension_semantics=("arbitrary",), vmem_limit_bytes=mib << 20,
        collective_id=collective_id, has_side_effects=True,
    )


def all_reduce_kernel(x_ref, o_ref, slots, send, recv):
    place = Place()
    place.greet(("all",), False)
    slots[place.me] = x_ref[...]
    place.greeted(("all",), False)
    hop = Hop(place, "all", lambda p: x_ref, slots, send, recv)
    hop.start()
    hop.wait()
    o_ref[...] = slot_sum(slots, place.n)


def slot_sum(slots, n):
    return lax.fori_loop(1, n, lambda j, total: total + slots[j], slots[0])


def all_reduce(x, collective_id):
    n = lax.axis_size("dp")
    return pl.pallas_call(
        all_reduce_kernel,
        in_specs=[VMEM],
        out_specs=VMEM,
        out_shape=shape(x.shape, x.dtype),
        scratch_shapes=slots_of(n, x.shape, f32),
        compiler_params=pltpu.CompilerParams(collective_id=collective_id, has_side_effects=True),
        name="all_reduce",
    )(x)


def ffn_up(n, halves, act_refs, slope_refs):
    total = None
    for (w1, w2), act_ref, slope_ref in zip(halves, act_refs, slope_refs):
        for c in range(0, w1.shape[1], 512):
            hid = dot(n, w1[:, c : c + 512])
            sg = jax.nn.sigmoid(hid)
            act = hid * sg
            act16 = act.astype(bf16)
            act_ref[:, c : c + 512] = act16
            slope_ref[:, c : c + 512] = (sg + act * (1.0 - sg)).astype(bf16)
            part = dot(act16, w2[c : c + 512, :])
            total = part if total is None else total + part
    return total


def ffn_down(gb, halves, slope_refs, ghid_refs):
    total = None
    for (w1, w2), slope_ref, ghid_ref in zip(halves, slope_refs, ghid_refs):
        for c in range(0, w1.shape[1], 512):
            gact = dot_nt(gb, w2[c : c + 512, :])
            ghid = (gact * slope_ref[:, c : c + 512].astype(f32)).astype(bf16)
            ghid_ref[:, c : c + 512] = ghid
            part = dot_nt(ghid, w1[:, c : c + 512])
            total = part if total is None else total + part
    return total


def first_kernel(m, x_ref, g1, w1o, w1x, w2o, w2x, ga, wqo, wqx,
                 x1_ref, xs_ref, act_ref, slo, slx, n1_ref, na_ref, q_ref, k_ref, v_ref):
    xs_ref[...] = x_ref[...]
    x = x_ref[...].astype(f32)
    xhat, _ = norm_parts(x)
    n = (xhat * g1[...]).astype(bf16)
    n1_ref[...] = n
    acts = (act_ref.at[1], act_ref.at[0])
    x1 = x + 0.5 * ffn_up(n, ((w1o, w2o), (w1x, w2x)), acts, (slo, slx))
    x1_ref[...] = x1
    xhat, _ = norm_parts(x1)
    na = (xhat * ga[...]).astype(bf16)
    na_ref[...] = na
    own = dot(na, wqo[...])
    oth = dot(na, wqx[...])
    w = own.shape[1] // 3
    q_ref[:, :w] = (own[:, :w].astype(bf16).astype(f32) * DH**-0.5).astype(bf16)
    q_ref[:, w:] = (oth[:, :w].astype(bf16).astype(f32) * DH**-0.5).astype(bf16)
    k_ref[:, :w] = own[:, w : 2 * w].astype(bf16)
    k_ref[:, w:] = oth[:, w : 2 * w].astype(bf16)
    v_ref[:, :w] = own[:, 2 * w :].astype(bf16)
    v_ref[:, w:] = oth[:, 2 * w :].astype(bf16)


def first_call(meta, frames, g1, w1o, w1x, w2o, w2x, ga, wqo, wqx):
    hid = w1o.shape[1]
    outs = [(D, f32), (D, bf16), None, (hid, bf16), (hid, bf16)] + [(D, bf16)] * 5
    return pl.pallas_call(
        first_kernel,
        grid_spec=pltpu.PrefetchScalarGridSpec(
            num_scalar_prefetch=1,
            grid=(SLAB // RB,),
            in_specs=[own_row(D)] + [fixed(*a.shape) for a in (g1, w1o, w1x, w2o, w2x, ga, wqo, wqx)],
            out_specs=[row(o[0]) if o else planes(2, hid) for o in outs],
        ),
        out_shape=[shape((SLAB, o[0]), o[1]) if o else shape((2, SLAB, hid), bf16) for o in outs],
        compiler_params=params(),
        name="ffn1_forward",
    )(meta, frames, g1, w1o, w1x, w2o, w2x, ga, wqo, wqx)


TI = 384


def halves_of(parity, rows, cols=128):
    lane = lax.broadcasted_iota(jnp.int32, (rows, cols), 1)
    return (lane >> 6) == parity


def pick(mask, a, b):
    return jnp.where(mask, a.astype(f32), b.astype(f32)).astype(bf16)


def attend_kernel(m, q_ref, k_ref, v_ref, relo_ref, relx_ref,
                  o16_ref, o32_ref, li_ref, p_ref, qa_ref, ka_ref, va_ref, e_ref, rel_ref):
    head = pl.program_id(0)
    parity = head % 2
    mine = halves_of(parity, SLAB)
    slot = lax.broadcasted_iota(jnp.int32, (SLAB, 128), 1) & 63
    frame = lax.broadcasted_iota(jnp.int32, (SLAB, 128), 0)
    label = jnp.where(frame < m[1], 0, jnp.where(frame < m[2], 1, 2))
    mq = jnp.where((slot < 3) & (slot != label), MASKED, 0.0)
    mk = jnp.where(slot == label, 1.0, 0.0)
    qa_ref[...] = jnp.where(mine, q_ref[...].astype(f32), mq).astype(bf16)
    ka_ref[...] = jnp.where(mine, k_ref[...].astype(f32), mk).astype(bf16)
    va_ref[...] = jnp.where(mine, v_ref[...].astype(f32), 1.0).astype(bf16)
    rel_ref[: 2 * RW + 1, :] = jnp.where(
        head < DH // 16, relo_ref[...].astype(f32), relx_ref[...].astype(f32)
    )
    rel_ref[2 * RW + 1 :, :] = jnp.broadcast_to(rel_ref[2 * RW : 2 * RW + 1, :], (255 - 2 * RW, 128))
    relz = jnp.where(halves_of(parity, 256), rel_ref[...], 0.0).astype(bf16)
    e_ref[...] = dot_nt(qa_ref[...], relz)
    lane = lax.broadcasted_iota(jnp.int32, (SUB, 128), 1)
    line = lax.broadcasted_iota(jnp.int32, (SUB, 128), 0)
    left_of = {0: lane < line, 64: lane < line + 64}
    tiles = SLAB // 128
    mine_ti = halves_of(parity, TI)
    for start in range(0, SLAB, TI):
        sc = dot_nt(qa_ref[start : start + TI, :], ka_ref[...])
        for r in range(0, TI, SUB):
            b = (start + r) // SUB
            off = 64 if b % 2 == 0 else 0
            first = b // 2 - 1 if b % 2 == 0 else b // 2
            eb = e_ref[b * SUB : (b + 1) * SUB, :]
            left, right = eb[:, 0:1], eb[:, 128:129]
            near = pltpu.roll(eb, off, 1, stride=1, stride_axis=0)
            near0 = jnp.where(left_of[off], left, near[:, :128])
            near1 = near[:, 128:]
            s = [sc[r : r + SUB, t * 128 : (t + 1) * 128] for t in range(tiles)]
            peak = None
            if first >= 0:
                s[first] = s[first] + near0
                peak = s[first]
            if first + 1 < tiles:
                s[first + 1] = s[first + 1] + near1
                peak = s[first + 1] if peak is None else jnp.maximum(peak, s[first + 1])
            lefts = list(range(0, max(first, 0)))
            rights = list(range(first + 2, tiles))
            for group, const in ((lefts, left), (rights, right)):
                if group:
                    far = s[group[0]]
                    for t in group[1:]:
                        far = jnp.maximum(far, s[t])
                    peak = jnp.maximum(peak, far + const)
            peak = jnp.max(peak, -1, keepdims=True)
            peak_left, peak_right = peak - left, peak - right
            for t in range(tiles):
                top = peak_left if t in lefts else peak_right if t in rights else peak
                p_ref[0, start + r : start + r + SUB, t * 128 : (t + 1) * 128] = jnp.exp(
                    s[t] - top
                ).astype(bf16)
        pv = dot(p_ref[0, start : start + TI, :], va_ref[...])
        li = 1.0 / pltpu.roll(pv, 64, 1)
        o = pv * li
        rows = slice(start, start + TI)
        o = jnp.where(mine_ti, o, o32_ref[rows, :])
        o32_ref[rows, :] = o
        o16_ref[rows, :] = o.astype(bf16)
        li_ref[rows, :] = jnp.where(mine_ti, li, li_ref[rows, :])


def pair(rows=SLAB):
    return pl.BlockSpec((rows, 128), lambda h, *m: (0, h // 2))


HEAD_MAP = pl.BlockSpec((1, SLAB, SLAB), lambda h, *m: (h, 0, 0))
TABLE_OWN = pl.BlockSpec((2 * RW + 1, 128), lambda h, *m: (0, jnp.minimum(h // 2, 1)))
TABLE_OTH = pl.BlockSpec((2 * RW + 1, 128), lambda h, *m: (0, jnp.maximum(h // 2, 2) - 2))


def attend_call(meta, q, k, v, relo, relx):
    heads = D // DH
    scratch = [
        pltpu.VMEM((SLAB, 128), bf16),
        pltpu.VMEM((SLAB, 128), bf16),
        pltpu.VMEM((SLAB, 128), bf16),
        pltpu.VMEM((SLAB, 256), f32),
        pltpu.VMEM((256, 128), f32),
    ]
    return pl.pallas_call(
        attend_kernel,
        grid_spec=pltpu.PrefetchScalarGridSpec(
            num_scalar_prefetch=1,
            grid=(heads,),
            in_specs=[pair(), pair(), pair(), TABLE_OWN, TABLE_OTH],
            out_specs=[pair(), pair(), pair(), HEAD_MAP],
            scratch_shapes=scratch,
        ),
        out_shape=[
            shape((SLAB, D), bf16),
            shape((SLAB, D), f32),
            shape((SLAB, D), f32),
            shape((heads, SLAB, SLAB), bf16),
        ],
        compiler_params=params(),
        name="attention_forward",
    )(meta, q, k, v, relo, relx)


def attend_back_kernel(q_ref, k_ref, v_ref, g_ref, o_ref, li_ref, p_ref, relo_ref, relx_ref, mid0, mid1, mid2, cg_ref,
                       gq_ref, gk_ref, gv_ref, gt_ref, f2_ref, c_ref,
                       ga_ref, va_ref, kz_ref, qt_ref, gt_scr, gs_ref, w_ref, n_ref, kt_ref, vt_ref,
                       flip_ref, rel_ref, relf_ref, cback, csems, cacc, *scr):
    head = pl.program_id(0)
    place = Place()
    scr = threes(scr)
    nv = len(PAIR_VIEWS)
    last = [v.second(place, mid, refs) for v, mid, refs in zip(PAIR_VIEWS, (mid0, mid1, mid2), scr[:nv])]
    cfirst = [v.first(place, cacc, refs) for v, refs in zip(CONV_VIEWS, scr[nv:])]
    nc = len(CONV_VIEWS)
    cmids = scr[nv + 2 * nc][:nc]
    csecond = [v.second(place, mid, refs) for v, mid, refs in zip(CONV_VIEWS, cmids, scr[nv + nc :])]
    cswap = core_copy(place, cg_ref.at[:, :, 1 - place.core], cback, csems)

    @pl.when(head == 0)
    def _():
        place.greet(("low", "high"))
        line = lax.broadcasted_iota(jnp.int32, (256, 256), 0)
        flip_ref[...] = jnp.where(line + lax.broadcasted_iota(jnp.int32, (256, 256), 1) == 255, 1.0, 0.0).astype(bf16)

    @pl.when(head == 1)
    def _():
        place.greeted(("low", "high"))
        for hop in last:
            hop.start()
        cswap.start()

    @pl.when(head == 2)
    def _():
        cswap.wait()
        cacc[...] = (cg_ref[:, :, place.core].astype(f32) + cback[...].astype(f32)).astype(bf16)
        for hop in cfirst:
            hop.start()

    @pl.when(head == 5)
    def _():
        for hop, mid in zip(cfirst, cmids):
            hop.wait()
            mid[...] = hop.total().astype(bf16)
        for hop in csecond:
            hop.start()
        for hop, v in zip(last, PAIR_VIEWS):
            hop.wait()
            at = v.index * 1024
            f2_ref[:, at + v.start : at + v.stop] = hop.total()

    @pl.when(head == 7)
    def _():
        for hop, v in zip(csecond, CONV_VIEWS):
            hop.wait()
            c_ref[:, v.start : v.stop] = hop.total()

    parity = pl.program_id(0) % 2
    base = (1 - parity) * 64
    mine = halves_of(parity, SLAB)
    lane = lax.broadcasted_iota(jnp.int32, (SLAB, 128), 1)
    go = g_ref[...].astype(f32) * li_ref[...]

    @pl.when(parity == 0)
    def _():
        gt_scr[...] = go.T.astype(bf16)
        qt_ref[...] = q_ref[...].astype(f32).T.astype(bf16)

    go16 = go.astype(bf16).astype(f32)
    inner = jnp.sum(jnp.where(mine, go16 * o_ref[...], 0.0), -1, keepdims=True)
    hi = inner.astype(bf16).astype(f32)
    lo = inner - hi
    extra = jnp.where(lane == base, -hi, jnp.where(lane == base + 1, -lo, 0.0))
    ga_ref[...] = jnp.where(mine, go16, extra).astype(bf16)
    ones = jnp.where((lane == base) | (lane == base + 1), 1.0, 0.0)
    va_ref[...] = jnp.where(mine, v_ref[...].astype(f32), ones).astype(bf16)
    kz_ref[...] = jnp.where(mine, k_ref[...].astype(f32), 0.0).astype(bf16)

    subl = lax.broadcasted_iota(jnp.int32, (SUB, 128), 1)
    line = lax.broadcasted_iota(jnp.int32, (SUB, 128), 0)
    tiles = SLAB // 128
    zero16 = jnp.zeros((SUB, 128), bf16)
    n_ref[:, 128:] = jnp.zeros((SLAB, 128), bf16)
    for start in range(0, SLAB, TI):
        gp = dot_nt(ga_ref[start : start + TI, :], va_ref[...])
        for r in range(0, TI, SUB):
            b = (start + r) // SUB
            off = 64 if b % 2 == 0 else 0
            first = b // 2 - 1 if b % 2 == 0 else b // 2
            rows = slice(start + r, start + r + SUB)
            sums = {0: jnp.zeros((SUB, 128), f32), 1: jnp.zeros((SUB, 128), f32)}
            for t in range(tiles):
                cols = slice(t * 128, (t + 1) * 128)
                gs = p_ref[0, rows, cols].astype(f32) * gp[r : r + SUB, cols]
                gs16 = gs.astype(bf16)
                gs_ref[rows, cols] = gs16
                if t < first:
                    sums[0] = sums[0] + gs
                elif t > first + 1:
                    sums[1] = sums[1] + gs
                elif t == first:
                    w_ref[rows, :128] = gs16
                    sums[0] = sums[0] + jnp.where(subl < line + off, gs, 0.0)
                else:
                    w_ref[rows, 128:] = gs16
                    sums[1] = sums[1] + jnp.where(subl >= line + off, gs, 0.0)
            if first < 0:
                w_ref[rows, :128] = zero16
            if first + 1 >= tiles:
                w_ref[rows, 128:] = zero16
            far_left = jnp.sum(sums[0], -1, keepdims=True)
            far_right = jnp.sum(sums[1], -1, keepdims=True)
            left_hi = far_left.astype(bf16).astype(f32)
            right_hi = far_right.astype(bf16).astype(f32)
            far = jnp.where(subl == 0, left_hi, 0.0)
            far = jnp.where(subl == 1, far_left - left_hi, far)
            far = jnp.where(subl == 2, right_hi, far)
            far = jnp.where(subl == 3, far_right - right_hi, far)
            n_ref[rows, 128:] = far.astype(bf16)
    flipped = dot(w_ref[...], flip_ref[...])
    for b in range(SLAB // SUB):
        off = 64 if b % 2 == 0 else 0
        rows = slice(b * SUB, (b + 1) * SUB)
        near = pltpu.roll(flipped[rows, :], (off + 128) % 256, 1, stride=1, stride_axis=0)
        n_ref[rows, :128] = near[:, :128].astype(bf16)
    rel_ref[: 2 * RW + 1, :] = jnp.where(
        head < DH // 16, relo_ref[...].astype(f32), relx_ref[...].astype(f32)
    )
    relf_ref[:128, :] = dot(flip_ref[128:, :128], rel_ref[:128, :].astype(bf16))
    line = lax.broadcasted_iota(jnp.int32, (128, 128), 0)
    relf_ref[128:, :] = jnp.where(
        line < 2, rel_ref[0:1, :], jnp.where(line < 4, rel_ref[2 * RW : 2 * RW + 1, :], 0.0)
    )
    relz = jnp.where(halves_of(parity, 256), relf_ref[...], 0.0).astype(bf16)
    half = pl.ds(pl.multiple_of(parity * 64, 64), 64)
    gq = dot(gs_ref[...], kz_ref[...]) + dot(n_ref[...], relz)
    gq_ref[...] = (
        jnp.where(mine, gq * DH**-0.5, gq_ref[...].astype(f32))
    ).astype(bf16)
    kt_ref[half, :] = dot(qt_ref[half, :], gs_ref[...])
    vt_ref[half, :] = dot(gt_scr[half, :], p_ref[0])
    gt_ref[half, :] = dot(qt_ref[half, :], n_ref[...])

    @pl.when(parity == 1)
    def _():
        gk_ref[...] = kt_ref[...].T.astype(bf16)
        gv_ref[...] = vt_ref[...].T.astype(bf16)


def attend_back_call(q, k, v, go, o32, li, p, relo, relx, mids, cg):
    heads = D // DH
    n, rows, crows = lax.axis_size("dp"), mids[0].shape[1], cg.shape[3]
    high, low = split_axis(n)
    cdims = (high, low, crows, CONV_C)
    return pl.pallas_call(
        attend_back_kernel,
        grid=(heads,),
        in_specs=[pair()] * 6 + [HEAD_MAP, TABLE_OWN, TABLE_OTH] + [fixed(*a.shape) for a in (*mids, cg)],
        out_specs=[pair(), pair(), pair(), pl.BlockSpec((128, 256), lambda h: (h // 2, 0)),
                   fixed(rows, 2048), fixed(crows, CONV_C)],
        out_shape=[shape((SLAB, D), bf16)] * 3
        + [shape((D, 256), f32), shape((rows, 2048), f32), shape((crows, CONV_C), f32)],
        scratch_shapes=[
            pltpu.VMEM((SLAB, 128), bf16),
            pltpu.VMEM((SLAB, 128), bf16),
            pltpu.VMEM((SLAB, 128), bf16),
            pltpu.VMEM((128, SLAB), bf16),
            pltpu.VMEM((128, SLAB), bf16),
            pltpu.VMEM((SLAB, SLAB), bf16),
            pltpu.VMEM((SLAB, 256), bf16),
            pltpu.VMEM((SLAB, 256), bf16),
            pltpu.VMEM((128, SLAB), f32),
            pltpu.VMEM((128, SLAB), f32),
            pltpu.VMEM((256, 256), bf16),
            pltpu.VMEM((136, 128), f32),
            pltpu.VMEM((256, 128), f32),
            pltpu.VMEM(cdims, bf16),
            pltpu.SemaphoreType.DMA((2,)),
            pltpu.VMEM(cdims, bf16),
        ]
        + seconds(PAIR_VIEWS, n, rows)
        + firsts(CONV_VIEWS, n, crows)
        + seconds(CONV_VIEWS, n, crows)
        + [pltpu.VMEM(v.mid(n, crows), bf16) for v in CONV_VIEWS],
        compiler_params=remote(4),
        name="attention_backward",
    )(q, k, v, go, o32, li, p, relo, relx, *mids, cg)


def spread_out(flat_ref, padded_ref, c, b1, b2):
    zeros = jnp.zeros((TOP, 128), f32)
    padded_ref[c, :TOP, :] = zeros
    padded_ref[c, TOP + PADDED :, :] = zeros
    for t0 in range(0, PADDED, CH):
        t = lax.broadcasted_iota(jnp.int32, (CH, 128), 0) + t0
        at = TOP + t0
        value = jnp.where(t < b1, flat_ref[c, at : at + CH, :], 0.0)
        middle = (t >= b1 + GAP) & (t < b2 + GAP)
        value = jnp.where(middle, flat_ref[c, at - GAP : at - GAP + CH, :], value)
        value = jnp.where(t >= b2 + 2 * GAP, flat_ref[c, at - 2 * GAP : at - 2 * GAP + CH, :], value)
        padded_ref[c, at : at + CH, :] = value


def lane_row(ref, r):
    return jnp.concatenate([ref[c, r : r + 1, :] for c in range(LT)], 1)


def draw_in(padded_ref, c, t0, rows, b1, b2):
    t = lax.broadcasted_iota(jnp.int32, (rows, 128), 0) + t0
    value = jnp.where(t < b1, padded_ref[c, t0 : t0 + rows, :], padded_ref[c, t0 + GAP : t0 + GAP + rows, :])
    return jnp.where(t < b2, value, padded_ref[c, t0 + 2 * GAP : t0 + 2 * GAP + rows, :])


GAIN_ROW, BN_GAIN_ROW, BN_BIAS_ROW = TAPS, TAPS + 1, TAPS + 2


def conv_kernel_fn(m, x1_ref, o_ref, woo, wox, pin, rest_ref,
                   x2_ref, cn_ref, u_ref, hd_ref, gp_ref, st_ref, taps_ref, flat_ref, out_ref):
    i = pl.program_id(0)

    @pl.when(i == 0)
    def _():
        across = rest_ref[...].astype(f32).T
        for c in range(LT):
            taps_ref[c] = across[:40, c * 128 : (c + 1) * 128]

    gain = lane_row(taps_ref, GAIN_ROW)
    w = woo.shape[0]
    x2 = x1_ref[...] + dot(o_ref[:, :w], woo[...]) + dot(o_ref[:, w:], wox[...])
    x2_ref[...] = x2
    xhat, _ = norm_parts(x2)
    cn = (xhat * gain).astype(bf16)
    cn_ref[...] = cn
    u = dot(cn, pin[...])
    u_ref[...] = u.astype(bf16)
    gl = u[:, :D] * jax.nn.sigmoid(u[:, D:])
    for c in range(LT):
        flat_ref[c, pl.ds(pl.multiple_of(TOP + i * RB, 8), RB), :] = gl[:, c * 128 : (c + 1) * 128]

    @pl.when(i == pl.num_programs(0) - 1)
    def _():
        b1, b2 = m[1], m[2]

        def tile(c, carry):
            flat_ref[c, TOP + SLAB :, :] = jnp.zeros((flat_ref.shape[1] - TOP - SLAB, 128), f32)
            spread_out(flat_ref, gp_ref, c, b1, b2)
            for t0 in range(0, PADDED, CH):
                acc = jnp.zeros((CH, 128), f32)
                for b in range(8):
                    at = TOP + t0 - TAPS // 2 + b
                    x = gp_ref[c, at : at + CH + 24, :]
                    for a in range(4):
                        acc = acc + x[8 * a : 8 * a + CH, :] * taps_ref[c, 8 * a + b : 8 * a + b + 1, :]
                out_ref[c, t0 : t0 + CH, :] = acc
            first = jnp.zeros((8, 128), f32)
            second = jnp.zeros((8, 128), f32)
            for t0 in range(0, SLAB, 128):
                hd = draw_in(out_ref, c, t0, 128, b1, b2)
                hd_ref[c, t0 : t0 + 128, :] = hd
                t = lax.broadcasted_iota(jnp.int32, (128, 128), 0) + t0
                hv = jnp.where(t < b2, hd, 0.0)
                first = first + rows_sum(hv)
                second = second + rows_sum(hv * hv)
            st_ref[pl.ds(c, 1), :] = jnp.sum(first, 0, keepdims=True)
            st_ref[pl.ds(LT + c, 1), :] = jnp.sum(second, 0, keepdims=True)
            return carry

        st_ref[2 * LT :, :] = jnp.full((8, 128), b2.astype(f32))

        lax.fori_loop(0, LT, tile, 0)


POINT_IN = pl.BlockSpec((D, 2 * D), lambda i, *m: (0, 0))
POINT_OUT = pl.BlockSpec((D, D), lambda i, *m: (0, 2))
REST = pl.BlockSpec((D, 128), lambda i, *m: (0, 3 * D // 128))


def conv_call(meta, x1, o16, woo, wox, gathered):
    return pl.pallas_call(
        conv_kernel_fn,
        grid_spec=pltpu.PrefetchScalarGridSpec(
            num_scalar_prefetch=1,
            grid=(SLAB // RB,),
            in_specs=[row(D), row(D), fixed(*woo.shape), fixed(*wox.shape), POINT_IN, REST],
            out_specs=[row(D), row(D), row(2 * D), fixed(LT, SLAB, 128),
                       fixed(LT, PADDED + 2 * TOP, 128), fixed(2 * LT + 8, 128), fixed(LT, 40, 128)],
            scratch_shapes=[
                pltpu.VMEM((LT, SLAB + 3 * TOP, 128), f32),
                pltpu.VMEM((LT, PADDED, 128), f32),
            ],
        ),
        out_shape=[
            shape((SLAB, D), f32),
            shape((SLAB, D), bf16),
            shape((SLAB, 2 * D), bf16),
            shape((LT, SLAB, 128), f32),
            shape((LT, PADDED + 2 * TOP, 128), f32),
            shape((2 * LT + 8, 128), f32),
            shape((LT, 40, 128), f32),
        ],
        compiler_params=params(),
        name="conv_forward",
    )(meta, x1, o16, woo, wox, gathered, gathered)


def lanes(ref, r):
    return jnp.concatenate([ref[r + c : r + c + 1, :] for c in range(LT)], 1)


def middle_kernel(m, hd_ref, x2_ref, ct_ref, st, taps_ref, pout, g2, w1o, w1x, w2o, w2x, gf,
                  out_ref, gx3_ref, gz_ref, wc_ref, gc_ref, left_ref, right_ref, sums_ref, slo, slx):
    i = pl.program_id(0)
    bng, bnb = lane_row(taps_ref, BN_GAIN_ROW), lane_row(taps_ref, BN_BIAS_ROW)
    ghx, actx, gho, acto = (right_ref.at[k] for k in range(4))
    t = lax.broadcasted_iota(jnp.int32, (RB, 1), 0) + i * RB
    valid = (t < m[2]).astype(f32)
    count = st[2 * LT : 2 * LT + 1, 0:1]
    centre = lanes(st, 0) / count
    inv_b = lax.rsqrt(lanes(st, LT) / count - centre * centre + BATCH_EPS)
    hd = jnp.concatenate([hd_ref[c] for c in range(LT)], 1)
    zh = (hd - centre) * inv_b
    z = zh * bng + bnb
    sgz = jax.nn.sigmoid(z)
    wcf = z * sgz
    slope_z = sgz + wcf * (1.0 - sgz)
    wc = wcf.astype(bf16)
    wc_ref[...] = wc
    x3 = x2_ref[...] + dot(wc, pout[...])
    xhat3, inv3 = norm_parts(x3)
    n2 = (xhat3 * g2[...]).astype(bf16)
    left_ref[0] = n2
    halves = ((w1o, w2o), (w1x, w2x))
    x4 = x3 + 0.5 * ffn_up(n2, halves, (acto, actx), (slo, slx))
    xhat4, inv4 = norm_parts(x4)
    out_ref[...] = (valid * xhat4 * gf[...]).astype(bf16)
    g = ct_ref[...].astype(f32) * valid
    gx4 = norm_back(g, gf[...], xhat4, inv4)
    gb = (0.5 * gx4).astype(bf16)
    left_ref[1] = gb
    gn = ffn_down(gb, halves, (slo, slx), (gho, ghx))
    gx3 = gx4 + norm_back(gn, g2[...], xhat3, inv3)
    gx3_ref[...] = gx3
    gc = gx3.astype(bf16)
    gc_ref[...] = gc
    gz = dot_nt(gc, pout[...]) * slope_z
    for c in range(LT):
        gz_ref[c] = gz[:, c * 128 : (c + 1) * 128]
    e = gz * bng * valid
    parts = (gz, gz * zh, e, e * zh, g * xhat4, gn * xhat3)
    sums = jnp.concatenate([jnp.sum(p, 0, keepdims=True) for p in parts] + [jnp.zeros((2, D), f32)], 0)
    accumulate(sums_ref, i, sums)


def middle_call(meta, hd, x2, cot, st, taps, gathered, g2, w1o, w1x, w2o, w2x, gf):
    hid = w1o.shape[1]
    consts = (g2, w1o, w1x, w2o, w2x, gf)
    tiled = planes(LT, 128)
    return pl.pallas_call(
        middle_kernel,
        grid_spec=pltpu.PrefetchScalarGridSpec(
            num_scalar_prefetch=1,
            grid=(SLAB // RB,),
            in_specs=[tiled, row(D), own_row(D), fixed(*st.shape), fixed(*taps.shape), POINT_OUT]
            + [fixed(*a.shape) for a in consts],
            out_specs=[row(D), row(D), tiled, row(D), row(D), planes(2, D), planes(4, hid), fixed(8, D)],
            scratch_shapes=[pltpu.VMEM((RB, hid), bf16), pltpu.VMEM((RB, hid), bf16)],
        ),
        out_shape=[
            shape((SLAB, D), bf16),
            shape((SLAB, D), f32),
            shape((LT, SLAB, 128), f32),
            shape((SLAB, D), bf16),
            shape((SLAB, D), bf16),
            shape((2, SLAB, D), bf16),
            shape((4, SLAB, hid), bf16),
            shape((8, D), f32),
        ],
        compiler_params=params(),
        name="ffn2_forward_backward",
    )(meta, hd, x2, cot, st, taps, gathered, *consts)


def conv_back_kernel(m, acc_in, gz_ref, hd_ref, gp_ref, st, back, taps_ref,
                     u_ref, x2_ref, gx3_ref, pin, woo, wox,
                     gu_ref, gx2_ref, ga_ref, go_ref, gtap_ref, gain_ref, mid0, mid1, mid2,
                     flat_ref, pad_ref, out_ref, acc_ref, *scr):
    i = pl.program_id(0)
    b1, b2 = m[1], m[2]
    gain = lane_row(taps_ref, GAIN_ROW)
    place = Place()
    hops = [v.first(place, acc_in, refs) for v, refs in zip(PAIR_VIEWS, threes(scr))]

    @pl.when(i == 0)
    def _():
        place.greet(("low", "high"), False)
        place.greeted(("low", "high"), False)
        for hop in hops:
            hop.start()

    @pl.when(i == 0)
    def _():
        def tile(c, carry):
            count = st[2 * LT : 2 * LT + 1, :]
            centre = st[pl.ds(c, 1), :] / count
            inv_b = lax.rsqrt(st[pl.ds(LT + c, 1), :] / count - centre * centre + BATCH_EPS)
            a1 = back[pl.ds(c, 1), :] / count
            a2 = back[pl.ds(LT + c, 1), :] / count
            for t0 in range(0, SLAB, 128):
                t = lax.broadcasted_iota(jnp.int32, (128, 128), 0) + t0
                zh = (hd_ref[c, t0 : t0 + 128, :] - centre) * inv_b
                away = jnp.where(t < b2, a1 + zh * a2, 0.0)
                flat_ref[c, TOP + t0 : TOP + t0 + 128, :] = inv_b * (
                    gz_ref[c, t0 : t0 + 128, :] * taps_ref[c, BN_GAIN_ROW : BN_GAIN_ROW + 1, :] - away
                )
            flat_ref[c, TOP + SLAB :, :] = jnp.zeros((flat_ref.shape[1] - TOP - SLAB, 128), f32)
            spread_out(flat_ref, pad_ref, c, b1, b2)
            acc_ref[...] = jnp.zeros(acc_ref.shape, f32)
            for t0 in range(0, PADDED, CH):
                acc = jnp.zeros((CH, 128), f32)
                gl = gp_ref[c, TOP + t0 : TOP + t0 + CH, :]
                for b in range(8):
                    at = TOP + t0 + TAPS // 2 - TAPS + 1 + b
                    x = pad_ref[c, at : at + CH + 24, :]
                    for a in range(4):
                        k = TAPS - 1 - (8 * a + b)
                        part = x[8 * a : 8 * a + CH, :]
                        acc = acc + part * taps_ref[c, k : k + 1, :]
                        acc_ref[8 * k : 8 * k + 8, :] += rows_sum(part * gl)
                out_ref[c, t0 : t0 + CH, :] = acc
            gtap_ref[c] = jnp.sum(acc_ref[...].reshape(TAPS, 8, 128), 1)
            for t0 in range(0, SLAB, 128):
                flat_ref[c, t0 : t0 + 128, :] = draw_in(out_ref, c, t0, 128, b1, b2)
            return carry

        lax.fori_loop(0, LT, tile, 0)

    at = pl.ds(pl.multiple_of(i * RB, 8), RB)
    ggl = jnp.concatenate([flat_ref[c, at, :] for c in range(LT)], 1)
    u1 = u_ref[:, :D].astype(f32)
    sg = jax.nn.sigmoid(u_ref[:, D:].astype(f32))
    gs = ggl * sg
    gu = jnp.concatenate([gs, gs * u1 * (1.0 - sg)], 1).astype(bf16)
    gu_ref[...] = gu
    gn = dot_nt(gu, pin[...])
    xhat, inv = norm_parts(x2_ref[...])
    gx2 = gx3_ref[...] + norm_back(gn, gain, xhat, inv)
    gx2_ref[...] = gx2
    ga = gx2.astype(bf16)
    ga_ref[...] = ga
    w = woo.shape[0]
    go_ref[:, :w] = dot_nt(ga, woo[...]).astype(bf16)
    go_ref[:, w:] = dot_nt(ga, wox[...]).astype(bf16)
    accumulate(gain_ref, i, rows_sum(gn * xhat))

    @pl.when(i == pl.num_programs(0) - 1)
    def _():
        for hop, mid in zip(hops, (mid0, mid1, mid2)):
            hop.wait()
            mid[...] = hop.total().astype(bf16)


def conv_back_call(meta, acc, gz, hd, gp, st, back, taps, u, x2, gx3, gathered, woo, wox):
    n, rows = lax.axis_size("dp"), acc.shape[3]
    first = (acc, gz, hd, gp, st, back, taps)
    return pl.pallas_call(
        conv_back_kernel,
        grid=(SLAB // RB,),
        in_specs=[SMEM] + [fixed(*a.shape) for a in first] + [row(2 * D), row(D), row(D)]
        + [POINT_IN, fixed(*woo.shape), fixed(*wox.shape)],
        out_specs=[row(2 * D), row(D), row(D), row(D), fixed(LT, TAPS, 128), fixed(8, D)]
        + [fixed(*v.mid(n, rows)) for v in PAIR_VIEWS],
        scratch_shapes=[
            pltpu.VMEM((LT, SLAB + 3 * TOP, 128), f32),
            pltpu.VMEM((LT, PADDED + 2 * TOP, 128), f32),
            pltpu.VMEM((LT, PADDED, 128), f32),
            pltpu.VMEM((TAPS * 8, 128), f32),
        ]
        + firsts(PAIR_VIEWS, n, rows),
        out_shape=[
            shape((SLAB, 2 * D), bf16),
            shape((SLAB, D), f32),
            shape((SLAB, D), bf16),
            shape((SLAB, D), bf16),
            shape((LT, TAPS, 128), f32),
            shape((8, D), f32),
        ]
        + [shape(v.mid(n, rows), bf16) for v in PAIR_VIEWS],
        compiler_params=remote(3),
        name="conv_backward",
    )(meta, *first, u, x2, gx3, gathered, woo, wox)


def last_kernel(x_ref, x1_ref, gx2_ref, gq_ref, gk_ref, gv_ref, slo, slx,
                g1, w1o, w1x, w2o, w2x, ga, wqo, wqx, acc, table_ref,
                gx_ref, left_ref, right_ref, gain_ref, a_ref, to_ref,
                tback, tsems, tsum, tmine, tslots, tsend, trecv, aslots, asend, arecv, *scr):
    i = pl.program_id(0)
    place = Place()
    scr = threes(scr)
    nv = len(FLAT_VIEWS)
    first = [v.first(place, acc, refs) for v, refs in zip(FLAT_VIEWS, scr)]
    mids = scr[2 * nv][:nv]
    second = [v.second(place, mid, refs) for v, mid, refs in zip(FLAT_VIEWS, mids, scr[nv:])]
    tswap = core_copy(place, table_ref.at[1], tback, tsems)
    scatter = Hop(place, "all", lambda p: tsum.at[p], tslots, tsend, trecv)
    spread = Hop(place, "all", lambda p: tmine, aslots, asend, arecv)

    @pl.when(i == 0)
    def _():
        place.greet(("all",))

    @pl.when(i == 1)
    def _():
        place.greeted(("all",))
        tswap.start()
        for hop in first:
            hop.start()

    @pl.when(i == 2)
    def _():
        tswap.wait()
        tsum[...] = table_ref[0] + tback[...]
        scatter.start()

    ghx, gho = right_ref.at[0], right_ref.at[1]
    w = wqo.shape[1] // 3
    gn = None
    for n, ref in enumerate((gq_ref, gk_ref, gv_ref)):
        cols = slice(n * w, (n + 1) * w)
        part = dot_nt(ref[:, :w], wqo[:, cols]) + dot_nt(ref[:, w:], wqx[:, cols])
        gn = part if gn is None else gn + part
    xhat, inv = norm_parts(x1_ref[...])
    gx1 = gx2_ref[...] + norm_back(gn, ga[...], xhat, inv)
    attn_gain = jnp.sum(gn * xhat, 0, keepdims=True)
    gb = (0.5 * gx1).astype(bf16)
    left_ref[...] = gb
    gn = ffn_down(gb, ((w1o, w2o), (w1x, w2x)), (slo, slx), (gho, ghx))
    xhat, inv = norm_parts(x_ref[...].astype(f32))
    gx_ref[...] = (gx1 + norm_back(gn, g1[...], xhat, inv)).astype(gx_ref.dtype)
    ffn_gain = jnp.sum(gn * xhat, 0, keepdims=True)
    accumulate(gain_ref, i, jnp.concatenate([attn_gain, ffn_gain, jnp.zeros((6, D), f32)], 0))

    @pl.when(i == 2)
    def _():
        scatter.wait()
        tmine[...] = scatter.total()
        aslots[place.me] = tmine[...]
        spread.start()
        for hop, mid in zip(first, mids):
            hop.wait()
            mid[...] = hop.total().astype(bf16)
        for hop in second:
            hop.start()

    @pl.when(i == 3)
    def _():
        for hop, v in zip(second, FLAT_VIEWS):
            hop.wait()
            a_ref[:, v.start : v.stop] = hop.total()
        spread.wait()
        to_ref[...] = aslots[...]


def last_call(x, x1, gx2, gq, gk, gv, slo, slx, g1, w1o, w1x, w2o, w2x, ga, wqo, wqx, acc, table):
    hid = w1o.shape[1]
    n, rows = lax.axis_size("dp"), acc.shape[2]
    tdims = table.shape[2:]
    consts = (g1, w1o, w1x, w2o, w2x, ga, wqo, wqx, acc, table)
    return pl.pallas_call(
        last_kernel,
        grid=(SLAB // RB,),
        in_specs=[row(D)] * 6 + [row(hid)] * 2 + [fixed(*a.shape) for a in consts],
        out_specs=[row(D), row(D), planes(2, hid), fixed(8, D), fixed(rows, 1024), fixed(n, *tdims)],
        out_shape=[
            shape((SLAB, D), bf16),
            shape((SLAB, D), bf16),
            shape((2, SLAB, hid), bf16),
            shape((8, D), f32),
            shape((rows, 1024), f32),
            shape((n, *tdims), f32),
        ],
        scratch_shapes=[
            pltpu.VMEM((n, *tdims), f32),
            pltpu.SemaphoreType.DMA((2,)),
            pltpu.VMEM((n, *tdims), f32),
            pltpu.VMEM(tdims, f32),
        ]
        + slots_of(n, tdims, f32)
        + slots_of(n, tdims, f32)
        + firsts(FLAT_VIEWS, n, rows)
        + seconds(FLAT_VIEWS, n, rows)
        + [pltpu.VMEM(v.mid(n, rows), bf16) for v in FLAT_VIEWS],
        compiler_params=remote(6),
        name="ffn1_backward",
    )(x, x1, gx2, gq, gk, gv, slo, slx, *consts)


def pair_grads_kernel(ends, *refs):
    if ends:
        left, left2, right, right2, x_ref, o_ref, f_ref, acc, *scr = refs
    else:
        left, right, x_ref, o_ref, acc, *scr = refs
        left2, right2 = left, right
    away, back, sems, xback, xsems, xsum, xslots, xsend, xrecv, *scr = scr
    j = pl.program_id(0)
    place = Place()
    kinds = ("all",)
    swaps = [core_copy(place, away.at[k], back.at[k], sems.at[k]) for k in range(2)]
    xswap = core_copy(place, x_ref, xback, xsems) if ends else None
    xhop = Hop(place, "all", lambda p: xsum, xslots, xsend, xrecv)
    dims = acc.shape[1:]

    def product(lhs, rhs):
        return dot_tn(lhs[0], rhs[0]).reshape(dims)

    @pl.when(j == 0)
    def _():
        place.greet(kinds)
        away[0] = product(left, right).astype(bf16)
        place.greeted(kinds)
        swaps[0].start()
        if ends:
            xswap.start()
        else:
            xsum[...] = x_ref[...]
            xslots[place.me] = x_ref[...]
            xhop.start()

    @pl.when(j == 1)
    def _():
        away[1] = product(left2, right2).astype(bf16)
        swaps[1].start()
        if ends:
            xswap.wait()
            xsum[...] = x_ref[...] + xback[...]
            xslots[place.me] = xsum[...]
            xhop.start()

    if ends:
        scr = threes(scr)
        nv = len(PAIR_VIEWS)
        first = [v.first(place, acc, r) for v, r in zip(PAIR_VIEWS, scr)]
        mids = scr[2 * nv]
        second = [v.second(place, mid, r) for v, mid, r in zip(PAIR_VIEWS, mids, scr[nv:])]

    @pl.when(j == 2)
    def _():
        mine = product(left, right)
        swaps[0].wait()
        acc[0] = (mine + back[0].astype(f32)).astype(bf16)
        if ends:
            first[0].start()

    @pl.when(j == 3)
    def _():
        mine = product(left2, right2)
        swaps[1].wait()
        acc[1] = (mine + back[1].astype(f32)).astype(bf16)
        if ends:
            for hop in first[1:]:
                hop.start()
            for hop, mid, on in zip(first, mids, second):
                hop.wait()
                mid[...] = hop.total().astype(bf16)
                on.start()
            for hop, v in zip(second, PAIR_VIEWS):
                hop.wait()
                at = v.index * 1024
                f_ref[:, at + v.start : at + v.stop] = hop.total()
        xhop.wait()
        o_ref[...] = slot_sum(xslots, place.n)


def pair_grads_scratch(n, dims, x):
    return [
        pltpu.VMEM((2, *dims), bf16),
        pltpu.VMEM((2, *dims), bf16),
        pltpu.SemaphoreType.DMA((2, 2)),
        pltpu.VMEM(x.shape, f32),
        pltpu.SemaphoreType.DMA((2,)),
        pltpu.VMEM(x.shape, f32),
    ] + slots_of(n, x.shape, f32)


def grad_dims(cols):
    n = lax.axis_size("dp")
    return n, (*split_axis(n), D // n, cols)


def pair_grads(left, right, x, collective_id):
    n, dims = grad_dims(right.shape[2])
    return pl.pallas_call(
        lambda *refs: pair_grads_kernel(False, *refs),
        grid=(4,),
        in_specs=[
            pl.BlockSpec((1, SLAB, D), lambda j: (j % 2, 0, 0)),
            pl.BlockSpec((1, SLAB, right.shape[2]), lambda j: (j, 0, 0)),
            fixed(*x.shape),
        ],
        out_specs=[fixed(*x.shape), fixed(2, *dims)],
        out_shape=[shape(x.shape, f32), shape((2, *dims), bf16)],
        scratch_shapes=pair_grads_scratch(n, dims, x),
        compiler_params=remote(collective_id),
        name="ffn2_gradients",
    )(left, right, x)


def pair_grads_end(left, left2, right, right2, x, collective_id):
    n, dims = grad_dims(right.shape[2])
    rows = dims[2]
    one = pl.BlockSpec((1, SLAB, D), lambda j: (0, 0, 0))
    half = pl.BlockSpec((1, SLAB, right.shape[2]), lambda j: (j // 2, 0, 0))
    return pl.pallas_call(
        lambda *refs: pair_grads_kernel(True, *refs),
        grid=(4,),
        in_specs=[one, one, half, half, fixed(*x.shape)],
        out_specs=[fixed(*x.shape), fixed(rows, 2048)],
        out_shape=[shape(x.shape, f32), shape((rows, 2048), f32)],
        scratch_shapes=[pltpu.VMEM((2, *dims), bf16)]
        + pair_grads_scratch(n, dims, x)
        + firsts(PAIR_VIEWS, n, rows)
        + seconds(PAIR_VIEWS, n, rows)
        + [pltpu.VMEM(v.mid(n, rows), bf16) for v in PAIR_VIEWS],
        compiler_params=remote(collective_id),
        name="ffn1_gradients",
    )(left[None], left2[None], right, right2, x)


def attn_grads_kernel(na_ref, ga_ref, gq, gk, gv, o_ref, acc, away, back, sems):
    j = pl.program_id(0)
    place = Place()
    swap_out = core_copy(place, away, back, sems)
    w = gq.shape[1]
    dims = (*acc.shape[:3], w)

    def product(k):
        lhs = ga_ref if k == 3 else na_ref
        return dot_tn(lhs[...], (gq, gk, gv, o_ref)[k][...]).reshape(dims)

    @pl.when(j == 0)
    def _():
        place.greet(())
        for k in range(4):
            away[:, :, :, k * w : (k + 1) * w] = product(k).astype(bf16)
        place.greeted(())
        swap_out.start()

    @pl.when(j == 1)
    def _():
        mine = [product(k) for k in range(4)]
        swap_out.wait()
        for k in range(4):
            cols = slice(k * w, (k + 1) * w)
            acc[:, :, :, cols] = (mine[k] + back[:, :, :, cols].astype(f32)).astype(bf16)


def attn_grads(na, ga, gq, gk, gv, o16):
    n, dims = grad_dims(1024)
    half = pl.BlockSpec((SLAB, D // 2), lambda j: (0, 1 - j))
    return pl.pallas_call(
        attn_grads_kernel,
        grid=(2,),
        in_specs=[fixed(SLAB, D), fixed(SLAB, D), half, half, half, half],
        out_specs=fixed(*dims),
        out_shape=shape(dims, bf16),
        scratch_shapes=[pltpu.VMEM(dims, bf16), pltpu.VMEM(dims, bf16), pltpu.SemaphoreType.DMA((2,))],
        compiler_params=remote(5),
        name="attention_gradients",
    )(na, ga, gq, gk, gv, o16)


def conv_grads_kernel(cn_ref, gu_ref, wc_ref, gc_ref, gtap_ref, gain_ref, sums_ref, out_ref):
    out_ref[:, : 2 * D] = dot_tn(cn_ref[...], gu_ref[...]).astype(bf16)
    out_ref[:, 2 * D : 3 * D] = dot_tn(wc_ref[...], gc_ref[...]).astype(bf16)
    gain = jnp.sum(gain_ref[...], 0, keepdims=True)
    for c in range(LT):
        cols = slice(c * 128, (c + 1) * 128)
        rows = [gtap_ref[c], gain[:, cols], sums_ref[1:2, cols], sums_ref[0:1, cols]]
        block = jnp.concatenate(rows + [jnp.zeros((128 - TAPS - 3, 128), f32)], 0)
        out_ref[c * 128 : (c + 1) * 128, 3 * D :] = block.T.astype(bf16)


def conv_grads(cn, gu, wc, gc, gtap, gain, sums):
    return pl.pallas_call(
        conv_grads_kernel,
        out_shape=shape((D, CONV_C), bf16),
        compiler_params=pltpu.CompilerParams(vmem_limit_bytes=60 << 20),
        name="conv_gradients",
    )(cn, gu, wc, gc, gtap, gain, sums)


def both_slabs_kernel(m, out_own, out_oth, gx_own, gx_oth, out_ref, gx_ref):
    blocks = SLAB // RB
    mine = pl.program_id(0) // blocks == m[0]

    @pl.when(mine)
    def _():
        out_ref[...] = out_own[...]
        gx_ref[...] = gx_own[...].astype(f32)

    @pl.when(jnp.logical_not(mine))
    def _():
        out_ref[...] = out_oth[...]
        gx_ref[...] = gx_oth[...].astype(f32)


def both_slabs(meta, out, gx):
    blocks = SLAB // RB

    def at(core):
        return pl.BlockSpec(
            (RB, D), lambda i, m: (jnp.clip(i - core(m[0]) * blocks, 0, blocks - 1), 0)
        )

    own, oth = at(lambda c: c), at(lambda c: 1 - c)
    return pl.pallas_call(
        both_slabs_kernel,
        grid_spec=pltpu.PrefetchScalarGridSpec(
            num_scalar_prefetch=1, grid=(2 * blocks,), in_specs=[own, oth, own, oth],
            out_specs=[row(D), row(D)],
        ),
        out_shape=[shape((2 * SLAB, D), bf16), shape((2 * SLAB, D), f32)],
        compiler_params=params(),
        name="both_slabs",
    )(meta, out, swap(out), gx, swap(gx))


def swap(x):
    return lax.ppermute(x, "mp", [(0, 1), (1, 0)])


def shards(
    frames, lengths, cotangent, ffn1_gain, ffn1_in, ffn1_out, attn_gain, query_weight, key_weight,
    value_weight, out_weight, rel_table, conv_gain, pointwise_in, conv_kernel, bn_gain, bn_bias,
    pointwise_out, ffn2_gain, ffn2_in, ffn2_out, final_gain,
):
    mp = lax.axis_index("mp")
    n = lax.axis_size("dp")
    high, low = split_axis(n)
    w1o, w2o = ffn1_in, ffn1_out
    w1x, w2x = swap(w1o), swap(w2o)
    wqo = jnp.concatenate([query_weight, key_weight, value_weight], 1)
    wqx = swap(wqo)
    relx = swap(rel_table)
    woo = out_weight
    wox = swap(woo)
    v1o, v2o = ffn2_in, ffn2_out
    v1x, v2x = swap(v1o), swap(v2o)
    column = jnp.arange(128 - TAPS)[None, :]
    vectors = sum(
        jnp.where(column == k, v[:, None], 0) for k, v in enumerate((conv_gain, bn_gain, bn_bias))
    )
    together = jnp.concatenate([pointwise_in, pointwise_out, conv_kernel, vectors.astype(bf16)], 1)
    gathered = lax.all_gather(together, ("dp", "mp"), axis=0, tiled=True)

    g1, ga, g2, gf = (g[None, :] for g in (ffn1_gain, attn_gain, ffn2_gain, final_gain))
    pair_lengths = jnp.where(mp == 0, lengths[0], lengths[1])
    first_end = pair_lengths[0]
    meta = jnp.stack([mp.astype(jnp.int32), first_end, first_end + pair_lengths[1]])

    x1, xs, act1, slo, slx, n1, na, q, k, v = first_call(meta, frames, g1, w1o, w1x, w2o, w2x, ga, wqo, wqx)
    o16, o32, li, p = attend_call(meta, q, k, v, rel_table, relx)
    x2, cn, u, hd, gp, st, taps = conv_call(meta, x1, o16, woo, wox, gathered)
    st = all_reduce(st, 0)
    out, gx3, gz, wc, gc, left2, right2, sums = middle_call(
        meta, hd, x2, cotangent, st, taps, gathered, g2, v1o, v1x, v2o, v2x, gf
    )
    back, acc2 = pair_grads(left2, right2, sums[2:4].reshape(2 * LT, 128), 2)
    gu, gx2, gatt, go, gtap, gcg, *mids = conv_back_call(
        meta, acc2, gz, hd, gp, st, back, taps, u, x2, gx3, gathered, woo, wox
    )
    conv_g = conv_grads(cn, gu, wc, gc, gtap, gcg, sums)
    conv_g = conv_g.reshape(high, low, 2, D // n // 2, CONV_C)
    gq, gk, gv, gtab, ffn2_s, conv_s = attend_back_call(
        q, k, v, go, o32, li, p, rel_table, relx, mids, conv_g
    )
    acc_a = attn_grads(na, gatt, gq, gk, gv, o16)
    h = D // 2
    gx, gb1, gh1, gains, attn_s, table = last_call(
        xs, x1, gx2, gq, gk, gv, slo, slx, g1, w1o, w1x, w2o, w2x, ga, wqo, wqx, acc_a,
        gtab.reshape(2, n, h // n, 256),
    )
    own_gains = jnp.stack([gains[1], gains[0], sums[5], sums[4]]).reshape(4 * LT, 128)
    gain_sums, ffn1_s = pair_grads_end(n1, gb1, gh1, act1, own_gains, 7)
    gain_sums = gain_sums.reshape(4, D)
    block_output, frames_grad = both_slabs(meta, out, gx)
    table = table.reshape(h, 256)
    near = table[:, :128][:, ::-1]
    first_row = near[:, :1] + table[:, 128:129] + table[:, 129:130]
    last_row = table[:, 130:131] + table[:, 131:132]
    table = jnp.concatenate([first_row, near[:, 1:], last_row], 1).T
    hid = ffn1_in.shape[1]
    w = query_weight.shape[1]
    c1 = 3 * D
    return (
        block_output,
        frames_grad,
        gain_sums[0],
        ffn1_s[:, :hid],
        ffn1_s[:, hid:].T,
        gain_sums[1],
        attn_s[:, :w],
        attn_s[:, w : 2 * w],
        attn_s[:, 2 * w : 3 * w],
        attn_s[:, 3 * w :].T,
        table,
        conv_s[:, c1 + TAPS],
        conv_s[:, : 2 * D],
        conv_s[:, c1 : c1 + TAPS],
        conv_s[:, c1 + TAPS + 1],
        conv_s[:, c1 + TAPS + 2],
        conv_s[:, 2 * D : 3 * D],
        gain_sums[2],
        ffn2_s[:, :hid],
        ffn2_s[:, hid:].T,
        gain_sums[3],
    )


def solution(mesh):
    return jax.shard_map(
        shards,
        mesh=mesh,
        in_specs=(
            P("dp", None), P("dp", None), P("dp", None), P(), P(None, "mp"), P("mp", None), P(),
            P(None, "mp"), P(None, "mp"), P(None, "mp"), P("mp", None), P(None, "mp"),
            P(("dp", "mp")), P(("dp", "mp"), None), P(("dp", "mp"), None), P(("dp", "mp")),
            P(("dp", "mp")), P(("dp", "mp"), None), P(), P(None, "mp"), P("mp", None), P(),
        ),
        out_specs=(
            P("dp", None), P("dp", None), P(), P("dp", "mp"), P("mp", "dp"), P(), P("dp", "mp"),
            P("dp", "mp"), P("dp", "mp"), P("mp", "dp"), P(None, "mp"), P(("dp", "mp")),
            P(("dp", "mp"), None), P(("dp", "mp"), None), P(("dp", "mp")), P(("dp", "mp")),
            P(("dp", "mp"), None), P(), P("dp", "mp"), P("mp", "dp"), P(),
        ),
        check_vma=False,
    )
```

```python
import jax
import jax.numpy as jnp
from jax import lax
from jax.experimental import pallas as pl
from jax.experimental.pallas import tpu as pltpu
from jax.sharding import PartitionSpec as P

D = 512
DH = 64
RW = 64
SLAB = 1152
TAPS = 32
NORM_EPS = 1e-05
BATCH_EPS = 1e-05
MASKED = -1e30

RB = 288
SUB = 64
GAP = 16
TOP = 32
PADDED = 1216
CH = 64
LT = D // 128

f32 = jnp.float32
bf16 = jnp.bfloat16


def params(mib=60):
    return pltpu.CompilerParams(
        dimension_semantics=("arbitrary",), vmem_limit_bytes=mib << 20
    )


def dot(a, b):
    return jnp.dot(a, b, preferred_element_type=f32)


def dot_nt(a, b):
    return lax.dot_general(a, b, (((1,), (1,)), ((), ())), preferred_element_type=f32)


def dot_tn(a, b):
    return lax.dot_general(a, b, (((0,), (0,)), ((), ())), preferred_element_type=f32)


def norm_parts(v):
    c = v - jnp.mean(v, -1, keepdims=True)
    inv = lax.rsqrt(jnp.mean(c * c, -1, keepdims=True) + NORM_EPS)
    return c * inv, inv


def norm_back(gy, gain, xhat, inv):
    e = gy * gain
    inner = jnp.mean(e * xhat, -1, keepdims=True)
    return inv * (e - jnp.mean(e, -1, keepdims=True) - xhat * inner)


def rows_sum(v):
    return jnp.sum(v.reshape(v.shape[0] // 8, 8, v.shape[1]), 0)


def accumulate(ref, step, value):
    @pl.when(step == 0)
    def _():
        ref[...] = value

    @pl.when(step > 0)
    def _():
        ref[...] += value


def row(shape_cols, rows=RB):
    return pl.BlockSpec((rows, shape_cols), lambda i, *m: (i, 0))


def own_row(cols, rows=RB):
    blocks = SLAB // rows
    return pl.BlockSpec((rows, cols), lambda i, m: (m[0] * blocks + i, 0))


def fixed(*shape):
    zeros = (0,) * len(shape)
    return pl.BlockSpec(shape, lambda i, *m: zeros)


def planes(count, cols, rows=RB):
    return pl.BlockSpec((count, rows, cols), lambda i, *m: (0, i, 0))


SMEM = pl.BlockSpec(memory_space=pltpu.SMEM)
VMEM = pl.BlockSpec(memory_space=pltpu.VMEM)


def shape(dims, dtype):
    return jax.ShapeDtypeStruct(dims, dtype)


MESH = pl.DeviceIdType.MESH


def split_axis(n):
    low = 4 if n % 4 == 0 else 1
    return n // low, low


class Place:
    def __init__(self):
        self.n = lax.axis_size("dp")
        self.high, self.low = split_axis(self.n)
        self.me = lax.axis_index("dp")
        self.core = lax.axis_index("mp")
        self.hi = self.me // self.low
        self.lo = self.me % self.low

    def size(self, kind):
        return {"all": self.n, "low": self.low, "high": self.high}[kind]

    def mine(self, kind):
        return {"all": self.me, "low": self.lo, "high": self.hi}[kind]

    def peer(self, kind, j):
        at = (self.mine(kind) + j) % self.size(kind)
        if kind == "low":
            return at, {"dp": self.hi * self.low + at}
        if kind == "high":
            return at, {"dp": at * self.low + self.lo}
        return at, {"dp": at}

    def each(self, kind, do):
        size = self.size(kind)
        if size <= 4:
            for j in range(1, size):
                do(j)
        else:

            def body(j, carry):
                do(j)
                return carry

            lax.fori_loop(1, size, body, 0)

    def greet(self, kinds, core=True):
        barrier = pltpu.get_barrier_semaphore()
        for kind in kinds:
            self.each(
                kind,
                lambda j: pl.semaphore_signal(
                    barrier, inc=1, device_id=self.peer(kind, j)[1], device_id_type=MESH
                ),
            )
        if core:
            pl.semaphore_signal(barrier, inc=1, device_id={"mp": 1 - self.core}, device_id_type=MESH)

    def greeted(self, kinds, core=True):
        count = sum(self.size(kind) - 1 for kind in kinds) + (1 if core else 0)
        if count:
            pl.semaphore_wait(pltpu.get_barrier_semaphore(), count)


class Hop:
    def __init__(self, place, kind, piece, slots, send, recv):
        self.place, self.kind, self.piece = place, kind, piece
        self.slots, self.send, self.recv = slots, send, recv

    def copy(self, j, slot):
        at, device = self.place.peer(self.kind, j)
        return pltpu.make_async_remote_copy(
            src_ref=self.piece(at), dst_ref=self.slots.at[slot], send_sem=self.send.at[j],
            recv_sem=self.recv.at[slot], device_id=device, device_id_type=MESH,
        )

    def start(self):
        mine = self.place.mine(self.kind)
        self.place.each(self.kind, lambda j: self.copy(j, mine).start())

    def wait(self):
        self.place.each(self.kind, lambda j: self.copy(j, self.place.peer(self.kind, j)[0]).wait())

    def total(self):
        total = self.piece(self.place.mine(self.kind))[...].astype(f32)
        size = self.place.size(self.kind)
        if size <= 4:
            for j in range(1, size):
                total = total + self.slots[self.place.peer(self.kind, j)[0]].astype(f32)
            return total
        return lax.fori_loop(
            1, size, lambda j, t: t + self.slots[self.place.peer(self.kind, j)[0]].astype(f32), total
        )


def core_copy(place, src, dst, sems):
    return pltpu.make_async_remote_copy(
        src_ref=src, dst_ref=dst, send_sem=sems.at[0], recv_sem=sems.at[1],
        device_id={"mp": 1 - place.core}, device_id_type=MESH,
    )


def slots_of(size, dims, dtype=bf16):
    return [
        pltpu.VMEM((size, *dims), dtype),
        pltpu.SemaphoreType.DMA((size,)),
        pltpu.SemaphoreType.DMA((size,)),
    ]


class View:
    def __init__(self, index, start, stop, order):
        self.index, self.start, self.stop, self.order = index, start, stop, order
        self.width = stop - start

    def kinds(self):
        return ("low", "high") if self.order == "low" else ("high", "low")

    def mid(self, n, rows):
        high, low = split_axis(n)
        return (high if self.order == "low" else low, rows, self.width)

    def first_scratch(self, n, rows):
        high, low = split_axis(n)
        return slots_of(low if self.order == "low" else high, self.mid(n, rows))

    def second_scratch(self, n, rows):
        size, *dims = self.mid(n, rows)
        return slots_of(size, dims)

    def first(self, place, acc, refs):
        cols = slice(self.start, self.stop)
        if self.index is not None:
            acc = acc.at[self.index]
        if self.order == "low":
            piece = lambda p: acc.at[:, p, :, cols]
        else:
            piece = lambda p: acc.at[p, :, :, cols]
        return Hop(place, self.kinds()[0], piece, *refs)

    def whole_first(self, place, acc, refs):
        if self.order == "low":
            return Hop(place, "low", lambda p: acc.at[:, p], *refs)
        return Hop(place, "high", lambda p: acc.at[p], *refs)

    def second(self, place, mid, refs):
        return Hop(place, self.kinds()[1], lambda p: mid.at[p], *refs)


PAIR_VIEWS = (View(0, 0, 1024, "low"), View(1, 0, 384, "low"), View(1, 384, 1024, "high"))
CONV_C = 2 * D + D + 128
CONV_VIEWS = (View(None, 0, 1024, "low"), View(None, 1024, CONV_C, "high"))


def firsts(views, n, rows):
    return [ref for v in views for ref in v.first_scratch(n, rows)]


def seconds(views, n, rows):
    return [ref for v in views for ref in v.second_scratch(n, rows)]


def threes(refs):
    return [refs[i : i + 3] for i in range(0, len(refs), 3)]


def remote(collective_id, mib=60):
    return pltpu.CompilerParams(
        vmem_limit_bytes=mib << 20, collective_id=collective_id, has_side_effects=True,
    )


def slot_sum(slots, n):
    return lax.fori_loop(1, n, lambda j, total: total + slots[j], slots[0])


TR = 32
UP = 512


def row_tiles(rows):
    return [slice(r, r + TR) for r in range(0, rows, TR)]


def tiles(rows, cols, width=256):
    return [(rs, slice(c, c + width)) for rs in row_tiles(rows) for c in range(0, cols, width)]


def transpose_into(dst, src):
    for r in range(0, src.shape[0], 128):
        dst[:, r : r + 128] = src[r : r + 128, :].astype(f32).T.astype(bf16)


class Copies:
    def __init__(self, sems):
        self.sems, self.count = sems, 0

    def start(self, src, dst):
        copy = pltpu.make_async_copy(src, dst, self.sems.at[self.count])
        self.count += 1
        copy.start()
        return copy


ANY = pl.BlockSpec(memory_space=pl.ANY)


def first_kernel(m, x_ref, g1, w1o, w1x, w2o, w2x, ga, wqo, wko, wvo, wqx, wkx, wvx,
                 x1_ref, hid_out, na_ref, q_ref, k_ref, v_ref, n_ref, act_ref, hid_ref, out_ref):
    for rs in row_tiles(RB):
        xhat, _ = norm_parts(x_ref[rs, :].astype(f32))
        n_ref[rs, :] = (xhat * g1[...]).astype(bf16)
    chunks = [(w1, w2, p, c) for w1, w2, p in ((w1x, w2x, 0), (w1o, w2o, 1)) for c in range(0, w1o.shape[1], UP)]

    def up(k):
        w1, _, _, c = chunks[k]
        hid_ref[k % 2] = dot(n_ref[...], w1[:, c : c + UP])

    def down(k):
        _, w2, _, c = chunks[k]
        part = dot(act_ref[k % 2], w2[c : c + UP, :])
        if k == 0:
            out_ref[...] = part
        else:
            out_ref[...] += part

    up(0)
    for k, (_, _, p, c) in enumerate(chunks):
        if k + 1 < len(chunks):
            up(k + 1)
        if k > 0:
            down(k - 1)
        for rs, cs in tiles(RB, UP):
            hid = hid_ref[k % 2, rs, cs]
            hid_out[p, rs, c + cs.start : c + cs.stop] = hid.astype(bf16)
            act_ref[k % 2, rs, cs] = (hid * jax.nn.sigmoid(hid)).astype(bf16)
    down(len(chunks) - 1)
    for rs in row_tiles(RB):
        x1 = x_ref[rs, :].astype(f32) + 0.5 * out_ref[rs, :]
        x1_ref[rs, :] = x1
        xhat, _ = norm_parts(x1)
        na_ref[rs, :] = (xhat * ga[...]).astype(bf16)
    w = wqo.shape[1]
    for ref, own, oth, scale in ((q_ref, wqo, wqx, DH**-0.5), (k_ref, wko, wkx, 1.0), (v_ref, wvo, wvx, 1.0)):
        for weight, cols in ((own, slice(0, w)), (oth, slice(w, 2 * w))):
            value = dot(na_ref[...], weight[...])
            if scale != 1.0:
                value = value.astype(bf16).astype(f32) * scale
            ref[:, cols] = value.astype(bf16)


def first_call(meta, frames, g1, w1o, w1x, w2o, w2x, ga, *qkv):
    hid = w1o.shape[1]
    consts = (g1, w1o, w1x, w2o, w2x, ga, *qkv)
    return pl.pallas_call(
        first_kernel,
        grid_spec=pltpu.PrefetchScalarGridSpec(
            num_scalar_prefetch=1,
            grid=(SLAB // RB,),
            in_specs=[own_row(D)] + [fixed(*a.shape) for a in consts],
            out_specs=[row(D), planes(2, hid)] + [row(D)] * 4,
            scratch_shapes=[
                pltpu.VMEM((RB, D), bf16),
                pltpu.VMEM((2, RB, UP), bf16),
                pltpu.VMEM((2, RB, UP), f32),
                pltpu.VMEM((RB, D), f32),
            ],
        ),
        out_shape=[shape((SLAB, D), f32), shape((2, SLAB, hid), bf16)] + [shape((SLAB, D), bf16)] * 4,
        compiler_params=params(),
        name="ffn1_forward",
    )(meta, frames, *consts)


TI = 384


def halves_of(parity, rows, cols=128):
    lane = lax.broadcasted_iota(jnp.int32, (rows, cols), 1)
    return (lane >> 6) == parity


def pick(mask, a, b):
    return jnp.where(mask, a.astype(f32), b.astype(f32)).astype(bf16)


def attend_kernel(m, q_ref, k_ref, v_ref, relo_ref, relx_ref,
                  o16_ref, o32_ref, li_ref, p_ref, qa_ref, ka_ref, va_ref, e_ref, rel_ref):
    head = pl.program_id(0)
    parity = head % 2
    mine = halves_of(parity, SLAB)
    slot = lax.broadcasted_iota(jnp.int32, (SLAB, 128), 1) & 63
    frame = lax.broadcasted_iota(jnp.int32, (SLAB, 128), 0)
    label = jnp.where(frame < m[1], 0, jnp.where(frame < m[2], 1, 2))
    mq = jnp.where((slot < 3) & (slot != label), MASKED, 0.0)
    mk = jnp.where(slot == label, 1.0, 0.0)
    qa_ref[...] = jnp.where(mine, q_ref[...].astype(f32), mq).astype(bf16)
    ka_ref[...] = jnp.where(mine, k_ref[...].astype(f32), mk).astype(bf16)
    va_ref[...] = jnp.where(mine, v_ref[...].astype(f32), 1.0).astype(bf16)
    rel_ref[: 2 * RW + 1, :] = jnp.where(
        head < DH // 16, relo_ref[...].astype(f32), relx_ref[...].astype(f32)
    )
    rel_ref[2 * RW + 1 :, :] = jnp.broadcast_to(rel_ref[2 * RW : 2 * RW + 1, :], (255 - 2 * RW, 128))
    relz = jnp.where(halves_of(parity, 256), rel_ref[...], 0.0).astype(bf16)
    e_ref[...] = dot_nt(qa_ref[...], relz)
    lane = lax.broadcasted_iota(jnp.int32, (SUB, 128), 1)
    line = lax.broadcasted_iota(jnp.int32, (SUB, 128), 0)
    left_of = {0: lane < line, 64: lane < line + 64}
    tiles = SLAB // 128
    mine_ti = halves_of(parity, TI)
    for start in range(0, SLAB, TI):
        sc = dot_nt(qa_ref[start : start + TI, :], ka_ref[...])
        for r in range(0, TI, SUB):
            b = (start + r) // SUB
            off = 64 if b % 2 == 0 else 0
            first = b // 2 - 1 if b % 2 == 0 else b // 2
            eb = e_ref[b * SUB : (b + 1) * SUB, :]
            left, right = eb[:, 0:1], eb[:, 128:129]
            near = pltpu.roll(eb, off, 1, stride=1, stride_axis=0)
            near0 = jnp.where(left_of[off], left, near[:, :128])
            near1 = near[:, 128:]
            s = [sc[r : r + SUB, t * 128 : (t + 1) * 128] for t in range(tiles)]
            peak = None
            if first >= 0:
                s[first] = s[first] + near0
                peak = s[first]
            if first + 1 < tiles:
                s[first + 1] = s[first + 1] + near1
                peak = s[first + 1] if peak is None else jnp.maximum(peak, s[first + 1])
            lefts = list(range(0, max(first, 0)))
            rights = list(range(first + 2, tiles))
            for group, const in ((lefts, left), (rights, right)):
                if group:
                    far = s[group[0]]
                    for t in group[1:]:
                        far = jnp.maximum(far, s[t])
                    peak = jnp.maximum(peak, far + const)
            peak = jnp.max(peak, -1, keepdims=True)
            peak_left, peak_right = peak - left, peak - right
            for t in range(tiles):
                top = peak_left if t in lefts else peak_right if t in rights else peak
                p_ref[0, start + r : start + r + SUB, t * 128 : (t + 1) * 128] = jnp.exp(
                    s[t] - top
                ).astype(bf16)
        pv = dot(p_ref[0, start : start + TI, :], va_ref[...])
        li = 1.0 / pltpu.roll(pv, 64, 1)
        o = pv * li
        rows = slice(start, start + TI)
        o = jnp.where(mine_ti, o, o32_ref[rows, :])
        o32_ref[rows, :] = o
        o16_ref[rows, :] = o.astype(bf16)
        li_ref[rows, :] = jnp.where(mine_ti, li, li_ref[rows, :])


def pair(rows=SLAB):
    return pl.BlockSpec((rows, 128), lambda h, *m: (0, h // 2))


HEAD_MAP = pl.BlockSpec((1, SLAB, SLAB), lambda h, *m: (h, 0, 0))
TABLE_OWN = pl.BlockSpec((2 * RW + 1, 128), lambda h, *m: (0, jnp.minimum(h // 2, 1)))
TABLE_OTH = pl.BlockSpec((2 * RW + 1, 128), lambda h, *m: (0, jnp.maximum(h // 2, 2) - 2))


def attend_call(meta, q, k, v, relo, relx):
    heads = D // DH
    scratch = [
        pltpu.VMEM((SLAB, 128), bf16),
        pltpu.VMEM((SLAB, 128), bf16),
        pltpu.VMEM((SLAB, 128), bf16),
        pltpu.VMEM((SLAB, 256), f32),
        pltpu.VMEM((256, 128), f32),
    ]
    return pl.pallas_call(
        attend_kernel,
        grid_spec=pltpu.PrefetchScalarGridSpec(
            num_scalar_prefetch=1,
            grid=(heads,),
            in_specs=[pair(), pair(), pair(), TABLE_OWN, TABLE_OTH],
            out_specs=[pair(), pair(), pair(), HEAD_MAP],
            scratch_shapes=scratch,
        ),
        out_shape=[
            shape((SLAB, D), bf16),
            shape((SLAB, D), f32),
            shape((SLAB, D), f32),
            shape((heads, SLAB, SLAB), bf16),
        ],
        compiler_params=params(),
        name="attention_forward",
    )(meta, q, k, v, relo, relx)


GAIN_ROW, BN_GAIN_ROW, BN_BIAS_ROW = TAPS, TAPS + 1, TAPS + 2
FLAT = SLAB + 3 * TOP
DEEP = PADDED + 2 * TOP


def spread_out(flat_ref, padded_ref, c, b1, b2):
    zeros = jnp.zeros((TOP, 128), f32)
    flat_ref[c, TOP + SLAB :, :] = jnp.zeros((FLAT - TOP - SLAB, 128), f32)
    padded_ref[c, :TOP, :] = zeros
    padded_ref[c, TOP + PADDED :, :] = zeros
    for t0 in range(0, PADDED, CH):
        t = lax.broadcasted_iota(jnp.int32, (CH, 128), 0) + t0
        at = TOP + t0
        value = jnp.where(t < b1, flat_ref[c, at : at + CH, :], 0.0)
        middle = (t >= b1 + GAP) & (t < b2 + GAP)
        value = jnp.where(middle, flat_ref[c, at - GAP : at - GAP + CH, :], value)
        value = jnp.where(t >= b2 + 2 * GAP, flat_ref[c, at - 2 * GAP : at - 2 * GAP + CH, :], value)
        padded_ref[c, at : at + CH, :] = value


def lane_row(ref, r):
    return jnp.concatenate([ref[c, r : r + 1, :] for c in range(LT)], 1)


def lanes(ref, r):
    return jnp.concatenate([ref[r + c : r + c + 1, :] for c in range(LT)], 1)


def draw_in(padded_ref, c, t0, rows, b1, b2):
    t = lax.broadcasted_iota(jnp.int32, (rows, 128), 0) + t0
    value = jnp.where(t < b1, padded_ref[c, t0 : t0 + rows, :], padded_ref[c, t0 + GAP : t0 + GAP + rows, :])
    return jnp.where(t < b2, value, padded_ref[c, t0 + 2 * GAP : t0 + 2 * GAP + rows, :])


def conv_kernel_fn(m, x1_in, o_in, woo, wox, weights, x2_out, u_out, hd_out, gp_out, st_ref, taps_ref,
                   x2_ref, o_ref, pin, rest, cn_ref, u_ref, u16_ref, hd_ref, gp_ref, flat_ref, out_ref,
                   mine, slots, send, recv, sems):
    place = Place()
    place.greet(("all",), False)
    copies = Copies(sems)
    cx = copies.start(x1_in, x2_ref)
    co = copies.start(o_in, o_ref)
    cr = copies.start(weights.at[:, 3 * D : 3 * D + 128], rest)
    cp = copies.start(weights.at[:, : 2 * D], pin)
    cr.wait()
    across = rest[...].astype(f32).T
    for c in range(LT):
        taps_ref[c] = across[:40, c * 128 : (c + 1) * 128]
    gain = lane_row(taps_ref, GAIN_ROW)
    w = woo.shape[0]
    cx.wait()
    co.wait()
    x2_ref[...] += dot(o_ref[:, :w], woo[...]) + dot(o_ref[:, w:], wox[...])
    for rs in row_tiles(SLAB):
        xhat, _ = norm_parts(x2_ref[rs, :])
        cn_ref[rs, :] = (xhat * gain).astype(bf16)
    ends = [copies.start(x2_ref, x2_out)]
    cp.wait()
    u_ref[...] = dot(cn_ref[...], pin[...])
    for rs in row_tiles(SLAB):
        for c in range(LT):
            cs, gs = slice(c * 128, c * 128 + 128), slice(D + c * 128, D + c * 128 + 128)
            u1, u2 = u_ref[rs, cs], u_ref[rs, gs]
            u16_ref[rs, cs] = u1.astype(bf16)
            u16_ref[rs, gs] = u2.astype(bf16)
            flat_ref[c, TOP + rs.start : TOP + rs.stop, :] = u1 * jax.nn.sigmoid(u2)
    ends.append(copies.start(u16_ref, u_out))
    b1, b2 = m[1], m[2]

    def tile(c, carry):
        spread_out(flat_ref, gp_ref, c, b1, b2)
        for t0 in range(0, PADDED, CH):
            acc = jnp.zeros((CH, 128), f32)
            for b in range(8):
                at = TOP + t0 - TAPS // 2 + b
                x = gp_ref[c, at : at + CH + 24, :]
                for a in range(4):
                    acc = acc + x[8 * a : 8 * a + CH, :] * taps_ref[c, 8 * a + b : 8 * a + b + 1, :]
            out_ref[c, t0 : t0 + CH, :] = acc
        first = jnp.zeros((8, 128), f32)
        second = jnp.zeros((8, 128), f32)
        for t0 in range(0, SLAB, 128):
            hd = draw_in(out_ref, c, t0, 128, b1, b2)
            hd_ref[c, t0 : t0 + 128, :] = hd
            t = lax.broadcasted_iota(jnp.int32, (128, 128), 0) + t0
            hv = jnp.where(t < b2, hd, 0.0)
            first = first + rows_sum(hv)
            second = second + rows_sum(hv * hv)
        mine[pl.ds(c, 1), :] = jnp.sum(first, 0, keepdims=True)
        mine[pl.ds(LT + c, 1), :] = jnp.sum(second, 0, keepdims=True)
        return carry

    lax.fori_loop(0, LT, tile, 0)
    mine[2 * LT :, :] = jnp.full((8, 128), b2.astype(f32))
    slots[place.me] = mine[...]
    place.greeted(("all",), False)
    hop = Hop(place, "all", lambda p: mine, slots, send, recv)
    hop.start()
    ends += [copies.start(hd_ref, hd_out), copies.start(gp_ref, gp_out)]
    hop.wait()
    st_ref[...] = slot_sum(slots, place.n)
    for copy in ends:
        copy.wait()


def conv_call(meta, x1, o16, woo, wox, gathered):
    n = lax.axis_size("dp")
    st = (2 * LT + 8, 128)
    return pl.pallas_call(
        conv_kernel_fn,
        in_specs=[SMEM, ANY, ANY, VMEM, VMEM, ANY],
        out_specs=[ANY, ANY, ANY, ANY, VMEM, VMEM],
        out_shape=[
            shape((SLAB, D), f32),
            shape((SLAB, 2 * D), bf16),
            shape((LT, SLAB, 128), f32),
            shape((LT, DEEP, 128), f32),
            shape(st, f32),
            shape((LT, 40, 128), f32),
        ],
        scratch_shapes=[
            pltpu.VMEM((SLAB, D), f32),
            pltpu.VMEM((SLAB, D), bf16),
            pltpu.VMEM((D, 2 * D), bf16),
            pltpu.VMEM((D, 128), bf16),
            pltpu.VMEM((SLAB, D), bf16),
            pltpu.VMEM((SLAB, 2 * D), f32),
            pltpu.VMEM((SLAB, 2 * D), bf16),
            pltpu.VMEM((LT, SLAB, 128), f32),
            pltpu.VMEM((LT, DEEP, 128), f32),
            pltpu.VMEM((LT, FLAT, 128), f32),
            pltpu.VMEM((LT, PADDED, 128), f32),
            pltpu.VMEM(st, f32),
        ]
        + slots_of(n, st, f32)
        + [pltpu.SemaphoreType.DMA((8,))],
        compiler_params=remote(0),
        name="conv_forward",
    )(meta, x1, o16, woo, wox, gathered)


def middle_kernel(m, hd_in, x2_in, ct_in, st, taps_ref, weights, g2, w1o_in, w1x_in, w2o_in, w2x_in, gf,
                  out_out, gx3_out, gz_out, acc, gpw_ref, back_ref, sums_ref,
                  hd_ref, x_ref, ct_ref, pout, w1, w2, wc_ref, n_ref, nt_ref, hid_ref, act_ref, slope_ref,
                  out_ref, out16_ref, gb_ref, gbt_ref, gn_ref, gc_ref, away, back, ssems, mine, slots, send, recv, sems):
    place = Place()
    place.greet(("all",))
    copies = Copies(sems)
    ch = copies.start(hd_in, hd_ref)
    cp = copies.start(weights.at[:, 2 * D : 3 * D], pout)
    cx = copies.start(x2_in, x_ref)
    cw = [copies.start(a, b) for a, b in ((w1x_in, w1.at[0]), (w1o_in, w1.at[1]), (w2x_in, w2.at[0]), (w2o_in, w2.at[1]))]
    start = pl.multiple_of(place.core * SLAB, SLAB)
    cc = copies.start(ct_in.at[pl.ds(start, SLAB)], ct_ref)

    bng, bnb = lane_row(taps_ref, BN_GAIN_ROW), lane_row(taps_ref, BN_BIAS_ROW)
    count = st[2 * LT : 2 * LT + 1, 0:1]
    centre = lanes(st, 0) / count
    inv_b = lax.rsqrt(lanes(st, LT) / count - centre * centre + BATCH_EPS)

    def normal(rs, c):
        cs = slice(c * 128, c * 128 + 128)
        zh = (hd_ref[c, rs, :] - centre[:, cs]) * inv_b[:, cs]
        z = zh * bng[:, cs] + bnb[:, cs]
        return cs, zh, z, jax.nn.sigmoid(z)

    ch.wait()
    for rs in row_tiles(SLAB):
        for c in range(LT):
            cs, _, z, sg = normal(rs, c)
            wc_ref[rs, cs] = (z * sg).astype(bf16)
    cp.wait()
    cx.wait()
    x_ref[...] += dot(wc_ref[...], pout[...])
    for rs in row_tiles(SLAB):
        xhat, _ = norm_parts(x_ref[rs, :])
        n_ref[rs, :] = (xhat * g2[...]).astype(bf16)
    for copy in cw:
        copy.wait()
    chunks = [(p, c) for p in (0, 1) for c in range(0, w1.shape[2], UP)]

    def up(k):
        p, c = chunks[k]
        hid_ref[k % 2] = dot(n_ref[...], w1[p, :, c : c + UP])

    def down(k):
        p, c = chunks[k]
        part = dot(act_ref[p, :, c : c + UP], w2[p, c : c + UP, :])
        if k == 0:
            out_ref[...] = part
        else:
            out_ref[...] += part

    up(0)
    for k, (p, c) in enumerate(chunks):
        if k + 1 < len(chunks):
            up(k + 1)
        if k > 0:
            down(k - 1)
        for rs, cs in tiles(SLAB, UP):
            hid = hid_ref[k % 2, rs, cs]
            sg = jax.nn.sigmoid(hid)
            act = hid * sg
            at = slice(c + cs.start, c + cs.stop)
            act_ref[p, rs, at] = act.astype(bf16)
            slope_ref[p, rs, at] = (sg + act * (1.0 - sg)).astype(bf16)
    down(len(chunks) - 1)
    transpose_into(nt_ref, n_ref)

    cc.wait()
    final_gain = jnp.zeros((8, D), f32)
    for rs in row_tiles(SLAB):
        t = lax.broadcasted_iota(jnp.int32, (TR, 1), 0) + rs.start
        valid = (t < m[2]).astype(f32)
        xhat, inv = norm_parts(x_ref[rs, :] + 0.5 * out_ref[rs, :])
        out16_ref[rs, :] = (valid * xhat * gf[...]).astype(bf16)
        g = ct_ref[rs, :].astype(f32) * valid
        gx4 = norm_back(g, gf[...], xhat, inv)
        out_ref[rs, :] = gx4
        gb_ref[rs, :] = (0.5 * gx4).astype(bf16)
        final_gain = final_gain + rows_sum(g * xhat)
    ends = [copies.start(out16_ref, out_out)]
    transpose_into(gbt_ref, gb_ref)

    def gup(k):
        p, c = chunks[k]
        hid_ref[k % 2] = dot_nt(gb_ref[...], w2[p, c : c + UP, :])

    def gdown(k):
        p, c = chunks[k]
        part = dot_nt(slope_ref[p, :, c : c + UP], w1[p, :, c : c + UP])
        if k == 0:
            gn_ref[...] = part
        else:
            gn_ref[...] += part

    gup(0)
    for k, (p, c) in enumerate(chunks):
        if k + 1 < len(chunks):
            gup(k + 1)
        if k > 0:
            gdown(k - 1)
        for rs, cs in tiles(SLAB, UP):
            at = slice(c + cs.start, c + cs.stop)
            slope_ref[p, rs, at] = (hid_ref[k % 2, rs, cs] * slope_ref[p, rs, at].astype(f32)).astype(bf16)
    gdown(len(chunks) - 1)

    ffn_gain = jnp.zeros((8, D), f32)
    for rs in row_tiles(SLAB):
        xhat, inv = norm_parts(x_ref[rs, :])
        gn = gn_ref[rs, :]
        gx3 = out_ref[rs, :] + norm_back(gn, g2[...], xhat, inv)
        x_ref[rs, :] = gx3
        gc_ref[rs, :] = gx3.astype(bf16)
        ffn_gain = ffn_gain + rows_sum(gn * xhat)
    ends.append(copies.start(x_ref, gx3_out))
    gn_ref[...] = dot_nt(gc_ref[...], pout[...])
    parts = [[jnp.zeros((8, 128), f32) for _ in range(4)] for _ in range(LT)]
    for rs in row_tiles(SLAB):
        t = lax.broadcasted_iota(jnp.int32, (TR, 1), 0) + rs.start
        valid = (t < m[2]).astype(f32)
        for c in range(LT):
            cs, zh, z, sg = normal(rs, c)
            gz = gn_ref[rs, cs] * (sg + z * sg * (1.0 - sg))
            hd_ref[c, rs, :] = gz
            e = gz * bng[:, cs] * valid
            for k, v in enumerate((gz, gz * zh, e, e * zh)):
                parts[c][k] = parts[c][k] + rows_sum(v)
    ends.append(copies.start(hd_ref, gz_out))
    sums_ref[...] = jnp.zeros(sums_ref.shape, f32)
    for c in range(LT):
        cs = slice(c * 128, c * 128 + 128)
        for k in range(4):
            total = jnp.sum(parts[c][k], 0, keepdims=True)
            sums_ref[k : k + 1, cs] = total
            if k >= 2:
                mine[(k - 2) * LT + c : (k - 2) * LT + c + 1, :] = total
    sums_ref[4:5, :] = jnp.sum(final_gain, 0, keepdims=True)
    sums_ref[5:6, :] = jnp.sum(ffn_gain, 0, keepdims=True)
    slots[place.me] = mine[...]
    place.greeted(("all",))
    hop = Hop(place, "all", lambda p: mine, slots, send, recv)
    hop.start()

    dims = acc.shape[1:]
    swaps = [core_copy(place, away.at[k], back.at[k], ssems.at[k]) for k in range(2)]
    lhs, rhs = (nt_ref, gbt_ref), (slope_ref, act_ref)
    for k in range(2):
        away[k] = dot(lhs[k][...], rhs[k][0]).reshape(dims).astype(bf16)
        swaps[k].start()
    gpw_ref[...] = dot_tn(wc_ref[...], gc_ref[...]).astype(bf16)
    for k in range(2):
        own = dot(lhs[k][...], rhs[k][1]).reshape(dims)
        swaps[k].wait()
        acc[k] = (own + back[k].astype(f32)).astype(bf16)
    hop.wait()
    back_ref[...] = slot_sum(slots, place.n)
    for copy in ends:
        copy.wait()


def grad_dims(cols):
    n = lax.axis_size("dp")
    return n, (*split_axis(n), D // n, cols)


def middle_call(meta, hd, x2, cot, st, taps, gathered, g2, w1o, w1x, w2o, w2x, gf):
    hid = w1o.shape[1]
    n, dims = grad_dims(hid)
    stat = (2 * LT, 128)
    return pl.pallas_call(
        middle_kernel,
        in_specs=[SMEM, ANY, ANY, ANY, VMEM, VMEM, ANY, VMEM, ANY, ANY, ANY, ANY, VMEM],
        out_specs=[ANY, ANY, ANY, VMEM, VMEM, VMEM, VMEM],
        out_shape=[
            shape((SLAB, D), bf16),
            shape((SLAB, D), f32),
            shape((LT, SLAB, 128), f32),
            shape((2, *dims), bf16),
            shape((D, D), bf16),
            shape(stat, f32),
            shape((8, D), f32),
        ],
        scratch_shapes=[
            pltpu.VMEM((LT, SLAB, 128), f32),
            pltpu.VMEM((SLAB, D), f32),
            pltpu.VMEM((SLAB, D), bf16),
            pltpu.VMEM((D, D), bf16),
            pltpu.VMEM((2, D, hid), bf16),
            pltpu.VMEM((2, hid, D), bf16),
            pltpu.VMEM((SLAB, D), bf16),
            pltpu.VMEM((SLAB, D), bf16),
            pltpu.VMEM((D, SLAB), bf16),
            pltpu.VMEM((2, SLAB, UP), f32),
            pltpu.VMEM((2, SLAB, hid), bf16),
            pltpu.VMEM((2, SLAB, hid), bf16),
            pltpu.VMEM((SLAB, D), f32),
            pltpu.VMEM((SLAB, D), bf16),
            pltpu.VMEM((SLAB, D), bf16),
            pltpu.VMEM((D, SLAB), bf16),
            pltpu.VMEM((SLAB, D), f32),
            pltpu.VMEM((SLAB, D), bf16),
            pltpu.VMEM((2, *dims), bf16),
            pltpu.VMEM((2, *dims), bf16),
            pltpu.SemaphoreType.DMA((2, 2)),
            pltpu.VMEM(stat, f32),
        ]
        + slots_of(n, stat, f32)
        + [pltpu.SemaphoreType.DMA((12,))],
        compiler_params=remote(1),
        name="ffn2_forward_backward",
    )(meta, hd, x2, cot, st, taps, gathered, g2, w1o, w1x, w2o, w2x, gf)


def conv_back_kernel(m, acc_in, gz_in, hd_in, gp_in, st, back, taps_ref, u_in, x2_in, gx3_in, weights, woo, wox,
                     gpw, sums, gx2_out, ga_out, go_out, cg_ref, mid0, mid1, mid2,
                     gz_ref, hd_ref, gp_ref, u_ref, x2_ref, gx_ref, pin, flat_ref, pad_ref, out_ref, acc_ref, gtap_ref,
                     gu_ref, gn_ref, cn_ref, ga_ref, go_ref, sems, *scr):
    place = Place()
    place.greet(("low", "high"), False)
    copies = Copies(sems)
    first = [copies.start(a, b) for a, b in ((gz_in, gz_ref), (hd_in, hd_ref), (gp_in, gp_ref))]
    rest = [copies.start(a, b) for a, b in (
        (u_in, u_ref), (weights.at[:, : 2 * D], pin), (x2_in, x2_ref), (gx3_in, gx_ref))]
    b1, b2 = m[1], m[2]
    gain = lane_row(taps_ref, GAIN_ROW)
    hops = [v.first(place, acc_in, refs) for v, refs in zip(PAIR_VIEWS, threes(scr))]
    place.greeted(("low", "high"), False)
    for hop in hops:
        hop.start()
    for copy in first:
        copy.wait()

    def tile(c, carry):
        count = st[2 * LT : 2 * LT + 1, :]
        centre = st[pl.ds(c, 1), :] / count
        inv_b = lax.rsqrt(st[pl.ds(LT + c, 1), :] / count - centre * centre + BATCH_EPS)
        a1 = back[pl.ds(c, 1), :] / count
        a2 = back[pl.ds(LT + c, 1), :] / count
        bn_gain = taps_ref[c, BN_GAIN_ROW : BN_GAIN_ROW + 1, :]
        for t0 in range(0, SLAB, 128):
            t = lax.broadcasted_iota(jnp.int32, (128, 128), 0) + t0
            zh = (hd_ref[c, t0 : t0 + 128, :] - centre) * inv_b
            away = jnp.where(t < b2, a1 + zh * a2, 0.0)
            flat_ref[c, TOP + t0 : TOP + t0 + 128, :] = inv_b * (gz_ref[c, t0 : t0 + 128, :] * bn_gain - away)
        spread_out(flat_ref, pad_ref, c, b1, b2)
        acc_ref[...] = jnp.zeros(acc_ref.shape, f32)
        for t0 in range(0, PADDED, CH):
            acc = jnp.zeros((CH, 128), f32)
            gl = gp_ref[c, TOP + t0 : TOP + t0 + CH, :]
            for b in range(8):
                at = TOP + t0 + TAPS // 2 - TAPS + 1 + b
                x = pad_ref[c, at : at + CH + 24, :]
                for a in range(4):
                    k = TAPS - 1 - (8 * a + b)
                    part = x[8 * a : 8 * a + CH, :]
                    acc = acc + part * taps_ref[c, k : k + 1, :]
                    acc_ref[8 * k : 8 * k + 8, :] += rows_sum(part * gl)
            out_ref[c, t0 : t0 + CH, :] = acc
        gtap_ref[c] = jnp.sum(acc_ref[...].reshape(TAPS, 8, 128), 1)
        for t0 in range(0, SLAB, 128):
            flat_ref[c, t0 : t0 + 128, :] = draw_in(out_ref, c, t0, 128, b1, b2)
        return carry

    lax.fori_loop(0, LT, tile, 0)
    for copy in rest:
        copy.wait()
    for rs in row_tiles(SLAB):
        for c in range(LT):
            cs, gs = slice(c * 128, c * 128 + 128), slice(D + c * 128, D + c * 128 + 128)
            sg = jax.nn.sigmoid(u_ref[rs, gs].astype(f32))
            g = flat_ref[c, rs, :] * sg
            gu_ref[rs, cs] = g.astype(bf16)
            gu_ref[rs, gs] = (g * u_ref[rs, cs].astype(f32) * (1.0 - sg)).astype(bf16)
    gn_ref[...] = dot_nt(gu_ref[...], pin[...])
    gain_sum = jnp.zeros((8, D), f32)
    for rs in row_tiles(SLAB):
        xhat, inv = norm_parts(x2_ref[rs, :])
        gn = gn_ref[rs, :]
        gx2 = gx_ref[rs, :] + norm_back(gn, gain, xhat, inv)
        gx_ref[rs, :] = gx2
        ga_ref[rs, :] = gx2.astype(bf16)
        cn_ref[rs, :] = (xhat * gain).astype(bf16)
        gain_sum = gain_sum + rows_sum(gn * xhat)
    ends = [copies.start(gx_ref, gx2_out), copies.start(ga_ref, ga_out)]
    w = woo.shape[0]
    go_ref[:, :w] = dot_nt(ga_ref[...], woo[...]).astype(bf16)
    go_ref[:, w:] = dot_nt(ga_ref[...], wox[...]).astype(bf16)
    ends.append(copies.start(go_ref, go_out))
    cg_ref[:, : 2 * D] = dot_tn(cn_ref[...], gu_ref[...]).astype(bf16)
    cg_ref[:, 2 * D : 3 * D] = gpw[...]
    gain_sum = jnp.sum(gain_sum, 0, keepdims=True)
    for c in range(LT):
        cols = slice(c * 128, (c + 1) * 128)
        rows = [gtap_ref[c], gain_sum[:, cols], sums[1:2, cols], sums[0:1, cols]]
        block = jnp.concatenate(rows + [jnp.zeros((128 - TAPS - 3, 128), f32)], 0)
        cg_ref[c * 128 : (c + 1) * 128, 3 * D :] = block.T.astype(bf16)
    for hop, mid in zip(hops, (mid0, mid1, mid2)):
        hop.wait()
        mid[...] = hop.total().astype(bf16)
    for copy in ends:
        copy.wait()


def conv_back_call(meta, acc, gz, hd, gp, st, back, taps, u, x2, gx3, gathered, woo, wox, gpw, sums):
    n, rows = lax.axis_size("dp"), acc.shape[3]
    return pl.pallas_call(
        conv_back_kernel,
        in_specs=[SMEM, VMEM, ANY, ANY, ANY, VMEM, VMEM, VMEM, ANY, ANY, ANY, ANY, VMEM, VMEM, VMEM, VMEM],
        out_specs=[ANY, ANY, ANY, VMEM, VMEM, VMEM, VMEM],
        out_shape=[
            shape((SLAB, D), f32),
            shape((SLAB, D), bf16),
            shape((SLAB, D), bf16),
            shape((D, CONV_C), bf16),
        ]
        + [shape(v.mid(n, rows), bf16) for v in PAIR_VIEWS],
        scratch_shapes=[
            pltpu.VMEM((LT, SLAB, 128), f32),
            pltpu.VMEM((LT, SLAB, 128), f32),
            pltpu.VMEM((LT, DEEP, 128), f32),
            pltpu.VMEM((SLAB, 2 * D), bf16),
            pltpu.VMEM((SLAB, D), f32),
            pltpu.VMEM((SLAB, D), f32),
            pltpu.VMEM((D, 2 * D), bf16),
            pltpu.VMEM((LT, FLAT, 128), f32),
            pltpu.VMEM((LT, DEEP, 128), f32),
            pltpu.VMEM((LT, PADDED, 128), f32),
            pltpu.VMEM((TAPS * 8, 128), f32),
            pltpu.VMEM((LT, TAPS, 128), f32),
            pltpu.VMEM((SLAB, 2 * D), bf16),
            pltpu.VMEM((SLAB, D), f32),
            pltpu.VMEM((SLAB, D), bf16),
            pltpu.VMEM((SLAB, D), bf16),
            pltpu.VMEM((SLAB, D), bf16),
            pltpu.SemaphoreType.DMA((10,)),
        ]
        + firsts(PAIR_VIEWS, n, rows),
        compiler_params=remote(2),
        name="conv_backward",
    )(meta, acc, gz, hd, gp, st, back, taps, u, x2, gx3, gathered, woo, wox, gpw, sums)


HEAD_VIEWS = (View(None, 0, 384, "low"), View(None, 384, 512, "high"))


def attend_back_kernel(q_ref, k_ref, v_ref, g_ref, o_ref, li_ref, p_ref, relo_ref, relx_ref,
                       wqo, wko, wvo, wqx, wkx, wvx, o16_ref, na_in, gatt_in, x1_in, gx2_in, gain,
                       mid0, mid1, mid2, cg_ref,
                       gt_ref, gx1_out, agains_ref, f2a_ref, f2b_ref, cpi_ref, cpo_ref, crest_ref, h0_ref, acc1_ref,
                       ga_ref, va_ref, kz_ref, qt_ref, gt_scr, gs_ref, w_ref, n_ref, kt_ref, vt_ref,
                       flip_ref, rel_ref, relf_ref, gqkv_ref, nat_ref, gat_ref, wide_ref, gn_ref, x1_ref, gx_ref,
                       away, hback, hsems, acc0_ref, sems, cback, csems, cacc, *scr):
    head = pl.program_id(0)
    place = Place()
    copies = Copies(sems)
    loads = [pltpu.make_async_copy(a, b, sems.at[k]) for k, (a, b) in enumerate((
        (na_in, wide_ref.at[0]), (gatt_in, wide_ref.at[1]), (x1_in, x1_ref), (gx2_in, gx_ref)))]
    gx1_copy = pltpu.make_async_copy(gx_ref, gx1_out, sems.at[4])
    scr = threes(scr)
    nv = len(PAIR_VIEWS)
    last = [v.second(place, mid, refs) for v, mid, refs in zip(PAIR_VIEWS, (mid0, mid1, mid2), scr[:nv])]
    cfirst = [v.first(place, cacc, refs) for v, refs in zip(CONV_VIEWS, scr[nv:])]
    nc = len(CONV_VIEWS)
    cmids = scr[nv + 2 * nc][:nc]
    assert len(cmids) == nc
    csecond = [v.second(place, mid, refs) for v, mid, refs in zip(CONV_VIEWS, cmids, scr[nv + nc :])]
    cswap = core_copy(place, cg_ref.at[:, :, 1 - place.core], cback, csems)
    hswaps = [core_copy(place, away.at[k], hback.at[k], hsems.at[k]) for k in range(2)]
    at = nv + 2 * nc + 1
    hfirst = [v.first(place, acc0_ref, refs) for v, refs in zip(HEAD_VIEWS, scr[at:])]
    nh = len(HEAD_VIEWS)
    hmids = scr[at + 2 * nh][:nh]
    hsecond = [v.second(place, mid, refs) for v, mid, refs in zip(HEAD_VIEWS, hmids, scr[at + nh :])]

    @pl.when(head == 0)
    def _():
        place.greet(("low", "high"))
        for copy in loads:
            copy.start()
        line = lax.broadcasted_iota(jnp.int32, (256, 256), 0)
        flip_ref[...] = jnp.where(line + lax.broadcasted_iota(jnp.int32, (256, 256), 1) == 255, 1.0, 0.0).astype(bf16)

    @pl.when(head == 1)
    def _():
        place.greeted(("low", "high"))
        for hop in last:
            hop.start()
        cswap.start()

    @pl.when(head == 2)
    def _():
        cswap.wait()
        cacc[...] = (cg_ref[:, :, place.core].astype(f32) + cback[...].astype(f32)).astype(bf16)
        for hop in cfirst:
            hop.start()

    @pl.when(head == 5)
    def _():
        for hop, mid in zip(cfirst, cmids):
            hop.wait()
            mid[...] = hop.total().astype(bf16)
        for hop in csecond:
            hop.start()
        for hop, v in zip(last, PAIR_VIEWS):
            hop.wait()
            if v.index == 0:
                f2a_ref[:, v.start : v.stop] = hop.total()
            else:
                f2b_ref[v.start : v.stop, :] = hop.total().T

    @pl.when(head == 7)
    def _():
        csecond[0].wait()
        cpi_ref[...] = csecond[0].total()
        csecond[1].wait()
        total = csecond[1].total()
        cpo_ref[...] = total[:, :D]
        crest_ref[...] = total[:, D:]
        for hop, mid, on in zip(hfirst, hmids, hsecond):
            hop.wait()
            mid[...] = hop.total().astype(bf16)
            on.start()

    parity = pl.program_id(0) % 2
    base = (1 - parity) * 64
    mine = halves_of(parity, SLAB)
    lane = lax.broadcasted_iota(jnp.int32, (SLAB, 128), 1)
    go = g_ref[...].astype(f32) * li_ref[...]

    @pl.when(parity == 0)
    def _():
        gt_scr[...] = go.T.astype(bf16)
        qt_ref[...] = q_ref[...].astype(f32).T.astype(bf16)

    go16 = go.astype(bf16).astype(f32)
    inner = jnp.sum(jnp.where(mine, go16 * o_ref[...], 0.0), -1, keepdims=True)
    hi = inner.astype(bf16).astype(f32)
    lo = inner - hi
    extra = jnp.where(lane == base, -hi, jnp.where(lane == base + 1, -lo, 0.0))
    ga_ref[...] = jnp.where(mine, go16, extra).astype(bf16)
    ones = jnp.where((lane == base) | (lane == base + 1), 1.0, 0.0)
    va_ref[...] = jnp.where(mine, v_ref[...].astype(f32), ones).astype(bf16)
    kz_ref[...] = jnp.where(mine, k_ref[...].astype(f32), 0.0).astype(bf16)

    subl = lax.broadcasted_iota(jnp.int32, (SUB, 128), 1)
    line = lax.broadcasted_iota(jnp.int32, (SUB, 128), 0)
    tiles = SLAB // 128
    zero16 = jnp.zeros((SUB, 128), bf16)
    n_ref[:, 128:] = jnp.zeros((SLAB, 128), bf16)
    for start in range(0, SLAB, TI):
        gp = dot_nt(ga_ref[start : start + TI, :], va_ref[...])
        for r in range(0, TI, SUB):
            b = (start + r) // SUB
            off = 64 if b % 2 == 0 else 0
            first = b // 2 - 1 if b % 2 == 0 else b // 2
            rows = slice(start + r, start + r + SUB)
            sums = {0: jnp.zeros((SUB, 128), f32), 1: jnp.zeros((SUB, 128), f32)}
            for t in range(tiles):
                cols = slice(t * 128, (t + 1) * 128)
                gs = p_ref[0, rows, cols].astype(f32) * gp[r : r + SUB, cols]
                gs16 = gs.astype(bf16)
                gs_ref[rows, cols] = gs16
                if t < first:
                    sums[0] = sums[0] + gs
                elif t > first + 1:
                    sums[1] = sums[1] + gs
                elif t == first:
                    w_ref[rows, :128] = gs16
                    sums[0] = sums[0] + jnp.where(subl < line + off, gs, 0.0)
                else:
                    w_ref[rows, 128:] = gs16
                    sums[1] = sums[1] + jnp.where(subl >= line + off, gs, 0.0)
            if first < 0:
                w_ref[rows, :128] = zero16
            if first + 1 >= tiles:
                w_ref[rows, 128:] = zero16
            far_left = jnp.sum(sums[0], -1, keepdims=True)
            far_right = jnp.sum(sums[1], -1, keepdims=True)
            left_hi = far_left.astype(bf16).astype(f32)
            right_hi = far_right.astype(bf16).astype(f32)
            far = jnp.where(subl == 0, left_hi, 0.0)
            far = jnp.where(subl == 1, far_left - left_hi, far)
            far = jnp.where(subl == 2, right_hi, far)
            far = jnp.where(subl == 3, far_right - right_hi, far)
            n_ref[rows, 128:] = far.astype(bf16)
    flipped = dot(w_ref[...], flip_ref[...])
    for b in range(SLAB // SUB):
        off = 64 if b % 2 == 0 else 0
        rows = slice(b * SUB, (b + 1) * SUB)
        near = pltpu.roll(flipped[rows, :], (off + 128) % 256, 1, stride=1, stride_axis=0)
        n_ref[rows, :128] = near[:, :128].astype(bf16)
    rel_ref[: 2 * RW + 1, :] = jnp.where(
        head >= 4, relo_ref[...].astype(f32), relx_ref[...].astype(f32)
    )
    relf_ref[:128, :] = dot(flip_ref[128:, :128], rel_ref[:128, :].astype(bf16))
    line = lax.broadcasted_iota(jnp.int32, (128, 128), 0)
    relf_ref[128:, :] = jnp.where(
        line < 2, rel_ref[0:1, :], jnp.where(line < 4, rel_ref[2 * RW : 2 * RW + 1, :], 0.0)
    )
    relz = jnp.where(halves_of(parity, 256), relf_ref[...], 0.0).astype(bf16)
    half = pl.ds(pl.multiple_of(parity * 64, 64), 64)
    gq = dot(gs_ref[...], kz_ref[...]) + dot(n_ref[...], relz)
    gqkv_ref[:, :128] = jnp.where(mine, gq * DH**-0.5, gqkv_ref[:, :128].astype(f32)).astype(bf16)
    kt_ref[half, :] = dot(qt_ref[half, :], gs_ref[...])
    vt_ref[half, :] = dot(gt_scr[half, :], p_ref[0])
    gt_ref[half, :] = dot(qt_ref[half, :], n_ref[...])

    @pl.when(head == 0)
    def _():
        loads[0].wait()
        loads[1].wait()
        transpose_into(nat_ref, wide_ref.at[0])
        transpose_into(gat_ref, wide_ref.at[1])

    own_pair = head >= 4

    def choose(own, oth):
        return jnp.where(own_pair, own[...].astype(f32), oth[...].astype(f32)).astype(bf16)

    dims = (*acc1_ref.shape[:3], 512)

    def pair_gradients():
        left = dot(nat_ref[...], gqkv_ref[...])
        right = dot(gat_ref[...], o16_ref[...])
        return jnp.concatenate([left, right], 1).reshape(dims)

    @pl.when(parity == 1)
    def _():
        gqkv_ref[:, 128:256] = kt_ref[...].T.astype(bf16)
        gqkv_ref[:, 256:] = vt_ref[...].T.astype(bf16)
        weights = jnp.concatenate([choose(wqo, wqx), choose(wko, wkx), choose(wvo, wvx)], 1)
        part = dot_nt(gqkv_ref[...], weights)

        @pl.when(head == 1)
        def _():
            gn_ref[...] = part

        @pl.when(head > 1)
        def _():
            gn_ref[...] += part

    for k in range(2):

        @pl.when(head == 2 * k + 1)
        def _(k=k):
            away[k] = pair_gradients().astype(bf16)
            hswaps[k].start()

        @pl.when(head == 2 * k + 5)
        def _(k=k):
            own = pair_gradients()
            hswaps[k].wait()
            (acc0_ref, acc1_ref)[k][...] = (own + hback[k].astype(f32)).astype(bf16)

    @pl.when(head == 5)
    def _():
        for hop in hfirst:
            hop.start()

    @pl.when(head == 7)
    def _():
        loads[2].wait()
        loads[3].wait()
        total = jnp.zeros((8, D), f32)
        for rs in row_tiles(SLAB):
            xhat, inv = norm_parts(x1_ref[rs, :])
            gn = gn_ref[rs, :]
            gx_ref[rs, :] = gx_ref[rs, :] + norm_back(gn, gain[...], xhat, inv)
            total = total + rows_sum(gn * xhat)
        gx1_copy.start()
        agains_ref[...] = total
        for hop, v in zip(hsecond, HEAD_VIEWS):
            hop.wait()
            h0_ref[:, v.start : v.stop] = hop.total()
        gx1_copy.wait()


def pair_of(h):
    return (h // 2 + 2) % 4


def attend_back_call(q, k, v, go, o32, li, p, relo, relx, weights, o16, na, gatt, x1, gx2, gain, mids, cg):
    heads = D // DH
    n, rows, crows = lax.axis_size("dp"), mids[0].shape[1], cg.shape[3]
    high, low = split_axis(n)
    cdims = (high, low, crows, CONV_C)
    hdims = (high, low, rows, 512)
    pair = pl.BlockSpec((SLAB, 128), lambda h: (0, pair_of(h)))
    head_map = pl.BlockSpec((1, SLAB, SLAB), lambda h: (2 * pair_of(h) + h % 2, 0, 0))
    own = lambda h: (0, jnp.maximum(h // 2, 2) - 2)
    oth = lambda h: (0, jnp.minimum(h // 2, 1))
    table_own, table_oth = pl.BlockSpec((2 * RW + 1, 128), own), pl.BlockSpec((2 * RW + 1, 128), oth)
    w_own, w_oth = pl.BlockSpec((D, 128), own), pl.BlockSpec((D, 128), oth)
    return pl.pallas_call(
        attend_back_kernel,
        grid=(heads,),
        in_specs=[pair] * 6 + [head_map, table_own, table_oth] + [w_own] * 3 + [w_oth] * 3 + [pair]
        + [ANY] * 4 + [fixed(1, D)] + [fixed(*a.shape) for a in (*mids, cg)],
        out_specs=[pl.BlockSpec((128, 256), lambda h: (pair_of(h), 0)), ANY, fixed(8, D), fixed(rows, 1024),
                   fixed(1024, rows), fixed(crows, 2 * D), fixed(crows, D), fixed(crows, 128),
                   fixed(rows, 512), fixed(*hdims)],
        out_shape=[
            shape((D, 256), f32),
            shape((SLAB, D), f32),
            shape((8, D), f32),
            shape((rows, 1024), f32),
            shape((1024, rows), f32),
            shape((crows, 2 * D), f32),
            shape((crows, D), f32),
            shape((crows, 128), f32),
            shape((rows, 512), f32),
            shape(hdims, bf16),
        ],
        scratch_shapes=[
            pltpu.VMEM((SLAB, 128), bf16),
            pltpu.VMEM((SLAB, 128), bf16),
            pltpu.VMEM((SLAB, 128), bf16),
            pltpu.VMEM((128, SLAB), bf16),
            pltpu.VMEM((128, SLAB), bf16),
            pltpu.VMEM((SLAB, SLAB), bf16),
            pltpu.VMEM((SLAB, 256), bf16),
            pltpu.VMEM((SLAB, 256), bf16),
            pltpu.VMEM((128, SLAB), f32),
            pltpu.VMEM((128, SLAB), f32),
            pltpu.VMEM((256, 256), bf16),
            pltpu.VMEM((136, 128), f32),
            pltpu.VMEM((256, 128), f32),
            pltpu.VMEM((SLAB, 384), bf16),
            pltpu.VMEM((D, SLAB), bf16),
            pltpu.VMEM((D, SLAB), bf16),
            pltpu.VMEM((2, SLAB, D), bf16),
            pltpu.VMEM((SLAB, D), f32),
            pltpu.VMEM((SLAB, D), f32),
            pltpu.VMEM((SLAB, D), f32),
            pltpu.VMEM((2, *hdims), bf16),
            pltpu.VMEM((2, *hdims), bf16),
            pltpu.SemaphoreType.DMA((2, 2)),
            pltpu.VMEM(hdims, bf16),
            pltpu.SemaphoreType.DMA((5,)),
            pltpu.VMEM(cdims, bf16),
            pltpu.SemaphoreType.DMA((2,)),
            pltpu.VMEM(cdims, bf16),
        ]
        + seconds(PAIR_VIEWS, n, rows)
        + firsts(CONV_VIEWS, n, crows)
        + seconds(CONV_VIEWS, n, crows)
        + padded_three([pltpu.VMEM(v.mid(n, crows), bf16) for v in CONV_VIEWS])
        + firsts(HEAD_VIEWS, n, rows)
        + seconds(HEAD_VIEWS, n, rows)
        + padded_three([pltpu.VMEM(v.mid(n, rows), bf16) for v in HEAD_VIEWS]),
        compiler_params=remote(3),
        name="attention_backward",
    )(q, k, v, go, o32, li, p, relo, relx, *weights, o16, na, gatt, x1, gx2, gain, *mids, cg)


CHUNK_VIEWS = (View(None, 0, 640, "low"), View(None, 640, 1024, "high"))


def last_kernel(gx1_in, x_in, hid_in, w1o_in, w1x_in, w2o_in, w2x_in, g1, sums, agains, acc1, table_ref,
                gx_out, fa_ref, fb_ref, gain0, gain1, gain2, gain3, h1_ref, to_ref,
                gx_ref, x_ref, hid_ref, w1, w2, gb_ref, gbt_ref, nt_ref, n_ref, gact_ref, act_ref, ghid_ref, gn_ref,
                gx16_ref, both_ref, away, back, ssems, xmine, xback, xsum, xsems, xslots, xsend, xrecv,
                tback, tsems, tsum, tmine, tslots, tsend, trecv, aslots, asend, arecv, sems, *scr):
    place = Place()
    place.greet(("all",))
    copies = Copies(sems)
    cg = copies.start(gx1_in, gx_ref)
    start = pl.multiple_of(place.core * SLAB, SLAB)
    cx = copies.start(x_in.at[pl.ds(start, SLAB)], x_ref)
    cw = [copies.start(a, b) for a, b in (
        (w2x_in, w2.at[0]), (hid_in.at[0], hid_ref.at[0]), (w1x_in, w1.at[0]),
        (w2o_in, w2.at[1]), (hid_in.at[1], hid_ref.at[1]), (w1o_in, w1.at[1]))]
    refs = threes(scr)
    nh, nc = len(HEAD_VIEWS), len(CHUNK_VIEWS)
    hfirst = [v.first(place, acc1, r) for v, r in zip(HEAD_VIEWS, refs)]
    refs = refs[nh:]
    hsecond_refs, refs = refs[:nh], refs[nh:]
    hmids, refs = refs[0][:nh], refs[1:]
    hsecond = [v.second(place, mid, r) for v, mid, r in zip(HEAD_VIEWS, hmids, hsecond_refs)]
    first, second, mids, accs = [], [], [], []
    for k in range(2):
        accs.append(refs[0][:nc])
        mids.append(refs[1][:nc])
        refs = refs[2:]
        first.append([v.whole_first(place, a, r) for v, a, r in zip(CHUNK_VIEWS, accs[k], refs)])
        refs = refs[nc:]
        second.append([v.second(place, mid, r) for v, mid, r in zip(CHUNK_VIEWS, mids[k], refs)])
        refs = refs[nc:]
    tswap = core_copy(place, table_ref.at[1], tback, tsems)
    scatter = Hop(place, "all", lambda p: tsum.at[p], tslots, tsend, trecv)
    gather = Hop(place, "all", lambda p: tmine, aslots, asend, arecv)
    xswap = core_copy(place, xmine, xback, xsems)
    xhop = Hop(place, "all", lambda p: xsum, xslots, xsend, xrecv)
    swaps = [core_copy(place, away.at[k], back.at[k], ssems.at[k]) for k in range(2)]

    cx.wait()
    for rs in row_tiles(SLAB):
        xhat, _ = norm_parts(x_ref[rs, :].astype(f32))
        n_ref[rs, :] = (xhat * g1[...]).astype(bf16)
    transpose_into(nt_ref, n_ref)
    place.greeted(("all",))
    tswap.start()
    for hop in hfirst:
        hop.start()
    cg.wait()
    for rs in row_tiles(SLAB):
        gb_ref[rs, :] = (0.5 * gx_ref[rs, :]).astype(bf16)
    transpose_into(gbt_ref, gb_ref)
    for copy in cw:
        copy.wait()
    dims = away.shape[1:]

    def side(p, k):
        cols = slice(k * UP, (k + 1) * UP)
        gact_ref[...] = dot_nt(gb_ref[...], w2[p, cols, :])
        for rs, cs in tiles(SLAB, UP):
            at = slice(k * UP + cs.start, k * UP + cs.stop)
            hid = hid_ref[p, rs, at].astype(f32)
            sg = jax.nn.sigmoid(hid)
            act = hid * sg
            act_ref[rs, cs] = act.astype(bf16)
            ghid_ref[rs, cs] = (gact_ref[rs, cs] * (sg + act * (1.0 - sg))).astype(bf16)
        part = dot_nt(ghid_ref[...], w1[p, :, cols])
        if p == 0 and k == 0:
            gn_ref[...] = part
        else:
            gn_ref[...] += part
        return dot(nt_ref[...], ghid_ref[...]), dot(gbt_ref[...], act_ref[...])

    half = (*dims[:3], UP)

    def send_side(k):
        left, right = side(0, k)
        away[k, :, :, :, :UP] = left.reshape(half).astype(bf16)
        away[k, :, :, :, UP:] = right.reshape(half).astype(bf16)
        swaps[k].start()

    def keep_side(k):
        left, right = side(1, k)
        swaps[k].wait()
        left = left.reshape(half) + back[k, :, :, :, :UP].astype(f32)
        right = right.reshape(half) + back[k, :, :, :, UP:].astype(f32)
        cut = CHUNK_VIEWS[0].stop
        accs[k][0][:, :, :, :UP] = left.astype(bf16)
        accs[k][0][:, :, :, UP:] = right[:, :, :, : cut - UP].astype(bf16)
        accs[k][1][...] = right[:, :, :, cut - UP :].astype(bf16)
        for hop in first[k]:
            hop.start()

    def turn(hops, mids, onward):
        for hop, mid, on in zip(hops, mids, onward):
            hop.wait()
            mid[...] = hop.total().astype(bf16)
            on.start()

    send_side(0)
    tswap.wait()
    tsum[...] = table_ref[0] + tback[...]
    scatter.start()
    keep_side(0)
    turn(hfirst, hmids, hsecond)
    scatter.wait()
    tmine[...] = scatter.total()
    aslots[place.me] = tmine[...]
    gather.start()
    send_side(1)
    keep_side(1)
    turn(first[0], mids[0], second[0])

    ffn_gain = jnp.zeros((8, D), f32)
    for rs in row_tiles(SLAB):
        xhat, inv = norm_parts(x_ref[rs, :].astype(f32))
        gn = gn_ref[rs, :]
        gx16_ref[rs, :] = (gx_ref[rs, :] + norm_back(gn, g1[...], xhat, inv)).astype(bf16)
        ffn_gain = ffn_gain + rows_sum(gn * xhat)
    out_copy = copies.start(gx16_ref, gx_out)
    gains = (
        jnp.sum(ffn_gain, 0, keepdims=True),
        jnp.sum(agains[...], 0, keepdims=True),
        sums[5:6, :],
        sums[4:5, :],
    )
    for r, g in enumerate(gains):
        for c in range(LT):
            xmine[r * LT + c : r * LT + c + 1, :] = g[:, c * 128 : (c + 1) * 128]
    xswap.start()
    for hop, v in zip(hsecond, HEAD_VIEWS):
        hop.wait()
        h1_ref[:, v.start : v.stop] = hop.total()
    gather.wait()
    line = lax.broadcasted_iota(jnp.int32, (136, 256), 0)
    slot = lax.broadcasted_iota(jnp.int32, (136, 256), 1)
    place_of = jnp.where(slot < 128, 127 - slot, jnp.where(slot < 130, 0, jnp.where(slot < 132, 128, -1)))
    choice = jnp.where(line == place_of, 1.0, 0.0)
    tall = aslots[...].reshape(-1, 256)
    to_ref[...] = lax.dot_general(
        choice, tall, (((1,), (1,)), ((), ())), preferred_element_type=f32, precision=lax.Precision.HIGHEST
    )[: 2 * RW + 1]
    xswap.wait()
    xsum[...] = xmine[...] + xback[...]
    xslots[place.me] = xsum[...]
    xhop.start()
    turn(first[1], mids[1], second[1])
    xhop.wait()
    total = slot_sum(xslots, place.n)
    for r, ref in enumerate((gain0, gain1, gain2, gain3)):
        for c in range(LT):
            ref[:, c * 128 : (c + 1) * 128] = total[r * LT + c : r * LT + c + 1, :]
    for k in range(2):
        for hop, v in zip(second[k], CHUNK_VIEWS):
            hop.wait()
            both_ref[:, v.start : v.stop] = hop.total()
        fa_ref[:, k * UP : (k + 1) * UP] = both_ref[:, :UP]
        fb_ref[k * UP : (k + 1) * UP, :] = both_ref[:, UP:].T
    out_copy.wait()


def padded_three(refs):
    return refs + [pltpu.SemaphoreType.DMA((1,))] * (-len(refs) % 3)


def last_call(gx1, frames, hid, w1o, w1x, w2o, w2x, g1, sums, agains, acc1, table):
    width = w1o.shape[1]
    n, dims = grad_dims(2 * UP)
    rows = dims[2]
    tdims = table.shape[2:]
    gains = (4 * LT, 128)
    chunk = []
    for _ in range(2):
        chunk += padded_three([pltpu.VMEM((*dims[:3], v.width), bf16) for v in CHUNK_VIEWS])
        chunk += padded_three([pltpu.VMEM(v.mid(n, rows), bf16) for v in CHUNK_VIEWS])
        chunk += firsts(CHUNK_VIEWS, n, rows) + seconds(CHUNK_VIEWS, n, rows)
    return pl.pallas_call(
        last_kernel,
        in_specs=[ANY] * 7 + [VMEM] * 5,
        out_specs=[ANY] + [VMEM] * 8,
        out_shape=[
            shape((SLAB, D), bf16),
            shape((rows, width), f32),
            shape((width, rows), f32),
        ]
        + [shape((1, D), f32)] * 4
        + [shape((rows, 512), f32), shape((2 * RW + 1, 256), f32)],
        scratch_shapes=[
            pltpu.VMEM((SLAB, D), f32),
            pltpu.VMEM((SLAB, D), bf16),
            pltpu.VMEM((2, SLAB, width), bf16),
            pltpu.VMEM((2, D, width), bf16),
            pltpu.VMEM((2, width, D), bf16),
            pltpu.VMEM((SLAB, D), bf16),
            pltpu.VMEM((D, SLAB), bf16),
            pltpu.VMEM((D, SLAB), bf16),
            pltpu.VMEM((SLAB, D), bf16),
            pltpu.VMEM((SLAB, UP), f32),
            pltpu.VMEM((SLAB, UP), bf16),
            pltpu.VMEM((SLAB, UP), bf16),
            pltpu.VMEM((SLAB, D), f32),
            pltpu.VMEM((SLAB, D), bf16),
            pltpu.VMEM((rows, 2 * UP), f32),
            pltpu.VMEM((2, *dims), bf16),
            pltpu.VMEM((2, *dims), bf16),
            pltpu.SemaphoreType.DMA((2, 2)),
            pltpu.VMEM(gains, f32),
            pltpu.VMEM(gains, f32),
            pltpu.VMEM(gains, f32),
            pltpu.SemaphoreType.DMA((2,)),
        ]
        + slots_of(n, gains, f32)
        + [
            pltpu.VMEM((n, *tdims), f32),
            pltpu.SemaphoreType.DMA((2,)),
            pltpu.VMEM((n, *tdims), f32),
            pltpu.VMEM(tdims, f32),
        ]
        + slots_of(n, tdims, f32)
        + slots_of(n, tdims, f32)
        + [pltpu.SemaphoreType.DMA((10,))]
        + firsts(HEAD_VIEWS, n, rows)
        + seconds(HEAD_VIEWS, n, rows)
        + padded_three([pltpu.VMEM(v.mid(n, rows), bf16) for v in HEAD_VIEWS])
        + chunk,
        compiler_params=remote(4),
        name="ffn1_backward",
    )(gx1, frames, hid, w1o, w1x, w2o, w2x, g1, sums, agains, acc1, table)


def both_slabs_kernel(m, out_own, out_oth, gx_own, gx_oth, out_ref, gx_ref):
    blocks = SLAB // RB
    mine = pl.program_id(0) // blocks == m[0]

    @pl.when(mine)
    def _():
        out_ref[...] = out_own[...]
        gx_ref[...] = gx_own[...].astype(f32)

    @pl.when(jnp.logical_not(mine))
    def _():
        out_ref[...] = out_oth[...]
        gx_ref[...] = gx_oth[...].astype(f32)


def both_slabs(meta, out, gx):
    blocks = SLAB // RB

    def at(core):
        return pl.BlockSpec(
            (RB, D), lambda i, m: (jnp.clip(i - core(m[0]) * blocks, 0, blocks - 1), 0)
        )

    own, oth = at(lambda c: c), at(lambda c: 1 - c)
    return pl.pallas_call(
        both_slabs_kernel,
        grid_spec=pltpu.PrefetchScalarGridSpec(
            num_scalar_prefetch=1, grid=(2 * blocks,), in_specs=[own, oth, own, oth],
            out_specs=[row(D), row(D)],
        ),
        out_shape=[shape((2 * SLAB, D), bf16), shape((2 * SLAB, D), f32)],
        compiler_params=params(),
        name="both_slabs",
    )(meta, out, swap(out), gx, swap(gx))


def swap(x):
    return lax.ppermute(x, "mp", [(0, 1), (1, 0)])


def shards(
    frames, lengths, cotangent, ffn1_gain, ffn1_in, ffn1_out, attn_gain, query_weight, key_weight,
    value_weight, out_weight, rel_table, conv_gain, pointwise_in, conv_kernel, bn_gain, bn_bias,
    pointwise_out, ffn2_gain, ffn2_in, ffn2_out, final_gain,
):
    mp = lax.axis_index("mp")
    n = lax.axis_size("dp")
    high, low = split_axis(n)
    w1o, w2o = ffn1_in, ffn1_out
    w1x, w2x = swap(w1o), swap(w2o)
    qkvo = (query_weight, key_weight, value_weight)
    qkvx = tuple(swap(w) for w in qkvo)
    relx = swap(rel_table)
    woo = out_weight
    wox = swap(woo)
    v1o, v2o = ffn2_in, ffn2_out
    v1x, v2x = swap(v1o), swap(v2o)
    column = jnp.arange(128 - TAPS)[None, :]
    vectors = sum(
        jnp.where(column == k, v[:, None], 0) for k, v in enumerate((conv_gain, bn_gain, bn_bias))
    )
    together = jnp.concatenate([pointwise_in, pointwise_out, conv_kernel, vectors.astype(bf16)], 1)
    gathered = lax.all_gather(together, ("dp", "mp"), axis=0, tiled=True)

    g1, ga, g2, gf = (g[None, :] for g in (ffn1_gain, attn_gain, ffn2_gain, final_gain))
    pair_lengths = jnp.where(mp == 0, lengths[0], lengths[1])
    first_end = pair_lengths[0]
    meta = jnp.stack([mp.astype(jnp.int32), first_end, first_end + pair_lengths[1]])

    x1, hid1, na, q, k, v = first_call(meta, frames, g1, w1o, w1x, w2o, w2x, ga, *qkvo, *qkvx)
    o16, o32, li, p = attend_call(meta, q, k, v, rel_table, relx)
    x2, u, hd, gp, st, taps = conv_call(meta, x1, o16, woo, wox, gathered)
    out, gx3, gz, acc2, gpw, back, sums = middle_call(
        meta, hd, x2, cotangent, st, taps, gathered, g2, v1o, v1x, v2o, v2x, gf
    )
    gx2, gatt, go, conv_g, *mids = conv_back_call(
        meta, acc2, gz, hd, gp, st, back, taps, u, x2, gx3, gathered, woo, wox, gpw, sums
    )
    conv_g = conv_g.reshape(high, low, 2, D // n // 2, CONV_C)
    gtab, gx1, agains, f2a, f2b, cpi, cpo, crest, h0, acc1 = attend_back_call(
        q, k, v, go, o32, li, p, rel_table, relx, (*qkvo, *qkvx), o16, na, gatt, x1, gx2, ga, mids, conv_g
    )
    h = D // 2
    gx, f1a, f1b, gain0, gain1, gain2, gain3, h1, table = last_call(
        gx1, frames, hid1, w1o, w1x, w2o, w2x, g1, sums, agains, acc1, gtab.reshape(2, n, h // n, 256)
    )
    block_output, frames_grad = both_slabs(meta, out, gx)
    q_grad, k_grad, v_grad, o_grad = (
        jnp.concatenate([h0[:, c : c + 128], h1[:, c : c + 128]], 1) for c in range(0, 512, 128)
    )
    return (
        block_output,
        frames_grad,
        gain0[0],
        f1a,
        f1b,
        gain1[0],
        q_grad,
        k_grad,
        v_grad,
        o_grad.T,
        table,
        crest[:, TAPS],
        cpi,
        crest[:, :TAPS],
        crest[:, TAPS + 1],
        crest[:, TAPS + 2],
        cpo,
        gain2[0],
        f2a,
        f2b,
        gain3[0],
    )


def solution(mesh):
    return jax.shard_map(
        shards,
        mesh=mesh,
        in_specs=(
            P("dp", None), P("dp", None), P("dp", None), P(), P(None, "mp"), P("mp", None), P(),
            P(None, "mp"), P(None, "mp"), P(None, "mp"), P("mp", None), P(None, "mp"),
            P(("dp", "mp")), P(("dp", "mp"), None), P(("dp", "mp"), None), P(("dp", "mp")),
            P(("dp", "mp")), P(("dp", "mp"), None), P(), P(None, "mp"), P("mp", None), P(),
        ),
        out_specs=(
            P("dp", None), P("dp", None), P(), P("dp", "mp"), P("mp", "dp"), P(), P("dp", "mp"),
            P("dp", "mp"), P("dp", "mp"), P("mp", "dp"), P(None, "mp"), P(("dp", "mp")),
            P(("dp", "mp"), None), P(("dp", "mp"), None), P(("dp", "mp")), P(("dp", "mp")),
            P(("dp", "mp"), None), P(), P("dp", "mp"), P("mp", "dp"), P(),
        ),
        check_vma=False,
    )
```

```python
import jax
import jax.numpy as jnp
from jax import lax
from jax.experimental import pallas as pl
from jax.experimental.pallas import tpu as pltpu
from jax.sharding import PartitionSpec as P

D = 512
DH = 64
RW = 64
SLAB = 1152
TAPS = 32
NORM_EPS = 1e-05
BATCH_EPS = 1e-05
MASKED = -1e30

SUB = 64
GAP = 16
TOP = 32
PADDED = 1216
CH = 64
LT = D // 128

f32 = jnp.float32
bf16 = jnp.bfloat16


def params(mib=60):
    return pltpu.CompilerParams(
        dimension_semantics=("arbitrary",), vmem_limit_bytes=mib << 20
    )


def dot(a, b):
    return jnp.dot(a, b, preferred_element_type=f32)


def dot_nt(a, b):
    return lax.dot_general(a, b, (((1,), (1,)), ((), ())), preferred_element_type=f32)


def dot_tn(a, b):
    return lax.dot_general(a, b, (((0,), (0,)), ((), ())), preferred_element_type=f32)


def norm_parts(v):
    c = v - jnp.mean(v, -1, keepdims=True)
    inv = lax.rsqrt(jnp.mean(c * c, -1, keepdims=True) + NORM_EPS)
    return c * inv, inv


def norm_back(gy, gain, xhat, inv):
    e = gy * gain
    inner = jnp.mean(e * xhat, -1, keepdims=True)
    return inv * (e - jnp.mean(e, -1, keepdims=True) - xhat * inner)


def rows_sum(v):
    return jnp.sum(v.reshape(v.shape[0] // 8, 8, v.shape[1]), 0)


def fixed(*shape):
    zeros = (0,) * len(shape)
    return pl.BlockSpec(shape, lambda i, *m: zeros)


SMEM = pl.BlockSpec(memory_space=pltpu.SMEM)
VMEM = pl.BlockSpec(memory_space=pltpu.VMEM)


def shape(dims, dtype):
    return jax.ShapeDtypeStruct(dims, dtype)


MESH = pl.DeviceIdType.MESH


def split_axis(n):
    low = 4 if n % 4 == 0 else 1
    return n // low, low


class Place:
    def __init__(self):
        self.n = lax.axis_size("dp")
        self.high, self.low = split_axis(self.n)
        self.me = lax.axis_index("dp")
        self.core = lax.axis_index("mp")
        self.hi = self.me // self.low
        self.lo = self.me % self.low

    def size(self, kind):
        return {"all": self.n, "low": self.low, "high": self.high}[kind]

    def mine(self, kind):
        return {"all": self.me, "low": self.lo, "high": self.hi}[kind]

    def peer(self, kind, j):
        at = (self.mine(kind) + j) % self.size(kind)
        if kind == "low":
            return at, {"dp": self.hi * self.low + at}
        if kind == "high":
            return at, {"dp": at * self.low + self.lo}
        return at, {"dp": at}

    def each(self, kind, do):
        size = self.size(kind)
        if size <= 4:
            for j in range(1, size):
                do(j)
        else:

            def body(j, carry):
                do(j)
                return carry

            lax.fori_loop(1, size, body, 0)

    def greet(self, kinds, core=True):
        barrier = pltpu.get_barrier_semaphore()
        for kind in kinds:
            self.each(
                kind,
                lambda j: pl.semaphore_signal(
                    barrier, inc=1, device_id=self.peer(kind, j)[1], device_id_type=MESH
                ),
            )
        if core:
            pl.semaphore_signal(barrier, inc=1, device_id={"mp": 1 - self.core}, device_id_type=MESH)

    def greeted(self, kinds, core=True):
        count = sum(self.size(kind) - 1 for kind in kinds) + (1 if core else 0)
        if count:
            pl.semaphore_wait(pltpu.get_barrier_semaphore(), count)


class Hop:
    def __init__(self, place, kind, piece, slots, send, recv):
        self.place, self.kind, self.piece = place, kind, piece
        self.slots, self.send, self.recv = slots, send, recv

    def copy(self, j, slot):
        at, device = self.place.peer(self.kind, j)
        return pltpu.make_async_remote_copy(
            src_ref=self.piece(at), dst_ref=self.slots.at[slot], send_sem=self.send.at[j],
            recv_sem=self.recv.at[slot], device_id=device, device_id_type=MESH,
        )

    def start(self):
        mine = self.place.mine(self.kind)
        self.place.each(self.kind, lambda j: self.copy(j, mine).start())

    def wait(self):
        self.place.each(self.kind, lambda j: self.copy(j, self.place.peer(self.kind, j)[0]).wait())

    def total(self):
        total = self.piece(self.place.mine(self.kind))[...].astype(f32)
        size = self.place.size(self.kind)
        if size <= 4:
            for j in range(1, size):
                total = total + self.slots[self.place.peer(self.kind, j)[0]].astype(f32)
            return total
        return lax.fori_loop(
            1, size, lambda j, t: t + self.slots[self.place.peer(self.kind, j)[0]].astype(f32), total
        )


def core_copy(place, src, dst, sems):
    return pltpu.make_async_remote_copy(
        src_ref=src, dst_ref=dst, send_sem=sems.at[0], recv_sem=sems.at[1],
        device_id={"mp": 1 - place.core}, device_id_type=MESH,
    )


def slots_of(size, dims, dtype=bf16):
    return [
        pltpu.VMEM((size, *dims), dtype),
        pltpu.SemaphoreType.DMA((size,)),
        pltpu.SemaphoreType.DMA((size,)),
    ]


class View:
    def __init__(self, index, start, stop, order):
        self.index, self.start, self.stop, self.order = index, start, stop, order
        self.width = stop - start

    def kinds(self):
        return ("low", "high") if self.order == "low" else ("high", "low")

    def mid(self, n, rows):
        high, low = split_axis(n)
        return (high if self.order == "low" else low, rows, self.width)

    def first_scratch(self, n, rows):
        high, low = split_axis(n)
        return slots_of(low if self.order == "low" else high, self.mid(n, rows))

    def second_scratch(self, n, rows):
        size, *dims = self.mid(n, rows)
        return slots_of(size, dims)

    def first(self, place, acc, refs):
        cols = slice(self.start, self.stop)
        if self.index is not None:
            acc = acc.at[self.index]
        if self.order == "low":
            piece = lambda p: acc.at[:, p, :, cols]
        else:
            piece = lambda p: acc.at[p, :, :, cols]
        return Hop(place, self.kinds()[0], piece, *refs)

    def whole_first(self, place, acc, refs):
        if self.order == "low":
            return Hop(place, "low", lambda p: acc.at[:, p], *refs)
        return Hop(place, "high", lambda p: acc.at[p], *refs)

    def second(self, place, mid, refs):
        return Hop(place, self.kinds()[1], lambda p: mid.at[p], *refs)


PAIR_VIEWS = (View(0, 0, 1024, "low"), View(1, 0, 384, "low"), View(1, 384, 1024, "high"))
CONV_C = 2 * D + D + 128
CONV_VIEWS = (View(None, 0, 1024, "low"), View(None, 1024, CONV_C, "high"))


def firsts(views, n, rows):
    return [ref for v in views for ref in v.first_scratch(n, rows)]


def seconds(views, n, rows):
    return [ref for v in views for ref in v.second_scratch(n, rows)]


def threes(refs):
    return [refs[i : i + 3] for i in range(0, len(refs), 3)]


def remote(collective_id, mib=60):
    return pltpu.CompilerParams(
        vmem_limit_bytes=mib << 20, collective_id=collective_id, has_side_effects=True,
    )


def slot_sum(slots, n):
    return lax.fori_loop(1, n, lambda j, total: total + slots[j], slots[0])


TR = 32
UP = 512


def row_tiles(rows):
    return [slice(r, r + TR) for r in range(0, rows, TR)]


def tiles(rows, cols, width=256):
    return [(rs, slice(c, c + width)) for rs in row_tiles(rows) for c in range(0, cols, width)]


def transpose_into(dst, src):
    for r in range(0, src.shape[0], 128):
        dst[:, r : r + 128] = src[r : r + 128, :].astype(f32).T.astype(bf16)


class Copies:
    def __init__(self, sems):
        self.sems, self.count = sems, 0

    def start(self, src, dst):
        copy = pltpu.make_async_copy(src, dst, self.sems.at[self.count])
        self.count += 1
        copy.start()
        return copy


ANY = pl.BlockSpec(memory_space=pl.ANY)


def bounds(len_ref, place):
    first = len_ref[place.core, 0]
    return first, first + len_ref[place.core, 1]


def first_kernel(x_in, g1, ga, w1_in, w2_in, wq_in, wk_in, wv_in, v1_in, v2_in, wo_in, rel_in,
                 x1_out, hid_out, na_out, q_out, k_out, v_out,
                 w1_out, w2_out, wq_out, wk_out, wv_out, v1_out, v2_out, wo_out, rel_out,
                 x_ref, w1, w2, wqkv, n_ref, act_ref, hid_ref, hid16_ref, x1_ref, na_ref, qkv_ref, sems, rsems):
    place = Place()
    place.greet(())
    copies = Copies(sems)
    cx = copies.start(x_in.at[pl.ds(pl.multiple_of(place.core * SLAB, SLAB), SLAB)], x_ref)
    qkv_in = (wq_in, wk_in, wv_in)
    mine = [copies.start(w1_in, w1.at[1]), copies.start(w2_in, w2.at[1])]
    mine_qkv = [copies.start(a, wqkv.at[1, k]) for k, a in enumerate(qkv_in)]
    place.greeted(())
    pairs = [(w1_in, w1.at[0]), (w2_in, w2.at[0])] + [(a, wqkv.at[0, k]) for k, a in enumerate(qkv_in)]
    pairs += [(v1_in, v1_out), (v2_in, v2_out), (wo_in, wo_out), (rel_in, rel_out)]
    swaps = [core_copy(place, a, b, rsems.at[k]) for k, (a, b) in enumerate(pairs)]
    for copy in swaps[:5]:
        copy.start()
    cx.wait()
    for rs in row_tiles(SLAB):
        xhat, _ = norm_parts(x_ref[rs, :].astype(f32))
        n_ref[rs, :] = (xhat * g1[...]).astype(bf16)
    for copy in mine:
        copy.wait()
    chunks = [(p, c) for p in (1, 0) for c in range(0, w1.shape[2], UP)]
    ends = []

    def up(k):
        p, c = chunks[k]
        hid_ref[k % 2] = dot(n_ref[...], w1[p, :, c : c + UP])

    def down(k):
        p, c = chunks[k]
        part = dot(act_ref[k % 2], w2[p, c : c + UP, :])
        if k == 0:
            x1_ref[...] = part
        else:
            x1_ref[...] += part

    up(0)
    for k, (p, c) in enumerate(chunks):
        for rs, cs in tiles(SLAB, UP):
            hid = hid_ref[k % 2, rs, cs]
            hid16_ref[p, rs, c + cs.start : c + cs.stop] = hid.astype(bf16)
            act_ref[k % 2, rs, cs] = (hid * jax.nn.sigmoid(hid)).astype(bf16)
        if k + 1 < len(chunks):
            if k + 1 == len(chunks) // 2:
                for copy in swaps[:5]:
                    copy.wait()
                for copy in swaps[5:]:
                    copy.start()
                ends.append(copies.start(hid16_ref.at[1], hid_out.at[1]))
                ends += [copies.start(w1.at[0], w1_out), copies.start(w2.at[0], w2_out)]
                ends += [copies.start(wqkv.at[0, n], out) for n, out in enumerate((wq_out, wk_out, wv_out))]
            up(k + 1)
        if k > 0:
            down(k - 1)
    ends.append(copies.start(hid16_ref.at[0], hid_out.at[0]))
    down(len(chunks) - 1)
    for rs in row_tiles(SLAB):
        x1 = x_ref[rs, :].astype(f32) + 0.5 * x1_ref[rs, :]
        x1_ref[rs, :] = x1
        xhat, _ = norm_parts(x1)
        na_ref[rs, :] = (xhat * ga[...]).astype(bf16)
    ends += [copies.start(x1_ref, x1_out), copies.start(na_ref, na_out)]
    for copy in mine_qkv:
        copy.wait()
    w = D // 2
    for n, out in enumerate((q_out, k_out, v_out)):
        for p in (0, 1):
            value = dot(na_ref[...], wqkv[p, n]).astype(bf16)
            if n == 0:
                value = (value.astype(f32) * DH**-0.5).astype(bf16)
            qkv_ref[n, :, (1 - p) * w : (2 - p) * w] = value
        ends.append(copies.start(qkv_ref.at[n], out))
    for copy in swaps[5:] + ends:
        copy.wait()


def first_call(frames, g1, ga, w1, w2, wq, wk, wv, v1, v2, wo, rel):
    hid = w1.shape[1]
    moved = (w1, w2, wq, wk, wv, v1, v2, wo, rel)
    return pl.pallas_call(
        first_kernel,
        in_specs=[ANY, VMEM, VMEM] + [ANY] * 9,
        out_specs=[ANY] * 15,
        out_shape=[shape((SLAB, D), f32), shape((2, SLAB, hid), bf16)]
        + [shape((SLAB, D), bf16)] * 4
        + [shape(a.shape, a.dtype) for a in moved],
        scratch_shapes=[
            pltpu.VMEM((SLAB, D), bf16),
            pltpu.VMEM((2, D, hid), bf16),
            pltpu.VMEM((2, hid, D), bf16),
            pltpu.VMEM((2, 3, D, D // 2), bf16),
            pltpu.VMEM((SLAB, D), bf16),
            pltpu.VMEM((2, SLAB, UP), bf16),
            pltpu.VMEM((2, SLAB, UP), f32),
            pltpu.VMEM((2, SLAB, hid), bf16),
            pltpu.VMEM((SLAB, D), f32),
            pltpu.VMEM((SLAB, D), bf16),
            pltpu.VMEM((3, SLAB, D), bf16),
            pltpu.SemaphoreType.DMA((20,)),
            pltpu.SemaphoreType.DMA((9, 2)),
        ],
        compiler_params=remote(5),
        name="ffn1_forward",
    )(frames, g1, ga, *moved)


TI = 384
STAGES = [(h, start) for h in (0, 1) for start in range(0, SLAB, TI)]


def low_lanes(rows, cols=128):
    return lax.broadcasted_iota(jnp.int32, (rows, cols), 1) < 64


def attend_kernel(len_ref, q_ref, k_ref, v_ref, relo_ref, relx_ref, pin, pout, ck, vec,
                  o16_ref, o32_ref, li_ref, p_ref, all_ref, qa_ref, ka_ref, va_ref, e_ref, rel_ref, s_ref, near_s, far_s, top_s,
                  piece_ref, far_ref, fsend, frecv, near_ref, nsend, nrecv, other_ref, osems):
    step = pl.program_id(0)
    place = Place()
    far = Hop(place, "high", lambda p: piece_ref, far_ref, fsend, frecv)
    near = Hop(place, "low", lambda p: far_ref, near_ref, nsend, nrecv)
    across = core_copy(place, near_ref, other_ref, osems)

    @pl.when(step == 0)
    def _():
        place.greet(("low", "high"))
        piece_ref[:, : 2 * D] = pin[...]
        piece_ref[:, 2 * D : 3 * D] = pout[...]
        piece_ref[:, 3 * D :] = jnp.concatenate([ck[...], vec[...]], 1)

    b1, b2 = bounds(len_ref, place)
    lane = lax.broadcasted_iota(jnp.int32, (SLAB, 128), 1)
    slot = lane & 63
    frame = lax.broadcasted_iota(jnp.int32, (SLAB, 128), 0)
    label = jnp.where(frame < b1, 0, jnp.where(frame < b2, 1, 2))
    mq = jnp.where((slot < 3) & (slot != label), MASKED, 0.0)
    mk = jnp.where(slot == label, 1.0, 0.0)
    rel_ref[: 2 * RW + 1, :] = jnp.where(step < 2, relo_ref[...].astype(f32), relx_ref[...].astype(f32))
    rel_ref[2 * RW + 1 :, :] = jnp.broadcast_to(rel_ref[2 * RW : 2 * RW + 1, :], (255 - 2 * RW, 128))
    q, k, v = (ref[...].astype(f32) for ref in (q_ref, k_ref, v_ref))
    for h in (0, 1):
        mine = (lane < 64) if h == 0 else (lane >= 64)
        qa_ref[h] = jnp.where(mine, q, mq).astype(bf16)
        ka_ref[h] = jnp.where(mine, k, mk).astype(bf16)
        va_ref[h] = jnp.where(mine, v, 1.0).astype(bf16)
        rel_mine = low_lanes(256) if h == 0 else jnp.logical_not(low_lanes(256))
        relz = jnp.where(rel_mine, rel_ref[...], 0.0).astype(bf16)
        e_ref[h] = dot_nt(qa_ref[h], relz)
    subl = lax.broadcasted_iota(jnp.int32, (SUB, 128), 1)
    line = lax.broadcasted_iota(jnp.int32, (SUB, 128), 0)
    left_of = {0: subl < line, 64: subl < line + 64}
    tiles = SLAB // 128

    def scores(t):
        h, start = STAGES[t]
        s_ref[t % 3] = dot_nt(qa_ref[h, start : start + TI, :], ka_ref[h])

    def shift(t):
        h, start = STAGES[t]
        for r in range(0, TI, SUB):
            b = (start + r) // SUB
            off = 64 if b % 2 == 0 else 0
            rows = slice(r, r + SUB)
            eb = e_ref[h, b * SUB : (b + 1) * SUB, :]
            near = pltpu.roll(eb, off, 1, stride=1, stride_axis=0)
            left = jnp.broadcast_to(eb[:, 0:1], (SUB, 128))
            near_s[t % 2, 0, rows, :] = jnp.where(left_of[off], left, near[:, :128])
            near_s[t % 2, 1, rows, :] = near[:, 128:]
            far_s[t % 2, 0, rows, :] = left
            far_s[t % 2, 1, rows, :] = jnp.broadcast_to(eb[:, 128:129], (SUB, 128))

    def groups(t, r):
        b = (STAGES[t][1] + r) // SUB
        first = b // 2 - 1 if b % 2 == 0 else b // 2
        near = [(n, n - first) for n in (first, first + 1) if 0 <= n < tiles]
        return near, list(range(0, max(first, 0))), list(range(first + 2, tiles))

    def find(t, r):
        rows = slice(r, r + SUB)
        near, lefts, rights = groups(t, r)
        s = {n: s_ref[t % 3, rows, n * 128 : (n + 1) * 128] for n in range(tiles)}
        peak = None
        for n, k in near:
            value = s[n] + near_s[t % 2, k, rows, :]
            s_ref[t % 3, rows, n * 128 : (n + 1) * 128] = value
            peak = value if peak is None else jnp.maximum(peak, value)
        far = [far_s[t % 2, k, rows, :] for k in (0, 1)]
        for group, const in ((lefts, far[0]), (rights, far[1])):
            if group:
                top = s[group[0]]
                for n in group[1:]:
                    top = jnp.maximum(top, s[n])
                peak = jnp.maximum(peak, top + const)
        peak = jnp.broadcast_to(jnp.max(peak, -1, keepdims=True), (SUB, 128))
        top_s[t % 2, 0, rows, :] = peak
        top_s[t % 2, 1, rows, :] = peak - far[0]
        top_s[t % 2, 2, rows, :] = peak - far[1]

    def power(t, r):
        h, start = STAGES[t]
        rows = slice(r, r + SUB)
        _, lefts, rights = groups(t, r)
        tops = [top_s[t % 2, k, rows, :] for k in range(3)]
        for n in range(tiles):
            top = tops[1] if n in lefts else tops[2] if n in rights else tops[0]
            s = s_ref[t % 3, rows, n * 128 : (n + 1) * 128]
            p_ref[h, start + r : start + r + SUB, n * 128 : (n + 1) * 128] = jnp.exp(s - top).astype(bf16)

    low = low_lanes(TI)

    def mix(t):
        h, start = STAGES[t]
        rows = slice(start, start + TI)
        pv = dot(p_ref[h, rows, :], va_ref[h])
        li = 1.0 / pltpu.roll(pv, 64, 1)
        o = pv * li
        if h == 1:
            o = jnp.where(low, o32_ref[rows, :], o)
            li = jnp.where(low, li_ref[rows, :], li)
            o16_ref[rows, :] = o.astype(bf16)
        o32_ref[rows, :] = o
        li_ref[rows, :] = li

    count = len(STAGES)
    scores(0)
    shift(0)
    for t in range(count + 2):
        if t + 1 < count:
            shift(t + 1)
        for r in range(0, TI, SUB):
            if t < count:
                find(t, r)
            if 0 < t <= count:
                power(t - 1, r)
        if t + 1 < count:
            scores(t + 1)
        if 2 <= t:
            mix(t - 2)

    @pl.when(step == 0)
    def _():
        place.greeted(("low", "high"))
        far.start()

    @pl.when(step == 1)
    def _():
        far.wait()
        far_ref[place.hi] = piece_ref[...]
        near.start()

    @pl.when(step == 2)
    def _():
        near.wait()
        near_ref[place.lo] = far_ref[...]
        across.start()

    @pl.when(step == 3)
    def _():
        across.wait()
        for l in range(place.low):
            all_ref[:, l, place.core] = near_ref[l]
            all_ref[:, l, 1 - place.core] = other_ref[l]


def attend_call(lengths, q, k, v, relo, relx, pin, pout, ck, vec):
    n, rows = lax.axis_size("dp"), pin.shape[0]
    high, low = split_axis(n)
    pair = pl.BlockSpec((SLAB, 128), lambda h: (0, h))
    table_own = pl.BlockSpec((2 * RW + 1, 128), lambda h: (0, jnp.minimum(h, 1)))
    table_oth = pl.BlockSpec((2 * RW + 1, 128), lambda h: (0, jnp.maximum(h, 2) - 2))
    smalls = (pin, pout, ck, vec)
    return pl.pallas_call(
        attend_kernel,
        grid=(D // 128,),
        in_specs=[SMEM, pair, pair, pair, table_own, table_oth] + [fixed(*a.shape) for a in smalls],
        out_specs=[pair, pair, pair, pl.BlockSpec((2, SLAB, SLAB), lambda h: (h, 0, 0)),
                   fixed(high, low, 2, rows, CONV_C)],
        out_shape=[
            shape((SLAB, D), bf16),
            shape((SLAB, D), f32),
            shape((SLAB, D), f32),
            shape((D // DH, SLAB, SLAB), bf16),
            shape((high, low, 2, rows, CONV_C), bf16),
        ],
        scratch_shapes=[
            pltpu.VMEM((2, SLAB, 128), bf16),
            pltpu.VMEM((2, SLAB, 128), bf16),
            pltpu.VMEM((2, SLAB, 128), bf16),
            pltpu.VMEM((2, SLAB, 256), f32),
            pltpu.VMEM((256, 128), f32),
            pltpu.VMEM((3, TI, SLAB), f32),
            pltpu.VMEM((2, 2, TI, 128), f32),
            pltpu.VMEM((2, 2, TI, 128), f32),
            pltpu.VMEM((2, 3, TI, 128), f32),
            pltpu.VMEM((rows, CONV_C), bf16),
        ]
        + slots_of(high, (rows, CONV_C))
        + slots_of(low, (high, rows, CONV_C))
        + [pltpu.VMEM((low, high, rows, CONV_C), bf16), pltpu.SemaphoreType.DMA((2,))],
        compiler_params=remote(6),
        name="attention_forward",
    )(lengths, q, k, v, relo, relx, *smalls)


GAIN_ROW, BN_GAIN_ROW, BN_BIAS_ROW = TAPS, TAPS + 1, TAPS + 2
FLAT = SLAB + 3 * TOP
DEEP = PADDED + 2 * TOP


def spread_out(flat_ref, padded_ref, c, b1, b2):
    zeros = jnp.zeros((TOP, 128), f32)
    flat_ref[c, TOP + SLAB :, :] = jnp.zeros((FLAT - TOP - SLAB, 128), f32)
    padded_ref[c, :TOP, :] = zeros
    padded_ref[c, TOP + PADDED :, :] = zeros
    for t0 in range(0, PADDED, CH):
        t = lax.broadcasted_iota(jnp.int32, (CH, 128), 0) + t0
        at = TOP + t0
        value = jnp.where(t < b1, flat_ref[c, at : at + CH, :], 0.0)
        middle = (t >= b1 + GAP) & (t < b2 + GAP)
        value = jnp.where(middle, flat_ref[c, at - GAP : at - GAP + CH, :], value)
        value = jnp.where(t >= b2 + 2 * GAP, flat_ref[c, at - 2 * GAP : at - 2 * GAP + CH, :], value)
        padded_ref[c, at : at + CH, :] = value


def lane_row(ref, r):
    return jnp.concatenate([ref[c, r : r + 1, :] for c in range(LT)], 1)


def lanes(ref, r):
    return jnp.concatenate([ref[r + c : r + c + 1, :] for c in range(LT)], 1)


def draw_in(padded_ref, c, t0, rows, b1, b2):
    t = lax.broadcasted_iota(jnp.int32, (rows, 128), 0) + t0
    value = jnp.where(t < b1, padded_ref[c, t0 : t0 + rows, :], padded_ref[c, t0 + GAP : t0 + GAP + rows, :])
    return jnp.where(t < b2, value, padded_ref[c, t0 + 2 * GAP : t0 + 2 * GAP + rows, :])


def conv_kernel_fn(len_ref, x1_in, o_in, woo, wox, weights, x2_out, u_out, hd_out, gp_out, st_ref, taps_ref,
                   x2_ref, o_ref, pin, rest, cn_ref, u_ref, u16_ref, hd_ref, gp_ref, flat_ref, out_ref,
                   mine, slots, send, recv, sems):
    place = Place()
    place.greet(("all",), False)
    copies = Copies(sems)
    cx = copies.start(x1_in, x2_ref)
    co = copies.start(o_in, o_ref)
    cr = copies.start(weights.at[:, 3 * D : 3 * D + 128], rest)
    cp = copies.start(weights.at[:, : 2 * D], pin)
    cr.wait()
    across = rest[...].astype(f32).T
    for c in range(LT):
        taps_ref[c] = across[:40, c * 128 : (c + 1) * 128]
    gain = lane_row(taps_ref, GAIN_ROW)
    w = woo.shape[0]
    cx.wait()
    co.wait()
    x2_ref[...] += dot(o_ref[:, :w], woo[...]) + dot(o_ref[:, w:], wox[...])
    for rs in row_tiles(SLAB):
        xhat, _ = norm_parts(x2_ref[rs, :])
        cn_ref[rs, :] = (xhat * gain).astype(bf16)
    ends = [copies.start(x2_ref, x2_out)]
    cp.wait()
    u_ref[...] = dot(cn_ref[...], pin[...])
    for rs in row_tiles(SLAB):
        for c in range(LT):
            cs, gs = slice(c * 128, c * 128 + 128), slice(D + c * 128, D + c * 128 + 128)
            u1, u2 = u_ref[rs, cs], u_ref[rs, gs]
            u16_ref[rs, cs] = u1.astype(bf16)
            u16_ref[rs, gs] = u2.astype(bf16)
            flat_ref[c, TOP + rs.start : TOP + rs.stop, :] = u1 * jax.nn.sigmoid(u2)
    ends.append(copies.start(u16_ref, u_out))
    b1, b2 = bounds(len_ref, place)

    def tile(c, carry):
        spread_out(flat_ref, gp_ref, c, b1, b2)
        for t0 in range(0, PADDED, CH):
            acc = jnp.zeros((CH, 128), f32)
            for b in range(8):
                at = TOP + t0 - TAPS // 2 + b
                x = gp_ref[c, at : at + CH + 24, :]
                for a in range(4):
                    acc = acc + x[8 * a : 8 * a + CH, :] * taps_ref[c, 8 * a + b : 8 * a + b + 1, :]
            out_ref[c, t0 : t0 + CH, :] = acc
        first = jnp.zeros((8, 128), f32)
        second = jnp.zeros((8, 128), f32)
        for t0 in range(0, SLAB, 128):
            hd = draw_in(out_ref, c, t0, 128, b1, b2)
            hd_ref[c, t0 : t0 + 128, :] = hd
            t = lax.broadcasted_iota(jnp.int32, (128, 128), 0) + t0
            hv = jnp.where(t < b2, hd, 0.0)
            first = first + rows_sum(hv)
            second = second + rows_sum(hv * hv)
        mine[pl.ds(c, 1), :] = jnp.sum(first, 0, keepdims=True)
        mine[pl.ds(LT + c, 1), :] = jnp.sum(second, 0, keepdims=True)
        return carry

    lax.fori_loop(0, LT, tile, 0)
    mine[2 * LT :, :] = jnp.full((8, 128), b2.astype(f32))
    slots[place.me] = mine[...]
    place.greeted(("all",), False)
    hop = Hop(place, "all", lambda p: mine, slots, send, recv)
    hop.start()
    ends += [copies.start(hd_ref, hd_out), copies.start(gp_ref, gp_out)]
    hop.wait()
    st_ref[...] = slot_sum(slots, place.n)
    for copy in ends:
        copy.wait()


def conv_call(lengths, x1, o16, woo, wox, gathered):
    n = lax.axis_size("dp")
    st = (2 * LT + 8, 128)
    return pl.pallas_call(
        conv_kernel_fn,
        in_specs=[SMEM, ANY, ANY, VMEM, VMEM, ANY],
        out_specs=[ANY, ANY, ANY, ANY, VMEM, VMEM],
        out_shape=[
            shape((SLAB, D), f32),
            shape((SLAB, 2 * D), bf16),
            shape((LT, SLAB, 128), f32),
            shape((LT, DEEP, 128), f32),
            shape(st, f32),
            shape((LT, 40, 128), f32),
        ],
        scratch_shapes=[
            pltpu.VMEM((SLAB, D), f32),
            pltpu.VMEM((SLAB, D), bf16),
            pltpu.VMEM((D, 2 * D), bf16),
            pltpu.VMEM((D, 128), bf16),
            pltpu.VMEM((SLAB, D), bf16),
            pltpu.VMEM((SLAB, 2 * D), f32),
            pltpu.VMEM((SLAB, 2 * D), bf16),
            pltpu.VMEM((LT, SLAB, 128), f32),
            pltpu.VMEM((LT, DEEP, 128), f32),
            pltpu.VMEM((LT, FLAT, 128), f32),
            pltpu.VMEM((LT, PADDED, 128), f32),
            pltpu.VMEM(st, f32),
        ]
        + slots_of(n, st, f32)
        + [pltpu.SemaphoreType.DMA((8,))],
        compiler_params=remote(0),
        name="conv_forward",
    )(lengths, x1, o16, woo, wox, gathered)


def middle_kernel(len_ref, hd_in, x2_in, ct_in, st, taps_ref, weights, g2, w1o_in, w1x_in, w2o_in, w2x_in, gf,
                  out_out, gx3_out, gz_out, acc, gpw_ref, back_ref, sums_ref,
                  hd_ref, x_ref, ct_ref, pout, w1, w2, wc_ref, n_ref, nt_ref, hid_ref, act_ref, slope_ref,
                  out_ref, out16_ref, gb_ref, gbt_ref, gn_ref, gc_ref, away, back, ssems, mine, slots, send, recv, sems):
    place = Place()
    place.greet(("all",))
    copies = Copies(sems)
    ch = copies.start(hd_in, hd_ref)
    cp = copies.start(weights.at[:, 2 * D : 3 * D], pout)
    cx = copies.start(x2_in, x_ref)
    cw = [copies.start(a, b) for a, b in ((w1x_in, w1.at[0]), (w1o_in, w1.at[1]), (w2x_in, w2.at[0]), (w2o_in, w2.at[1]))]
    start = pl.multiple_of(place.core * SLAB, SLAB)
    cc = copies.start(ct_in.at[pl.ds(start, SLAB)], ct_ref)

    _, b2 = bounds(len_ref, place)
    bng, bnb = lane_row(taps_ref, BN_GAIN_ROW), lane_row(taps_ref, BN_BIAS_ROW)
    count = st[2 * LT : 2 * LT + 1, 0:1]
    centre = lanes(st, 0) / count
    inv_b = lax.rsqrt(lanes(st, LT) / count - centre * centre + BATCH_EPS)

    def normal(rs, c):
        cs = slice(c * 128, c * 128 + 128)
        zh = (hd_ref[c, rs, :] - centre[:, cs]) * inv_b[:, cs]
        z = zh * bng[:, cs] + bnb[:, cs]
        return cs, zh, z, jax.nn.sigmoid(z)

    ch.wait()
    for rs in row_tiles(SLAB):
        for c in range(LT):
            cs, _, z, sg = normal(rs, c)
            wc_ref[rs, cs] = (z * sg).astype(bf16)
    cp.wait()
    cx.wait()
    x_ref[...] += dot(wc_ref[...], pout[...])
    for rs in row_tiles(SLAB):
        xhat, _ = norm_parts(x_ref[rs, :])
        n_ref[rs, :] = (xhat * g2[...]).astype(bf16)
    for copy in cw:
        copy.wait()
    chunks = [(p, c) for p in (0, 1) for c in range(0, w1.shape[2], UP)]

    def up(k):
        p, c = chunks[k]
        hid_ref[k % 2] = dot(n_ref[...], w1[p, :, c : c + UP])

    def down(k):
        p, c = chunks[k]
        part = dot(act_ref[p, :, c : c + UP], w2[p, c : c + UP, :])
        if k == 0:
            out_ref[...] = part
        else:
            out_ref[...] += part

    up(0)
    for k, (p, c) in enumerate(chunks):
        for rs, cs in tiles(SLAB, UP):
            hid = hid_ref[k % 2, rs, cs]
            sg = jax.nn.sigmoid(hid)
            act = hid * sg
            at = slice(c + cs.start, c + cs.stop)
            act_ref[p, rs, at] = act.astype(bf16)
            slope_ref[p, rs, at] = (sg + act * (1.0 - sg)).astype(bf16)
        if k + 1 < len(chunks):
            up(k + 1)
        if k > 0:
            down(k - 1)
    down(len(chunks) - 1)
    transpose_into(nt_ref, n_ref)

    cc.wait()
    final_gain = jnp.zeros((8, D), f32)
    for rs in row_tiles(SLAB):
        t = lax.broadcasted_iota(jnp.int32, (TR, 1), 0) + rs.start
        valid = (t < b2).astype(f32)
        xhat, inv = norm_parts(x_ref[rs, :] + 0.5 * out_ref[rs, :])
        out16_ref[rs, :] = (valid * xhat * gf[...]).astype(bf16)
        g = ct_ref[rs, :].astype(f32) * valid
        gx4 = norm_back(g, gf[...], xhat, inv)
        out_ref[rs, :] = gx4
        gb_ref[rs, :] = (0.5 * gx4).astype(bf16)
        final_gain = final_gain + rows_sum(g * xhat)
    ends = [copies.start(out16_ref, out_out)]
    transpose_into(gbt_ref, gb_ref)

    def gup(k):
        p, c = chunks[k]
        hid_ref[k % 2] = dot_nt(gb_ref[...], w2[p, c : c + UP, :])

    def gdown(k):
        p, c = chunks[k]
        part = dot_nt(slope_ref[p, :, c : c + UP], w1[p, :, c : c + UP])
        if k == 0:
            gn_ref[...] = part
        else:
            gn_ref[...] += part

    gup(0)
    for k, (p, c) in enumerate(chunks):
        for rs, cs in tiles(SLAB, UP):
            at = slice(c + cs.start, c + cs.stop)
            slope_ref[p, rs, at] = (hid_ref[k % 2, rs, cs] * slope_ref[p, rs, at].astype(f32)).astype(bf16)
        if k + 1 < len(chunks):
            gup(k + 1)
        if k > 0:
            gdown(k - 1)
    gdown(len(chunks) - 1)

    ffn_gain = jnp.zeros((8, D), f32)
    for rs in row_tiles(SLAB):
        xhat, inv = norm_parts(x_ref[rs, :])
        gn = gn_ref[rs, :]
        gx3 = out_ref[rs, :] + norm_back(gn, g2[...], xhat, inv)
        x_ref[rs, :] = gx3
        gc_ref[rs, :] = gx3.astype(bf16)
        ffn_gain = ffn_gain + rows_sum(gn * xhat)
    ends.append(copies.start(x_ref, gx3_out))
    gn_ref[...] = dot_nt(gc_ref[...], pout[...])
    parts = [[jnp.zeros((8, 128), f32) for _ in range(4)] for _ in range(LT)]
    for rs in row_tiles(SLAB):
        t = lax.broadcasted_iota(jnp.int32, (TR, 1), 0) + rs.start
        valid = (t < b2).astype(f32)
        for c in range(LT):
            cs, zh, z, sg = normal(rs, c)
            gz = gn_ref[rs, cs] * (sg + z * sg * (1.0 - sg))
            hd_ref[c, rs, :] = gz
            e = gz * bng[:, cs] * valid
            for k, v in enumerate((gz, gz * zh, e, e * zh)):
                parts[c][k] = parts[c][k] + rows_sum(v)
    ends.append(copies.start(hd_ref, gz_out))
    sums_ref[...] = jnp.zeros(sums_ref.shape, f32)
    for c in range(LT):
        cs = slice(c * 128, c * 128 + 128)
        for k in range(4):
            total = jnp.sum(parts[c][k], 0, keepdims=True)
            sums_ref[k : k + 1, cs] = total
            if k >= 2:
                mine[(k - 2) * LT + c : (k - 2) * LT + c + 1, :] = total
    sums_ref[4:5, :] = jnp.sum(final_gain, 0, keepdims=True)
    sums_ref[5:6, :] = jnp.sum(ffn_gain, 0, keepdims=True)
    slots[place.me] = mine[...]
    place.greeted(("all",))
    hop = Hop(place, "all", lambda p: mine, slots, send, recv)
    hop.start()

    dims = acc.shape[1:]
    swaps = [core_copy(place, away.at[k], back.at[k], ssems.at[k]) for k in range(2)]
    lhs, rhs = (nt_ref, gbt_ref), (slope_ref, act_ref)
    for k in range(2):
        away[k] = dot(lhs[k][...], rhs[k][0]).reshape(dims).astype(bf16)
        swaps[k].start()
    gpw_ref[...] = dot_tn(wc_ref[...], gc_ref[...]).astype(bf16)
    for k in range(2):
        own = dot(lhs[k][...], rhs[k][1]).reshape(dims)
        swaps[k].wait()
        acc[k] = (own + back[k].astype(f32)).astype(bf16)
    hop.wait()
    back_ref[...] = slot_sum(slots, place.n)
    for copy in ends:
        copy.wait()


def grad_dims(cols):
    n = lax.axis_size("dp")
    return n, (*split_axis(n), D // n, cols)


def middle_call(lengths, hd, x2, cot, st, taps, gathered, g2, w1o, w1x, w2o, w2x, gf):
    hid = w1o.shape[1]
    n, dims = grad_dims(hid)
    stat = (2 * LT, 128)
    return pl.pallas_call(
        middle_kernel,
        in_specs=[SMEM, ANY, ANY, ANY, VMEM, VMEM, ANY, VMEM, ANY, ANY, ANY, ANY, VMEM],
        out_specs=[ANY, ANY, ANY, VMEM, VMEM, VMEM, VMEM],
        out_shape=[
            shape((SLAB, D), bf16),
            shape((SLAB, D), f32),
            shape((LT, SLAB, 128), f32),
            shape((2, *dims), bf16),
            shape((D, D), bf16),
            shape(stat, f32),
            shape((8, D), f32),
        ],
        scratch_shapes=[
            pltpu.VMEM((LT, SLAB, 128), f32),
            pltpu.VMEM((SLAB, D), f32),
            pltpu.VMEM((SLAB, D), bf16),
            pltpu.VMEM((D, D), bf16),
            pltpu.VMEM((2, D, hid), bf16),
            pltpu.VMEM((2, hid, D), bf16),
            pltpu.VMEM((SLAB, D), bf16),
            pltpu.VMEM((SLAB, D), bf16),
            pltpu.VMEM((D, SLAB), bf16),
            pltpu.VMEM((2, SLAB, UP), f32),
            pltpu.VMEM((2, SLAB, hid), bf16),
            pltpu.VMEM((2, SLAB, hid), bf16),
            pltpu.VMEM((SLAB, D), f32),
            pltpu.VMEM((SLAB, D), bf16),
            pltpu.VMEM((SLAB, D), bf16),
            pltpu.VMEM((D, SLAB), bf16),
            pltpu.VMEM((SLAB, D), f32),
            pltpu.VMEM((SLAB, D), bf16),
            pltpu.VMEM((2, *dims), bf16),
            pltpu.VMEM((2, *dims), bf16),
            pltpu.SemaphoreType.DMA((2, 2)),
            pltpu.VMEM(stat, f32),
        ]
        + slots_of(n, stat, f32)
        + [pltpu.SemaphoreType.DMA((12,))],
        compiler_params=remote(1),
        name="ffn2_forward_backward",
    )(lengths, hd, x2, cot, st, taps, gathered, g2, w1o, w1x, w2o, w2x, gf)


def conv_back_kernel(len_ref, acc_in, gz_in, hd_in, gp_in, st, back, taps_ref, u_in, x2_in, gx3_in, weights, woo, wox,
                     gpw, sums, gx2_out, ga_out, go_out, cg_ref, mid0, mid1, mid2,
                     gz_ref, hd_ref, gp_ref, u_ref, x2_ref, gx_ref, pin, flat_ref, pad_ref, out_ref, acc_ref, gtap_ref,
                     gu_ref, gn_ref, cn_ref, ga_ref, go_ref, sems, *scr):
    place = Place()
    place.greet(("low", "high"), False)
    copies = Copies(sems)
    first = [copies.start(a, b) for a, b in ((gz_in, gz_ref), (hd_in, hd_ref), (gp_in, gp_ref))]
    rest = [copies.start(a, b) for a, b in (
        (u_in, u_ref), (weights.at[:, : 2 * D], pin), (x2_in, x2_ref), (gx3_in, gx_ref))]
    b1, b2 = bounds(len_ref, place)
    gain = lane_row(taps_ref, GAIN_ROW)
    hops = [v.first(place, acc_in, refs) for v, refs in zip(PAIR_VIEWS, threes(scr))]
    place.greeted(("low", "high"), False)
    for hop in hops:
        hop.start()
    for copy in first:
        copy.wait()

    def tile(c, carry):
        count = st[2 * LT : 2 * LT + 1, :]
        centre = st[pl.ds(c, 1), :] / count
        inv_b = lax.rsqrt(st[pl.ds(LT + c, 1), :] / count - centre * centre + BATCH_EPS)
        a1 = back[pl.ds(c, 1), :] / count
        a2 = back[pl.ds(LT + c, 1), :] / count
        bn_gain = taps_ref[c, BN_GAIN_ROW : BN_GAIN_ROW + 1, :]
        for t0 in range(0, SLAB, 128):
            t = lax.broadcasted_iota(jnp.int32, (128, 128), 0) + t0
            zh = (hd_ref[c, t0 : t0 + 128, :] - centre) * inv_b
            away = jnp.where(t < b2, a1 + zh * a2, 0.0)
            flat_ref[c, TOP + t0 : TOP + t0 + 128, :] = inv_b * (gz_ref[c, t0 : t0 + 128, :] * bn_gain - away)
        spread_out(flat_ref, pad_ref, c, b1, b2)
        acc_ref[...] = jnp.zeros(acc_ref.shape, f32)
        for t0 in range(0, PADDED, CH):
            acc = jnp.zeros((CH, 128), f32)
            gl = gp_ref[c, TOP + t0 : TOP + t0 + CH, :]
            for b in range(8):
                at = TOP + t0 + TAPS // 2 - TAPS + 1 + b
                x = pad_ref[c, at : at + CH + 24, :]
                for a in range(4):
                    k = TAPS - 1 - (8 * a + b)
                    part = x[8 * a : 8 * a + CH, :]
                    acc = acc + part * taps_ref[c, k : k + 1, :]
                    acc_ref[8 * k : 8 * k + 8, :] += rows_sum(part * gl)
            out_ref[c, t0 : t0 + CH, :] = acc
        gtap_ref[c] = jnp.sum(acc_ref[...].reshape(TAPS, 8, 128), 1)
        for t0 in range(0, SLAB, 128):
            flat_ref[c, t0 : t0 + 128, :] = draw_in(out_ref, c, t0, 128, b1, b2)
        return carry

    lax.fori_loop(0, LT, tile, 0)
    for copy in rest:
        copy.wait()
    for rs in row_tiles(SLAB):
        for c in range(LT):
            cs, gs = slice(c * 128, c * 128 + 128), slice(D + c * 128, D + c * 128 + 128)
            sg = jax.nn.sigmoid(u_ref[rs, gs].astype(f32))
            g = flat_ref[c, rs, :] * sg
            gu_ref[rs, cs] = g.astype(bf16)
            gu_ref[rs, gs] = (g * u_ref[rs, cs].astype(f32) * (1.0 - sg)).astype(bf16)
    gn_ref[...] = dot_nt(gu_ref[...], pin[...])
    gain_sum = jnp.zeros((8, D), f32)
    for rs in row_tiles(SLAB):
        xhat, inv = norm_parts(x2_ref[rs, :])
        gn = gn_ref[rs, :]
        gx2 = gx_ref[rs, :] + norm_back(gn, gain, xhat, inv)
        gx_ref[rs, :] = gx2
        ga_ref[rs, :] = gx2.astype(bf16)
        cn_ref[rs, :] = (xhat * gain).astype(bf16)
        gain_sum = gain_sum + rows_sum(gn * xhat)
    ends = [copies.start(gx_ref, gx2_out), copies.start(ga_ref, ga_out)]
    w = woo.shape[0]
    go_ref[:, :w] = dot_nt(ga_ref[...], woo[...]).astype(bf16)
    go_ref[:, w:] = dot_nt(ga_ref[...], wox[...]).astype(bf16)
    ends.append(copies.start(go_ref, go_out))
    cg_ref[:, : 2 * D] = dot_tn(cn_ref[...], gu_ref[...]).astype(bf16)
    cg_ref[:, 2 * D : 3 * D] = gpw[...]
    gain_sum = jnp.sum(gain_sum, 0, keepdims=True)
    for c in range(LT):
        cols = slice(c * 128, (c + 1) * 128)
        rows = [gtap_ref[c], gain_sum[:, cols], sums[1:2, cols], sums[0:1, cols]]
        block = jnp.concatenate(rows + [jnp.zeros((128 - TAPS - 3, 128), f32)], 0)
        cg_ref[c * 128 : (c + 1) * 128, 3 * D :] = block.T.astype(bf16)
    for hop, mid in zip(hops, (mid0, mid1, mid2)):
        hop.wait()
        mid[...] = hop.total().astype(bf16)
    for copy in ends:
        copy.wait()


def conv_back_call(lengths, acc, gz, hd, gp, st, back, taps, u, x2, gx3, gathered, woo, wox, gpw, sums):
    n, rows = lax.axis_size("dp"), acc.shape[3]
    return pl.pallas_call(
        conv_back_kernel,
        in_specs=[SMEM, VMEM, ANY, ANY, ANY, VMEM, VMEM, VMEM, ANY, ANY, ANY, ANY, VMEM, VMEM, VMEM, VMEM],
        out_specs=[ANY, ANY, ANY, VMEM, VMEM, VMEM, VMEM],
        out_shape=[
            shape((SLAB, D), f32),
            shape((SLAB, D), bf16),
            shape((SLAB, D), bf16),
            shape((D, CONV_C), bf16),
        ]
        + [shape(v.mid(n, rows), bf16) for v in PAIR_VIEWS],
        scratch_shapes=[
            pltpu.VMEM((LT, SLAB, 128), f32),
            pltpu.VMEM((LT, SLAB, 128), f32),
            pltpu.VMEM((LT, DEEP, 128), f32),
            pltpu.VMEM((SLAB, 2 * D), bf16),
            pltpu.VMEM((SLAB, D), f32),
            pltpu.VMEM((SLAB, D), f32),
            pltpu.VMEM((D, 2 * D), bf16),
            pltpu.VMEM((LT, FLAT, 128), f32),
            pltpu.VMEM((LT, DEEP, 128), f32),
            pltpu.VMEM((LT, PADDED, 128), f32),
            pltpu.VMEM((TAPS * 8, 128), f32),
            pltpu.VMEM((LT, TAPS, 128), f32),
            pltpu.VMEM((SLAB, 2 * D), bf16),
            pltpu.VMEM((SLAB, D), f32),
            pltpu.VMEM((SLAB, D), bf16),
            pltpu.VMEM((SLAB, D), bf16),
            pltpu.VMEM((SLAB, D), bf16),
            pltpu.SemaphoreType.DMA((10,)),
        ]
        + firsts(PAIR_VIEWS, n, rows),
        compiler_params=remote(2),
        name="conv_backward",
    )(lengths, acc, gz, hd, gp, st, back, taps, u, x2, gx3, gathered, woo, wox, gpw, sums)


HEAD_VIEWS = (View(None, 0, 384, "low"), View(None, 384, 512, "high"))


def attend_back_kernel(q_ref, k_ref, v_ref, g_ref, o_ref, li_ref, p_ref, relo_ref, relx_ref,
                       wqo, wko, wvo, wqx, wkx, wvx, o16_ref, na_in, gatt_in, x1_in, gx2_in, gain,
                       mid0, mid1, mid2, cg_ref,
                       gt_ref, gx1_out, agains_ref, f2a_ref, f2b_ref, cpi_ref, cpo_ref, crest_ref, h0_ref, acc1_ref,
                       ga_ref, va_ref, kz_ref, qt_ref, got_ref, gs_ref, gp_ref, w_ref, fl_ref, n_ref, kt_ref, vt_ref,
                       dq_ref, far_s, flip_ref, rel_ref, relf_ref, gqkv_ref, nat_ref, gat_ref, wide_ref, gn_ref, x1_ref, gx_ref,
                       pg_ref, away, hback, hsems, acc0_ref, sems, cback, csems, cacc, *scr):
    step = pl.program_id(0)
    place = Place()
    loads = [pltpu.make_async_copy(a, b, sems.at[k]) for k, (a, b) in enumerate((
        (na_in, wide_ref.at[0]), (gatt_in, wide_ref.at[1]), (x1_in, x1_ref), (gx2_in, gx_ref)))]
    gx1_copy = pltpu.make_async_copy(gx_ref, gx1_out, sems.at[4])
    scr = threes(scr)
    nv = len(PAIR_VIEWS)
    last = [v.second(place, mid, refs) for v, mid, refs in zip(PAIR_VIEWS, (mid0, mid1, mid2), scr[:nv])]
    cfirst = [v.first(place, cacc, refs) for v, refs in zip(CONV_VIEWS, scr[nv:])]
    nc = len(CONV_VIEWS)
    cmids = scr[nv + 2 * nc][:nc]
    csecond = [v.second(place, mid, refs) for v, mid, refs in zip(CONV_VIEWS, cmids, scr[nv + nc :])]
    cswap = core_copy(place, cg_ref.at[:, :, 1 - place.core], cback, csems)
    hswaps = [core_copy(place, away.at[k], hback.at[k], hsems.at[k]) for k in range(2)]
    at = nv + 2 * nc + 1
    hfirst = [v.first(place, acc0_ref, refs) for v, refs in zip(HEAD_VIEWS, scr[at:])]
    nh = len(HEAD_VIEWS)
    hmids = scr[at + 2 * nh][:nh]
    hsecond = [v.second(place, mid, refs) for v, mid, refs in zip(HEAD_VIEWS, hmids, scr[at + nh :])]
    kinds = ("low", "high")

    @pl.when(step == 0)
    def _():
        place.greet(kinds)
        for copy in loads:
            copy.start()
        line = lax.broadcasted_iota(jnp.int32, (256, 256), 0)
        flip_ref[...] = jnp.where(line + lax.broadcasted_iota(jnp.int32, (256, 256), 1) == 255, 1.0, 0.0).astype(bf16)
        loads[0].wait()
        loads[1].wait()
        transpose_into(nat_ref, wide_ref.at[0])
        transpose_into(gat_ref, wide_ref.at[1])

    lane = lax.broadcasted_iota(jnp.int32, (SLAB, 128), 1)
    go = g_ref[...].astype(f32) * li_ref[...]
    got_ref[...] = go.T.astype(bf16)
    qt_ref[...] = q_ref[...].astype(f32).T.astype(bf16)
    go = go.astype(bf16).astype(f32)
    product = go * o_ref[...]
    own_pair = step >= 2
    rel_ref[: 2 * RW + 1, :] = jnp.where(own_pair, relo_ref[...].astype(f32), relx_ref[...].astype(f32))
    relf_ref[:128, :] = dot(flip_ref[128:, :128], rel_ref[:128, :].astype(bf16))
    line = lax.broadcasted_iota(jnp.int32, (128, 128), 0)
    relf_ref[128:, :] = jnp.where(
        line < 2, rel_ref[0:1, :], jnp.where(line < 4, rel_ref[2 * RW : 2 * RW + 1, :], 0.0)
    )
    relz = []
    for h in (0, 1):
        mine = (lane < 64) if h == 0 else (lane >= 64)
        base = 64 - 64 * h
        inner = jnp.sum(jnp.where(mine, product, 0.0), -1, keepdims=True)
        hi = inner.astype(bf16).astype(f32)
        extra = jnp.where(lane == base, -hi, jnp.where(lane == base + 1, hi - inner, 0.0))
        ga_ref[h] = jnp.where(mine, go, extra).astype(bf16)
        ones = jnp.where((lane == base) | (lane == base + 1), 1.0, 0.0)
        va_ref[h] = jnp.where(mine, v_ref[...].astype(f32), ones).astype(bf16)
        kz_ref[h] = jnp.where(mine, k_ref[...].astype(f32), 0.0).astype(bf16)
        rel_mine = low_lanes(256) if h == 0 else jnp.logical_not(low_lanes(256))
        relz.append(jnp.where(rel_mine, relf_ref[...], 0.0).astype(bf16))

    subl = lax.broadcasted_iota(jnp.int32, (SUB, 128), 1)
    line = lax.broadcasted_iota(jnp.int32, (SUB, 128), 0)
    left_of = {0: subl < line, 64: subl < line + 64}
    tiles = SLAB // 128
    zero16 = jnp.zeros((SUB, 128), bf16)

    def grow(t):
        h, start = STAGES[t]
        gp_ref[t % 2] = dot_nt(ga_ref[h, start : start + TI, :], va_ref[h])

    def weigh(t):
        h, start = STAGES[t]
        for r in range(0, TI, SUB):
            b = (start + r) // SUB
            off = 64 if b % 2 == 0 else 0
            first = b // 2 - 1 if b % 2 == 0 else b // 2
            rows = slice(start + r, start + r + SUB)
            near = slice(r, r + SUB)
            sums = [jnp.zeros((SUB, 128), f32), jnp.zeros((SUB, 128), f32)]
            for n in range(tiles):
                cols = slice(n * 128, (n + 1) * 128)
                gs = p_ref[h, rows, cols].astype(f32) * gp_ref[t % 2, near, cols]
                gs16 = gs.astype(bf16)
                gs_ref[h, rows, cols] = gs16
                if n < first:
                    sums[0] = sums[0] + gs
                elif n > first + 1:
                    sums[1] = sums[1] + gs
                elif n == first:
                    w_ref[t % 2, near, :128] = gs16
                    sums[0] = sums[0] + jnp.where(left_of[off], gs, 0.0)
                else:
                    w_ref[t % 2, near, 128:] = gs16
                    sums[1] = sums[1] + jnp.where(left_of[off], 0.0, gs)
            if first < 0:
                w_ref[t % 2, near, :128] = zero16
            if first + 1 >= tiles:
                w_ref[t % 2, near, 128:] = zero16
            far_s[t % 2, 0, near, :] = sums[0]
            far_s[t % 2, 1, near, :] = sums[1]

    def flip(t):
        fl_ref[t % 2] = dot(w_ref[t % 2], flip_ref[...])

    def unroll(t):
        h, start = STAGES[t]
        for r in range(0, TI, SUB):
            off = 64 if ((start + r) // SUB) % 2 == 0 else 0
            near = pltpu.roll(fl_ref[t % 2, r : r + SUB, :], (off + 128) % 256, 1, stride=1, stride_axis=0)
            n_ref[h, start + r : start + r + SUB, :128] = near[:, :128].astype(bf16)
            far_left = jnp.sum(far_s[t % 2, 0, r : r + SUB, :], -1, keepdims=True)
            far_right = jnp.sum(far_s[t % 2, 1, r : r + SUB, :], -1, keepdims=True)
            left_hi = far_left.astype(bf16).astype(f32)
            right_hi = far_right.astype(bf16).astype(f32)
            far = jnp.where(subl == 0, left_hi, 0.0)
            far = jnp.where(subl == 1, far_left - left_hi, far)
            far = jnp.where(subl == 2, right_hi, far)
            far = jnp.where(subl == 3, far_right - right_hi, far)
            n_ref[h, start + r : start + r + SUB, 128:] = far.astype(bf16)

    def query(t):
        h, start = STAGES[t]
        rows = slice(start, start + TI)
        part = dot(gs_ref[h, rows, :], kz_ref[h]) + dot(n_ref[h, rows, :], relz[h])
        if h == 0:
            dq_ref[rows, :] = part
        else:
            gqkv_ref[rows, :128] = ((dq_ref[rows, :] + part) * DH**-0.5).astype(bf16)

    def key(h):
        half = slice(64 * h, 64 * h + 64)
        kt_ref[half, :] = dot(qt_ref[half, :], gs_ref[h])
        gt_ref[half, :] = dot(qt_ref[half, :], n_ref[h])

    def value(h):
        half = slice(64 * h, 64 * h + 64)
        vt_ref[half, :] = dot(got_ref[half, :], p_ref[h])

    grow(0)
    for t in range(len(STAGES)):
        weigh(t)
        if t > 0:
            unroll(t - 1)
        if t + 1 < len(STAGES):
            grow(t + 1)
        flip(t)
        if t > 0:
            query(t - 1)
        if t == 1:
            value(0)
        if t == 2:
            value(1)
        if t == 3:
            key(0)
        if t == 4:
            gqkv_ref[:, 256:] = vt_ref[...].T.astype(bf16)
            pg_ref[:, 384:] = dot(gat_ref[...], o16_ref[...])
    unroll(len(STAGES) - 1)
    key(1)
    gqkv_ref[:, 128:256] = kt_ref[...].T.astype(bf16)
    query(len(STAGES) - 1)

    def choose(own, oth):
        return jnp.where(own_pair, own[...].astype(f32), oth[...].astype(f32)).astype(bf16)

    weights = jnp.concatenate([choose(wqo, wqx), choose(wko, wkx), choose(wvo, wvx)], 1)
    gn_ref[...] = jnp.where(step == 0, 0.0, gn_ref[...]) + dot_nt(gqkv_ref[...], weights)
    pg_ref[:, :384] = dot(nat_ref[...], gqkv_ref[...])
    dims = acc1_ref.shape

    @pl.when(step == 0)
    def _():
        place.greeted(kinds)
        for hop in last:
            hop.start()
        cswap.start()
        away[0] = pg_ref[...].reshape(dims).astype(bf16)
        hswaps[0].start()

    @pl.when(step == 1)
    def _():
        away[1] = pg_ref[...].reshape(dims).astype(bf16)
        hswaps[1].start()
        cswap.wait()
        cacc[...] = (cg_ref[:, :, place.core].astype(f32) + cback[...].astype(f32)).astype(bf16)
        for hop in cfirst:
            hop.start()
        for hop, v in zip(last, PAIR_VIEWS):
            hop.wait()
            if v.index == 0:
                f2a_ref[:, v.start : v.stop] = hop.total()
            else:
                f2b_ref[:, v.start : v.stop] = hop.total()

    @pl.when(step == 2)
    def _():
        hswaps[0].wait()
        acc0_ref[...] = (pg_ref[...].reshape(dims) + hback[0].astype(f32)).astype(bf16)
        for hop in hfirst:
            hop.start()
        for hop, mid, on in zip(cfirst, cmids, csecond):
            hop.wait()
            mid[...] = hop.total().astype(bf16)
            on.start()

    @pl.when(step == 3)
    def _():
        hswaps[1].wait()
        acc1_ref[...] = (pg_ref[...].reshape(dims) + hback[1].astype(f32)).astype(bf16)
        csecond[0].wait()
        cpi_ref[...] = csecond[0].total()
        csecond[1].wait()
        total = csecond[1].total()
        cpo_ref[...] = total[:, :D]
        crest_ref[...] = total[:, D:]
        for hop, mid, on in zip(hfirst, hmids, hsecond):
            hop.wait()
            mid[...] = hop.total().astype(bf16)
            on.start()
        loads[2].wait()
        loads[3].wait()
        total = jnp.zeros((8, D), f32)
        for rs in row_tiles(SLAB):
            xhat, inv = norm_parts(x1_ref[rs, :])
            gn = gn_ref[rs, :]
            gx_ref[rs, :] = gx_ref[rs, :] + norm_back(gn, gain[...], xhat, inv)
            total = total + rows_sum(gn * xhat)
        gx1_copy.start()
        agains_ref[...] = total
        for hop, v in zip(hsecond, HEAD_VIEWS):
            hop.wait()
            h0_ref[:, v.start : v.stop] = hop.total()
        gx1_copy.wait()


def pair_of(s):
    return (s + 2) % 4


def attend_back_call(q, k, v, go, o32, li, p, relo, relx, weights, o16, na, gatt, x1, gx2, gain, mids, cg):
    n, rows, crows = lax.axis_size("dp"), mids[0].shape[1], cg.shape[3]
    high, low = split_axis(n)
    cdims = (high, low, crows, CONV_C)
    hdims = (high, low, rows, 512)
    pair = pl.BlockSpec((SLAB, 128), lambda s: (0, pair_of(s)))
    head_map = pl.BlockSpec((2, SLAB, SLAB), lambda s: (pair_of(s), 0, 0))
    own = lambda s: (0, jnp.maximum(s, 2) - 2)
    oth = lambda s: (0, jnp.minimum(s, 1))
    table_own, table_oth = pl.BlockSpec((2 * RW + 1, 128), own), pl.BlockSpec((2 * RW + 1, 128), oth)
    w_own, w_oth = pl.BlockSpec((D, 128), own), pl.BlockSpec((D, 128), oth)
    return pl.pallas_call(
        attend_back_kernel,
        grid=(D // 128,),
        in_specs=[pair] * 6 + [head_map, table_own, table_oth] + [w_own] * 3 + [w_oth] * 3 + [pair]
        + [ANY] * 4 + [fixed(1, D)] + [fixed(*a.shape) for a in (*mids, cg)],
        out_specs=[pl.BlockSpec((128, 256), lambda s: (pair_of(s), 0)), ANY, fixed(8, D), fixed(rows, 1024),
                   fixed(rows, 1024), fixed(crows, 2 * D), fixed(crows, D), fixed(crows, 128),
                   fixed(rows, 512), fixed(*hdims)],
        out_shape=[
            shape((D, 256), f32),
            shape((SLAB, D), f32),
            shape((8, D), f32),
            shape((rows, 1024), f32),
            shape((rows, 1024), f32),
            shape((crows, 2 * D), f32),
            shape((crows, D), f32),
            shape((crows, 128), f32),
            shape((rows, 512), f32),
            shape(hdims, bf16),
        ],
        scratch_shapes=[
            pltpu.VMEM((2, SLAB, 128), bf16),
            pltpu.VMEM((2, SLAB, 128), bf16),
            pltpu.VMEM((2, SLAB, 128), bf16),
            pltpu.VMEM((128, SLAB), bf16),
            pltpu.VMEM((128, SLAB), bf16),
            pltpu.VMEM((2, SLAB, SLAB), bf16),
            pltpu.VMEM((2, TI, SLAB), f32),
            pltpu.VMEM((2, TI, 256), bf16),
            pltpu.VMEM((2, TI, 256), f32),
            pltpu.VMEM((2, SLAB, 256), bf16),
            pltpu.VMEM((128, SLAB), f32),
            pltpu.VMEM((128, SLAB), f32),
            pltpu.VMEM((SLAB, 128), f32),
            pltpu.VMEM((2, 2, TI, 128), f32),
            pltpu.VMEM((256, 256), bf16),
            pltpu.VMEM((136, 128), f32),
            pltpu.VMEM((256, 128), f32),
            pltpu.VMEM((SLAB, 384), bf16),
            pltpu.VMEM((D, SLAB), bf16),
            pltpu.VMEM((D, SLAB), bf16),
            pltpu.VMEM((2, SLAB, D), bf16),
            pltpu.VMEM((SLAB, D), f32),
            pltpu.VMEM((SLAB, D), f32),
            pltpu.VMEM((SLAB, D), f32),
            pltpu.VMEM((D, 512), f32),
            pltpu.VMEM((2, *hdims), bf16),
            pltpu.VMEM((2, *hdims), bf16),
            pltpu.SemaphoreType.DMA((2, 2)),
            pltpu.VMEM(hdims, bf16),
            pltpu.SemaphoreType.DMA((5,)),
            pltpu.VMEM(cdims, bf16),
            pltpu.SemaphoreType.DMA((2,)),
            pltpu.VMEM(cdims, bf16),
        ]
        + seconds(PAIR_VIEWS, n, rows)
        + firsts(CONV_VIEWS, n, crows)
        + seconds(CONV_VIEWS, n, crows)
        + padded_three([pltpu.VMEM(v.mid(n, crows), bf16) for v in CONV_VIEWS])
        + firsts(HEAD_VIEWS, n, rows)
        + seconds(HEAD_VIEWS, n, rows)
        + padded_three([pltpu.VMEM(v.mid(n, rows), bf16) for v in HEAD_VIEWS]),
        compiler_params=remote(3),
        name="attention_backward",
    )(q, k, v, go, o32, li, p, relo, relx, *weights, o16, na, gatt, x1, gx2, gain, *mids, cg)


PART = 256
PARTS = 4


def last_kernel(gx1_in, x_in, hid_in, w1o_in, w1x_in, w2o_in, w2x_in, g1, sums, agains, acc1, table_ref,
                gx_out, gxx_out, fa_ref, fb_ref, gain0, gain1, gain2, gain3, h1_ref, to_ref,
                gx_ref, x_ref, hid_ref, w1, w2, gb_ref, gbt_ref, nt_ref, n_ref, gact_ref, act_ref, ghid_ref, gn_ref,
                gx16_ref, both_ref, away, back, ssems, gsems, xmine, xback, xsum, xsems, xmid, x1s, x1a, x1b, x2s, x2a, x2b,
                tnear, tback, tsems, tsum, t1, t2, t1s, t1a, t1b, t2s, t2a, t2b, t3s, t3a, t3b, t4s, t4a, t4b, sems, *scr):
    place = Place()
    place.greet(("low", "high"))
    copies = Copies(sems)
    cx = copies.start(x_in.at[pl.ds(pl.multiple_of(place.core * SLAB, SLAB), SLAB)], x_ref)
    cg = copies.start(gx1_in, gx_ref)
    cw = [copies.start(a, b) for a, b in (
        (w2x_in, w2.at[0]), (hid_in.at[0], hid_ref.at[0]), (w1x_in, w1.at[0]),
        (w2o_in, w2.at[1]), (hid_in.at[1], hid_ref.at[1]), (w1o_in, w1.at[1]))]
    refs = threes(scr)
    nh = len(HEAD_VIEWS)

    def chain(acc):
        nonlocal refs
        first = [v.first(place, acc, r) for v, r in zip(HEAD_VIEWS, refs)]
        mids = refs[2 * nh][:nh]
        second = [v.second(place, mid, r) for v, mid, r in zip(HEAD_VIEWS, mids, refs[nh:])]
        refs = refs[2 * nh + 1 :]
        return first, mids, second

    def chain_split(accs):
        nonlocal refs
        first = [v.whole_first(place, a, r) for v, a, r in zip(HEAD_VIEWS, accs, refs)]
        mids = refs[2 * nh][:nh]
        second = [v.second(place, mid, r) for v, mid, r in zip(HEAD_VIEWS, mids, refs[nh:])]
        refs = refs[2 * nh + 1 :]
        return first, mids, second

    heads = chain(acc1)
    accs, chains = [], []
    for k in range(PARTS):
        accs.append(refs[0][:nh])
        refs = refs[1:]
        chains.append(chain_split(accs[k]))

    def begin(chain):
        for hop in chain[0]:
            hop.start()

    def turn(chain):
        for hop, mid, on in zip(*chain):
            hop.wait()
            mid[...] = hop.total().astype(bf16)
            on.start()

    tswap = core_copy(place, tnear.at[1], tback, tsems)
    scatter1 = Hop(place, "low", lambda p: tsum.at[:, p], t1s, t1a, t1b)
    scatter2 = Hop(place, "high", lambda p: t1.at[p], t2s, t2a, t2b)
    gather1 = Hop(place, "high", lambda p: t2, t3s, t3a, t3b)
    gather2 = Hop(place, "low", lambda p: t3s, t4s, t4a, t4b)
    xswap = core_copy(place, xmine, xback, xsems)
    xhop1 = Hop(place, "low", lambda p: xsum, x1s, x1a, x1b)
    xhop2 = Hop(place, "high", lambda p: xmid, x2s, x2a, x2b)
    swaps = [core_copy(place, away.at[k], back.at[k], ssems.at[k]) for k in range(PARTS)]

    slot = lax.broadcasted_iota(jnp.int32, (256, 128), 1)
    diagonal = (lax.broadcasted_iota(jnp.int32, (256, 128), 0) & 127) == slot
    for half in (0, 1):
        block = table_ref[half].reshape(256, 256)
        far = block[:, 128:]
        left = far[:, 0:1] + far[:, 1:2]
        right = far[:, 2:3] + far[:, 3:4]
        tnear[half] = (block[:, :128] + jnp.where(slot == 127, left, 0.0)).reshape(tnear.shape[1:])
        spread = jnp.where(diagonal, right, 0.0)
        for r in (0, 1):
            at = 4 * LT + 2 * half + r
            xmine[at : at + 1, :] = jnp.sum(spread[r * 128 : (r + 1) * 128], 0, keepdims=True)
    place.greeted(("low", "high"))
    tswap.start()
    begin(heads)
    cx.wait()
    for rs in row_tiles(SLAB):
        xhat, _ = norm_parts(x_ref[rs, :].astype(f32))
        n_ref[rs, :] = (xhat * g1[...]).astype(bf16)
    transpose_into(nt_ref, n_ref)
    tswap.wait()
    tsum[...] = tnear[0] + tback[...]
    scatter1.start()
    cg.wait()
    for rs in row_tiles(SLAB):
        gb_ref[rs, :] = (0.5 * gx_ref[rs, :]).astype(bf16)
    transpose_into(gbt_ref, gb_ref)
    for copy in cw:
        copy.wait()
    dims = away.shape[1:]
    half_dims = (*dims[:3], PART)

    order = [(0, 0), (0, 1), (1, 0), (0, 2), (1, 1), (0, 3), (1, 2), (1, 3)]

    def up(i):
        p, k = order[i]
        gact_ref[i % 2] = dot_nt(gb_ref[...], w2[p, k * PART : (k + 1) * PART, :])

    def weigh(i):
        p, k = order[i]
        for rs in row_tiles(SLAB):
            hid = hid_ref[p, rs, k * PART : (k + 1) * PART].astype(f32)
            sg = jax.nn.sigmoid(hid)
            act = hid * sg
            act_ref[rs, :] = act.astype(bf16)
            ghid_ref[rs, :] = (gact_ref[i % 2, rs, :] * (sg + act * (1.0 - sg))).astype(bf16)

    def down(i):
        p, k = order[i]
        part = dot_nt(ghid_ref[...], w1[p, :, k * PART : (k + 1) * PART])
        if i == 0:
            gn_ref[...] = part
        else:
            gn_ref[...] += part
        return dot(nt_ref[...], ghid_ref[...]), dot(gbt_ref[...], act_ref[...])

    up(0)
    for i, (p, k) in enumerate(order):
        weigh(i)
        if i + 1 < len(order):
            up(i + 1)
        left, right = down(i)
        if p == 0:
            away[k, :, :, :, :PART] = left.reshape(half_dims).astype(bf16)
            away[k, :, :, :, PART:] = right.reshape(half_dims).astype(bf16)
            swaps[k].start()
        else:
            swaps[k].wait()
            left = left.reshape(half_dims) + back[k, :, :, :, :PART].astype(f32)
            right = right.reshape(half_dims) + back[k, :, :, :, PART:].astype(f32)
            accs[k][0][:, :, :, :PART] = left.astype(bf16)
            accs[k][0][:, :, :, PART:] = right[:, :, :, : 384 - PART].astype(bf16)
            accs[k][1][...] = right[:, :, :, 384 - PART :].astype(bf16)
            begin(chains[k])
        if i == 1:
            scatter1.wait()
            t1[...] = scatter1.total()
            scatter2.start()
        elif i == 2:
            scatter2.wait()
            t2[...] = scatter2.total()
            t3s[place.hi] = t2[...]
            gather1.start()
            turn(heads)
        elif i == 3:
            gather1.wait()
            t4s[place.lo] = t3s[...]
            gather2.start()
        elif i == 5:
            turn(chains[0])
        elif i == 7:
            turn(chains[1])

    ffn_gain = jnp.zeros((8, D), f32)
    for rs in row_tiles(SLAB):
        xhat, inv = norm_parts(x_ref[rs, :].astype(f32))
        gn = gn_ref[rs, :]
        gx16_ref[rs, :] = (gx_ref[rs, :] + norm_back(gn, g1[...], xhat, inv)).astype(bf16)
        ffn_gain = ffn_gain + rows_sum(gn * xhat)
    gains = (
        jnp.sum(ffn_gain, 0, keepdims=True),
        jnp.sum(agains[...], 0, keepdims=True),
        sums[5:6, :],
        sums[4:5, :],
    )
    for r, g in enumerate(gains):
        for c in range(LT):
            xmine[r * LT + c : r * LT + c + 1, :] = g[:, c * 128 : (c + 1) * 128]
    xmine[4 * LT + 4 :, :] = jnp.zeros((4, 128), f32)
    xswap.start()
    out_copy = copies.start(gx16_ref, gx_out)
    gxswap = core_copy(place, gx16_ref, gxx_out, gsems)
    gxswap.start()
    xswap.wait()
    xsum[...] = xmine[...] + xback[...]
    at = 4 * LT
    xsum[at : at + 2, :] = xmine[at : at + 2, :] + xback[at + 2 : at + 4, :]
    x1s[place.lo] = xsum[...]
    xhop1.start()
    turn(chains[PARTS - 2])
    xhop1.wait()
    xmid[...] = slot_sum(x1s, place.low)
    x2s[place.hi] = xmid[...]
    xhop2.start()
    turn(chains[PARTS - 1])
    for hop, v in zip(heads[2], HEAD_VIEWS):
        hop.wait()
        h1_ref[:, v.start : v.stop] = hop.total()
    gather2.wait()
    xhop2.wait()
    total = slot_sum(x2s, place.high)
    for r, ref in enumerate((gain0, gain1, gain2, gain3)):
        for c in range(LT):
            ref[:, c * 128 : (c + 1) * 128] = total[r * LT + c : r * LT + c + 1, :]
    line = lax.broadcasted_iota(jnp.int32, (128, 128), 0)
    choice = jnp.where(line + lax.broadcasted_iota(jnp.int32, (128, 128), 1) == 127, 1.0, 0.0)
    tall = jnp.stack([t4s[l, h] for h in range(place.high) for l in range(place.low)]).reshape(256, 128)
    to_ref[: 2 * RW, :] = lax.dot_general(
        choice, tall, (((1,), (1,)), ((), ())), preferred_element_type=f32, precision=lax.Precision.HIGHEST
    )
    for r in (0, 1):
        to_ref[2 * RW : 2 * RW + 1, r * 128 : (r + 1) * 128] = total[at + r : at + r + 1, :]
    for k in range(PARTS):
        for hop, v in zip(chains[k][2], HEAD_VIEWS):
            hop.wait()
            both_ref[:, v.start : v.stop] = hop.total()
        fa_ref[:, k * PART : (k + 1) * PART] = both_ref[:, :PART]
        fb_ref[:, k * PART : (k + 1) * PART] = both_ref[:, PART:]
    out_copy.wait()
    gxswap.wait()


def padded_three(refs):
    return refs + [pltpu.SemaphoreType.DMA((1,))] * (-len(refs) % 3)


def last_call(gx1, frames, hid, w1o, w1x, w2o, w2x, g1, sums, agains, acc1, table):
    width = w1o.shape[1]
    n, dims = grad_dims(2 * PART)
    rows = dims[2]
    high, low = split_axis(n)
    trows = table.shape[3]
    gains = (4 * LT + 8, 128)
    link = firsts(HEAD_VIEWS, n, rows) + seconds(HEAD_VIEWS, n, rows)
    link = link + padded_three([pltpu.VMEM(v.mid(n, rows), bf16) for v in HEAD_VIEWS])
    part = padded_three([pltpu.VMEM((*dims[:3], v.width), bf16) for v in HEAD_VIEWS]) + link
    return pl.pallas_call(
        last_kernel,
        in_specs=[ANY] * 7 + [VMEM] * 5,
        out_specs=[ANY] * 2 + [VMEM] * 8,
        out_shape=[
            shape((SLAB, D), bf16),
            shape((SLAB, D), bf16),
            shape((rows, width), f32),
            shape((rows, width), f32),
        ]
        + [shape((1, D), f32)] * 4
        + [shape((rows, 512), f32), shape((2 * RW + 1, 256), f32)],
        scratch_shapes=[
            pltpu.VMEM((SLAB, D), f32),
            pltpu.VMEM((SLAB, D), bf16),
            pltpu.VMEM((2, SLAB, width), bf16),
            pltpu.VMEM((2, D, width), bf16),
            pltpu.VMEM((2, width, D), bf16),
            pltpu.VMEM((SLAB, D), bf16),
            pltpu.VMEM((D, SLAB), bf16),
            pltpu.VMEM((D, SLAB), bf16),
            pltpu.VMEM((SLAB, D), bf16),
            pltpu.VMEM((2, SLAB, PART), f32),
            pltpu.VMEM((SLAB, PART), bf16),
            pltpu.VMEM((SLAB, PART), bf16),
            pltpu.VMEM((SLAB, D), f32),
            pltpu.VMEM((SLAB, D), bf16),
            pltpu.VMEM((rows, 2 * PART), f32),
            pltpu.VMEM((PARTS, *dims), bf16),
            pltpu.VMEM((PARTS, *dims), bf16),
            pltpu.SemaphoreType.DMA((PARTS, 2)),
            pltpu.SemaphoreType.DMA((2,)),
            pltpu.VMEM(gains, f32),
            pltpu.VMEM(gains, f32),
            pltpu.VMEM(gains, f32),
            pltpu.SemaphoreType.DMA((2,)),
            pltpu.VMEM(gains, f32),
        ]
        + slots_of(low, gains, f32)
        + slots_of(high, gains, f32)
        + [
            pltpu.VMEM((2, high, low, trows, 128), f32),
            pltpu.VMEM((high, low, trows, 128), f32),
            pltpu.SemaphoreType.DMA((2,)),
            pltpu.VMEM((high, low, trows, 128), f32),
            pltpu.VMEM((high, trows, 128), f32),
            pltpu.VMEM((trows, 128), f32),
        ]
        + slots_of(low, (high, trows, 128), f32)
        + slots_of(high, (trows, 128), f32)
        + slots_of(high, (trows, 128), f32)
        + slots_of(low, (high, trows, 128), f32)
        + [pltpu.SemaphoreType.DMA((10,))]
        + link
        + part * PARTS,
        compiler_params=remote(4),
        name="ffn1_backward",
    )(gx1, frames, hid, w1o, w1x, w2o, w2x, g1, sums, agains, acc1, table)


def results_kernel(out_own, out_oth, gx_own, gx_oth, *refs):
    count = len(SMALL)
    smalls, (out_ref, gx_out), outs, (load_ref, gx_ref, sems) = (
        refs[:count], refs[count : count + 2], refs[count + 2 : -3], refs[-3:]
    )
    core = lax.axis_index("mp")
    own = pl.ds(pl.multiple_of(core * SLAB, SLAB), SLAB)
    oth = pl.ds(pl.multiple_of((1 - core) * SLAB, SLAB), SLAB)
    copies = Copies(sems)
    loads = [copies.start(gx_own, load_ref.at[0]), copies.start(gx_oth, load_ref.at[1])]
    loads += [copies.start(out_own, load_ref.at[2]), copies.start(out_oth, load_ref.at[3])]
    ends = []
    for k, rows in ((0, own), (1, oth)):
        loads[k].wait()
        for rs in row_tiles(SLAB):
            gx_ref[k, rs, :] = load_ref[k, rs, :].astype(f32)
        ends.append(copies.start(gx_ref.at[k], gx_out.at[rows]))
    for k, rows in ((2, own), (3, oth)):
        loads[k].wait()
        ends.append(copies.start(load_ref.at[k], out_ref.at[rows]))
    (f1a, f1b, f2a, f2b, h0, h1, cpi, cpo, crest, table, gain0, gain1, gain2, gain3) = smalls
    (of1a, of1b, of2a, of2b, oq, ok, ov, oo, ocpi, ocpo, ock, ov0, ov1, ov2, otable, og0, og1, og2, og3) = outs
    for dst, src in ((of1a, f1a), (of1b, f1b), (of2a, f2a), (of2b, f2b), (ocpi, cpi), (ocpo, cpo), (otable, table),
                     (og0, gain0), (og1, gain1), (og2, gain2), (og3, gain3)):
        dst[...] = src[...]
    for n, dst in enumerate((oq, ok, ov, oo)):
        dst[:, :128] = h0[:, n * 128 : (n + 1) * 128]
        dst[:, 128:] = h1[:, n * 128 : (n + 1) * 128]
    ock[...] = crest[:, :TAPS]
    across = crest[...].T
    for n, dst in enumerate((ov0, ov1, ov2)):
        dst[...] = across[TAPS + n : TAPS + n + 1, :]
    for copy in ends:
        copy.wait()


SMALL = range(14)


def results(out, out_oth, gx, gx_oth, smalls):
    rows, crows = smalls[0].shape[0], smalls[6].shape[0]
    outs = [shape(a.shape, f32) for a in smalls[:4]]
    outs += [shape((rows, D // 2), f32)] * 4
    outs += [shape((crows, 2 * D), f32), shape((crows, D), f32), shape((crows, TAPS), f32)]
    outs += [shape((1, crows), f32)] * 3 + [shape(a.shape, f32) for a in smalls[9:]]
    return pl.pallas_call(
        results_kernel,
        in_specs=[ANY] * 4 + [VMEM] * len(smalls),
        out_specs=[ANY] * 2 + [VMEM] * len(outs),
        out_shape=[shape((2 * SLAB, D), bf16), shape((2 * SLAB, D), f32)] + outs,
        scratch_shapes=[
            pltpu.VMEM((4, SLAB, D), bf16),
            pltpu.VMEM((2, SLAB, D), f32),
            pltpu.SemaphoreType.DMA((8,)),
        ],
        compiler_params=pltpu.CompilerParams(vmem_limit_bytes=60 << 20),
        name="results",
    )(out, out_oth, gx, gx_oth, *smalls)


def shards(
    frames, lengths, cotangent, ffn1_gain, ffn1_in, ffn1_out, attn_gain, query_weight, key_weight,
    value_weight, out_weight, rel_table, conv_gain, pointwise_in, conv_kernel, bn_gain, bn_bias,
    pointwise_out, ffn2_gain, ffn2_in, ffn2_out, final_gain,
):
    n = lax.axis_size("dp")
    high, low = split_axis(n)
    column = jnp.arange(128 - TAPS)[None, :]
    vectors = sum(
        jnp.where(column == k, v[:, None], 0) for k, v in enumerate((conv_gain, bn_gain, bn_bias))
    ).astype(bf16)
    g1, ga, g2, gf = (g[None, :] for g in (ffn1_gain, attn_gain, ffn2_gain, final_gain))
    qkvo = (query_weight, key_weight, value_weight)

    x1, hid1, na, q, k, v, w1x, w2x, wqx, wkx, wvx, v1x, v2x, wox, relx = first_call(
        frames, g1, ga, ffn1_in, ffn1_out, *qkvo, ffn2_in, ffn2_out, out_weight, rel_table
    )
    o16, o32, li, p, gathered = attend_call(
        lengths, q, k, v, rel_table, relx, pointwise_in, pointwise_out, conv_kernel, vectors
    )
    gathered = gathered.reshape(D, CONV_C)
    x2, u, hd, gp, st, taps = conv_call(lengths, x1, o16, out_weight, wox, gathered)
    out, gx3, gz, acc2, gpw, back, sums = middle_call(
        lengths, hd, x2, cotangent, st, taps, gathered, g2, ffn2_in, v1x, ffn2_out, v2x, gf
    )
    gx2, gatt, go, conv_g, *mids = conv_back_call(
        lengths, acc2, gz, hd, gp, st, back, taps, u, x2, gx3, gathered, out_weight, wox, gpw, sums
    )
    conv_g = conv_g.reshape(high, low, 2, D // n // 2, CONV_C)
    gtab, gx1, agains, f2a, f2b, cpi, cpo, crest, h0, acc1 = attend_back_call(
        q, k, v, go, o32, li, p, rel_table, relx, (*qkvo, wqx, wkx, wvx), o16, na, gatt, x1, gx2, ga, mids, conv_g
    )
    gx, gx_oth, f1a, f1b, gain0, gain1, gain2, gain3, h1, table = last_call(
        gx1, frames, hid1, ffn1_in, w1x, ffn1_out, w2x, g1, sums, agains, acc1,
        gtab.reshape(2, high, low, D // 2 // n, 256),
    )
    (block_output, frames_grad, f1a, f1b, f2a, f2b, q_grad, k_grad, v_grad, o_grad, cpi, cpo, ck, cg, bg, bb,
     table, gain0, gain1, gain2, gain3) = results(
        out, lax.ppermute(out, "mp", [(0, 1), (1, 0)]), gx, gx_oth,
        (f1a, f1b, f2a, f2b, h0, h1, cpi, cpo, crest, table, gain0, gain1, gain2, gain3),
    )
    return (
        block_output, frames_grad, gain0[0], f1a, f1b.T, gain1[0], q_grad, k_grad, v_grad, o_grad.T, table, cg[0],
        cpi, ck, bg[0], bb[0], cpo, gain2[0], f2a, f2b.T, gain3[0],
    )


def solution(mesh):
    return jax.shard_map(
        shards,
        mesh=mesh,
        in_specs=(
            P("dp", None), P("dp", None), P("dp", None), P(), P(None, "mp"), P("mp", None), P(),
            P(None, "mp"), P(None, "mp"), P(None, "mp"), P("mp", None), P(None, "mp"),
            P(("dp", "mp")), P(("dp", "mp"), None), P(("dp", "mp"), None), P(("dp", "mp")),
            P(("dp", "mp")), P(("dp", "mp"), None), P(), P(None, "mp"), P("mp", None), P(),
        ),
        out_specs=(
            P("dp", None), P("dp", None), P(), P("dp", "mp"), P("mp", "dp"), P(), P("dp", "mp"),
            P("dp", "mp"), P("dp", "mp"), P("mp", "dp"), P(None, "mp"), P(("dp", "mp")),
            P(("dp", "mp"), None), P(("dp", "mp"), None), P(("dp", "mp")), P(("dp", "mp")),
            P(("dp", "mp"), None), P(), P("dp", "mp"), P("mp", "dp"), P(),
        ),
        check_vma=False,
    )
```

```python
import jax
import jax.numpy as jnp
from jax import lax
from jax.experimental import pallas as pl
from jax.experimental.pallas import tpu as pltpu
from jax.sharding import PartitionSpec as P

D = 512
DH = 64
RW = 64
SLAB = 1152
TAPS = 32
NORM_EPS = 1e-05
BATCH_EPS = 1e-05
MASKED = -1e30

SUB = 64
GAP = 16
TOP = 32
PADDED = 1216
CH = 64
LT = D // 128

f32 = jnp.float32
bf16 = jnp.bfloat16


def params(mib=60):
    return pltpu.CompilerParams(
        dimension_semantics=("arbitrary",), vmem_limit_bytes=mib << 20
    )


def dot(a, b):
    return jnp.dot(a, b, preferred_element_type=f32)


def dot_nt(a, b):
    return lax.dot_general(a, b, (((1,), (1,)), ((), ())), preferred_element_type=f32)


def dot_tn(a, b):
    return lax.dot_general(a, b, (((0,), (0,)), ((), ())), preferred_element_type=f32)


def norm_parts(v):
    c = v - jnp.mean(v, -1, keepdims=True)
    inv = lax.rsqrt(jnp.mean(c * c, -1, keepdims=True) + NORM_EPS)
    return c * inv, inv


def norm_back(gy, gain, xhat, inv):
    e = gy * gain
    inner = jnp.mean(e * xhat, -1, keepdims=True)
    return inv * (e - jnp.mean(e, -1, keepdims=True) - xhat * inner)


def rows_sum(v):
    return jnp.sum(v.reshape(v.shape[0] // 8, 8, v.shape[1]), 0)


def fixed(*shape):
    zeros = (0,) * len(shape)
    return pl.BlockSpec(shape, lambda i, *m: zeros)


SMEM = pl.BlockSpec(memory_space=pltpu.SMEM)
VMEM = pl.BlockSpec(memory_space=pltpu.VMEM)


def shape(dims, dtype):
    return jax.ShapeDtypeStruct(dims, dtype)


MESH = pl.DeviceIdType.MESH


def split_axis(n):
    low = 4 if n % 4 == 0 else 1
    return n // low, low


class Place:
    def __init__(self):
        self.n = lax.axis_size("dp")
        self.high, self.low = split_axis(self.n)
        self.me = lax.axis_index("dp")
        self.core = lax.axis_index("mp")
        self.hi = self.me // self.low
        self.lo = self.me % self.low

    def size(self, kind):
        return {"all": self.n, "low": self.low, "high": self.high}[kind]

    def mine(self, kind):
        return {"all": self.me, "low": self.lo, "high": self.hi}[kind]

    def peer(self, kind, j):
        at = (self.mine(kind) + j) % self.size(kind)
        if kind == "low":
            return at, {"dp": self.hi * self.low + at}
        if kind == "high":
            return at, {"dp": at * self.low + self.lo}
        return at, {"dp": at}

    def each(self, kind, do):
        size = self.size(kind)
        if size <= 4:
            for j in range(1, size):
                do(j)
        else:

            def body(j, carry):
                do(j)
                return carry

            lax.fori_loop(1, size, body, 0)

    def greet(self, kinds, core=True):
        barrier = pltpu.get_barrier_semaphore()
        for kind in kinds:
            self.each(
                kind,
                lambda j: pl.semaphore_signal(
                    barrier, inc=1, device_id=self.peer(kind, j)[1], device_id_type=MESH
                ),
            )
        if core:
            pl.semaphore_signal(barrier, inc=1, device_id={"mp": 1 - self.core}, device_id_type=MESH)

    def greeted(self, kinds, core=True):
        count = sum(self.size(kind) - 1 for kind in kinds) + (1 if core else 0)
        if count:
            pl.semaphore_wait(pltpu.get_barrier_semaphore(), count)


class Hop:
    def __init__(self, place, kind, piece, slots, send, recv):
        self.place, self.kind, self.piece = place, kind, piece
        self.slots, self.send, self.recv = slots, send, recv

    def copy(self, j, slot):
        at, device = self.place.peer(self.kind, j)
        return pltpu.make_async_remote_copy(
            src_ref=self.piece(at), dst_ref=self.slots.at[slot], send_sem=self.send.at[j],
            recv_sem=self.recv.at[slot], device_id=device, device_id_type=MESH,
        )

    def start(self):
        mine = self.place.mine(self.kind)
        self.place.each(self.kind, lambda j: self.copy(j, mine).start())

    def wait(self):
        self.place.each(self.kind, lambda j: self.copy(j, self.place.peer(self.kind, j)[0]).wait())

    def total(self):
        total = self.piece(self.place.mine(self.kind))[...].astype(f32)
        size = self.place.size(self.kind)
        if size <= 4:
            for j in range(1, size):
                total = total + self.slots[self.place.peer(self.kind, j)[0]].astype(f32)
            return total
        return lax.fori_loop(
            1, size, lambda j, t: t + self.slots[self.place.peer(self.kind, j)[0]].astype(f32), total
        )


def core_copy(place, src, dst, sems):
    return pltpu.make_async_remote_copy(
        src_ref=src, dst_ref=dst, send_sem=sems.at[0], recv_sem=sems.at[1],
        device_id={"mp": 1 - place.core}, device_id_type=MESH,
    )


def slots_of(size, dims, dtype=bf16):
    return [
        pltpu.VMEM((size, *dims), dtype),
        pltpu.SemaphoreType.DMA((size,)),
        pltpu.SemaphoreType.DMA((size,)),
    ]


class View:
    def __init__(self, index, start, stop, order):
        self.index, self.start, self.stop, self.order = index, start, stop, order
        self.width = stop - start

    def kinds(self):
        return ("low", "high") if self.order == "low" else ("high", "low")

    def mid(self, n, rows):
        high, low = split_axis(n)
        return (high if self.order == "low" else low, rows, self.width)

    def first_scratch(self, n, rows):
        high, low = split_axis(n)
        return slots_of(low if self.order == "low" else high, self.mid(n, rows))

    def second_scratch(self, n, rows):
        size, *dims = self.mid(n, rows)
        return slots_of(size, dims)

    def first(self, place, acc, refs):
        cols = slice(self.start, self.stop)
        if self.index is not None:
            acc = acc.at[self.index]
        if self.order == "low":
            piece = lambda p: acc.at[:, p, :, cols]
        else:
            piece = lambda p: acc.at[p, :, :, cols]
        return Hop(place, self.kinds()[0], piece, *refs)

    def whole_first(self, place, acc, refs):
        if self.order == "low":
            return Hop(place, "low", lambda p: acc.at[:, p], *refs)
        return Hop(place, "high", lambda p: acc.at[p], *refs)

    def second(self, place, mid, refs):
        return Hop(place, self.kinds()[1], lambda p: mid.at[p], *refs)


PAIR_VIEWS = (View(0, 0, 1024, "low"), View(1, 0, 384, "low"), View(1, 384, 1024, "high"))
CONV_C = 2 * D + D + 128
CONV_VIEWS = (View(None, 0, 1024, "low"), View(None, 1024, CONV_C, "high"))


def firsts(views, n, rows):
    return [ref for v in views for ref in v.first_scratch(n, rows)]


def seconds(views, n, rows):
    return [ref for v in views for ref in v.second_scratch(n, rows)]


def threes(refs):
    return [refs[i : i + 3] for i in range(0, len(refs), 3)]


def remote(collective_id, mib=60):
    return pltpu.CompilerParams(
        vmem_limit_bytes=mib << 20, collective_id=collective_id, has_side_effects=True,
    )


def slot_sum(slots, n):
    return lax.fori_loop(1, n, lambda j, total: total + slots[j], slots[0])


TR = 128
UP = 512


def row_tiles(rows):
    return [slice(r, r + TR) for r in range(0, rows, TR)]


def tiles(rows, cols, width=256):
    return [(rs, slice(c, c + width)) for rs in row_tiles(rows) for c in range(0, cols, width)]


def transpose_into(dst, src):
    for r in range(0, src.shape[0], 128):
        dst[:, r : r + 128] = src[r : r + 128, :].astype(f32).T.astype(bf16)


class Copies:
    def __init__(self, sems):
        self.sems, self.count = sems, 0

    def start(self, src, dst):
        copy = pltpu.make_async_copy(src, dst, self.sems.at[self.count])
        self.count += 1
        copy.start()
        return copy


ANY = pl.BlockSpec(memory_space=pl.ANY)


def bounds(len_ref, place):
    first = len_ref[place.core, 0]
    return first, first + len_ref[place.core, 1]


def first_kernel(x_in, g1, ga, pin, pout, ck, vec, w1_in, w2_in, wq_in, wk_in, wv_in, v1_in, v2_in, wo_in, rel_in,
                 x1_out, hid_out, na_out, q_out, k_out, v_out,
                 w1_out, w2_out, wq_out, wk_out, wv_out, v1_out, v2_out, wo_out, rel_out, far_out,
                 x_ref, w1, w2, wqkv, n_ref, act_ref, hid_ref, hid16_ref, x1_ref, na_ref, qkv_ref, sems, rsems, piece_ref, far_ref, fsend, frecv):
    place = Place()
    place.greet(("high",))
    copies = Copies(sems)
    cx = copies.start(x_in.at[pl.ds(pl.multiple_of(place.core * SLAB, SLAB), SLAB)], x_ref)
    qkv_in = (wq_in, wk_in, wv_in)
    mine = [copies.start(w1_in, w1.at[1]), copies.start(w2_in, w2.at[1])]
    mine_qkv = [copies.start(a, wqkv.at[1, k]) for k, a in enumerate(qkv_in)]
    piece_ref[:, : 2 * D] = pin[...]
    piece_ref[:, 2 * D : 3 * D] = pout[...]
    piece_ref[:, 3 * D :] = jnp.concatenate([ck[...], vec[...]], 1)
    far = Hop(place, "high", lambda p: piece_ref, far_ref, fsend, frecv)
    pairs = [(w1_in, w1.at[0]), (w2_in, w2.at[0])] + [(a, wqkv.at[0, k]) for k, a in enumerate(qkv_in)]
    pairs += [(v1_in, v1_out), (v2_in, v2_out), (wo_in, wo_out), (rel_in, rel_out)]
    swaps = [core_copy(place, a, b, rsems.at[k]) for k, (a, b) in enumerate(pairs)]
    cx.wait()
    for rs in row_tiles(SLAB):
        xhat, _ = norm_parts(x_ref[rs, :].astype(f32))
        n_ref[rs, :] = (xhat * g1[...]).astype(bf16)
    for copy in mine:
        copy.wait()
    chunks = [(p, c) for p in (1, 0) for c in range(0, w1.shape[2], UP)]
    ends = []

    def up(k):
        p, c = chunks[k]
        hid_ref[k % 2] = dot(n_ref[...], w1[p, :, c : c + UP])

    def down(k):
        p, c = chunks[k]
        part = dot(act_ref[k % 2], w2[p, c : c + UP, :])
        if k == 0:
            x1_ref[...] = part
        else:
            x1_ref[...] += part

    up(0)
    place.greeted(("high",))
    for copy in swaps[:5]:
        copy.start()
    far.start()
    for k, (p, c) in enumerate(chunks):
        for rs, cs in tiles(SLAB, UP):
            hid = hid_ref[k % 2, rs, cs]
            hid16_ref[p, rs, c + cs.start : c + cs.stop] = hid.astype(bf16)
            act_ref[k % 2, rs, cs] = (hid * jax.nn.sigmoid(hid)).astype(bf16)
        if k + 1 < len(chunks):
            if k + 1 == len(chunks) // 2:
                for copy in swaps[:5]:
                    copy.wait()
                for copy in swaps[5:]:
                    copy.start()
                ends.append(copies.start(hid16_ref.at[1], hid_out.at[1]))
                ends += [copies.start(w1.at[0], w1_out), copies.start(w2.at[0], w2_out)]
                ends += [copies.start(wqkv.at[0, n], out) for n, out in enumerate((wq_out, wk_out, wv_out))]
            up(k + 1)
        if k > 0:
            down(k - 1)
    ends.append(copies.start(hid16_ref.at[0], hid_out.at[0]))
    down(len(chunks) - 1)
    for rs in row_tiles(SLAB):
        x1 = x_ref[rs, :].astype(f32) + 0.5 * x1_ref[rs, :]
        x1_ref[rs, :] = x1
        xhat, _ = norm_parts(x1)
        na_ref[rs, :] = (xhat * ga[...]).astype(bf16)
    ends += [copies.start(x1_ref, x1_out), copies.start(na_ref, na_out)]
    for copy in mine_qkv:
        copy.wait()
    w = D // 2
    for n, out in enumerate((q_out, k_out, v_out)):
        for p in (0, 1):
            value = dot(na_ref[...], wqkv[p, n]).astype(bf16)
            if n == 0:
                value = (value.astype(f32) * DH**-0.5).astype(bf16)
            qkv_ref[n, :, (1 - p) * w : (2 - p) * w] = value
        ends.append(copies.start(qkv_ref.at[n], out))
    far.wait()
    far_ref[place.hi] = piece_ref[...]
    far_out[...] = far_ref[...]
    for copy in swaps[5:] + ends:
        copy.wait()


def first_call(frames, g1, ga, pin, pout, ck, vec, w1, w2, wq, wk, wv, v1, v2, wo, rel):
    hid = w1.shape[1]
    moved = (w1, w2, wq, wk, wv, v1, v2, wo, rel)
    high, _ = split_axis(lax.axis_size("dp"))
    piece = (pin.shape[0], CONV_C)
    return pl.pallas_call(
        first_kernel,
        in_specs=[ANY] + [VMEM] * 6 + [ANY] * 9,
        out_specs=[ANY] * 15 + [VMEM],
        out_shape=[shape((SLAB, D), f32), shape((2, SLAB, hid), bf16)]
        + [shape((SLAB, D), bf16)] * 4
        + [shape(a.shape, a.dtype) for a in moved]
        + [shape((high, *piece), bf16)],
        scratch_shapes=[
            pltpu.VMEM((SLAB, D), bf16),
            pltpu.VMEM((2, D, hid), bf16),
            pltpu.VMEM((2, hid, D), bf16),
            pltpu.VMEM((2, 3, D, D // 2), bf16),
            pltpu.VMEM((SLAB, D), bf16),
            pltpu.VMEM((2, SLAB, UP), bf16),
            pltpu.VMEM((2, SLAB, UP), f32),
            pltpu.VMEM((2, SLAB, hid), bf16),
            pltpu.VMEM((SLAB, D), f32),
            pltpu.VMEM((SLAB, D), bf16),
            pltpu.VMEM((3, SLAB, D), bf16),
            pltpu.SemaphoreType.DMA((20,)),
            pltpu.SemaphoreType.DMA((9, 2)),
            pltpu.VMEM(piece, bf16),
        ]
        + slots_of(high, piece),
        compiler_params=remote(5),
        name="ffn1_forward",
    )(frames, g1, ga, pin, pout, ck, vec, *moved)


TI = 384
STAGES = [(h, start) for h in (0, 1) for start in range(0, SLAB, TI)]


def low_lanes(rows, cols=128):
    return lax.broadcasted_iota(jnp.int32, (rows, cols), 1) < 64


def attend_kernel(len_ref, q_ref, k_ref, v_ref, relo_ref, relx_ref, far_ref,
                  o16_ref, o32_ref, li_ref, p_ref, all_ref, qa_ref, ka_ref, va_ref, e_ref, rel_ref, s_ref, near_s, far_s, top_s,
                  near_ref, nsend, nrecv, other_ref, osems):
    step = pl.program_id(0)
    place = Place()
    near = Hop(place, "low", lambda p: far_ref, near_ref, nsend, nrecv)
    across = core_copy(place, near_ref, other_ref, osems)

    @pl.when(step == 0)
    def _():
        place.greet(("low",))

    b1, b2 = bounds(len_ref, place)
    lane = lax.broadcasted_iota(jnp.int32, (SLAB, 128), 1)
    slot = lane & 63
    frame = lax.broadcasted_iota(jnp.int32, (SLAB, 128), 0)
    label = jnp.where(frame < b1, 0, jnp.where(frame < b2, 1, 2))
    mq = jnp.where((slot < 3) & (slot != label), MASKED, 0.0)
    mk = jnp.where(slot == label, 1.0, 0.0)
    rel_ref[: 2 * RW + 1, :] = jnp.where(step < 2, relo_ref[...].astype(f32), relx_ref[...].astype(f32))
    rel_ref[2 * RW + 1 :, :] = jnp.broadcast_to(rel_ref[2 * RW : 2 * RW + 1, :], (255 - 2 * RW, 128))
    q, k, v = (ref[...].astype(f32) for ref in (q_ref, k_ref, v_ref))
    for h in (0, 1):
        mine = (lane < 64) if h == 0 else (lane >= 64)
        qa_ref[h] = jnp.where(mine, q, mq).astype(bf16)
        ka_ref[h] = jnp.where(mine, k, mk).astype(bf16)
        va_ref[h] = jnp.where(mine, v, 1.0).astype(bf16)
        rel_mine = low_lanes(256) if h == 0 else jnp.logical_not(low_lanes(256))
        relz = jnp.where(rel_mine, rel_ref[...], 0.0).astype(bf16)
        e_ref[h] = dot_nt(qa_ref[h], relz)
    subl = lax.broadcasted_iota(jnp.int32, (SUB, 128), 1)
    line = lax.broadcasted_iota(jnp.int32, (SUB, 128), 0)
    left_of = {0: subl < line, 64: subl < line + 64}
    tiles = SLAB // 128

    def scores(t):
        h, start = STAGES[t]
        s_ref[t % 3] = dot_nt(qa_ref[h, start : start + TI, :], ka_ref[h])

    def shift(t):
        h, start = STAGES[t]
        for r in range(0, TI, SUB):
            b = (start + r) // SUB
            off = 64 if b % 2 == 0 else 0
            rows = slice(r, r + SUB)
            eb = e_ref[h, b * SUB : (b + 1) * SUB, :]
            near = pltpu.roll(eb, off, 1, stride=1, stride_axis=0)
            left = jnp.broadcast_to(eb[:, 0:1], (SUB, 128))
            near_s[t % 2, 0, rows, :] = jnp.where(left_of[off], left, near[:, :128])
            near_s[t % 2, 1, rows, :] = near[:, 128:]
            far_s[t % 2, 0, rows, :] = left
            far_s[t % 2, 1, rows, :] = jnp.broadcast_to(eb[:, 128:129], (SUB, 128))

    def groups(t, r):
        b = (STAGES[t][1] + r) // SUB
        first = b // 2 - 1 if b % 2 == 0 else b // 2
        near = [(n, n - first) for n in (first, first + 1) if 0 <= n < tiles]
        return near, list(range(0, max(first, 0))), list(range(first + 2, tiles))

    def find(t, r):
        rows = slice(r, r + SUB)
        near, lefts, rights = groups(t, r)
        s = {n: s_ref[t % 3, rows, n * 128 : (n + 1) * 128] for n in range(tiles)}
        peak = None
        for n, k in near:
            value = s[n] + near_s[t % 2, k, rows, :]
            s_ref[t % 3, rows, n * 128 : (n + 1) * 128] = value
            peak = value if peak is None else jnp.maximum(peak, value)
        far = [far_s[t % 2, k, rows, :] for k in (0, 1)]
        for group, const in ((lefts, far[0]), (rights, far[1])):
            if group:
                top = s[group[0]]
                for n in group[1:]:
                    top = jnp.maximum(top, s[n])
                peak = jnp.maximum(peak, top + const)
        peak = jnp.broadcast_to(jnp.max(peak, -1, keepdims=True), (SUB, 128))
        top_s[t % 2, 0, rows, :] = peak
        top_s[t % 2, 1, rows, :] = peak - far[0]
        top_s[t % 2, 2, rows, :] = peak - far[1]

    def power(t, r):
        h, start = STAGES[t]
        rows = slice(r, r + SUB)
        _, lefts, rights = groups(t, r)
        tops = [top_s[t % 2, k, rows, :] for k in range(3)]
        for n in range(tiles):
            top = tops[1] if n in lefts else tops[2] if n in rights else tops[0]
            s = s_ref[t % 3, rows, n * 128 : (n + 1) * 128]
            p_ref[h, start + r : start + r + SUB, n * 128 : (n + 1) * 128] = jnp.exp(s - top).astype(bf16)

    low = low_lanes(TI)

    def mix(t):
        h, start = STAGES[t]
        rows = slice(start, start + TI)
        pv = dot(p_ref[h, rows, :], va_ref[h])
        li = 1.0 / pltpu.roll(pv, 64, 1)
        o = pv * li
        if h == 1:
            o = jnp.where(low, o32_ref[rows, :], o)
            li = jnp.where(low, li_ref[rows, :], li)
            o16_ref[rows, :] = o.astype(bf16)
        o32_ref[rows, :] = o
        li_ref[rows, :] = li

    count = len(STAGES)
    scores(0)
    shift(0)
    for t in range(count + 2):
        if t + 1 < count:
            shift(t + 1)
        for r in range(0, TI, SUB):
            if t < count:
                find(t, r)
            if 0 < t <= count:
                power(t - 1, r)
        if t + 1 < count:
            scores(t + 1)
        if 2 <= t:
            mix(t - 2)

    @pl.when(step == 0)
    def _():
        place.greeted(("low",))
        near.start()

    @pl.when(step == 2)
    def _():
        near.wait()
        near_ref[place.lo] = far_ref[...]
        across.start()

    @pl.when(step == 3)
    def _():
        across.wait()
        for l in range(place.low):
            all_ref[:, l, place.core] = near_ref[l]
            all_ref[:, l, 1 - place.core] = other_ref[l]


def attend_call(lengths, q, k, v, relo, relx, far):
    n, rows = lax.axis_size("dp"), far.shape[1]
    high, low = split_axis(n)
    pair = pl.BlockSpec((SLAB, 128), lambda h: (0, h))
    table_own = pl.BlockSpec((2 * RW + 1, 128), lambda h: (0, jnp.minimum(h, 1)))
    table_oth = pl.BlockSpec((2 * RW + 1, 128), lambda h: (0, jnp.maximum(h, 2) - 2))
    return pl.pallas_call(
        attend_kernel,
        grid=(D // 128,),
        in_specs=[SMEM, pair, pair, pair, table_own, table_oth, fixed(*far.shape)],
        out_specs=[pair, pair, pair, pl.BlockSpec((2, SLAB, SLAB), lambda h: (h, 0, 0)),
                   fixed(high, low, 2, rows, CONV_C)],
        out_shape=[
            shape((SLAB, D), bf16),
            shape((SLAB, D), f32),
            shape((SLAB, D), f32),
            shape((D // DH, SLAB, SLAB), bf16),
            shape((high, low, 2, rows, CONV_C), bf16),
        ],
        scratch_shapes=[
            pltpu.VMEM((2, SLAB, 128), bf16),
            pltpu.VMEM((2, SLAB, 128), bf16),
            pltpu.VMEM((2, SLAB, 128), bf16),
            pltpu.VMEM((2, SLAB, 256), f32),
            pltpu.VMEM((256, 128), f32),
            pltpu.VMEM((3, TI, SLAB), f32),
            pltpu.VMEM((2, 2, TI, 128), f32),
            pltpu.VMEM((2, 2, TI, 128), f32),
            pltpu.VMEM((2, 3, TI, 128), f32),
        ]
        + slots_of(low, (high, rows, CONV_C))
        + [pltpu.VMEM((low, high, rows, CONV_C), bf16), pltpu.SemaphoreType.DMA((2,))],
        compiler_params=remote(6),
        name="attention_forward",
    )(lengths, q, k, v, relo, relx, far)


GAIN_ROW, BN_GAIN_ROW, BN_BIAS_ROW = TAPS, TAPS + 1, TAPS + 2
FLAT = SLAB + 3 * TOP
DEEP = PADDED + 2 * TOP


def spread_out(flat_ref, padded_ref, c, b1, b2):
    zeros = jnp.zeros((TOP, 128), f32)
    flat_ref[c, TOP + SLAB :, :] = jnp.zeros((FLAT - TOP - SLAB, 128), f32)
    padded_ref[c, :TOP, :] = zeros
    padded_ref[c, TOP + PADDED :, :] = zeros
    for t0 in range(0, PADDED, CH):
        t = lax.broadcasted_iota(jnp.int32, (CH, 128), 0) + t0
        at = TOP + t0
        value = jnp.where(t < b1, flat_ref[c, at : at + CH, :], 0.0)
        middle = (t >= b1 + GAP) & (t < b2 + GAP)
        value = jnp.where(middle, flat_ref[c, at - GAP : at - GAP + CH, :], value)
        value = jnp.where(t >= b2 + 2 * GAP, flat_ref[c, at - 2 * GAP : at - 2 * GAP + CH, :], value)
        padded_ref[c, at : at + CH, :] = value


def lane_row(ref, r):
    return jnp.concatenate([ref[c, r : r + 1, :] for c in range(LT)], 1)


def lanes(ref, r):
    return jnp.concatenate([ref[r + c : r + c + 1, :] for c in range(LT)], 1)


def draw_in(padded_ref, c, t0, rows, b1, b2):
    t = lax.broadcasted_iota(jnp.int32, (rows, 128), 0) + t0
    value = jnp.where(t < b1, padded_ref[c, t0 : t0 + rows, :], padded_ref[c, t0 + GAP : t0 + GAP + rows, :])
    return jnp.where(t < b2, value, padded_ref[c, t0 + 2 * GAP : t0 + 2 * GAP + rows, :])


def conv_kernel_fn(len_ref, x1_in, o_in, woo, wox, weights, x2_out, u_out, hd_out, gp_out, st_ref, taps_ref,
                   x2_ref, o_ref, pin, rest, cn_ref, u_ref, u16_ref, hd_ref, gp_ref, flat_ref, out_ref,
                   mine, slots, send, recv, sems):
    place = Place()
    place.greet(("all",), False)
    copies = Copies(sems)
    cx = copies.start(x1_in, x2_ref)
    co = copies.start(o_in, o_ref)
    cr = copies.start(weights.at[:, 3 * D : 3 * D + 128], rest)
    cp = copies.start(weights.at[:, : 2 * D], pin)
    cr.wait()
    across = rest[...].astype(f32).T
    for c in range(LT):
        taps_ref[c] = across[:40, c * 128 : (c + 1) * 128]
    gain = lane_row(taps_ref, GAIN_ROW)
    w = woo.shape[0]
    cx.wait()
    co.wait()
    x2_ref[...] += dot(o_ref[:, :w], woo[...]) + dot(o_ref[:, w:], wox[...])
    for rs in row_tiles(SLAB):
        xhat, _ = norm_parts(x2_ref[rs, :])
        cn_ref[rs, :] = (xhat * gain).astype(bf16)
    ends = [copies.start(x2_ref, x2_out)]
    cp.wait()
    u_ref[...] = dot(cn_ref[...], pin[...])
    for rs in row_tiles(SLAB):
        for c in range(LT):
            cs, gs = slice(c * 128, c * 128 + 128), slice(D + c * 128, D + c * 128 + 128)
            u1, u2 = u_ref[rs, cs], u_ref[rs, gs]
            u16_ref[rs, cs] = u1.astype(bf16)
            u16_ref[rs, gs] = u2.astype(bf16)
            flat_ref[c, TOP + rs.start : TOP + rs.stop, :] = u1 * jax.nn.sigmoid(u2)
    ends.append(copies.start(u16_ref, u_out))
    b1, b2 = bounds(len_ref, place)

    def tile(c, carry):
        spread_out(flat_ref, gp_ref, c, b1, b2)
        for t0 in range(0, PADDED, CH):
            acc = jnp.zeros((CH, 128), f32)
            for b in range(8):
                at = TOP + t0 - TAPS // 2 + b
                x = gp_ref[c, at : at + CH + 24, :]
                for a in range(4):
                    acc = acc + x[8 * a : 8 * a + CH, :] * taps_ref[c, 8 * a + b : 8 * a + b + 1, :]
            out_ref[c, t0 : t0 + CH, :] = acc
        first = jnp.zeros((8, 128), f32)
        second = jnp.zeros((8, 128), f32)
        for t0 in range(0, SLAB, 128):
            hd = draw_in(out_ref, c, t0, 128, b1, b2)
            hd_ref[c, t0 : t0 + 128, :] = hd
            t = lax.broadcasted_iota(jnp.int32, (128, 128), 0) + t0
            hv = jnp.where(t < b2, hd, 0.0)
            first = first + rows_sum(hv)
            second = second + rows_sum(hv * hv)
        mine[pl.ds(c, 1), :] = jnp.sum(first, 0, keepdims=True)
        mine[pl.ds(LT + c, 1), :] = jnp.sum(second, 0, keepdims=True)
        return carry

    lax.fori_loop(0, LT, tile, 0)
    mine[2 * LT :, :] = jnp.full((8, 128), b2.astype(f32))
    slots[place.me] = mine[...]
    place.greeted(("all",), False)
    hop = Hop(place, "all", lambda p: mine, slots, send, recv)
    hop.start()
    ends += [copies.start(hd_ref, hd_out), copies.start(gp_ref, gp_out)]
    hop.wait()
    st_ref[...] = slot_sum(slots, place.n)
    for copy in ends:
        copy.wait()


def conv_call(lengths, x1, o16, woo, wox, gathered):
    n = lax.axis_size("dp")
    st = (2 * LT + 8, 128)
    return pl.pallas_call(
        conv_kernel_fn,
        in_specs=[SMEM, ANY, ANY, VMEM, VMEM, ANY],
        out_specs=[ANY, ANY, ANY, ANY, VMEM, VMEM],
        out_shape=[
            shape((SLAB, D), f32),
            shape((SLAB, 2 * D), bf16),
            shape((LT, SLAB, 128), f32),
            shape((LT, DEEP, 128), f32),
            shape(st, f32),
            shape((LT, 40, 128), f32),
        ],
        scratch_shapes=[
            pltpu.VMEM((SLAB, D), f32),
            pltpu.VMEM((SLAB, D), bf16),
            pltpu.VMEM((D, 2 * D), bf16),
            pltpu.VMEM((D, 128), bf16),
            pltpu.VMEM((SLAB, D), bf16),
            pltpu.VMEM((SLAB, 2 * D), f32),
            pltpu.VMEM((SLAB, 2 * D), bf16),
            pltpu.VMEM((LT, SLAB, 128), f32),
            pltpu.VMEM((LT, DEEP, 128), f32),
            pltpu.VMEM((LT, FLAT, 128), f32),
            pltpu.VMEM((LT, PADDED, 128), f32),
            pltpu.VMEM(st, f32),
        ]
        + slots_of(n, st, f32)
        + [pltpu.SemaphoreType.DMA((8,))],
        compiler_params=remote(0),
        name="conv_forward",
    )(lengths, x1, o16, woo, wox, gathered)


def middle_kernel(len_ref, hd_in, x2_in, ct_in, st, taps_ref, weights, g2, w1o_in, w1x_in, w2o_in, w2x_in, gf,
                  out_out, gx3_out, gz_out, acc, gpw_ref, back_ref, sums_ref,
                  hd_ref, x_ref, ct_ref, pout, w1, w2, wc_ref, n_ref, nt_ref, hid_ref, act_ref, slope_ref,
                  out_ref, out16_ref, gb_ref, gbt_ref, gn_ref, gc_ref, away, back, ssems, mine, slots, send, recv, sems):
    place = Place()
    place.greet(("all",))
    copies = Copies(sems)
    ch = copies.start(hd_in, hd_ref)
    cp = copies.start(weights.at[:, 2 * D : 3 * D], pout)
    cx = copies.start(x2_in, x_ref)
    cw = [copies.start(a, b) for a, b in ((w1x_in, w1.at[0]), (w1o_in, w1.at[1]), (w2x_in, w2.at[0]), (w2o_in, w2.at[1]))]
    start = pl.multiple_of(place.core * SLAB, SLAB)
    cc = copies.start(ct_in.at[pl.ds(start, SLAB)], ct_ref)

    _, b2 = bounds(len_ref, place)
    bng, bnb = lane_row(taps_ref, BN_GAIN_ROW), lane_row(taps_ref, BN_BIAS_ROW)
    count = st[2 * LT : 2 * LT + 1, 0:1]
    centre = lanes(st, 0) / count
    inv_b = lax.rsqrt(lanes(st, LT) / count - centre * centre + BATCH_EPS)

    def normal(rs, c):
        cs = slice(c * 128, c * 128 + 128)
        zh = (hd_ref[c, rs, :] - centre[:, cs]) * inv_b[:, cs]
        z = zh * bng[:, cs] + bnb[:, cs]
        return cs, zh, z, jax.nn.sigmoid(z)

    ch.wait()
    for rs in row_tiles(SLAB):
        for c in range(LT):
            cs, _, z, sg = normal(rs, c)
            wc_ref[rs, cs] = (z * sg).astype(bf16)
    cp.wait()
    cx.wait()
    x_ref[...] += dot(wc_ref[...], pout[...])
    for rs in row_tiles(SLAB):
        xhat, _ = norm_parts(x_ref[rs, :])
        n_ref[rs, :] = (xhat * g2[...]).astype(bf16)
    for copy in cw:
        copy.wait()
    chunks = [(p, c) for p in (0, 1) for c in range(0, w1.shape[2], UP)]

    def up(k):
        p, c = chunks[k]
        hid_ref[k % 2] = dot(n_ref[...], w1[p, :, c : c + UP])

    def down(k):
        p, c = chunks[k]
        part = dot(act_ref[p, :, c : c + UP], w2[p, c : c + UP, :])
        if k == 0:
            out_ref[...] = part
        else:
            out_ref[...] += part

    up(0)
    for k, (p, c) in enumerate(chunks):
        for rs, cs in tiles(SLAB, UP):
            hid = hid_ref[k % 2, rs, cs]
            sg = jax.nn.sigmoid(hid)
            act = hid * sg
            at = slice(c + cs.start, c + cs.stop)
            act_ref[p, rs, at] = act.astype(bf16)
            slope_ref[p, rs, at] = (sg + act * (1.0 - sg)).astype(bf16)
        if k + 1 < len(chunks):
            up(k + 1)
        if k > 0:
            down(k - 1)
    down(len(chunks) - 1)
    transpose_into(nt_ref, n_ref)

    cc.wait()
    final_gain = jnp.zeros((8, D), f32)
    for rs in row_tiles(SLAB):
        t = lax.broadcasted_iota(jnp.int32, (TR, 1), 0) + rs.start
        valid = (t < b2).astype(f32)
        xhat, inv = norm_parts(x_ref[rs, :] + 0.5 * out_ref[rs, :])
        out16_ref[rs, :] = (valid * xhat * gf[...]).astype(bf16)
        g = ct_ref[rs, :].astype(f32) * valid
        gx4 = norm_back(g, gf[...], xhat, inv)
        out_ref[rs, :] = gx4
        gb_ref[rs, :] = (0.5 * gx4).astype(bf16)
        final_gain = final_gain + rows_sum(g * xhat)
    ends = [copies.start(out16_ref, out_out)]
    transpose_into(gbt_ref, gb_ref)

    def gup(k):
        p, c = chunks[k]
        hid_ref[k % 2] = dot_nt(gb_ref[...], w2[p, c : c + UP, :])

    def gdown(k):
        p, c = chunks[k]
        part = dot_nt(slope_ref[p, :, c : c + UP], w1[p, :, c : c + UP])
        if k == 0:
            gn_ref[...] = part
        else:
            gn_ref[...] += part

    gup(0)
    for k, (p, c) in enumerate(chunks):
        for rs, cs in tiles(SLAB, UP):
            at = slice(c + cs.start, c + cs.stop)
            slope_ref[p, rs, at] = (hid_ref[k % 2, rs, cs] * slope_ref[p, rs, at].astype(f32)).astype(bf16)
        if k + 1 < len(chunks):
            gup(k + 1)
        if k > 0:
            gdown(k - 1)
    gdown(len(chunks) - 1)

    ffn_gain = jnp.zeros((8, D), f32)
    for rs in row_tiles(SLAB):
        xhat, inv = norm_parts(x_ref[rs, :])
        gn = gn_ref[rs, :]
        gx3 = out_ref[rs, :] + norm_back(gn, g2[...], xhat, inv)
        x_ref[rs, :] = gx3
        gc_ref[rs, :] = gx3.astype(bf16)
        ffn_gain = ffn_gain + rows_sum(gn * xhat)
    ends.append(copies.start(x_ref, gx3_out))
    gn_ref[...] = dot_nt(gc_ref[...], pout[...])
    parts = [[jnp.zeros((8, 128), f32) for _ in range(4)] for _ in range(LT)]
    for rs in row_tiles(SLAB):
        t = lax.broadcasted_iota(jnp.int32, (TR, 1), 0) + rs.start
        valid = (t < b2).astype(f32)
        for c in range(LT):
            cs, zh, z, sg = normal(rs, c)
            gz = gn_ref[rs, cs] * (sg + z * sg * (1.0 - sg))
            hd_ref[c, rs, :] = gz
            e = gz * bng[:, cs] * valid
            for k, v in enumerate((gz, gz * zh, e, e * zh)):
                parts[c][k] = parts[c][k] + rows_sum(v)
    ends.append(copies.start(hd_ref, gz_out))
    sums_ref[...] = jnp.zeros(sums_ref.shape, f32)
    for c in range(LT):
        cs = slice(c * 128, c * 128 + 128)
        for k in range(4):
            total = jnp.sum(parts[c][k], 0, keepdims=True)
            sums_ref[k : k + 1, cs] = total
            if k >= 2:
                mine[(k - 2) * LT + c : (k - 2) * LT + c + 1, :] = total
    sums_ref[4:5, :] = jnp.sum(final_gain, 0, keepdims=True)
    sums_ref[5:6, :] = jnp.sum(ffn_gain, 0, keepdims=True)
    slots[place.me] = mine[...]
    place.greeted(("all",))
    hop = Hop(place, "all", lambda p: mine, slots, send, recv)
    hop.start()

    dims = acc.shape[1:]
    swaps = [core_copy(place, away.at[k], back.at[k], ssems.at[k]) for k in range(2)]
    lhs, rhs = (nt_ref, gbt_ref), (slope_ref, act_ref)
    for k in range(2):
        away[k] = dot(lhs[k][...], rhs[k][0]).reshape(dims).astype(bf16)
        swaps[k].start()
    gpw_ref[...] = dot_tn(wc_ref[...], gc_ref[...]).astype(bf16)
    for k in range(2):
        own = dot(lhs[k][...], rhs[k][1]).reshape(dims)
        swaps[k].wait()
        acc[k] = (own + back[k].astype(f32)).astype(bf16)
    hop.wait()
    back_ref[...] = slot_sum(slots, place.n)
    for copy in ends:
        copy.wait()


def grad_dims(cols):
    n = lax.axis_size("dp")
    return n, (*split_axis(n), D // n, cols)


def middle_call(lengths, hd, x2, cot, st, taps, gathered, g2, w1o, w1x, w2o, w2x, gf):
    hid = w1o.shape[1]
    n, dims = grad_dims(hid)
    stat = (2 * LT, 128)
    return pl.pallas_call(
        middle_kernel,
        in_specs=[SMEM, ANY, ANY, ANY, VMEM, VMEM, ANY, VMEM, ANY, ANY, ANY, ANY, VMEM],
        out_specs=[ANY, ANY, ANY, VMEM, VMEM, VMEM, VMEM],
        out_shape=[
            shape((SLAB, D), bf16),
            shape((SLAB, D), f32),
            shape((LT, SLAB, 128), f32),
            shape((2, *dims), bf16),
            shape((D, D), bf16),
            shape(stat, f32),
            shape((8, D), f32),
        ],
        scratch_shapes=[
            pltpu.VMEM((LT, SLAB, 128), f32),
            pltpu.VMEM((SLAB, D), f32),
            pltpu.VMEM((SLAB, D), bf16),
            pltpu.VMEM((D, D), bf16),
            pltpu.VMEM((2, D, hid), bf16),
            pltpu.VMEM((2, hid, D), bf16),
            pltpu.VMEM((SLAB, D), bf16),
            pltpu.VMEM((SLAB, D), bf16),
            pltpu.VMEM((D, SLAB), bf16),
            pltpu.VMEM((2, SLAB, UP), f32),
            pltpu.VMEM((2, SLAB, hid), bf16),
            pltpu.VMEM((2, SLAB, hid), bf16),
            pltpu.VMEM((SLAB, D), f32),
            pltpu.VMEM((SLAB, D), bf16),
            pltpu.VMEM((SLAB, D), bf16),
            pltpu.VMEM((D, SLAB), bf16),
            pltpu.VMEM((SLAB, D), f32),
            pltpu.VMEM((SLAB, D), bf16),
            pltpu.VMEM((2, *dims), bf16),
            pltpu.VMEM((2, *dims), bf16),
            pltpu.SemaphoreType.DMA((2, 2)),
            pltpu.VMEM(stat, f32),
        ]
        + slots_of(n, stat, f32)
        + [pltpu.SemaphoreType.DMA((12,))],
        compiler_params=remote(1),
        name="ffn2_forward_backward",
    )(lengths, hd, x2, cot, st, taps, gathered, g2, w1o, w1x, w2o, w2x, gf)


def conv_back_kernel(len_ref, acc_in, gz_in, hd_in, gp_in, st, back, taps_ref, u_in, x2_in, gx3_in, weights, woo, wox,
                     gpw, sums, gx2_out, ga_out, go_out, cg_ref, mid0, mid1, mid2,
                     gz_ref, hd_ref, gp_ref, u_ref, x2_ref, gx_ref, pin, flat_ref, pad_ref, out_ref, acc_ref, gtap_ref,
                     gu_ref, gn_ref, cn_ref, ga_ref, go_ref, sems, tsems, *scr):
    place = Place()
    place.greet(("low", "high"), False)
    copies = Copies(sems)
    def tile_copies(c):
        pairs = ((gz_in, gz_ref), (hd_in, hd_ref), (gp_in, gp_ref))
        return [pltpu.make_async_copy(a.at[c], b.at[c], tsems.at[k, c]) for k, (a, b) in enumerate(pairs)]

    for c in range(LT):
        for copy in tile_copies(c):
            copy.start()
    rest = [copies.start(a, b) for a, b in (
        (u_in, u_ref), (weights.at[:, : 2 * D], pin), (x2_in, x2_ref), (gx3_in, gx_ref))]
    b1, b2 = bounds(len_ref, place)
    gain = lane_row(taps_ref, GAIN_ROW)
    hops = [v.first(place, acc_in, refs) for v, refs in zip(PAIR_VIEWS, threes(scr))]
    place.greeted(("low", "high"), False)
    for hop in hops:
        hop.start()

    def tile(c, carry):
        for copy in tile_copies(c):
            copy.wait()
        count = st[2 * LT : 2 * LT + 1, :]
        centre = st[pl.ds(c, 1), :] / count
        inv_b = lax.rsqrt(st[pl.ds(LT + c, 1), :] / count - centre * centre + BATCH_EPS)
        a1 = back[pl.ds(c, 1), :] / count
        a2 = back[pl.ds(LT + c, 1), :] / count
        bn_gain = taps_ref[c, BN_GAIN_ROW : BN_GAIN_ROW + 1, :]
        for t0 in range(0, SLAB, 128):
            t = lax.broadcasted_iota(jnp.int32, (128, 128), 0) + t0
            zh = (hd_ref[c, t0 : t0 + 128, :] - centre) * inv_b
            away = jnp.where(t < b2, a1 + zh * a2, 0.0)
            flat_ref[c, TOP + t0 : TOP + t0 + 128, :] = inv_b * (gz_ref[c, t0 : t0 + 128, :] * bn_gain - away)
        spread_out(flat_ref, pad_ref, c, b1, b2)
        acc_ref[...] = jnp.zeros(acc_ref.shape, f32)
        for t0 in range(0, PADDED, CH):
            acc = jnp.zeros((CH, 128), f32)
            gl = gp_ref[c, TOP + t0 : TOP + t0 + CH, :]
            for b in range(8):
                at = TOP + t0 + TAPS // 2 - TAPS + 1 + b
                x = pad_ref[c, at : at + CH + 24, :]
                for a in range(4):
                    k = TAPS - 1 - (8 * a + b)
                    part = x[8 * a : 8 * a + CH, :]
                    acc = acc + part * taps_ref[c, k : k + 1, :]
                    acc_ref[8 * k : 8 * k + 8, :] += rows_sum(part * gl)
            out_ref[c, t0 : t0 + CH, :] = acc
        gtap_ref[c] = jnp.sum(acc_ref[...].reshape(TAPS, 8, 128), 1)
        for t0 in range(0, SLAB, 128):
            flat_ref[c, t0 : t0 + 128, :] = draw_in(out_ref, c, t0, 128, b1, b2)
        return carry

    lax.fori_loop(0, LT, tile, 0)
    for copy in rest:
        copy.wait()
    for rs in row_tiles(SLAB):
        for c in range(LT):
            cs, gs = slice(c * 128, c * 128 + 128), slice(D + c * 128, D + c * 128 + 128)
            sg = jax.nn.sigmoid(u_ref[rs, gs].astype(f32))
            g = flat_ref[c, rs, :] * sg
            gu_ref[rs, cs] = g.astype(bf16)
            gu_ref[rs, gs] = (g * u_ref[rs, cs].astype(f32) * (1.0 - sg)).astype(bf16)
    gn_ref[...] = dot_nt(gu_ref[...], pin[...])
    gain_sum = jnp.zeros((8, D), f32)
    for rs in row_tiles(SLAB):
        xhat, inv = norm_parts(x2_ref[rs, :])
        gn = gn_ref[rs, :]
        gx2 = gx_ref[rs, :] + norm_back(gn, gain, xhat, inv)
        gx_ref[rs, :] = gx2
        ga_ref[rs, :] = gx2.astype(bf16)
        cn_ref[rs, :] = (xhat * gain).astype(bf16)
        gain_sum = gain_sum + rows_sum(gn * xhat)
    ends = [copies.start(gx_ref, gx2_out), copies.start(ga_ref, ga_out)]
    w = woo.shape[0]
    go_ref[:, :w] = dot_nt(ga_ref[...], woo[...]).astype(bf16)
    go_ref[:, w:] = dot_nt(ga_ref[...], wox[...]).astype(bf16)
    ends.append(copies.start(go_ref, go_out))
    cg_ref[:, : 2 * D] = dot_tn(cn_ref[...], gu_ref[...]).astype(bf16)
    cg_ref[:, 2 * D : 3 * D] = gpw[...]
    gain_sum = jnp.sum(gain_sum, 0, keepdims=True)
    for c in range(LT):
        cols = slice(c * 128, (c + 1) * 128)
        rows = [gtap_ref[c], gain_sum[:, cols], sums[1:2, cols], sums[0:1, cols]]
        block = jnp.concatenate(rows + [jnp.zeros((128 - TAPS - 3, 128), f32)], 0)
        cg_ref[c * 128 : (c + 1) * 128, 3 * D :] = block.T.astype(bf16)
    for hop, mid in zip(hops, (mid0, mid1, mid2)):
        hop.wait()
        mid[...] = hop.total().astype(bf16)
    for copy in ends:
        copy.wait()


def conv_back_call(lengths, acc, gz, hd, gp, st, back, taps, u, x2, gx3, gathered, woo, wox, gpw, sums):
    n, rows = lax.axis_size("dp"), acc.shape[3]
    return pl.pallas_call(
        conv_back_kernel,
        in_specs=[SMEM, VMEM, ANY, ANY, ANY, VMEM, VMEM, VMEM, ANY, ANY, ANY, ANY, VMEM, VMEM, VMEM, VMEM],
        out_specs=[ANY, ANY, ANY, VMEM, VMEM, VMEM, VMEM],
        out_shape=[
            shape((SLAB, D), f32),
            shape((SLAB, D), bf16),
            shape((SLAB, D), bf16),
            shape((D, CONV_C), bf16),
        ]
        + [shape(v.mid(n, rows), bf16) for v in PAIR_VIEWS],
        scratch_shapes=[
            pltpu.VMEM((LT, SLAB, 128), f32),
            pltpu.VMEM((LT, SLAB, 128), f32),
            pltpu.VMEM((LT, DEEP, 128), f32),
            pltpu.VMEM((SLAB, 2 * D), bf16),
            pltpu.VMEM((SLAB, D), f32),
            pltpu.VMEM((SLAB, D), f32),
            pltpu.VMEM((D, 2 * D), bf16),
            pltpu.VMEM((LT, FLAT, 128), f32),
            pltpu.VMEM((LT, DEEP, 128), f32),
            pltpu.VMEM((LT, PADDED, 128), f32),
            pltpu.VMEM((TAPS * 8, 128), f32),
            pltpu.VMEM((LT, TAPS, 128), f32),
            pltpu.VMEM((SLAB, 2 * D), bf16),
            pltpu.VMEM((SLAB, D), f32),
            pltpu.VMEM((SLAB, D), bf16),
            pltpu.VMEM((SLAB, D), bf16),
            pltpu.VMEM((SLAB, D), bf16),
            pltpu.SemaphoreType.DMA((10,)),
            pltpu.SemaphoreType.DMA((3, LT)),
        ]
        + firsts(PAIR_VIEWS, n, rows),
        compiler_params=remote(2),
        name="conv_backward",
    )(lengths, acc, gz, hd, gp, st, back, taps, u, x2, gx3, gathered, woo, wox, gpw, sums)


HEAD_VIEWS = (View(None, 0, 384, "low"), View(None, 384, 512, "high"))


def attend_back_kernel(q_ref, k_ref, v_ref, g_ref, o_ref, li_ref, p_ref, relo_ref, relx_ref,
                       wqo, wko, wvo, wqx, wkx, wvx, o16_ref, na_in, gatt_in, x1_in, gx2_in, gain,
                       mid0, mid1, mid2, cg_ref,
                       gt_ref, gx1_out, agains_ref, f2a_ref, f2b_ref, cpi_ref, cpo_ref, crest_ref, h0_ref, acc1_ref,
                       ga_ref, va_ref, kt_ref, qt_ref, got_ref, gs_ref, gp_ref, w_ref, fl_ref, n_ref, all_ref, other_ref,
                       relt_ref, far_s, flip_ref, rel_ref, relf_ref, wide_ref, gn_ref, x1_ref, gx_ref,
                       pg_ref, away, hback, hsems, acc0_ref, sems, cback, csems, cacc, *scr):
    step = pl.program_id(0)
    place = Place()
    loads = [pltpu.make_async_copy(a, b, sems.at[k]) for k, (a, b) in enumerate((
        (na_in, wide_ref.at[0]), (gatt_in, wide_ref.at[1]), (x1_in, x1_ref), (gx2_in, gx_ref)))]
    gx1_copy = pltpu.make_async_copy(gx_ref, gx1_out, sems.at[4])
    scr = threes(scr)
    nv = len(PAIR_VIEWS)
    last = [v.second(place, mid, refs) for v, mid, refs in zip(PAIR_VIEWS, (mid0, mid1, mid2), scr[:nv])]
    cfirst = [v.first(place, cacc, refs) for v, refs in zip(CONV_VIEWS, scr[nv:])]
    nc = len(CONV_VIEWS)
    cmids = scr[nv + 2 * nc][:nc]
    csecond = [v.second(place, mid, refs) for v, mid, refs in zip(CONV_VIEWS, cmids, scr[nv + nc :])]
    cswap = core_copy(place, cg_ref.at[:, :, 1 - place.core], cback, csems)
    hswaps = [core_copy(place, away.at[k], hback.at[k], hsems.at[k]) for k in range(2)]
    at = nv + 2 * nc + 1
    hfirst = [v.first(place, acc0_ref, refs) for v, refs in zip(HEAD_VIEWS, scr[at:])]
    nh = len(HEAD_VIEWS)
    hmids = scr[at + 2 * nh][:nh]
    hsecond = [v.second(place, mid, refs) for v, mid, refs in zip(HEAD_VIEWS, hmids, scr[at + nh :])]
    kinds = ("low", "high")

    @pl.when(step == 0)
    def _():
        place.greet(kinds)
        for copy in loads:
            copy.start()
        line = lax.broadcasted_iota(jnp.int32, (256, 256), 0)
        flip_ref[...] = jnp.where(line + lax.broadcasted_iota(jnp.int32, (256, 256), 1) == 255, 1.0, 0.0).astype(bf16)
        line = lax.broadcasted_iota(jnp.int32, (128, 128), 0)
        other = (line < 64) != (lax.broadcasted_iota(jnp.int32, (128, 128), 1) < 64)
        other_ref[...] = jnp.where(other, 1.0, 0.0).astype(bf16)

    lane = lax.broadcasted_iota(jnp.int32, (SLAB, 128), 1)
    go = g_ref[...].astype(f32) * li_ref[...]
    got_ref[...] = go.T.astype(bf16)
    qt_ref[...] = q_ref[...].astype(f32).T.astype(bf16)
    kt_ref[...] = k_ref[...].astype(f32).T.astype(bf16)
    go = go.astype(bf16).astype(f32)
    product = go * o_ref[...]
    product_hi = product.astype(bf16)
    product_lo = (product - product_hi.astype(f32)).astype(bf16)
    inner = dot(product_hi, other_ref[...]) + dot(product_lo, other_ref[...])
    inner_hi = inner.astype(bf16).astype(f32)
    inner_lo = inner - inner_hi
    own_pair = step >= 2
    rel_ref[: 2 * RW + 1, :] = jnp.where(own_pair, relo_ref[...].astype(f32), relx_ref[...].astype(f32))
    relf_ref[:128, :] = dot(flip_ref[128:, :128], rel_ref[:128, :].astype(bf16))
    line = lax.broadcasted_iota(jnp.int32, (128, 128), 0)
    relf_ref[128:, :] = jnp.where(
        line < 2, rel_ref[0:1, :], jnp.where(line < 4, rel_ref[2 * RW : 2 * RW + 1, :], 0.0)
    )
    relt_ref[...] = relf_ref[...].T.astype(bf16)
    for h in (0, 1):
        mine = (lane < 64) if h == 0 else (lane >= 64)
        base = 64 - 64 * h
        extra = jnp.where(lane == base, -inner_hi, jnp.where(lane == base + 1, -inner_lo, 0.0))
        ga_ref[h] = jnp.where(mine, go, extra).astype(bf16)
        ones = jnp.where((lane == base) | (lane == base + 1), 1.0, 0.0)
        va_ref[h] = jnp.where(mine, v_ref[...].astype(f32), ones).astype(bf16)

    subl = lax.broadcasted_iota(jnp.int32, (SUB, 128), 1)
    line = lax.broadcasted_iota(jnp.int32, (SUB, 128), 0)
    left_of = {0: subl < line, 64: subl < line + 64}
    tiles = SLAB // 128
    zero16 = jnp.zeros((SUB, 128), bf16)

    def grow(t):
        h, start = STAGES[t]
        gp_ref[t % 2] = dot_nt(ga_ref[h, start : start + TI, :], va_ref[h])

    def weigh(t):
        h, start = STAGES[t]
        for r in range(0, TI, SUB):
            b = (start + r) // SUB
            off = 64 if b % 2 == 0 else 0
            first = b // 2 - 1 if b % 2 == 0 else b // 2
            rows = slice(start + r, start + r + SUB)
            near = slice(r, r + SUB)
            sums = [jnp.zeros((SUB, 128), f32), jnp.zeros((SUB, 128), f32)]
            for n in range(tiles):
                cols = slice(n * 128, (n + 1) * 128)
                gs = p_ref[h, rows, cols].astype(f32) * gp_ref[t % 2, near, cols]
                gs16 = gs.astype(bf16)
                gs_ref[h, rows, cols] = gs16
                if n < first:
                    sums[0] = sums[0] + gs
                elif n > first + 1:
                    sums[1] = sums[1] + gs
                elif n == first:
                    w_ref[t % 2, near, :128] = gs16
                    sums[0] = sums[0] + jnp.where(left_of[off], gs, 0.0)
                else:
                    w_ref[t % 2, near, 128:] = gs16
                    sums[1] = sums[1] + jnp.where(left_of[off], 0.0, gs)
            if first < 0:
                w_ref[t % 2, near, :128] = zero16
            if first + 1 >= tiles:
                w_ref[t % 2, near, 128:] = zero16
            far_s[t % 2, 0, near, :] = sums[0]
            far_s[t % 2, 1, near, :] = sums[1]

    def flip(t):
        fl_ref[t % 2] = dot(w_ref[t % 2], flip_ref[...])

    def unroll(t):
        h, start = STAGES[t]
        for r in range(0, TI, SUB):
            off = 64 if ((start + r) // SUB) % 2 == 0 else 0
            near = pltpu.roll(fl_ref[t % 2, r : r + SUB, :], (off + 128) % 256, 1, stride=1, stride_axis=0)
            n_ref[h, start + r : start + r + SUB, :128] = near[:, :128].astype(bf16)
            far_left = jnp.sum(far_s[t % 2, 0, r : r + SUB, :], -1, keepdims=True)
            far_right = jnp.sum(far_s[t % 2, 1, r : r + SUB, :], -1, keepdims=True)
            left_hi = far_left.astype(bf16).astype(f32)
            right_hi = far_right.astype(bf16).astype(f32)
            far = jnp.where(subl == 0, left_hi, 0.0)
            far = jnp.where(subl == 1, far_left - left_hi, far)
            far = jnp.where(subl == 2, right_hi, far)
            far = jnp.where(subl == 3, far_right - right_hi, far)
            n_ref[h, start + r : start + r + SUB, 128:] = far.astype(bf16)

    def query(t):
        h, start = STAGES[t]
        rows = slice(start, start + TI)
        half = slice(64 * h, 64 * h + 64)
        part = dot_nt(kt_ref[half, :], gs_ref[h, rows, :]) + dot_nt(relt_ref[half, :], n_ref[h, rows, :])
        all_ref[half, rows] = (part * DH**-0.5).astype(bf16)

    def key(h):
        half = slice(64 * h, 64 * h + 64)
        all_ref[128 + 64 * h : 192 + 64 * h, :] = dot(qt_ref[half, :], gs_ref[h]).astype(bf16)
        gt_ref[half, :] = dot(qt_ref[half, :], n_ref[h])

    def value(h):
        half = slice(64 * h, 64 * h + 64)
        all_ref[256 + 64 * h : 320 + 64 * h, :] = dot(got_ref[half, :], p_ref[h]).astype(bf16)

    grow(0)
    for t in range(len(STAGES)):
        weigh(t)
        if t > 0:
            unroll(t - 1)
        if t + 1 < len(STAGES):
            grow(t + 1)
        flip(t)
        if t > 0:
            query(t - 1)
        if t == 1:
            value(0)
        if t == 2:
            value(1)
        if t == 3:
            key(0)
        if t == 4:
            all_ref[384:, :] = o16_ref[...].astype(f32).T.astype(bf16)
    unroll(len(STAGES) - 1)
    query(len(STAGES) - 1)
    key(1)

    @pl.when(step == 0)
    def _():
        loads[0].wait()
        loads[1].wait()

    def choose(own, oth):
        return jnp.where(own_pair, own[...].astype(f32), oth[...].astype(f32)).astype(bf16)

    weights = jnp.concatenate([choose(wqo, wqx), choose(wko, wkx), choose(wvo, wvx)], 1)
    gn_ref[...] = jnp.where(step == 0, 0.0, gn_ref[...]) + dot(weights, all_ref[:384, :])
    pg_ref[:384, :] = dot(all_ref[:384, :], wide_ref[0])
    pg_ref[384:, :] = dot(all_ref[384:, :], wide_ref[1])
    pg_ref[...] = pg_ref[...].T
    dims = acc1_ref.shape

    @pl.when(step == 0)
    def _():
        place.greeted(kinds)
        for hop in last:
            hop.start()
        cswap.start()
        away[0] = pg_ref[...].reshape(dims).astype(bf16)
        hswaps[0].start()

    @pl.when(step == 1)
    def _():
        away[1] = pg_ref[...].reshape(dims).astype(bf16)
        hswaps[1].start()
        cswap.wait()
        cacc[...] = (cg_ref[:, :, place.core].astype(f32) + cback[...].astype(f32)).astype(bf16)
        for hop in cfirst:
            hop.start()
        for hop, v in zip(last, PAIR_VIEWS):
            hop.wait()
            if v.index == 0:
                f2a_ref[:, v.start : v.stop] = hop.total()
            else:
                f2b_ref[:, v.start : v.stop] = hop.total()

    @pl.when(step == 2)
    def _():
        hswaps[0].wait()
        acc0_ref[...] = (pg_ref[...].reshape(dims) + hback[0].astype(f32)).astype(bf16)
        for hop in hfirst:
            hop.start()
        for hop, mid, on in zip(cfirst, cmids, csecond):
            hop.wait()
            mid[...] = hop.total().astype(bf16)
            on.start()

    @pl.when(step == 3)
    def _():
        hswaps[1].wait()
        acc1_ref[...] = (pg_ref[...].reshape(dims) + hback[1].astype(f32)).astype(bf16)
        csecond[0].wait()
        cpi_ref[...] = csecond[0].total()
        csecond[1].wait()
        total = csecond[1].total()
        cpo_ref[...] = total[:, :D]
        crest_ref[...] = total[:, D:]
        for hop, mid, on in zip(hfirst, hmids, hsecond):
            hop.wait()
            mid[...] = hop.total().astype(bf16)
            on.start()
        loads[2].wait()
        loads[3].wait()
        total = jnp.zeros((8, D), f32)
        for rs in row_tiles(SLAB):
            xhat, inv = norm_parts(x1_ref[rs, :])
            gn = gn_ref[:, rs].T
            gx_ref[rs, :] = gx_ref[rs, :] + norm_back(gn, gain[...], xhat, inv)
            total = total + rows_sum(gn * xhat)
        gx1_copy.start()
        agains_ref[...] = total
        for hop, v in zip(hsecond, HEAD_VIEWS):
            hop.wait()
            h0_ref[:, v.start : v.stop] = hop.total()
        gx1_copy.wait()


def pair_of(s):
    return (s + 2) % 4


def attend_back_call(q, k, v, go, o32, li, p, relo, relx, weights, o16, na, gatt, x1, gx2, gain, mids, cg):
    n, rows, crows = lax.axis_size("dp"), mids[0].shape[1], cg.shape[3]
    high, low = split_axis(n)
    cdims = (high, low, crows, CONV_C)
    hdims = (high, low, rows, 512)
    pair = pl.BlockSpec((SLAB, 128), lambda s: (0, pair_of(s)))
    head_map = pl.BlockSpec((2, SLAB, SLAB), lambda s: (pair_of(s), 0, 0))
    own = lambda s: (0, jnp.maximum(s, 2) - 2)
    oth = lambda s: (0, jnp.minimum(s, 1))
    table_own, table_oth = pl.BlockSpec((2 * RW + 1, 128), own), pl.BlockSpec((2 * RW + 1, 128), oth)
    w_own, w_oth = pl.BlockSpec((D, 128), own), pl.BlockSpec((D, 128), oth)
    return pl.pallas_call(
        attend_back_kernel,
        grid=(D // 128,),
        in_specs=[pair] * 6 + [head_map, table_own, table_oth] + [w_own] * 3 + [w_oth] * 3 + [pair]
        + [ANY] * 4 + [fixed(1, D)] + [fixed(*a.shape) for a in (*mids, cg)],
        out_specs=[pl.BlockSpec((128, 256), lambda s: (pair_of(s), 0)), ANY, fixed(8, D), fixed(rows, 1024),
                   fixed(rows, 1024), fixed(crows, 2 * D), fixed(crows, D), fixed(crows, 128),
                   fixed(rows, 512), fixed(*hdims)],
        out_shape=[
            shape((D, 256), f32),
            shape((SLAB, D), f32),
            shape((8, D), f32),
            shape((rows, 1024), f32),
            shape((rows, 1024), f32),
            shape((crows, 2 * D), f32),
            shape((crows, D), f32),
            shape((crows, 128), f32),
            shape((rows, 512), f32),
            shape(hdims, bf16),
        ],
        scratch_shapes=[
            pltpu.VMEM((2, SLAB, 128), bf16),
            pltpu.VMEM((2, SLAB, 128), bf16),
            pltpu.VMEM((128, SLAB), bf16),
            pltpu.VMEM((128, SLAB), bf16),
            pltpu.VMEM((128, SLAB), bf16),
            pltpu.VMEM((2, SLAB, SLAB), bf16),
            pltpu.VMEM((2, TI, SLAB), f32),
            pltpu.VMEM((2, TI, 256), bf16),
            pltpu.VMEM((2, TI, 256), f32),
            pltpu.VMEM((2, SLAB, 256), bf16),
            pltpu.VMEM((512, SLAB), bf16),
            pltpu.VMEM((128, 128), bf16),
            pltpu.VMEM((128, 256), bf16),
            pltpu.VMEM((2, 2, TI, 128), f32),
            pltpu.VMEM((256, 256), bf16),
            pltpu.VMEM((136, 128), f32),
            pltpu.VMEM((256, 128), f32),
            pltpu.VMEM((2, SLAB, D), bf16),
            pltpu.VMEM((D, SLAB), f32),
            pltpu.VMEM((SLAB, D), f32),
            pltpu.VMEM((SLAB, D), f32),
            pltpu.VMEM((D, 512), f32),
            pltpu.VMEM((2, *hdims), bf16),
            pltpu.VMEM((2, *hdims), bf16),
            pltpu.SemaphoreType.DMA((2, 2)),
            pltpu.VMEM(hdims, bf16),
            pltpu.SemaphoreType.DMA((5,)),
            pltpu.VMEM(cdims, bf16),
            pltpu.SemaphoreType.DMA((2,)),
            pltpu.VMEM(cdims, bf16),
        ]
        + seconds(PAIR_VIEWS, n, rows)
        + firsts(CONV_VIEWS, n, crows)
        + seconds(CONV_VIEWS, n, crows)
        + padded_three([pltpu.VMEM(v.mid(n, crows), bf16) for v in CONV_VIEWS])
        + firsts(HEAD_VIEWS, n, rows)
        + seconds(HEAD_VIEWS, n, rows)
        + padded_three([pltpu.VMEM(v.mid(n, rows), bf16) for v in HEAD_VIEWS]),
        compiler_params=remote(3),
        name="attention_backward",
    )(q, k, v, go, o32, li, p, relo, relx, *weights, o16, na, gatt, x1, gx2, gain, *mids, cg)


PART = 256
PARTS = 4


def last_kernel(gx1_in, x_in, hid_in, w1o_in, w1x_in, w2o_in, w2x_in, g1, sums, agains, acc1, table_ref,
                gx_out, gxx_out, fa_ref, fb_ref, gain0, gain1, gain2, gain3, h1_ref, to_ref,
                gx_ref, x_ref, hid_ref, w1, w2, gb_ref, gbt_ref, nt_ref, n_ref, gact_ref, act_ref, ghid_ref, gn_ref,
                gx16_ref, both_ref, away, back, ssems, gsems, xmine, xback, xsum, xsems, xmid, x1s, x1a, x1b, x2s, x2a, x2b,
                tnear, tback, tsems, tsum, t1, t2, t1s, t1a, t1b, t2s, t2a, t2b, t3s, t3a, t3b, t4s, t4a, t4b, sems, *scr):
    place = Place()
    place.greet(("low", "high"))
    copies = Copies(sems)
    cx = copies.start(x_in.at[pl.ds(pl.multiple_of(place.core * SLAB, SLAB), SLAB)], x_ref)
    cg = copies.start(gx1_in, gx_ref)
    cw = [copies.start(a, b) for a, b in (
        (w2x_in, w2.at[0]), (hid_in.at[0], hid_ref.at[0]), (w1x_in, w1.at[0]),
        (w2o_in, w2.at[1]), (hid_in.at[1], hid_ref.at[1]), (w1o_in, w1.at[1]))]
    refs = threes(scr)
    nh = len(HEAD_VIEWS)

    def chain(acc):
        nonlocal refs
        first = [v.first(place, acc, r) for v, r in zip(HEAD_VIEWS, refs)]
        mids = refs[2 * nh][:nh]
        second = [v.second(place, mid, r) for v, mid, r in zip(HEAD_VIEWS, mids, refs[nh:])]
        refs = refs[2 * nh + 1 :]
        return first, mids, second

    def chain_split(accs):
        nonlocal refs
        first = [v.whole_first(place, a, r) for v, a, r in zip(HEAD_VIEWS, accs, refs)]
        mids = refs[2 * nh][:nh]
        second = [v.second(place, mid, r) for v, mid, r in zip(HEAD_VIEWS, mids, refs[nh:])]
        refs = refs[2 * nh + 1 :]
        return first, mids, second

    heads = chain(acc1)
    accs, chains = [], []
    for k in range(PARTS):
        accs.append(refs[0][:nh])
        refs = refs[1:]
        chains.append(chain_split(accs[k]))

    def begin(chain):
        for hop in chain[0]:
            hop.start()

    def turn(chain):
        for hop, mid, on in zip(*chain):
            hop.wait()
            mid[...] = hop.total().astype(bf16)
            on.start()

    tswap = core_copy(place, tnear.at[1], tback, tsems)
    scatter1 = Hop(place, "low", lambda p: tsum.at[:, p], t1s, t1a, t1b)
    scatter2 = Hop(place, "high", lambda p: t1.at[p], t2s, t2a, t2b)
    gather1 = Hop(place, "high", lambda p: t2, t3s, t3a, t3b)
    gather2 = Hop(place, "low", lambda p: t3s, t4s, t4a, t4b)
    xswap = core_copy(place, xmine, xback, xsems)
    xhop1 = Hop(place, "low", lambda p: xsum, x1s, x1a, x1b)
    xhop2 = Hop(place, "high", lambda p: xmid, x2s, x2a, x2b)
    swaps = [core_copy(place, away.at[k], back.at[k], ssems.at[k]) for k in range(PARTS)]

    slot = lax.broadcasted_iota(jnp.int32, (256, 128), 1)
    diagonal = (lax.broadcasted_iota(jnp.int32, (256, 128), 0) & 127) == slot
    for half in (0, 1):
        block = table_ref[half].reshape(256, 256)
        far = block[:, 128:]
        left = far[:, 0:1] + far[:, 1:2]
        right = far[:, 2:3] + far[:, 3:4]
        tnear[half] = (block[:, :128] + jnp.where(slot == 127, left, 0.0)).reshape(tnear.shape[1:])
        spread = jnp.where(diagonal, right, 0.0)
        for r in (0, 1):
            at = 4 * LT + 2 * half + r
            xmine[at : at + 1, :] = jnp.sum(spread[r * 128 : (r + 1) * 128], 0, keepdims=True)
    cx.wait()
    for rs in row_tiles(SLAB):
        xhat, _ = norm_parts(x_ref[rs, :].astype(f32))
        n_ref[rs, :] = (xhat * g1[...]).astype(bf16)
    transpose_into(nt_ref, n_ref)
    cg.wait()
    for rs in row_tiles(SLAB):
        gb_ref[rs, :] = (0.5 * gx_ref[rs, :]).astype(bf16)
    transpose_into(gbt_ref, gb_ref)
    place.greeted(("low", "high"))
    tswap.start()
    begin(heads)
    for copy in cw:
        copy.wait()
    dims = away.shape[1:]
    half_dims = (*dims[:3], PART)

    order = [(0, 0), (1, 0), (0, 1), (0, 2), (1, 1), (0, 3), (1, 2), (1, 3)]

    def up(i):
        p, k = order[i]
        gact_ref[i % 2] = dot_nt(gb_ref[...], w2[p, k * PART : (k + 1) * PART, :])

    def weigh(i):
        p, k = order[i]
        for rs in row_tiles(SLAB):
            hid = hid_ref[p, rs, k * PART : (k + 1) * PART].astype(f32)
            sg = jax.nn.sigmoid(hid)
            act = hid * sg
            act_ref[rs, :] = act.astype(bf16)
            ghid_ref[rs, :] = (gact_ref[i % 2, rs, :] * (sg + act * (1.0 - sg))).astype(bf16)

    def down(i):
        p, k = order[i]
        part = dot_nt(ghid_ref[...], w1[p, :, k * PART : (k + 1) * PART])
        if i == 0:
            gn_ref[...] = part
        else:
            gn_ref[...] += part
        return dot(nt_ref[...], ghid_ref[...]), dot(gbt_ref[...], act_ref[...])

    up(0)
    for i, (p, k) in enumerate(order):
        weigh(i)
        if i + 1 < len(order):
            up(i + 1)
        left, right = down(i)
        if p == 0:
            away[k, :, :, :, :PART] = left.reshape(half_dims).astype(bf16)
            away[k, :, :, :, PART:] = right.reshape(half_dims).astype(bf16)
            swaps[k].start()
        else:
            swaps[k].wait()
            left = left.reshape(half_dims) + back[k, :, :, :, :PART].astype(f32)
            right = right.reshape(half_dims) + back[k, :, :, :, PART:].astype(f32)
            accs[k][0][:, :, :, :PART] = left.astype(bf16)
            accs[k][0][:, :, :, PART:] = right[:, :, :, : 384 - PART].astype(bf16)
            accs[k][1][...] = right[:, :, :, 384 - PART :].astype(bf16)
            begin(chains[k])
        if i == 0:
            tswap.wait()
            tsum[...] = tnear[0] + tback[...]
            scatter1.start()
        elif i == 2:
            scatter1.wait()
            t1[...] = scatter1.total()
            scatter2.start()
            turn(heads)
        elif i == 4:
            scatter2.wait()
            t2[...] = scatter2.total()
            t3s[place.hi] = t2[...]
            gather1.start()
        elif i == 5:
            turn(chains[0])
        elif i == 6:
            gather1.wait()
            t4s[place.lo] = t3s[...]
            gather2.start()
        elif i == 7:
            turn(chains[1])

    ffn_gain = jnp.zeros((8, D), f32)
    for rs in row_tiles(SLAB):
        xhat, inv = norm_parts(x_ref[rs, :].astype(f32))
        gn = gn_ref[rs, :]
        gx16_ref[rs, :] = (gx_ref[rs, :] + norm_back(gn, g1[...], xhat, inv)).astype(bf16)
        ffn_gain = ffn_gain + rows_sum(gn * xhat)
    gains = (
        jnp.sum(ffn_gain, 0, keepdims=True),
        jnp.sum(agains[...], 0, keepdims=True),
        sums[5:6, :],
        sums[4:5, :],
    )
    for r, g in enumerate(gains):
        for c in range(LT):
            xmine[r * LT + c : r * LT + c + 1, :] = g[:, c * 128 : (c + 1) * 128]
    xmine[4 * LT + 4 :, :] = jnp.zeros((4, 128), f32)
    xswap.start()
    out_copy = copies.start(gx16_ref, gx_out)
    gxswap = core_copy(place, gx16_ref, gxx_out, gsems)
    gxswap.start()
    xswap.wait()
    xsum[...] = xmine[...] + xback[...]
    at = 4 * LT
    xsum[at : at + 2, :] = xmine[at : at + 2, :] + xback[at + 2 : at + 4, :]
    x1s[place.lo] = xsum[...]
    xhop1.start()
    turn(chains[PARTS - 2])
    xhop1.wait()
    xmid[...] = slot_sum(x1s, place.low)
    x2s[place.hi] = xmid[...]
    xhop2.start()
    turn(chains[PARTS - 1])
    for hop, v in zip(heads[2], HEAD_VIEWS):
        hop.wait()
        h1_ref[:, v.start : v.stop] = hop.total()
    gather2.wait()
    xhop2.wait()
    total = slot_sum(x2s, place.high)
    for r, ref in enumerate((gain0, gain1, gain2, gain3)):
        for c in range(LT):
            ref[:, c * 128 : (c + 1) * 128] = total[r * LT + c : r * LT + c + 1, :]
    line = lax.broadcasted_iota(jnp.int32, (128, 128), 0)
    choice = jnp.where(line + lax.broadcasted_iota(jnp.int32, (128, 128), 1) == 127, 1.0, 0.0)
    tall = jnp.stack([t4s[l, h] for h in range(place.high) for l in range(place.low)]).reshape(256, 128)
    to_ref[: 2 * RW, :] = lax.dot_general(
        choice, tall, (((1,), (1,)), ((), ())), preferred_element_type=f32, precision=lax.Precision.HIGHEST
    )
    for r in (0, 1):
        to_ref[2 * RW : 2 * RW + 1, r * 128 : (r + 1) * 128] = total[at + r : at + r + 1, :]
    for k in range(PARTS):
        for hop, v in zip(chains[k][2], HEAD_VIEWS):
            hop.wait()
            both_ref[:, v.start : v.stop] = hop.total()
        fa_ref[:, k * PART : (k + 1) * PART] = both_ref[:, :PART]
        fb_ref[:, k * PART : (k + 1) * PART] = both_ref[:, PART:]
    out_copy.wait()
    gxswap.wait()


def padded_three(refs):
    return refs + [pltpu.SemaphoreType.DMA((1,))] * (-len(refs) % 3)


def last_call(gx1, frames, hid, w1o, w1x, w2o, w2x, g1, sums, agains, acc1, table):
    width = w1o.shape[1]
    n, dims = grad_dims(2 * PART)
    rows = dims[2]
    high, low = split_axis(n)
    trows = table.shape[3]
    gains = (4 * LT + 8, 128)
    link = firsts(HEAD_VIEWS, n, rows) + seconds(HEAD_VIEWS, n, rows)
    link = link + padded_three([pltpu.VMEM(v.mid(n, rows), bf16) for v in HEAD_VIEWS])
    part = padded_three([pltpu.VMEM((*dims[:3], v.width), bf16) for v in HEAD_VIEWS]) + link
    return pl.pallas_call(
        last_kernel,
        in_specs=[ANY] * 7 + [VMEM] * 5,
        out_specs=[ANY] * 2 + [VMEM] * 8,
        out_shape=[
            shape((SLAB, D), bf16),
            shape((SLAB, D), bf16),
            shape((rows, width), f32),
            shape((rows, width), f32),
        ]
        + [shape((1, D), f32)] * 4
        + [shape((rows, 512), f32), shape((2 * RW + 1, 256), f32)],
        scratch_shapes=[
            pltpu.VMEM((SLAB, D), f32),
            pltpu.VMEM((SLAB, D), bf16),
            pltpu.VMEM((2, SLAB, width), bf16),
            pltpu.VMEM((2, D, width), bf16),
            pltpu.VMEM((2, width, D), bf16),
            pltpu.VMEM((SLAB, D), bf16),
            pltpu.VMEM((D, SLAB), bf16),
            pltpu.VMEM((D, SLAB), bf16),
            pltpu.VMEM((SLAB, D), bf16),
            pltpu.VMEM((2, SLAB, PART), f32),
            pltpu.VMEM((SLAB, PART), bf16),
            pltpu.VMEM((SLAB, PART), bf16),
            pltpu.VMEM((SLAB, D), f32),
            pltpu.VMEM((SLAB, D), bf16),
            pltpu.VMEM((rows, 2 * PART), f32),
            pltpu.VMEM((PARTS, *dims), bf16),
            pltpu.VMEM((PARTS, *dims), bf16),
            pltpu.SemaphoreType.DMA((PARTS, 2)),
            pltpu.SemaphoreType.DMA((2,)),
            pltpu.VMEM(gains, f32),
            pltpu.VMEM(gains, f32),
            pltpu.VMEM(gains, f32),
            pltpu.SemaphoreType.DMA((2,)),
            pltpu.VMEM(gains, f32),
        ]
        + slots_of(low, gains, f32)
        + slots_of(high, gains, f32)
        + [
            pltpu.VMEM((2, high, low, trows, 128), f32),
            pltpu.VMEM((high, low, trows, 128), f32),
            pltpu.SemaphoreType.DMA((2,)),
            pltpu.VMEM((high, low, trows, 128), f32),
            pltpu.VMEM((high, trows, 128), f32),
            pltpu.VMEM((trows, 128), f32),
        ]
        + slots_of(low, (high, trows, 128), f32)
        + slots_of(high, (trows, 128), f32)
        + slots_of(high, (trows, 128), f32)
        + slots_of(low, (high, trows, 128), f32)
        + [pltpu.SemaphoreType.DMA((10,))]
        + link
        + part * PARTS,
        compiler_params=remote(4),
        name="ffn1_backward",
    )(gx1, frames, hid, w1o, w1x, w2o, w2x, g1, sums, agains, acc1, table)


def results_kernel(out_own, out_oth, gx_own, gx_oth, *refs):
    count = len(SMALL)
    smalls, (out_ref, gx_out), outs, (load_ref, gx_ref, sems) = (
        refs[:count], refs[count : count + 2], refs[count + 2 : -3], refs[-3:]
    )
    core = lax.axis_index("mp")
    own = pl.ds(pl.multiple_of(core * SLAB, SLAB), SLAB)
    oth = pl.ds(pl.multiple_of((1 - core) * SLAB, SLAB), SLAB)
    copies = Copies(sems)
    loads = [copies.start(gx_own, load_ref.at[0]), copies.start(gx_oth, load_ref.at[1])]
    loads += [copies.start(out_own, load_ref.at[2]), copies.start(out_oth, load_ref.at[3])]
    ends = []
    for k, rows in ((0, own), (1, oth)):
        loads[k].wait()
        for rs in row_tiles(SLAB):
            gx_ref[k, rs, :] = load_ref[k, rs, :].astype(f32)
        ends.append(copies.start(gx_ref.at[k], gx_out.at[rows]))
    for k, rows in ((2, own), (3, oth)):
        loads[k].wait()
        ends.append(copies.start(load_ref.at[k], out_ref.at[rows]))
    (f1a, f1b, f2a, f2b, h0, h1, cpi, cpo, crest, table, gain0, gain1, gain2, gain3) = smalls
    (of1a, of1b, of2a, of2b, oq, ok, ov, oo, ocpi, ocpo, ock, ov0, ov1, ov2, otable, og0, og1, og2, og3) = outs
    for dst, src in ((of1a, f1a), (of1b, f1b), (of2a, f2a), (of2b, f2b), (ocpi, cpi), (ocpo, cpo), (otable, table),
                     (og0, gain0), (og1, gain1), (og2, gain2), (og3, gain3)):
        dst[...] = src[...]
    for n, dst in enumerate((oq, ok, ov, oo)):
        dst[:, :128] = h0[:, n * 128 : (n + 1) * 128]
        dst[:, 128:] = h1[:, n * 128 : (n + 1) * 128]
    ock[...] = crest[:, :TAPS]
    across = crest[...].T
    for n, dst in enumerate((ov0, ov1, ov2)):
        dst[...] = across[TAPS + n : TAPS + n + 1, :]
    for copy in ends:
        copy.wait()


SMALL = range(14)


def results(out, out_oth, gx, gx_oth, smalls):
    rows, crows = smalls[0].shape[0], smalls[6].shape[0]
    outs = [shape(a.shape, f32) for a in smalls[:4]]
    outs += [shape((rows, D // 2), f32)] * 4
    outs += [shape((crows, 2 * D), f32), shape((crows, D), f32), shape((crows, TAPS), f32)]
    outs += [shape((1, crows), f32)] * 3 + [shape(a.shape, f32) for a in smalls[9:]]
    return pl.pallas_call(
        results_kernel,
        in_specs=[ANY] * 4 + [VMEM] * len(smalls),
        out_specs=[ANY] * 2 + [VMEM] * len(outs),
        out_shape=[shape((2 * SLAB, D), bf16), shape((2 * SLAB, D), f32)] + outs,
        scratch_shapes=[
            pltpu.VMEM((4, SLAB, D), bf16),
            pltpu.VMEM((2, SLAB, D), f32),
            pltpu.SemaphoreType.DMA((8,)),
        ],
        compiler_params=pltpu.CompilerParams(vmem_limit_bytes=60 << 20),
        name="results",
    )(out, out_oth, gx, gx_oth, *smalls)


def shards(
    frames, lengths, cotangent, ffn1_gain, ffn1_in, ffn1_out, attn_gain, query_weight, key_weight,
    value_weight, out_weight, rel_table, conv_gain, pointwise_in, conv_kernel, bn_gain, bn_bias,
    pointwise_out, ffn2_gain, ffn2_in, ffn2_out, final_gain,
):
    n = lax.axis_size("dp")
    high, low = split_axis(n)
    column = jnp.arange(128 - TAPS)[None, :]
    vectors = sum(
        jnp.where(column == k, v[:, None], 0) for k, v in enumerate((conv_gain, bn_gain, bn_bias))
    ).astype(bf16)
    g1, ga, g2, gf = (g[None, :] for g in (ffn1_gain, attn_gain, ffn2_gain, final_gain))
    qkvo = (query_weight, key_weight, value_weight)

    x1, hid1, na, q, k, v, w1x, w2x, wqx, wkx, wvx, v1x, v2x, wox, relx, far = first_call(
        frames, g1, ga, pointwise_in, pointwise_out, conv_kernel, vectors, ffn1_in, ffn1_out, *qkvo, ffn2_in, ffn2_out, out_weight, rel_table
    )
    o16, o32, li, p, gathered = attend_call(lengths, q, k, v, rel_table, relx, far)
    gathered = gathered.reshape(D, CONV_C)
    x2, u, hd, gp, st, taps = conv_call(lengths, x1, o16, out_weight, wox, gathered)
    out, gx3, gz, acc2, gpw, back, sums = middle_call(
        lengths, hd, x2, cotangent, st, taps, gathered, g2, ffn2_in, v1x, ffn2_out, v2x, gf
    )
    gx2, gatt, go, conv_g, *mids = conv_back_call(
        lengths, acc2, gz, hd, gp, st, back, taps, u, x2, gx3, gathered, out_weight, wox, gpw, sums
    )
    conv_g = conv_g.reshape(high, low, 2, D // n // 2, CONV_C)
    gtab, gx1, agains, f2a, f2b, cpi, cpo, crest, h0, acc1 = attend_back_call(
        q, k, v, go, o32, li, p, rel_table, relx, (*qkvo, wqx, wkx, wvx), o16, na, gatt, x1, gx2, ga, mids, conv_g
    )
    gx, gx_oth, f1a, f1b, gain0, gain1, gain2, gain3, h1, table = last_call(
        gx1, frames, hid1, ffn1_in, w1x, ffn1_out, w2x, g1, sums, agains, acc1,
        gtab.reshape(2, high, low, D // 2 // n, 256),
    )
    (block_output, frames_grad, f1a, f1b, f2a, f2b, q_grad, k_grad, v_grad, o_grad, cpi, cpo, ck, cg, bg, bb,
     table, gain0, gain1, gain2, gain3) = results(
        out, lax.ppermute(out, "mp", [(0, 1), (1, 0)]), gx, gx_oth,
        (f1a, f1b, f2a, f2b, h0, h1, cpi, cpo, crest, table, gain0, gain1, gain2, gain3),
    )
    return (
        block_output, frames_grad, gain0[0], f1a, f1b.T, gain1[0], q_grad, k_grad, v_grad, o_grad.T, table, cg[0],
        cpi, ck, bg[0], bb[0], cpo, gain2[0], f2a, f2b.T, gain3[0],
    )


def solution(mesh):
    return jax.shard_map(
        shards,
        mesh=mesh,
        in_specs=(
            P("dp", None), P("dp", None), P("dp", None), P(), P(None, "mp"), P("mp", None), P(),
            P(None, "mp"), P(None, "mp"), P(None, "mp"), P("mp", None), P(None, "mp"),
            P(("dp", "mp")), P(("dp", "mp"), None), P(("dp", "mp"), None), P(("dp", "mp")),
            P(("dp", "mp")), P(("dp", "mp"), None), P(), P(None, "mp"), P("mp", None), P(),
        ),
        out_specs=(
            P("dp", None), P("dp", None), P(), P("dp", "mp"), P("mp", "dp"), P(), P("dp", "mp"),
            P("dp", "mp"), P("dp", "mp"), P("mp", "dp"), P(None, "mp"), P(("dp", "mp")),
            P(("dp", "mp"), None), P(("dp", "mp"), None), P(("dp", "mp")), P(("dp", "mp")),
            P(("dp", "mp"), None), P(), P("dp", "mp"), P("mp", "dp"), P(),
        ),
        check_vma=False,
    )
```

```python
import jax
import jax.numpy as jnp
from jax import lax
from jax.experimental import pallas as pl
from jax.experimental.pallas import tpu as pltpu
from jax.sharding import PartitionSpec as P

D = 512
DH = 64
RW = 64
SLAB = 1152
TAPS = 32
NORM_EPS = 1e-05
BATCH_EPS = 1e-05
MASKED = -1e30

SUB = 64
GAP = 16
TOP = 32
PADDED = 1216
CH = 64
LT = D // 128

f32 = jnp.float32
bf16 = jnp.bfloat16


def params(mib=60):
    return pltpu.CompilerParams(
        dimension_semantics=("arbitrary",), vmem_limit_bytes=mib << 20
    )


def dot(a, b):
    return jnp.dot(a, b, preferred_element_type=f32)


def dot_nt(a, b):
    return lax.dot_general(a, b, (((1,), (1,)), ((), ())), preferred_element_type=f32)


def dot_tn(a, b):
    return lax.dot_general(a, b, (((0,), (0,)), ((), ())), preferred_element_type=f32)


def norm_parts(v):
    c = v - jnp.mean(v, -1, keepdims=True)
    inv = lax.rsqrt(jnp.mean(c * c, -1, keepdims=True) + NORM_EPS)
    return c * inv, inv


def norm_back(gy, gain, xhat, inv):
    e = gy * gain
    inner = jnp.mean(e * xhat, -1, keepdims=True)
    return inv * (e - jnp.mean(e, -1, keepdims=True) - xhat * inner)


def rows_sum(v):
    return jnp.sum(v.reshape(v.shape[0] // 8, 8, v.shape[1]), 0)


def fixed(*shape):
    zeros = (0,) * len(shape)
    return pl.BlockSpec(shape, lambda i, *m: zeros)


SMEM = pl.BlockSpec(memory_space=pltpu.SMEM)
VMEM = pl.BlockSpec(memory_space=pltpu.VMEM)


def shape(dims, dtype):
    return jax.ShapeDtypeStruct(dims, dtype)


MESH = pl.DeviceIdType.MESH


def split_axis(n):
    low = 4 if n % 4 == 0 else 1
    return n // low, low


class Place:
    def __init__(self):
        self.n = lax.axis_size("dp")
        self.high, self.low = split_axis(self.n)
        self.me = lax.axis_index("dp")
        self.core = lax.axis_index("mp")
        self.hi = self.me // self.low
        self.lo = self.me % self.low

    def size(self, kind):
        return {"all": self.n, "low": self.low, "high": self.high}[kind]

    def mine(self, kind):
        return {"all": self.me, "low": self.lo, "high": self.hi}[kind]

    def peer(self, kind, j):
        at = (self.mine(kind) + j) % self.size(kind)
        if kind == "low":
            return at, {"dp": self.hi * self.low + at}
        if kind == "high":
            return at, {"dp": at * self.low + self.lo}
        return at, {"dp": at}

    def each(self, kind, do):
        size = self.size(kind)
        if size <= 4:
            for j in range(1, size):
                do(j)
        else:

            def body(j, carry):
                do(j)
                return carry

            lax.fori_loop(1, size, body, 0)

    def greet(self, kinds, core=True):
        barrier = pltpu.get_barrier_semaphore()
        for kind in kinds:
            self.each(
                kind,
                lambda j: pl.semaphore_signal(
                    barrier, inc=1, device_id=self.peer(kind, j)[1], device_id_type=MESH
                ),
            )
        if core:
            pl.semaphore_signal(barrier, inc=1, device_id={"mp": 1 - self.core}, device_id_type=MESH)

    def greeted(self, kinds, core=True):
        count = sum(self.size(kind) - 1 for kind in kinds) + (1 if core else 0)
        if count:
            pl.semaphore_wait(pltpu.get_barrier_semaphore(), count)


class Hop:
    def __init__(self, place, kind, piece, slots, send, recv):
        self.place, self.kind, self.piece = place, kind, piece
        self.slots, self.send, self.recv = slots, send, recv

    def copy(self, j, slot):
        at, device = self.place.peer(self.kind, j)
        return pltpu.make_async_remote_copy(
            src_ref=self.piece(at), dst_ref=self.slots.at[slot], send_sem=self.send.at[j],
            recv_sem=self.recv.at[slot], device_id=device, device_id_type=MESH,
        )

    def start(self):
        mine = self.place.mine(self.kind)
        self.place.each(self.kind, lambda j: self.copy(j, mine).start())

    def wait(self):
        self.place.each(self.kind, lambda j: self.copy(j, self.place.peer(self.kind, j)[0]).wait())

    def total(self):
        total = self.piece(self.place.mine(self.kind))[...].astype(f32)
        size = self.place.size(self.kind)
        if size <= 4:
            for j in range(1, size):
                total = total + self.slots[self.place.peer(self.kind, j)[0]].astype(f32)
            return total
        return lax.fori_loop(
            1, size, lambda j, t: t + self.slots[self.place.peer(self.kind, j)[0]].astype(f32), total
        )


def core_copy(place, src, dst, sems):
    return pltpu.make_async_remote_copy(
        src_ref=src, dst_ref=dst, send_sem=sems.at[0], recv_sem=sems.at[1],
        device_id={"mp": 1 - place.core}, device_id_type=MESH,
    )


def slots_of(size, dims, dtype=bf16):
    return [
        pltpu.VMEM((size, *dims), dtype),
        pltpu.SemaphoreType.DMA((size,)),
        pltpu.SemaphoreType.DMA((size,)),
    ]


class View:
    def __init__(self, index, start, stop, order):
        self.index, self.start, self.stop, self.order = index, start, stop, order
        self.width = stop - start

    def kinds(self):
        return ("low", "high") if self.order == "low" else ("high", "low")

    def mid(self, n, rows):
        high, low = split_axis(n)
        return (high if self.order == "low" else low, rows, self.width)

    def first_scratch(self, n, rows):
        high, low = split_axis(n)
        return slots_of(low if self.order == "low" else high, self.mid(n, rows))

    def second_scratch(self, n, rows):
        size, *dims = self.mid(n, rows)
        return slots_of(size, dims)

    def first(self, place, acc, refs):
        cols = slice(self.start, self.stop)
        if self.index is not None:
            acc = acc.at[self.index]
        if self.order == "low":
            piece = lambda p: acc.at[:, p, :, cols]
        else:
            piece = lambda p: acc.at[p, :, :, cols]
        return Hop(place, self.kinds()[0], piece, *refs)

    def whole_first(self, place, acc, refs):
        if self.order == "low":
            return Hop(place, "low", lambda p: acc.at[:, p], *refs)
        return Hop(place, "high", lambda p: acc.at[p], *refs)

    def second(self, place, mid, refs):
        return Hop(place, self.kinds()[1], lambda p: mid.at[p], *refs)


PAIR_VIEWS = (View(0, 0, 1024, "low"), View(1, 0, 384, "low"), View(1, 384, 1024, "high"))
CONV_C = 2 * D + D + 128
CONV_VIEWS = (View(None, 0, 1024, "low"), View(None, 1024, CONV_C, "high"))


def firsts(views, n, rows):
    return [ref for v in views for ref in v.first_scratch(n, rows)]


def seconds(views, n, rows):
    return [ref for v in views for ref in v.second_scratch(n, rows)]


def threes(refs):
    return [refs[i : i + 3] for i in range(0, len(refs), 3)]


def remote(collective_id, mib=60):
    return pltpu.CompilerParams(
        vmem_limit_bytes=mib << 20, collective_id=collective_id, has_side_effects=True,
    )


def slot_sum(slots, n):
    return lax.fori_loop(1, n, lambda j, total: total + slots[j], slots[0])


TR = 128
UP = 512


def row_tiles(rows):
    return [slice(r, r + TR) for r in range(0, rows, TR)]


def tiles(rows, cols, width=256):
    return [(rs, slice(c, c + width)) for rs in row_tiles(rows) for c in range(0, cols, width)]


def transpose_into(dst, src):
    for r in range(0, src.shape[0], 128):
        dst[:, r : r + 128] = src[r : r + 128, :].astype(f32).T.astype(bf16)


class Copies:
    def __init__(self, sems):
        self.sems, self.count = sems, 0

    def start(self, src, dst):
        copy = pltpu.make_async_copy(src, dst, self.sems.at[self.count])
        self.count += 1
        copy.start()
        return copy


ANY = pl.BlockSpec(memory_space=pl.ANY)


def bounds(len_ref, place):
    first = len_ref[place.core, 0]
    return first, first + len_ref[place.core, 1]


def first_kernel(x_in, g1, ga, pin, pout, ck, vec, w1_in, w2_in, wq_in, wk_in, wv_in, v1_in, v2_in, wo_in, rel_in,
                 x1_out, hid_out, na_out, q_out, k_out, v_out,
                 w1_out, w2_out, wq_out, wk_out, wv_out, v1_out, v2_out, wo_out, rel_out, far_out,
                 x_ref, w1, w2, wqkv, n_ref, act_ref, hid_ref, hid16_ref, x1_ref, na_ref, qkv_ref, sems, rsems, piece_ref, far_ref, fsend, frecv):
    place = Place()
    place.greet(("high",))
    copies = Copies(sems)
    cx = copies.start(x_in.at[pl.ds(pl.multiple_of(place.core * SLAB, SLAB), SLAB)], x_ref)
    qkv_in = (wq_in, wk_in, wv_in)
    mine = [copies.start(w1_in, w1.at[1]), copies.start(w2_in, w2.at[1])]
    mine_qkv = [copies.start(a, wqkv.at[1, k]) for k, a in enumerate(qkv_in)]
    piece_ref[:, : 2 * D] = pin[...]
    piece_ref[:, 2 * D : 3 * D] = pout[...]
    piece_ref[:, 3 * D :] = jnp.concatenate([ck[...], vec[...]], 1)
    far = Hop(place, "high", lambda p: piece_ref, far_ref, fsend, frecv)
    pairs = [(w1_in, w1.at[0]), (w2_in, w2.at[0])] + [(a, wqkv.at[0, k]) for k, a in enumerate(qkv_in)]
    pairs += [(v1_in, v1_out), (v2_in, v2_out), (wo_in, wo_out), (rel_in, rel_out)]
    swaps = [core_copy(place, a, b, rsems.at[k]) for k, (a, b) in enumerate(pairs)]
    cx.wait()
    for rs in row_tiles(SLAB):
        xhat, _ = norm_parts(x_ref[rs, :].astype(f32))
        n_ref[rs, :] = (xhat * g1[...]).astype(bf16)
    for copy in mine:
        copy.wait()
    chunks = [(p, c) for p in (1, 0) for c in range(0, w1.shape[2], UP)]
    ends = []

    def up(k):
        p, c = chunks[k]
        hid_ref[k % 2] = dot(n_ref[...], w1[p, :, c : c + UP])

    def down(k):
        p, c = chunks[k]
        part = dot(act_ref[k % 2], w2[p, c : c + UP, :])
        if k == 0:
            x1_ref[...] = part
        else:
            x1_ref[...] += part

    up(0)
    place.greeted(("high",))
    for copy in swaps[:2]:
        copy.start()
    far.start()
    for k, (p, c) in enumerate(chunks):
        for rs, cs in tiles(SLAB, UP):
            hid = hid_ref[k % 2, rs, cs]
            hid16_ref[p, rs, c + cs.start : c + cs.stop] = hid.astype(bf16)
            act_ref[k % 2, rs, cs] = (hid * jax.nn.sigmoid(hid)).astype(bf16)
        if k + 1 < len(chunks):
            if k + 1 == len(chunks) // 2:
                for copy in swaps[:2]:
                    copy.wait()
                for copy in swaps[2:]:
                    copy.start()
                ends.append(copies.start(hid16_ref.at[1], hid_out.at[1]))
                ends += [copies.start(w1.at[0], w1_out), copies.start(w2.at[0], w2_out)]
            up(k + 1)
        if k > 0:
            down(k - 1)
    ends.append(copies.start(hid16_ref.at[0], hid_out.at[0]))
    down(len(chunks) - 1)
    for rs in row_tiles(SLAB):
        x1 = x_ref[rs, :].astype(f32) + 0.5 * x1_ref[rs, :]
        x1_ref[rs, :] = x1
        xhat, _ = norm_parts(x1)
        na_ref[rs, :] = (xhat * ga[...]).astype(bf16)
    ends += [copies.start(x1_ref, x1_out), copies.start(na_ref, na_out)]
    for copy in mine_qkv + swaps[2:5]:
        copy.wait()
    ends += [copies.start(wqkv.at[0, n], out) for n, out in enumerate((wq_out, wk_out, wv_out))]
    w = D // 2
    for n, out in enumerate((q_out, k_out, v_out)):
        for p in (0, 1):
            value = dot(na_ref[...], wqkv[p, n]).astype(bf16)
            if n == 0:
                value = (value.astype(f32) * DH**-0.5).astype(bf16)
            qkv_ref[n, :, (1 - p) * w : (2 - p) * w] = value
        ends.append(copies.start(qkv_ref.at[n], out))
    far.wait()
    far_ref[place.hi] = piece_ref[...]
    far_out[...] = far_ref[...]
    for copy in swaps[5:] + ends:
        copy.wait()


def first_call(frames, g1, ga, pin, pout, ck, vec, w1, w2, wq, wk, wv, v1, v2, wo, rel):
    hid = w1.shape[1]
    moved = (w1, w2, wq, wk, wv, v1, v2, wo, rel)
    high, _ = split_axis(lax.axis_size("dp"))
    piece = (pin.shape[0], CONV_C)
    return pl.pallas_call(
        first_kernel,
        in_specs=[ANY] + [VMEM] * 6 + [ANY] * 9,
        out_specs=[ANY] * 15 + [VMEM],
        out_shape=[shape((SLAB, D), f32), shape((2, SLAB, hid), bf16)]
        + [shape((SLAB, D), bf16)] * 4
        + [shape(a.shape, a.dtype) for a in moved]
        + [shape((high, *piece), bf16)],
        scratch_shapes=[
            pltpu.VMEM((SLAB, D), bf16),
            pltpu.VMEM((2, D, hid), bf16),
            pltpu.VMEM((2, hid, D), bf16),
            pltpu.VMEM((2, 3, D, D // 2), bf16),
            pltpu.VMEM((SLAB, D), bf16),
            pltpu.VMEM((2, SLAB, UP), bf16),
            pltpu.VMEM((2, SLAB, UP), f32),
            pltpu.VMEM((2, SLAB, hid), bf16),
            pltpu.VMEM((SLAB, D), f32),
            pltpu.VMEM((SLAB, D), bf16),
            pltpu.VMEM((3, SLAB, D), bf16),
            pltpu.SemaphoreType.DMA((20,)),
            pltpu.SemaphoreType.DMA((9, 2)),
            pltpu.VMEM(piece, bf16),
        ]
        + slots_of(high, piece),
        compiler_params=remote(5),
        name="ffn1_forward",
    )(frames, g1, ga, pin, pout, ck, vec, *moved)


TI = 384
STAGES = [(h, start) for h in (0, 1) for start in range(0, SLAB, TI)]


def low_lanes(rows, cols=128):
    return lax.broadcasted_iota(jnp.int32, (rows, cols), 1) < 64


def attend_kernel(len_ref, q_ref, k_ref, v_ref, relo_ref, relx_ref, far_ref,
                  o16_ref, o32_ref, li_ref, p_ref, all_ref, qa_ref, ka_ref, va_ref, e_ref, rel_ref, s_ref, near_s, far_s, top_s,
                  near_ref, nsend, nrecv, other_ref, osems):
    step = pl.program_id(0)
    place = Place()
    near = Hop(place, "low", lambda p: far_ref, near_ref, nsend, nrecv)
    across = core_copy(place, near_ref, other_ref, osems)

    @pl.when(step == 0)
    def _():
        place.greet(("low",))

    b1, b2 = bounds(len_ref, place)
    lane = lax.broadcasted_iota(jnp.int32, (SLAB, 128), 1)
    slot = lane & 63
    frame = lax.broadcasted_iota(jnp.int32, (SLAB, 128), 0)
    label = jnp.where(frame < b1, 0, jnp.where(frame < b2, 1, 2))
    mq = jnp.where((slot < 3) & (slot != label), MASKED, 0.0)
    mk = jnp.where(slot == label, 1.0, 0.0)
    rel_ref[: 2 * RW + 1, :] = jnp.where(step < 2, relo_ref[...].astype(f32), relx_ref[...].astype(f32))
    rel_ref[2 * RW + 1 :, :] = jnp.broadcast_to(rel_ref[2 * RW : 2 * RW + 1, :], (255 - 2 * RW, 128))
    q, k, v = (ref[...].astype(f32) for ref in (q_ref, k_ref, v_ref))
    for h in (0, 1):
        mine = (lane < 64) if h == 0 else (lane >= 64)
        qa_ref[h] = jnp.where(mine, q, mq).astype(bf16)
        ka_ref[h] = jnp.where(mine, k, mk).astype(bf16)
        va_ref[h] = jnp.where(mine, v, 1.0).astype(bf16)
        rel_mine = low_lanes(256) if h == 0 else jnp.logical_not(low_lanes(256))
        relz = jnp.where(rel_mine, rel_ref[...], 0.0).astype(bf16)
        e_ref[h] = dot_nt(qa_ref[h], relz)
    subl = lax.broadcasted_iota(jnp.int32, (SUB, 128), 1)
    line = lax.broadcasted_iota(jnp.int32, (SUB, 128), 0)
    left_of = {0: subl < line, 64: subl < line + 64}
    tiles = SLAB // 128

    def scores(t):
        h, start = STAGES[t]
        s_ref[t % 3] = dot_nt(qa_ref[h, start : start + TI, :], ka_ref[h])

    def shift(t):
        h, start = STAGES[t]
        for r in range(0, TI, SUB):
            b = (start + r) // SUB
            off = 64 if b % 2 == 0 else 0
            rows = slice(r, r + SUB)
            eb = e_ref[h, b * SUB : (b + 1) * SUB, :]
            near = pltpu.roll(eb, off, 1, stride=1, stride_axis=0)
            left = jnp.broadcast_to(eb[:, 0:1], (SUB, 128))
            near_s[t % 2, 0, rows, :] = jnp.where(left_of[off], left, near[:, :128])
            near_s[t % 2, 1, rows, :] = near[:, 128:]
            far_s[t % 2, 0, rows, :] = left
            far_s[t % 2, 1, rows, :] = jnp.broadcast_to(eb[:, 128:129], (SUB, 128))

    def groups(t, r):
        b = (STAGES[t][1] + r) // SUB
        first = b // 2 - 1 if b % 2 == 0 else b // 2
        near = [(n, n - first) for n in (first, first + 1) if 0 <= n < tiles]
        return near, list(range(0, max(first, 0))), list(range(first + 2, tiles))

    def find(t, r):
        rows = slice(r, r + SUB)
        near, lefts, rights = groups(t, r)
        s = {n: s_ref[t % 3, rows, n * 128 : (n + 1) * 128] for n in range(tiles)}
        peak = None
        for n, k in near:
            value = s[n] + near_s[t % 2, k, rows, :]
            s_ref[t % 3, rows, n * 128 : (n + 1) * 128] = value
            peak = value if peak is None else jnp.maximum(peak, value)
        far = [far_s[t % 2, k, rows, :] for k in (0, 1)]
        for group, const in ((lefts, far[0]), (rights, far[1])):
            if group:
                top = s[group[0]]
                for n in group[1:]:
                    top = jnp.maximum(top, s[n])
                peak = jnp.maximum(peak, top + const)
        peak = jnp.broadcast_to(jnp.max(peak, -1, keepdims=True), (SUB, 128))
        top_s[t % 2, 0, rows, :] = peak
        top_s[t % 2, 1, rows, :] = peak - far[0]
        top_s[t % 2, 2, rows, :] = peak - far[1]

    def power(t, r):
        h, start = STAGES[t]
        rows = slice(r, r + SUB)
        _, lefts, rights = groups(t, r)
        tops = [top_s[t % 2, k, rows, :] for k in range(3)]
        for n in range(tiles):
            top = tops[1] if n in lefts else tops[2] if n in rights else tops[0]
            s = s_ref[t % 3, rows, n * 128 : (n + 1) * 128]
            p_ref[h, start + r : start + r + SUB, n * 128 : (n + 1) * 128] = jnp.exp(s - top).astype(bf16)

    low = low_lanes(TI)

    def mix(t):
        h, start = STAGES[t]
        rows = slice(start, start + TI)
        pv = dot(p_ref[h, rows, :], va_ref[h])
        li = 1.0 / pltpu.roll(pv, 64, 1)
        o = pv * li
        if h == 1:
            o = jnp.where(low, o32_ref[rows, :], o)
            li = jnp.where(low, li_ref[rows, :], li)
            o16_ref[rows, :] = o.astype(bf16)
        o32_ref[rows, :] = o
        li_ref[rows, :] = li

    count = len(STAGES)
    scores(0)
    shift(0)
    for t in range(count + 2):
        if t + 1 < count:
            shift(t + 1)
        for r in range(0, TI, SUB):
            if t < count:
                find(t, r)
            if 0 < t <= count:
                power(t - 1, r)
        if t + 1 < count:
            scores(t + 1)
        if 2 <= t:
            mix(t - 2)

    @pl.when(step == 0)
    def _():
        place.greeted(("low",))
        near.start()

    @pl.when(step == 2)
    def _():
        near.wait()
        near_ref[place.lo] = far_ref[...]
        across.start()

    @pl.when(step == 3)
    def _():
        across.wait()
        for l in range(place.low):
            all_ref[:, l, place.core] = near_ref[l]
            all_ref[:, l, 1 - place.core] = other_ref[l]


def attend_call(lengths, q, k, v, relo, relx, far):
    n, rows = lax.axis_size("dp"), far.shape[1]
    high, low = split_axis(n)
    pair = pl.BlockSpec((SLAB, 128), lambda h: (0, h))
    table_own = pl.BlockSpec((2 * RW + 1, 128), lambda h: (0, jnp.minimum(h, 1)))
    table_oth = pl.BlockSpec((2 * RW + 1, 128), lambda h: (0, jnp.maximum(h, 2) - 2))
    return pl.pallas_call(
        attend_kernel,
        grid=(D // 128,),
        in_specs=[SMEM, pair, pair, pair, table_own, table_oth, fixed(*far.shape)],
        out_specs=[pair, pair, pair, pl.BlockSpec((2, SLAB, SLAB), lambda h: (h, 0, 0)),
                   fixed(high, low, 2, rows, CONV_C)],
        out_shape=[
            shape((SLAB, D), bf16),
            shape((SLAB, D), f32),
            shape((SLAB, D), f32),
            shape((D // DH, SLAB, SLAB), bf16),
            shape((high, low, 2, rows, CONV_C), bf16),
        ],
        scratch_shapes=[
            pltpu.VMEM((2, SLAB, 128), bf16),
            pltpu.VMEM((2, SLAB, 128), bf16),
            pltpu.VMEM((2, SLAB, 128), bf16),
            pltpu.VMEM((2, SLAB, 256), f32),
            pltpu.VMEM((256, 128), f32),
            pltpu.VMEM((3, TI, SLAB), f32),
            pltpu.VMEM((2, 2, TI, 128), f32),
            pltpu.VMEM((2, 2, TI, 128), f32),
            pltpu.VMEM((2, 3, TI, 128), f32),
        ]
        + slots_of(low, (high, rows, CONV_C))
        + [pltpu.VMEM((low, high, rows, CONV_C), bf16), pltpu.SemaphoreType.DMA((2,))],
        compiler_params=remote(6),
        name="attention_forward",
    )(lengths, q, k, v, relo, relx, far)


GAIN_ROW, BN_GAIN_ROW, BN_BIAS_ROW = TAPS, TAPS + 1, TAPS + 2
FLAT = SLAB + 3 * TOP
DEEP = PADDED + 2 * TOP


def spread_out(flat_ref, padded_ref, c, b1, b2):
    zeros = jnp.zeros((TOP, 128), f32)
    flat_ref[c, TOP + SLAB :, :] = jnp.zeros((FLAT - TOP - SLAB, 128), f32)
    padded_ref[c, :TOP, :] = zeros
    padded_ref[c, TOP + PADDED :, :] = zeros
    for t0 in range(0, PADDED, CH):
        t = lax.broadcasted_iota(jnp.int32, (CH, 128), 0) + t0
        at = TOP + t0
        value = jnp.where(t < b1, flat_ref[c, at : at + CH, :], 0.0)
        middle = (t >= b1 + GAP) & (t < b2 + GAP)
        value = jnp.where(middle, flat_ref[c, at - GAP : at - GAP + CH, :], value)
        value = jnp.where(t >= b2 + 2 * GAP, flat_ref[c, at - 2 * GAP : at - 2 * GAP + CH, :], value)
        padded_ref[c, at : at + CH, :] = value


def lane_row(ref, r):
    return jnp.concatenate([ref[c, r : r + 1, :] for c in range(LT)], 1)


def lanes(ref, r):
    return jnp.concatenate([ref[r + c : r + c + 1, :] for c in range(LT)], 1)


def draw_in(padded_ref, c, t0, rows, b1, b2):
    t = lax.broadcasted_iota(jnp.int32, (rows, 128), 0) + t0
    value = jnp.where(t < b1, padded_ref[c, t0 : t0 + rows, :], padded_ref[c, t0 + GAP : t0 + GAP + rows, :])
    return jnp.where(t < b2, value, padded_ref[c, t0 + 2 * GAP : t0 + 2 * GAP + rows, :])


def conv_kernel_fn(len_ref, x1_in, o_in, woo, wox, weights, x2_out, u_out, hd_out, gp_out, st_ref, taps_ref,
                   x2_ref, o_ref, pin, rest, cn_ref, u_ref, u16_ref, hd_ref, gp_ref, flat_ref, out_ref,
                   mine, slots, send, recv, sems):
    place = Place()
    place.greet(("all",), False)
    copies = Copies(sems)
    cx = copies.start(x1_in, x2_ref)
    co = copies.start(o_in, o_ref)
    cr = copies.start(weights.at[:, 3 * D : 3 * D + 128], rest)
    cp = copies.start(weights.at[:, : 2 * D], pin)
    cr.wait()
    across = rest[...].astype(f32).T
    for c in range(LT):
        taps_ref[c] = across[:40, c * 128 : (c + 1) * 128]
    gain = lane_row(taps_ref, GAIN_ROW)
    w = woo.shape[0]
    cx.wait()
    co.wait()
    x2_ref[...] += dot(o_ref[:, :w], woo[...]) + dot(o_ref[:, w:], wox[...])
    for rs in row_tiles(SLAB):
        xhat, _ = norm_parts(x2_ref[rs, :])
        cn_ref[rs, :] = (xhat * gain).astype(bf16)
    ends = [copies.start(x2_ref, x2_out)]
    cp.wait()
    u_ref[...] = dot(cn_ref[...], pin[...])
    for rs in row_tiles(SLAB):
        for c in range(LT):
            cs, gs = slice(c * 128, c * 128 + 128), slice(D + c * 128, D + c * 128 + 128)
            u1, u2 = u_ref[rs, cs], u_ref[rs, gs]
            u16_ref[rs, cs] = u1.astype(bf16)
            u16_ref[rs, gs] = u2.astype(bf16)
            flat_ref[c, TOP + rs.start : TOP + rs.stop, :] = u1 * jax.nn.sigmoid(u2)
    ends.append(copies.start(u16_ref, u_out))
    b1, b2 = bounds(len_ref, place)

    def tile(c, carry):
        spread_out(flat_ref, gp_ref, c, b1, b2)
        for t0 in range(0, PADDED, CH):
            acc = jnp.zeros((CH, 128), f32)
            for b in range(8):
                at = TOP + t0 - TAPS // 2 + b
                x = gp_ref[c, at : at + CH + 24, :]
                for a in range(4):
                    acc = acc + x[8 * a : 8 * a + CH, :] * taps_ref[c, 8 * a + b : 8 * a + b + 1, :]
            out_ref[c, t0 : t0 + CH, :] = acc
        first = jnp.zeros((8, 128), f32)
        second = jnp.zeros((8, 128), f32)
        for t0 in range(0, SLAB, 128):
            hd = draw_in(out_ref, c, t0, 128, b1, b2)
            hd_ref[c, t0 : t0 + 128, :] = hd
            t = lax.broadcasted_iota(jnp.int32, (128, 128), 0) + t0
            hv = jnp.where(t < b2, hd, 0.0)
            first = first + rows_sum(hv)
            second = second + rows_sum(hv * hv)
        mine[pl.ds(c, 1), :] = jnp.sum(first, 0, keepdims=True)
        mine[pl.ds(LT + c, 1), :] = jnp.sum(second, 0, keepdims=True)
        return carry

    lax.fori_loop(0, LT, tile, 0)
    mine[2 * LT :, :] = jnp.full((8, 128), b2.astype(f32))
    slots[place.me] = mine[...]
    place.greeted(("all",), False)
    hop = Hop(place, "all", lambda p: mine, slots, send, recv)
    hop.start()
    ends += [copies.start(hd_ref, hd_out), copies.start(gp_ref, gp_out)]
    hop.wait()
    st_ref[...] = slot_sum(slots, place.n)
    for copy in ends:
        copy.wait()


def conv_call(lengths, x1, o16, woo, wox, gathered):
    n = lax.axis_size("dp")
    st = (2 * LT + 8, 128)
    return pl.pallas_call(
        conv_kernel_fn,
        in_specs=[SMEM, ANY, ANY, VMEM, VMEM, ANY],
        out_specs=[ANY, ANY, ANY, ANY, VMEM, VMEM],
        out_shape=[
            shape((SLAB, D), f32),
            shape((SLAB, 2 * D), bf16),
            shape((LT, SLAB, 128), f32),
            shape((LT, DEEP, 128), f32),
            shape(st, f32),
            shape((LT, 40, 128), f32),
        ],
        scratch_shapes=[
            pltpu.VMEM((SLAB, D), f32),
            pltpu.VMEM((SLAB, D), bf16),
            pltpu.VMEM((D, 2 * D), bf16),
            pltpu.VMEM((D, 128), bf16),
            pltpu.VMEM((SLAB, D), bf16),
            pltpu.VMEM((SLAB, 2 * D), f32),
            pltpu.VMEM((SLAB, 2 * D), bf16),
            pltpu.VMEM((LT, SLAB, 128), f32),
            pltpu.VMEM((LT, DEEP, 128), f32),
            pltpu.VMEM((LT, FLAT, 128), f32),
            pltpu.VMEM((LT, PADDED, 128), f32),
            pltpu.VMEM(st, f32),
        ]
        + slots_of(n, st, f32)
        + [pltpu.SemaphoreType.DMA((8,))],
        compiler_params=remote(0),
        name="conv_forward",
    )(lengths, x1, o16, woo, wox, gathered)


def middle_kernel(len_ref, hd_in, x2_in, ct_in, st, taps_ref, weights, g2, w1o_in, w1x_in, w2o_in, w2x_in, gf,
                  out_out, gx3_out, gz_out, acc, gpw_ref, back_ref, sums_ref,
                  hd_ref, x_ref, ct_ref, pout, w1, w2, wc_ref, n_ref, nt_ref, hid_ref, act_ref, slope_ref,
                  out_ref, out16_ref, gb_ref, gbt_ref, gn_ref, gc_ref, away, back, ssems, mine, slots, send, recv, sems):
    place = Place()
    place.greet(("all",))
    copies = Copies(sems)
    ch = copies.start(hd_in, hd_ref)
    cp = copies.start(weights.at[:, 2 * D : 3 * D], pout)
    cx = copies.start(x2_in, x_ref)
    cw = [copies.start(a, b) for a, b in ((w1x_in, w1.at[0]), (w1o_in, w1.at[1]), (w2x_in, w2.at[0]), (w2o_in, w2.at[1]))]
    start = pl.multiple_of(place.core * SLAB, SLAB)
    cc = copies.start(ct_in.at[pl.ds(start, SLAB)], ct_ref)

    _, b2 = bounds(len_ref, place)
    bng, bnb = lane_row(taps_ref, BN_GAIN_ROW), lane_row(taps_ref, BN_BIAS_ROW)
    count = st[2 * LT : 2 * LT + 1, 0:1]
    centre = lanes(st, 0) / count
    inv_b = lax.rsqrt(lanes(st, LT) / count - centre * centre + BATCH_EPS)

    def normal(rs, c):
        cs = slice(c * 128, c * 128 + 128)
        zh = (hd_ref[c, rs, :] - centre[:, cs]) * inv_b[:, cs]
        z = zh * bng[:, cs] + bnb[:, cs]
        return cs, zh, z, jax.nn.sigmoid(z)

    ch.wait()
    for rs in row_tiles(SLAB):
        for c in range(LT):
            cs, _, z, sg = normal(rs, c)
            wc_ref[rs, cs] = (z * sg).astype(bf16)
    cp.wait()
    cx.wait()
    x_ref[...] += dot(wc_ref[...], pout[...])
    for rs in row_tiles(SLAB):
        xhat, _ = norm_parts(x_ref[rs, :])
        n_ref[rs, :] = (xhat * g2[...]).astype(bf16)
    for copy in cw:
        copy.wait()
    chunks = [(p, c) for p in (0, 1) for c in range(0, w1.shape[2], UP)]

    def up(k):
        p, c = chunks[k]
        hid_ref[k % 2] = dot(n_ref[...], w1[p, :, c : c + UP])

    def down(k):
        p, c = chunks[k]
        part = dot(act_ref[p, :, c : c + UP], w2[p, c : c + UP, :])
        if k == 0:
            out_ref[...] = part
        else:
            out_ref[...] += part

    up(0)
    for k, (p, c) in enumerate(chunks):
        for rs, cs in tiles(SLAB, UP):
            hid = hid_ref[k % 2, rs, cs]
            sg = jax.nn.sigmoid(hid)
            act = hid * sg
            at = slice(c + cs.start, c + cs.stop)
            act_ref[p, rs, at] = act.astype(bf16)
            slope_ref[p, rs, at] = (sg + act * (1.0 - sg)).astype(bf16)
        if k + 1 < len(chunks):
            up(k + 1)
        if k > 0:
            down(k - 1)
    down(len(chunks) - 1)
    transpose_into(nt_ref, n_ref)

    cc.wait()
    final_gain = jnp.zeros((8, D), f32)
    for rs in row_tiles(SLAB):
        t = lax.broadcasted_iota(jnp.int32, (TR, 1), 0) + rs.start
        valid = (t < b2).astype(f32)
        xhat, inv = norm_parts(x_ref[rs, :] + 0.5 * out_ref[rs, :])
        out16_ref[rs, :] = (valid * xhat * gf[...]).astype(bf16)
        g = ct_ref[rs, :].astype(f32) * valid
        gx4 = norm_back(g, gf[...], xhat, inv)
        out_ref[rs, :] = gx4
        gb_ref[rs, :] = (0.5 * gx4).astype(bf16)
        final_gain = final_gain + rows_sum(g * xhat)
    ends = [copies.start(out16_ref, out_out)]
    transpose_into(gbt_ref, gb_ref)

    def gup(k):
        p, c = chunks[k]
        hid_ref[k % 2] = dot_nt(gb_ref[...], w2[p, c : c + UP, :])

    def gdown(k):
        p, c = chunks[k]
        part = dot_nt(slope_ref[p, :, c : c + UP], w1[p, :, c : c + UP])
        if k == 0:
            gn_ref[...] = part
        else:
            gn_ref[...] += part

    gup(0)
    for k, (p, c) in enumerate(chunks):
        for rs, cs in tiles(SLAB, UP):
            at = slice(c + cs.start, c + cs.stop)
            slope_ref[p, rs, at] = (hid_ref[k % 2, rs, cs] * slope_ref[p, rs, at].astype(f32)).astype(bf16)
        if k + 1 < len(chunks):
            gup(k + 1)
        if k > 0:
            gdown(k - 1)
    gdown(len(chunks) - 1)

    ffn_gain = jnp.zeros((8, D), f32)
    for rs in row_tiles(SLAB):
        xhat, inv = norm_parts(x_ref[rs, :])
        gn = gn_ref[rs, :]
        gx3 = out_ref[rs, :] + norm_back(gn, g2[...], xhat, inv)
        x_ref[rs, :] = gx3
        gc_ref[rs, :] = gx3.astype(bf16)
        ffn_gain = ffn_gain + rows_sum(gn * xhat)
    ends.append(copies.start(x_ref, gx3_out))
    gn_ref[...] = dot_nt(gc_ref[...], pout[...])
    parts = [[jnp.zeros((8, 128), f32) for _ in range(4)] for _ in range(LT)]
    for rs in row_tiles(SLAB):
        t = lax.broadcasted_iota(jnp.int32, (TR, 1), 0) + rs.start
        valid = (t < b2).astype(f32)
        for c in range(LT):
            cs, zh, z, sg = normal(rs, c)
            gz = gn_ref[rs, cs] * (sg + z * sg * (1.0 - sg))
            hd_ref[c, rs, :] = gz
            e = gz * bng[:, cs] * valid
            for k, v in enumerate((gz, gz * zh, e, e * zh)):
                parts[c][k] = parts[c][k] + rows_sum(v)
    ends.append(copies.start(hd_ref, gz_out))
    sums_ref[...] = jnp.zeros(sums_ref.shape, f32)
    for c in range(LT):
        cs = slice(c * 128, c * 128 + 128)
        for k in range(4):
            total = jnp.sum(parts[c][k], 0, keepdims=True)
            sums_ref[k : k + 1, cs] = total
            if k >= 2:
                mine[(k - 2) * LT + c : (k - 2) * LT + c + 1, :] = total
    sums_ref[4:5, :] = jnp.sum(final_gain, 0, keepdims=True)
    sums_ref[5:6, :] = jnp.sum(ffn_gain, 0, keepdims=True)
    slots[place.me] = mine[...]
    place.greeted(("all",))
    hop = Hop(place, "all", lambda p: mine, slots, send, recv)
    hop.start()

    dims = acc.shape[1:]
    swaps = [core_copy(place, away.at[k], back.at[k], ssems.at[k]) for k in range(2)]
    lhs, rhs = (nt_ref, gbt_ref), (slope_ref, act_ref)
    for k in range(2):
        away[k] = dot(lhs[k][...], rhs[k][0]).reshape(dims).astype(bf16)
        swaps[k].start()
    gpw_ref[...] = dot_tn(wc_ref[...], gc_ref[...]).astype(bf16)
    for k in range(2):
        own = dot(lhs[k][...], rhs[k][1]).reshape(dims)
        swaps[k].wait()
        acc[k] = (own + back[k].astype(f32)).astype(bf16)
    hop.wait()
    back_ref[...] = slot_sum(slots, place.n)
    for copy in ends:
        copy.wait()


def grad_dims(cols):
    n = lax.axis_size("dp")
    return n, (*split_axis(n), D // n, cols)


def middle_call(lengths, hd, x2, cot, st, taps, gathered, g2, w1o, w1x, w2o, w2x, gf):
    hid = w1o.shape[1]
    n, dims = grad_dims(hid)
    stat = (2 * LT, 128)
    return pl.pallas_call(
        middle_kernel,
        in_specs=[SMEM, ANY, ANY, ANY, VMEM, VMEM, ANY, VMEM, ANY, ANY, ANY, ANY, VMEM],
        out_specs=[ANY, ANY, ANY, VMEM, VMEM, VMEM, VMEM],
        out_shape=[
            shape((SLAB, D), bf16),
            shape((SLAB, D), f32),
            shape((LT, SLAB, 128), f32),
            shape((2, *dims), bf16),
            shape((D, D), bf16),
            shape(stat, f32),
            shape((8, D), f32),
        ],
        scratch_shapes=[
            pltpu.VMEM((LT, SLAB, 128), f32),
            pltpu.VMEM((SLAB, D), f32),
            pltpu.VMEM((SLAB, D), bf16),
            pltpu.VMEM((D, D), bf16),
            pltpu.VMEM((2, D, hid), bf16),
            pltpu.VMEM((2, hid, D), bf16),
            pltpu.VMEM((SLAB, D), bf16),
            pltpu.VMEM((SLAB, D), bf16),
            pltpu.VMEM((D, SLAB), bf16),
            pltpu.VMEM((2, SLAB, UP), f32),
            pltpu.VMEM((2, SLAB, hid), bf16),
            pltpu.VMEM((2, SLAB, hid), bf16),
            pltpu.VMEM((SLAB, D), f32),
            pltpu.VMEM((SLAB, D), bf16),
            pltpu.VMEM((SLAB, D), bf16),
            pltpu.VMEM((D, SLAB), bf16),
            pltpu.VMEM((SLAB, D), f32),
            pltpu.VMEM((SLAB, D), bf16),
            pltpu.VMEM((2, *dims), bf16),
            pltpu.VMEM((2, *dims), bf16),
            pltpu.SemaphoreType.DMA((2, 2)),
            pltpu.VMEM(stat, f32),
        ]
        + slots_of(n, stat, f32)
        + [pltpu.SemaphoreType.DMA((12,))],
        compiler_params=remote(1),
        name="ffn2_forward_backward",
    )(lengths, hd, x2, cot, st, taps, gathered, g2, w1o, w1x, w2o, w2x, gf)


def conv_back_kernel(len_ref, acc_in, gz_in, hd_in, gp_in, st, back, taps_ref, u_in, x2_in, gx3_in, weights, woo, wox,
                     gpw, sums, gx2_out, ga_out, go_out, cg_ref, mid0, mid1, mid2,
                     gz_ref, hd_ref, gp_ref, u_ref, x2_ref, gx_ref, pin, flat_ref, pad_ref, out_ref, acc_ref, gtap_ref,
                     gu_ref, gn_ref, cn_ref, ga_ref, go_ref, sems, tsems, *scr):
    place = Place()
    place.greet(("low", "high"), False)
    copies = Copies(sems)
    def tile_copies(c):
        pairs = ((gz_in, gz_ref), (hd_in, hd_ref), (gp_in, gp_ref))
        return [pltpu.make_async_copy(a.at[c], b.at[c], tsems.at[k, c]) for k, (a, b) in enumerate(pairs)]

    for c in range(LT):
        for copy in tile_copies(c):
            copy.start()
    rest = [copies.start(a, b) for a, b in (
        (u_in, u_ref), (weights.at[:, : 2 * D], pin), (x2_in, x2_ref), (gx3_in, gx_ref))]
    b1, b2 = bounds(len_ref, place)
    gain = lane_row(taps_ref, GAIN_ROW)
    hops = [v.first(place, acc_in, refs) for v, refs in zip(PAIR_VIEWS, threes(scr))]
    place.greeted(("low", "high"), False)
    for hop in hops:
        hop.start()

    def tile(c, carry):
        for copy in tile_copies(c):
            copy.wait()
        count = st[2 * LT : 2 * LT + 1, :]
        centre = st[pl.ds(c, 1), :] / count
        inv_b = lax.rsqrt(st[pl.ds(LT + c, 1), :] / count - centre * centre + BATCH_EPS)
        a1 = back[pl.ds(c, 1), :] / count
        a2 = back[pl.ds(LT + c, 1), :] / count
        bn_gain = taps_ref[c, BN_GAIN_ROW : BN_GAIN_ROW + 1, :]
        for t0 in range(0, SLAB, 128):
            t = lax.broadcasted_iota(jnp.int32, (128, 128), 0) + t0
            zh = (hd_ref[c, t0 : t0 + 128, :] - centre) * inv_b
            away = jnp.where(t < b2, a1 + zh * a2, 0.0)
            flat_ref[c, TOP + t0 : TOP + t0 + 128, :] = inv_b * (gz_ref[c, t0 : t0 + 128, :] * bn_gain - away)
        spread_out(flat_ref, pad_ref, c, b1, b2)
        acc_ref[...] = jnp.zeros(acc_ref.shape, f32)
        for t0 in range(0, PADDED, CH):
            acc = jnp.zeros((CH, 128), f32)
            gl = gp_ref[c, TOP + t0 : TOP + t0 + CH, :]
            for b in range(8):
                at = TOP + t0 + TAPS // 2 - TAPS + 1 + b
                x = pad_ref[c, at : at + CH + 24, :]
                for a in range(4):
                    k = TAPS - 1 - (8 * a + b)
                    part = x[8 * a : 8 * a + CH, :]
                    acc = acc + part * taps_ref[c, k : k + 1, :]
                    acc_ref[8 * k : 8 * k + 8, :] += rows_sum(part * gl)
            out_ref[c, t0 : t0 + CH, :] = acc
        gtap_ref[c] = jnp.sum(acc_ref[...].reshape(TAPS, 8, 128), 1)
        for t0 in range(0, SLAB, 128):
            flat_ref[c, t0 : t0 + 128, :] = draw_in(out_ref, c, t0, 128, b1, b2)
        return carry

    lax.fori_loop(0, LT, tile, 0)
    for copy in rest:
        copy.wait()
    for rs in row_tiles(SLAB):
        for c in range(LT):
            cs, gs = slice(c * 128, c * 128 + 128), slice(D + c * 128, D + c * 128 + 128)
            sg = jax.nn.sigmoid(u_ref[rs, gs].astype(f32))
            g = flat_ref[c, rs, :] * sg
            gu_ref[rs, cs] = g.astype(bf16)
            gu_ref[rs, gs] = (g * u_ref[rs, cs].astype(f32) * (1.0 - sg)).astype(bf16)
    gn_ref[...] = dot_nt(gu_ref[...], pin[...])
    gain_sum = jnp.zeros((8, D), f32)
    for rs in row_tiles(SLAB):
        xhat, inv = norm_parts(x2_ref[rs, :])
        gn = gn_ref[rs, :]
        gx2 = gx_ref[rs, :] + norm_back(gn, gain, xhat, inv)
        gx_ref[rs, :] = gx2
        ga_ref[rs, :] = gx2.astype(bf16)
        cn_ref[rs, :] = (xhat * gain).astype(bf16)
        gain_sum = gain_sum + rows_sum(gn * xhat)
    ends = [copies.start(gx_ref, gx2_out), copies.start(ga_ref, ga_out)]
    w = woo.shape[0]
    go_ref[:, :w] = dot_nt(ga_ref[...], woo[...]).astype(bf16)
    go_ref[:, w:] = dot_nt(ga_ref[...], wox[...]).astype(bf16)
    ends.append(copies.start(go_ref, go_out))
    cg_ref[:, : 2 * D] = dot_tn(cn_ref[...], gu_ref[...]).astype(bf16)
    cg_ref[:, 2 * D : 3 * D] = gpw[...]
    gain_sum = jnp.sum(gain_sum, 0, keepdims=True)
    for c in range(LT):
        cols = slice(c * 128, (c + 1) * 128)
        rows = [gtap_ref[c], gain_sum[:, cols], sums[1:2, cols], sums[0:1, cols]]
        block = jnp.concatenate(rows + [jnp.zeros((128 - TAPS - 3, 128), f32)], 0)
        cg_ref[c * 128 : (c + 1) * 128, 3 * D :] = block.T.astype(bf16)
    for hop, mid in zip(hops, (mid0, mid1, mid2)):
        hop.wait()
        mid[...] = hop.total().astype(bf16)
    for copy in ends:
        copy.wait()


def conv_back_call(lengths, acc, gz, hd, gp, st, back, taps, u, x2, gx3, gathered, woo, wox, gpw, sums):
    n, rows = lax.axis_size("dp"), acc.shape[3]
    return pl.pallas_call(
        conv_back_kernel,
        in_specs=[SMEM, VMEM, ANY, ANY, ANY, VMEM, VMEM, VMEM, ANY, ANY, ANY, ANY, VMEM, VMEM, VMEM, VMEM],
        out_specs=[ANY, ANY, ANY, VMEM, VMEM, VMEM, VMEM],
        out_shape=[
            shape((SLAB, D), f32),
            shape((SLAB, D), bf16),
            shape((SLAB, D), bf16),
            shape((D, CONV_C), bf16),
        ]
        + [shape(v.mid(n, rows), bf16) for v in PAIR_VIEWS],
        scratch_shapes=[
            pltpu.VMEM((LT, SLAB, 128), f32),
            pltpu.VMEM((LT, SLAB, 128), f32),
            pltpu.VMEM((LT, DEEP, 128), f32),
            pltpu.VMEM((SLAB, 2 * D), bf16),
            pltpu.VMEM((SLAB, D), f32),
            pltpu.VMEM((SLAB, D), f32),
            pltpu.VMEM((D, 2 * D), bf16),
            pltpu.VMEM((LT, FLAT, 128), f32),
            pltpu.VMEM((LT, DEEP, 128), f32),
            pltpu.VMEM((LT, PADDED, 128), f32),
            pltpu.VMEM((TAPS * 8, 128), f32),
            pltpu.VMEM((LT, TAPS, 128), f32),
            pltpu.VMEM((SLAB, 2 * D), bf16),
            pltpu.VMEM((SLAB, D), f32),
            pltpu.VMEM((SLAB, D), bf16),
            pltpu.VMEM((SLAB, D), bf16),
            pltpu.VMEM((SLAB, D), bf16),
            pltpu.SemaphoreType.DMA((10,)),
            pltpu.SemaphoreType.DMA((3, LT)),
        ]
        + firsts(PAIR_VIEWS, n, rows),
        compiler_params=remote(2),
        name="conv_backward",
    )(lengths, acc, gz, hd, gp, st, back, taps, u, x2, gx3, gathered, woo, wox, gpw, sums)


HEAD_VIEWS = (View(None, 0, 384, "low"), View(None, 384, 512, "high"))


def attend_back_kernel(q_ref, k_ref, v_ref, g_ref, o_ref, li_ref, p_ref, relo_ref, relx_ref,
                       wqo, wko, wvo, wqx, wkx, wvx, o16_ref, na_in, gatt_in, x1_in, gx2_in, gain,
                       mid0, mid1, mid2, cg_ref,
                       gt_ref, gx1_out, agains_ref, f2a_ref, f2b_ref, cpi_ref, cpo_ref, crest_ref, h0_ref, acc1_ref,
                       ga_ref, va_ref, kt_ref, qt_ref, got_ref, gs_ref, gp_ref, w_ref, fl_ref, n_ref, all_ref, other_ref,
                       relt_ref, far_s, flip_ref, rel_ref, relf_ref, wide_ref, gn_ref, x1_ref, gx_ref,
                       pg_ref, away, hback, hsems, acc0_ref, sems, cback, csems, cacc, *scr):
    step = pl.program_id(0)
    place = Place()
    loads = [pltpu.make_async_copy(a, b, sems.at[k]) for k, (a, b) in enumerate((
        (na_in, wide_ref.at[0]), (gatt_in, wide_ref.at[1]), (x1_in, x1_ref), (gx2_in, gx_ref)))]
    gx1_copy = pltpu.make_async_copy(gx_ref, gx1_out, sems.at[4])
    scr = threes(scr)
    nv = len(PAIR_VIEWS)
    last = [v.second(place, mid, refs) for v, mid, refs in zip(PAIR_VIEWS, (mid0, mid1, mid2), scr[:nv])]
    cfirst = [v.first(place, cacc, refs) for v, refs in zip(CONV_VIEWS, scr[nv:])]
    nc = len(CONV_VIEWS)
    cmids = scr[nv + 2 * nc][:nc]
    csecond = [v.second(place, mid, refs) for v, mid, refs in zip(CONV_VIEWS, cmids, scr[nv + nc :])]
    cswap = core_copy(place, cg_ref.at[:, :, 1 - place.core], cback, csems)
    hswaps = [core_copy(place, away.at[k], hback.at[k], hsems.at[k]) for k in range(2)]
    at = nv + 2 * nc + 1
    hfirst = [v.first(place, acc0_ref, refs) for v, refs in zip(HEAD_VIEWS, scr[at:])]
    nh = len(HEAD_VIEWS)
    hmids = scr[at + 2 * nh][:nh]
    hsecond = [v.second(place, mid, refs) for v, mid, refs in zip(HEAD_VIEWS, hmids, scr[at + nh :])]
    kinds = ("low", "high")

    @pl.when(step == 0)
    def _():
        place.greet(kinds)
        for copy in loads:
            copy.start()
        line = lax.broadcasted_iota(jnp.int32, (256, 256), 0)
        flip_ref[...] = jnp.where(line + lax.broadcasted_iota(jnp.int32, (256, 256), 1) == 255, 1.0, 0.0).astype(bf16)
        line = lax.broadcasted_iota(jnp.int32, (128, 128), 0)
        other = (line < 64) != (lax.broadcasted_iota(jnp.int32, (128, 128), 1) < 64)
        other_ref[...] = jnp.where(other, 1.0, 0.0).astype(bf16)

    lane = lax.broadcasted_iota(jnp.int32, (SLAB, 128), 1)
    go = g_ref[...].astype(f32) * li_ref[...]
    got_ref[...] = go.T.astype(bf16)
    qt_ref[...] = q_ref[...].astype(f32).T.astype(bf16)
    kt_ref[...] = k_ref[...].astype(f32).T.astype(bf16)
    go = go.astype(bf16).astype(f32)
    product = go * o_ref[...]
    product_hi = product.astype(bf16)
    product_lo = (product - product_hi.astype(f32)).astype(bf16)
    inner = dot(product_hi, other_ref[...]) + dot(product_lo, other_ref[...])
    inner_hi = inner.astype(bf16).astype(f32)
    inner_lo = inner - inner_hi
    own_pair = step >= 2
    rel_ref[: 2 * RW + 1, :] = jnp.where(own_pair, relo_ref[...].astype(f32), relx_ref[...].astype(f32))
    relf_ref[:128, :] = dot(flip_ref[128:, :128], rel_ref[:128, :].astype(bf16))
    line = lax.broadcasted_iota(jnp.int32, (128, 128), 0)
    relf_ref[128:, :] = jnp.where(
        line < 2, rel_ref[0:1, :], jnp.where(line < 4, rel_ref[2 * RW : 2 * RW + 1, :], 0.0)
    )
    relt_ref[...] = relf_ref[...].T.astype(bf16)
    for h in (0, 1):
        mine = (lane < 64) if h == 0 else (lane >= 64)
        base = 64 - 64 * h
        extra = jnp.where(lane == base, -inner_hi, jnp.where(lane == base + 1, -inner_lo, 0.0))
        ga_ref[h] = jnp.where(mine, go, extra).astype(bf16)
        ones = jnp.where((lane == base) | (lane == base + 1), 1.0, 0.0)
        va_ref[h] = jnp.where(mine, v_ref[...].astype(f32), ones).astype(bf16)

    subl = lax.broadcasted_iota(jnp.int32, (SUB, 128), 1)
    line = lax.broadcasted_iota(jnp.int32, (SUB, 128), 0)
    left_of = {0: subl < line, 64: subl < line + 64}
    tiles = SLAB // 128
    zero16 = jnp.zeros((SUB, 128), bf16)

    def grow(t):
        h, start = STAGES[t]
        gp_ref[t % 2] = dot_nt(ga_ref[h, start : start + TI, :], va_ref[h])

    def weigh(t):
        h, start = STAGES[t]
        for r in range(0, TI, SUB):
            b = (start + r) // SUB
            off = 64 if b % 2 == 0 else 0
            first = b // 2 - 1 if b % 2 == 0 else b // 2
            rows = slice(start + r, start + r + SUB)
            near = slice(r, r + SUB)
            sums = [jnp.zeros((SUB, 128), f32), jnp.zeros((SUB, 128), f32)]
            for n in range(tiles):
                cols = slice(n * 128, (n + 1) * 128)
                gs = p_ref[h, rows, cols].astype(f32) * gp_ref[t % 2, near, cols]
                gs16 = gs.astype(bf16)
                gs_ref[h, rows, cols] = gs16
                if n < first:
                    sums[0] = sums[0] + gs
                elif n > first + 1:
                    sums[1] = sums[1] + gs
                elif n == first:
                    w_ref[t % 2, near, :128] = gs16
                    sums[0] = sums[0] + jnp.where(left_of[off], gs, 0.0)
                else:
                    w_ref[t % 2, near, 128:] = gs16
                    sums[1] = sums[1] + jnp.where(left_of[off], 0.0, gs)
            if first < 0:
                w_ref[t % 2, near, :128] = zero16
            if first + 1 >= tiles:
                w_ref[t % 2, near, 128:] = zero16
            far_s[t % 2, 0, near, :] = sums[0]
            far_s[t % 2, 1, near, :] = sums[1]

    def flip(t):
        fl_ref[t % 2] = dot(w_ref[t % 2], flip_ref[...])

    def unroll(t):
        h, start = STAGES[t]
        for r in range(0, TI, SUB):
            off = 64 if ((start + r) // SUB) % 2 == 0 else 0
            near = pltpu.roll(fl_ref[t % 2, r : r + SUB, :], (off + 128) % 256, 1, stride=1, stride_axis=0)
            n_ref[h, start + r : start + r + SUB, :128] = near[:, :128].astype(bf16)
            far_left = jnp.sum(far_s[t % 2, 0, r : r + SUB, :], -1, keepdims=True)
            far_right = jnp.sum(far_s[t % 2, 1, r : r + SUB, :], -1, keepdims=True)
            left_hi = far_left.astype(bf16).astype(f32)
            right_hi = far_right.astype(bf16).astype(f32)
            far = jnp.where(subl == 0, left_hi, 0.0)
            far = jnp.where(subl == 1, far_left - left_hi, far)
            far = jnp.where(subl == 2, right_hi, far)
            far = jnp.where(subl == 3, far_right - right_hi, far)
            n_ref[h, start + r : start + r + SUB, 128:] = far.astype(bf16)

    def query(t):
        h, start = STAGES[t]
        rows = slice(start, start + TI)
        half = slice(64 * h, 64 * h + 64)
        part = dot_nt(kt_ref[half, :], gs_ref[h, rows, :]) + dot_nt(relt_ref[half, :], n_ref[h, rows, :])
        all_ref[half, rows] = (part * DH**-0.5).astype(bf16)

    def key(h):
        half = slice(64 * h, 64 * h + 64)
        all_ref[128 + 64 * h : 192 + 64 * h, :] = dot(qt_ref[half, :], gs_ref[h]).astype(bf16)
        gt_ref[half, :] = dot(qt_ref[half, :], n_ref[h])

    def value(h):
        half = slice(64 * h, 64 * h + 64)
        all_ref[256 + 64 * h : 320 + 64 * h, :] = dot(got_ref[half, :], p_ref[h]).astype(bf16)

    grow(0)
    for t in range(len(STAGES)):
        weigh(t)
        if t > 0:
            unroll(t - 1)
        if t + 1 < len(STAGES):
            grow(t + 1)
        flip(t)
        if t > 0:
            query(t - 1)
        if t == 1:
            value(0)
        if t == 2:
            value(1)
        if t == 3:
            key(0)
        if t == 4:
            all_ref[384:, :] = o16_ref[...].astype(f32).T.astype(bf16)
    unroll(len(STAGES) - 1)
    query(len(STAGES) - 1)
    key(1)

    @pl.when(step == 0)
    def _():
        loads[0].wait()
        loads[1].wait()

    def choose(own, oth):
        return jnp.where(own_pair, own[...].astype(f32), oth[...].astype(f32)).astype(bf16)

    weights = jnp.concatenate([choose(wqo, wqx), choose(wko, wkx), choose(wvo, wvx)], 1)
    gn_ref[...] = jnp.where(step == 0, 0.0, gn_ref[...]) + dot(weights, all_ref[:384, :])
    pg_ref[:384, :] = dot(all_ref[:384, :], wide_ref[0])
    pg_ref[384:, :] = dot(all_ref[384:, :], wide_ref[1])
    pg_ref[...] = pg_ref[...].T
    dims = acc1_ref.shape

    @pl.when(step == 0)
    def _():
        place.greeted(kinds)
        for hop in last:
            hop.start()
        cswap.start()
        away[0] = pg_ref[...].reshape(dims).astype(bf16)
        hswaps[0].start()

    @pl.when(step == 1)
    def _():
        away[1] = pg_ref[...].reshape(dims).astype(bf16)
        hswaps[1].start()
        cswap.wait()
        cacc[...] = (cg_ref[:, :, place.core].astype(f32) + cback[...].astype(f32)).astype(bf16)
        for hop in cfirst:
            hop.start()
        for hop, v in zip(last, PAIR_VIEWS):
            hop.wait()
            if v.index == 0:
                f2a_ref[:, v.start : v.stop] = hop.total()
            else:
                f2b_ref[:, v.start : v.stop] = hop.total()

    @pl.when(step == 2)
    def _():
        hswaps[0].wait()
        acc0_ref[...] = (pg_ref[...].reshape(dims) + hback[0].astype(f32)).astype(bf16)
        for hop in hfirst:
            hop.start()
        for hop, mid, on in zip(cfirst, cmids, csecond):
            hop.wait()
            mid[...] = hop.total().astype(bf16)
            on.start()

    @pl.when(step == 3)
    def _():
        hswaps[1].wait()
        acc1_ref[...] = (pg_ref[...].reshape(dims) + hback[1].astype(f32)).astype(bf16)
        csecond[0].wait()
        cpi_ref[...] = csecond[0].total()
        csecond[1].wait()
        total = csecond[1].total()
        cpo_ref[...] = total[:, :D]
        crest_ref[...] = total[:, D:]
        for hop, mid, on in zip(hfirst, hmids, hsecond):
            hop.wait()
            mid[...] = hop.total().astype(bf16)
            on.start()
        loads[2].wait()
        loads[3].wait()
        total = jnp.zeros((8, D), f32)
        for rs in row_tiles(SLAB):
            xhat, inv = norm_parts(x1_ref[rs, :])
            gn = gn_ref[:, rs].T
            gx_ref[rs, :] = gx_ref[rs, :] + norm_back(gn, gain[...], xhat, inv)
            total = total + rows_sum(gn * xhat)
        gx1_copy.start()
        agains_ref[...] = total
        for hop, v in zip(hsecond, HEAD_VIEWS):
            hop.wait()
            h0_ref[:, v.start : v.stop] = hop.total()
        gx1_copy.wait()


def pair_of(s):
    return (s + 2) % 4


def attend_back_call(q, k, v, go, o32, li, p, relo, relx, weights, o16, na, gatt, x1, gx2, gain, mids, cg):
    n, rows, crows = lax.axis_size("dp"), mids[0].shape[1], cg.shape[3]
    high, low = split_axis(n)
    cdims = (high, low, crows, CONV_C)
    hdims = (high, low, rows, 512)
    pair = pl.BlockSpec((SLAB, 128), lambda s: (0, pair_of(s)))
    head_map = pl.BlockSpec((2, SLAB, SLAB), lambda s: (pair_of(s), 0, 0))
    own = lambda s: (0, jnp.maximum(s, 2) - 2)
    oth = lambda s: (0, jnp.minimum(s, 1))
    table_own, table_oth = pl.BlockSpec((2 * RW + 1, 128), own), pl.BlockSpec((2 * RW + 1, 128), oth)
    w_own, w_oth = pl.BlockSpec((D, 128), own), pl.BlockSpec((D, 128), oth)
    return pl.pallas_call(
        attend_back_kernel,
        grid=(D // 128,),
        in_specs=[pair] * 6 + [head_map, table_own, table_oth] + [w_own] * 3 + [w_oth] * 3 + [pair]
        + [ANY] * 4 + [fixed(1, D)] + [fixed(*a.shape) for a in (*mids, cg)],
        out_specs=[pl.BlockSpec((128, 256), lambda s: (pair_of(s), 0)), ANY, fixed(8, D), fixed(rows, 1024),
                   fixed(rows, 1024), fixed(crows, 2 * D), fixed(crows, D), fixed(crows, 128),
                   fixed(rows, 512), fixed(*hdims)],
        out_shape=[
            shape((D, 256), f32),
            shape((SLAB, D), f32),
            shape((8, D), f32),
            shape((rows, 1024), f32),
            shape((rows, 1024), f32),
            shape((crows, 2 * D), f32),
            shape((crows, D), f32),
            shape((crows, 128), f32),
            shape((rows, 512), f32),
            shape(hdims, bf16),
        ],
        scratch_shapes=[
            pltpu.VMEM((2, SLAB, 128), bf16),
            pltpu.VMEM((2, SLAB, 128), bf16),
            pltpu.VMEM((128, SLAB), bf16),
            pltpu.VMEM((128, SLAB), bf16),
            pltpu.VMEM((128, SLAB), bf16),
            pltpu.VMEM((2, SLAB, SLAB), bf16),
            pltpu.VMEM((2, TI, SLAB), f32),
            pltpu.VMEM((2, TI, 256), bf16),
            pltpu.VMEM((2, TI, 256), f32),
            pltpu.VMEM((2, SLAB, 256), bf16),
            pltpu.VMEM((512, SLAB), bf16),
            pltpu.VMEM((128, 128), bf16),
            pltpu.VMEM((128, 256), bf16),
            pltpu.VMEM((2, 2, TI, 128), f32),
            pltpu.VMEM((256, 256), bf16),
            pltpu.VMEM((136, 128), f32),
            pltpu.VMEM((256, 128), f32),
            pltpu.VMEM((2, SLAB, D), bf16),
            pltpu.VMEM((D, SLAB), f32),
            pltpu.VMEM((SLAB, D), f32),
            pltpu.VMEM((SLAB, D), f32),
            pltpu.VMEM((D, 512), f32),
            pltpu.VMEM((2, *hdims), bf16),
            pltpu.VMEM((2, *hdims), bf16),
            pltpu.SemaphoreType.DMA((2, 2)),
            pltpu.VMEM(hdims, bf16),
            pltpu.SemaphoreType.DMA((5,)),
            pltpu.VMEM(cdims, bf16),
            pltpu.SemaphoreType.DMA((2,)),
            pltpu.VMEM(cdims, bf16),
        ]
        + seconds(PAIR_VIEWS, n, rows)
        + firsts(CONV_VIEWS, n, crows)
        + seconds(CONV_VIEWS, n, crows)
        + padded_three([pltpu.VMEM(v.mid(n, crows), bf16) for v in CONV_VIEWS])
        + firsts(HEAD_VIEWS, n, rows)
        + seconds(HEAD_VIEWS, n, rows)
        + padded_three([pltpu.VMEM(v.mid(n, rows), bf16) for v in HEAD_VIEWS]),
        compiler_params=remote(3),
        name="attention_backward",
    )(q, k, v, go, o32, li, p, relo, relx, *weights, o16, na, gatt, x1, gx2, gain, *mids, cg)


PART = 256
PARTS = 4


def last_kernel(gx1_in, x_in, hid_in, w1o_in, w1x_in, w2o_in, w2x_in, g1, sums, agains, acc1, table_ref,
                gx_out, gxx_out, fa_ref, fb_ref, gain0, gain1, gain2, gain3, h1_ref, to_ref,
                gx_ref, x_ref, hid_ref, w1, w2, gb_ref, gbt_ref, nt_ref, n_ref, gact_ref, act_ref, ghid_ref, gn_ref,
                gx16_ref, both_ref, away, back, ssems, gsems, xmine, xback, xsum, xsems, xmid, x1s, x1a, x1b, x2s, x2a, x2b,
                tnear, tback, tsems, tsum, t1, t2, t1s, t1a, t1b, t2s, t2a, t2b, t3s, t3a, t3b, t4s, t4a, t4b, sems, *scr):
    place = Place()
    place.greet(("low", "high"))
    copies = Copies(sems)
    cx = copies.start(x_in.at[pl.ds(pl.multiple_of(place.core * SLAB, SLAB), SLAB)], x_ref)
    cg = copies.start(gx1_in, gx_ref)
    cw = [copies.start(a, b) for a, b in (
        (w2x_in, w2.at[0]), (hid_in.at[0], hid_ref.at[0]), (w1x_in, w1.at[0]),
        (w2o_in, w2.at[1]), (hid_in.at[1], hid_ref.at[1]), (w1o_in, w1.at[1]))]
    refs = threes(scr)
    nh = len(HEAD_VIEWS)

    def chain(acc):
        nonlocal refs
        first = [v.first(place, acc, r) for v, r in zip(HEAD_VIEWS, refs)]
        mids = refs[2 * nh][:nh]
        second = [v.second(place, mid, r) for v, mid, r in zip(HEAD_VIEWS, mids, refs[nh:])]
        refs = refs[2 * nh + 1 :]
        return first, mids, second

    def chain_split(accs):
        nonlocal refs
        first = [v.whole_first(place, a, r) for v, a, r in zip(HEAD_VIEWS, accs, refs)]
        mids = refs[2 * nh][:nh]
        second = [v.second(place, mid, r) for v, mid, r in zip(HEAD_VIEWS, mids, refs[nh:])]
        refs = refs[2 * nh + 1 :]
        return first, mids, second

    heads = chain(acc1)
    accs, chains = [], []
    for k in range(PARTS):
        accs.append(refs[0][:nh])
        refs = refs[1:]
        chains.append(chain_split(accs[k]))

    def begin(chain):
        for hop in chain[0]:
            hop.start()

    def turn(chain):
        for hop, mid, on in zip(*chain):
            hop.wait()
            mid[...] = hop.total().astype(bf16)
            on.start()

    tswap = core_copy(place, tnear.at[1], tback, tsems)
    scatter1 = Hop(place, "low", lambda p: tsum.at[:, p], t1s, t1a, t1b)
    scatter2 = Hop(place, "high", lambda p: t1.at[p], t2s, t2a, t2b)
    gather1 = Hop(place, "high", lambda p: t2, t3s, t3a, t3b)
    gather2 = Hop(place, "low", lambda p: t3s, t4s, t4a, t4b)
    xswap = core_copy(place, xmine, xback, xsems)
    xhop1 = Hop(place, "low", lambda p: xsum, x1s, x1a, x1b)
    xhop2 = Hop(place, "high", lambda p: xmid, x2s, x2a, x2b)
    swaps = [core_copy(place, away.at[k], back.at[k], ssems.at[k]) for k in range(PARTS)]

    slot = lax.broadcasted_iota(jnp.int32, (256, 128), 1)
    diagonal = (lax.broadcasted_iota(jnp.int32, (256, 128), 0) & 127) == slot
    for half in (0, 1):
        block = table_ref[half].reshape(256, 256)
        far = block[:, 128:]
        left = far[:, 0:1] + far[:, 1:2]
        right = far[:, 2:3] + far[:, 3:4]
        tnear[half] = (block[:, :128] + jnp.where(slot == 127, left, 0.0)).reshape(tnear.shape[1:])
        spread = jnp.where(diagonal, right, 0.0)
        for r in (0, 1):
            at = 4 * LT + 2 * half + r
            xmine[at : at + 1, :] = jnp.sum(spread[r * 128 : (r + 1) * 128], 0, keepdims=True)
    cx.wait()
    for rs in row_tiles(SLAB):
        xhat, _ = norm_parts(x_ref[rs, :].astype(f32))
        n_ref[rs, :] = (xhat * g1[...]).astype(bf16)
    transpose_into(nt_ref, n_ref)
    cg.wait()
    for rs in row_tiles(SLAB):
        gb_ref[rs, :] = (0.5 * gx_ref[rs, :]).astype(bf16)
    transpose_into(gbt_ref, gb_ref)
    place.greeted(("low", "high"))
    tswap.start()
    begin(heads)
    for copy in cw:
        copy.wait()
    dims = away.shape[1:]
    half_dims = (*dims[:3], PART)

    order = [(0, 0), (1, 0), (0, 1), (0, 2), (1, 1), (0, 3), (1, 2), (1, 3)]

    def up(i):
        p, k = order[i]
        gact_ref[i % 2] = dot_nt(gb_ref[...], w2[p, k * PART : (k + 1) * PART, :])

    def weigh(i):
        p, k = order[i]
        for rs in row_tiles(SLAB):
            hid = hid_ref[p, rs, k * PART : (k + 1) * PART].astype(f32)
            sg = jax.nn.sigmoid(hid)
            act = hid * sg
            act_ref[rs, :] = act.astype(bf16)
            ghid_ref[rs, :] = (gact_ref[i % 2, rs, :] * (sg + act * (1.0 - sg))).astype(bf16)

    def down(i):
        p, k = order[i]
        part = dot_nt(ghid_ref[...], w1[p, :, k * PART : (k + 1) * PART])
        if i == 0:
            gn_ref[...] = part
        else:
            gn_ref[...] += part
        return dot(nt_ref[...], ghid_ref[...]), dot(gbt_ref[...], act_ref[...])

    up(0)
    for i, (p, k) in enumerate(order):
        weigh(i)
        if i + 1 < len(order):
            up(i + 1)
        left, right = down(i)
        if p == 0:
            away[k, :, :, :, :PART] = left.reshape(half_dims).astype(bf16)
            away[k, :, :, :, PART:] = right.reshape(half_dims).astype(bf16)
            swaps[k].start()
        else:
            swaps[k].wait()
            left = left.reshape(half_dims) + back[k, :, :, :, :PART].astype(f32)
            right = right.reshape(half_dims) + back[k, :, :, :, PART:].astype(f32)
            accs[k][0][:, :, :, :PART] = left.astype(bf16)
            accs[k][0][:, :, :, PART:] = right[:, :, :, : 384 - PART].astype(bf16)
            accs[k][1][...] = right[:, :, :, 384 - PART :].astype(bf16)
            begin(chains[k])
        if i == 0:
            tswap.wait()
            tsum[...] = tnear[0] + tback[...]
            scatter1.start()
        elif i == 2:
            scatter1.wait()
            t1[...] = scatter1.total()
            scatter2.start()
            turn(heads)
        elif i == 4:
            scatter2.wait()
            t2[...] = scatter2.total()
            t3s[place.hi] = t2[...]
            gather1.start()
        elif i == 5:
            turn(chains[0])
        elif i == 6:
            gather1.wait()
            t4s[place.lo] = t3s[...]
            gather2.start()
        elif i == 7:
            turn(chains[1])

    ffn_gain = jnp.zeros((8, D), f32)
    for rs in row_tiles(SLAB):
        xhat, inv = norm_parts(x_ref[rs, :].astype(f32))
        gn = gn_ref[rs, :]
        gx16_ref[rs, :] = (gx_ref[rs, :] + norm_back(gn, g1[...], xhat, inv)).astype(bf16)
        ffn_gain = ffn_gain + rows_sum(gn * xhat)
    gains = (
        jnp.sum(ffn_gain, 0, keepdims=True),
        jnp.sum(agains[...], 0, keepdims=True),
        sums[5:6, :],
        sums[4:5, :],
    )
    for r, g in enumerate(gains):
        for c in range(LT):
            xmine[r * LT + c : r * LT + c + 1, :] = g[:, c * 128 : (c + 1) * 128]
    xmine[4 * LT + 4 :, :] = jnp.zeros((4, 128), f32)
    xswap.start()
    out_copy = copies.start(gx16_ref, gx_out)
    gxswap = core_copy(place, gx16_ref, gxx_out, gsems)
    gxswap.start()
    xswap.wait()
    xsum[...] = xmine[...] + xback[...]
    at = 4 * LT
    xsum[at : at + 2, :] = xmine[at : at + 2, :] + xback[at + 2 : at + 4, :]
    x1s[place.lo] = xsum[...]
    xhop1.start()
    turn(chains[PARTS - 2])
    xhop1.wait()
    xmid[...] = slot_sum(x1s, place.low)
    x2s[place.hi] = xmid[...]
    xhop2.start()
    turn(chains[PARTS - 1])
    for hop, v in zip(heads[2], HEAD_VIEWS):
        hop.wait()
        h1_ref[:, v.start : v.stop] = hop.total()
    gather2.wait()
    xhop2.wait()
    total = slot_sum(x2s, place.high)
    for r, ref in enumerate((gain0, gain1, gain2, gain3)):
        for c in range(LT):
            ref[:, c * 128 : (c + 1) * 128] = total[r * LT + c : r * LT + c + 1, :]
    line = lax.broadcasted_iota(jnp.int32, (128, 128), 0)
    choice = jnp.where(line + lax.broadcasted_iota(jnp.int32, (128, 128), 1) == 127, 1.0, 0.0)
    tall = jnp.stack([t4s[l, h] for h in range(place.high) for l in range(place.low)]).reshape(256, 128)
    to_ref[: 2 * RW, :] = lax.dot_general(
        choice, tall, (((1,), (1,)), ((), ())), preferred_element_type=f32, precision=lax.Precision.HIGHEST
    )
    for r in (0, 1):
        to_ref[2 * RW : 2 * RW + 1, r * 128 : (r + 1) * 128] = total[at + r : at + r + 1, :]
    for k in range(PARTS):
        for hop, v in zip(chains[k][2], HEAD_VIEWS):
            hop.wait()
            both_ref[:, v.start : v.stop] = hop.total()
        fa_ref[:, k * PART : (k + 1) * PART] = both_ref[:, :PART]
        fb_ref[:, k * PART : (k + 1) * PART] = both_ref[:, PART:]
    out_copy.wait()
    gxswap.wait()


def padded_three(refs):
    return refs + [pltpu.SemaphoreType.DMA((1,))] * (-len(refs) % 3)


def last_call(gx1, frames, hid, w1o, w1x, w2o, w2x, g1, sums, agains, acc1, table):
    width = w1o.shape[1]
    n, dims = grad_dims(2 * PART)
    rows = dims[2]
    high, low = split_axis(n)
    trows = table.shape[3]
    gains = (4 * LT + 8, 128)
    link = firsts(HEAD_VIEWS, n, rows) + seconds(HEAD_VIEWS, n, rows)
    link = link + padded_three([pltpu.VMEM(v.mid(n, rows), bf16) for v in HEAD_VIEWS])
    part = padded_three([pltpu.VMEM((*dims[:3], v.width), bf16) for v in HEAD_VIEWS]) + link
    return pl.pallas_call(
        last_kernel,
        in_specs=[ANY] * 7 + [VMEM] * 5,
        out_specs=[ANY] * 2 + [VMEM] * 8,
        out_shape=[
            shape((SLAB, D), bf16),
            shape((SLAB, D), bf16),
            shape((rows, width), f32),
            shape((rows, width), f32),
        ]
        + [shape((1, D), f32)] * 4
        + [shape((rows, 512), f32), shape((2 * RW + 1, 256), f32)],
        scratch_shapes=[
            pltpu.VMEM((SLAB, D), f32),
            pltpu.VMEM((SLAB, D), bf16),
            pltpu.VMEM((2, SLAB, width), bf16),
            pltpu.VMEM((2, D, width), bf16),
            pltpu.VMEM((2, width, D), bf16),
            pltpu.VMEM((SLAB, D), bf16),
            pltpu.VMEM((D, SLAB), bf16),
            pltpu.VMEM((D, SLAB), bf16),
            pltpu.VMEM((SLAB, D), bf16),
            pltpu.VMEM((2, SLAB, PART), f32),
            pltpu.VMEM((SLAB, PART), bf16),
            pltpu.VMEM((SLAB, PART), bf16),
            pltpu.VMEM((SLAB, D), f32),
            pltpu.VMEM((SLAB, D), bf16),
            pltpu.VMEM((rows, 2 * PART), f32),
            pltpu.VMEM((PARTS, *dims), bf16),
            pltpu.VMEM((PARTS, *dims), bf16),
            pltpu.SemaphoreType.DMA((PARTS, 2)),
            pltpu.SemaphoreType.DMA((2,)),
            pltpu.VMEM(gains, f32),
            pltpu.VMEM(gains, f32),
            pltpu.VMEM(gains, f32),
            pltpu.SemaphoreType.DMA((2,)),
            pltpu.VMEM(gains, f32),
        ]
        + slots_of(low, gains, f32)
        + slots_of(high, gains, f32)
        + [
            pltpu.VMEM((2, high, low, trows, 128), f32),
            pltpu.VMEM((high, low, trows, 128), f32),
            pltpu.SemaphoreType.DMA((2,)),
            pltpu.VMEM((high, low, trows, 128), f32),
            pltpu.VMEM((high, trows, 128), f32),
            pltpu.VMEM((trows, 128), f32),
        ]
        + slots_of(low, (high, trows, 128), f32)
        + slots_of(high, (trows, 128), f32)
        + slots_of(high, (trows, 128), f32)
        + slots_of(low, (high, trows, 128), f32)
        + [pltpu.SemaphoreType.DMA((10,))]
        + link
        + part * PARTS,
        compiler_params=remote(4),
        name="ffn1_backward",
    )(gx1, frames, hid, w1o, w1x, w2o, w2x, g1, sums, agains, acc1, table)


def results_kernel(out_own, out_oth, gx_own, gx_oth, *refs):
    count = len(SMALL)
    smalls, (out_ref, gx_out), outs, (load_ref, gx_ref, sems) = (
        refs[:count], refs[count : count + 2], refs[count + 2 : -3], refs[-3:]
    )
    core = lax.axis_index("mp")
    own = pl.ds(pl.multiple_of(core * SLAB, SLAB), SLAB)
    oth = pl.ds(pl.multiple_of((1 - core) * SLAB, SLAB), SLAB)
    copies = Copies(sems)
    loads = [copies.start(gx_own, load_ref.at[0]), copies.start(gx_oth, load_ref.at[1])]
    loads += [copies.start(out_own, load_ref.at[2]), copies.start(out_oth, load_ref.at[3])]
    ends = []
    for k, rows in ((0, own), (1, oth)):
        loads[k].wait()
        for rs in row_tiles(SLAB):
            gx_ref[k, rs, :] = load_ref[k, rs, :].astype(f32)
        ends.append(copies.start(gx_ref.at[k], gx_out.at[rows]))
    for k, rows in ((2, own), (3, oth)):
        loads[k].wait()
        ends.append(copies.start(load_ref.at[k], out_ref.at[rows]))
    (f1a, f1b, f2a, f2b, h0, h1, cpi, cpo, crest, table, gain0, gain1, gain2, gain3) = smalls
    (of1a, of1b, of2a, of2b, oq, ok, ov, oo, ocpi, ocpo, ock, ov0, ov1, ov2, otable, og0, og1, og2, og3) = outs
    for dst, src in ((of1a, f1a), (of1b, f1b), (of2a, f2a), (of2b, f2b), (ocpi, cpi), (ocpo, cpo), (otable, table),
                     (og0, gain0), (og1, gain1), (og2, gain2), (og3, gain3)):
        dst[...] = src[...]
    for n, dst in enumerate((oq, ok, ov, oo)):
        dst[:, :128] = h0[:, n * 128 : (n + 1) * 128]
        dst[:, 128:] = h1[:, n * 128 : (n + 1) * 128]
    ock[...] = crest[:, :TAPS]
    across = crest[...].T
    for n, dst in enumerate((ov0, ov1, ov2)):
        dst[...] = across[TAPS + n : TAPS + n + 1, :]
    for copy in ends:
        copy.wait()


SMALL = range(14)


def results(out, out_oth, gx, gx_oth, smalls):
    rows, crows = smalls[0].shape[0], smalls[6].shape[0]
    outs = [shape(a.shape, f32) for a in smalls[:4]]
    outs += [shape((rows, D // 2), f32)] * 4
    outs += [shape((crows, 2 * D), f32), shape((crows, D), f32), shape((crows, TAPS), f32)]
    outs += [shape((1, crows), f32)] * 3 + [shape(a.shape, f32) for a in smalls[9:]]
    return pl.pallas_call(
        results_kernel,
        in_specs=[ANY] * 4 + [VMEM] * len(smalls),
        out_specs=[ANY] * 2 + [VMEM] * len(outs),
        out_shape=[shape((2 * SLAB, D), bf16), shape((2 * SLAB, D), f32)] + outs,
        scratch_shapes=[
            pltpu.VMEM((4, SLAB, D), bf16),
            pltpu.VMEM((2, SLAB, D), f32),
            pltpu.SemaphoreType.DMA((8,)),
        ],
        compiler_params=pltpu.CompilerParams(vmem_limit_bytes=60 << 20),
        name="results",
    )(out, out_oth, gx, gx_oth, *smalls)


def shards(
    frames, lengths, cotangent, ffn1_gain, ffn1_in, ffn1_out, attn_gain, query_weight, key_weight,
    value_weight, out_weight, rel_table, conv_gain, pointwise_in, conv_kernel, bn_gain, bn_bias,
    pointwise_out, ffn2_gain, ffn2_in, ffn2_out, final_gain,
):
    n = lax.axis_size("dp")
    high, low = split_axis(n)
    column = jnp.arange(128 - TAPS)[None, :]
    vectors = sum(
        jnp.where(column == k, v[:, None], 0) for k, v in enumerate((conv_gain, bn_gain, bn_bias))
    ).astype(bf16)
    g1, ga, g2, gf = (g[None, :] for g in (ffn1_gain, attn_gain, ffn2_gain, final_gain))
    qkvo = (query_weight, key_weight, value_weight)

    x1, hid1, na, q, k, v, w1x, w2x, wqx, wkx, wvx, v1x, v2x, wox, relx, far = first_call(
        frames, g1, ga, pointwise_in, pointwise_out, conv_kernel, vectors, ffn1_in, ffn1_out, *qkvo, ffn2_in, ffn2_out, out_weight, rel_table
    )
    o16, o32, li, p, gathered = attend_call(lengths, q, k, v, rel_table, relx, far)
    gathered = gathered.reshape(D, CONV_C)
    x2, u, hd, gp, st, taps = conv_call(lengths, x1, o16, out_weight, wox, gathered)
    out, gx3, gz, acc2, gpw, back, sums = middle_call(
        lengths, hd, x2, cotangent, st, taps, gathered, g2, ffn2_in, v1x, ffn2_out, v2x, gf
    )
    gx2, gatt, go, conv_g, *mids = conv_back_call(
        lengths, acc2, gz, hd, gp, st, back, taps, u, x2, gx3, gathered, out_weight, wox, gpw, sums
    )
    conv_g = conv_g.reshape(high, low, 2, D // n // 2, CONV_C)
    gtab, gx1, agains, f2a, f2b, cpi, cpo, crest, h0, acc1 = attend_back_call(
        q, k, v, go, o32, li, p, rel_table, relx, (*qkvo, wqx, wkx, wvx), o16, na, gatt, x1, gx2, ga, mids, conv_g
    )
    gx, gx_oth, f1a, f1b, gain0, gain1, gain2, gain3, h1, table = last_call(
        gx1, frames, hid1, ffn1_in, w1x, ffn1_out, w2x, g1, sums, agains, acc1,
        gtab.reshape(2, high, low, D // 2 // n, 256),
    )
    (block_output, frames_grad, f1a, f1b, f2a, f2b, q_grad, k_grad, v_grad, o_grad, cpi, cpo, ck, cg, bg, bb,
     table, gain0, gain1, gain2, gain3) = results(
        out, lax.ppermute(out, "mp", [(0, 1), (1, 0)]), gx, gx_oth,
        (f1a, f1b, f2a, f2b, h0, h1, cpi, cpo, crest, table, gain0, gain1, gain2, gain3),
    )
    return (
        block_output, frames_grad, gain0[0], f1a, f1b.T, gain1[0], q_grad, k_grad, v_grad, o_grad.T, table, cg[0],
        cpi, ck, bg[0], bb[0], cpo, gain2[0], f2a, f2b.T, gain3[0],
    )


def solution(mesh):
    return jax.shard_map(
        shards,
        mesh=mesh,
        in_specs=(
            P("dp", None), P("dp", None), P("dp", None), P(), P(None, "mp"), P("mp", None), P(),
            P(None, "mp"), P(None, "mp"), P(None, "mp"), P("mp", None), P(None, "mp"),
            P(("dp", "mp")), P(("dp", "mp"), None), P(("dp", "mp"), None), P(("dp", "mp")),
            P(("dp", "mp")), P(("dp", "mp"), None), P(), P(None, "mp"), P("mp", None), P(),
        ),
        out_specs=(
            P("dp", None), P("dp", None), P(), P("dp", "mp"), P("mp", "dp"), P(), P("dp", "mp"),
            P("dp", "mp"), P("dp", "mp"), P("mp", "dp"), P(None, "mp"), P(("dp", "mp")),
            P(("dp", "mp"), None), P(("dp", "mp"), None), P(("dp", "mp")), P(("dp", "mp")),
            P(("dp", "mp"), None), P(), P("dp", "mp"), P("mp", "dp"), P(),
        ),
        check_vma=False,
    )
```

```python
import jax
import jax.numpy as jnp
from jax import lax
from jax.experimental import pallas as pl
from jax.experimental.pallas import tpu as pltpu
from jax.sharding import PartitionSpec as P

D = 512
DH = 64
RW = 64
SLAB = 1152
TAPS = 32
NORM_EPS = 1e-05
BATCH_EPS = 1e-05
MASKED = -1e30

SUB = 64
GAP = 16
TOP = 32
PADDED = 1216
CH = 64
LT = D // 128

f32 = jnp.float32
bf16 = jnp.bfloat16


def params(mib=60):
    return pltpu.CompilerParams(
        dimension_semantics=("arbitrary",), vmem_limit_bytes=mib << 20
    )


def dot(a, b):
    return jnp.dot(a, b, preferred_element_type=f32)


def dot_nt(a, b):
    return lax.dot_general(a, b, (((1,), (1,)), ((), ())), preferred_element_type=f32)


def dot_tn(a, b):
    return lax.dot_general(a, b, (((0,), (0,)), ((), ())), preferred_element_type=f32)


def norm_parts(v):
    c = v - jnp.mean(v, -1, keepdims=True)
    inv = lax.rsqrt(jnp.mean(c * c, -1, keepdims=True) + NORM_EPS)
    return c * inv, inv


def norm_back(gy, gain, xhat, inv):
    e = gy * gain
    inner = jnp.mean(e * xhat, -1, keepdims=True)
    return inv * (e - jnp.mean(e, -1, keepdims=True) - xhat * inner)


def rows_sum(v):
    return jnp.sum(v.reshape(v.shape[0] // 8, 8, v.shape[1]), 0)


def fixed(*shape):
    zeros = (0,) * len(shape)
    return pl.BlockSpec(shape, lambda i, *m: zeros)


SMEM = pl.BlockSpec(memory_space=pltpu.SMEM)
VMEM = pl.BlockSpec(memory_space=pltpu.VMEM)


def shape(dims, dtype):
    return jax.ShapeDtypeStruct(dims, dtype)


MESH = pl.DeviceIdType.MESH


def split_axis(n):
    low = 4 if n % 4 == 0 else 1
    return n // low, low


class Place:
    def __init__(self):
        self.n = lax.axis_size("dp")
        self.high, self.low = split_axis(self.n)
        self.me = lax.axis_index("dp")
        self.core = lax.axis_index("mp")
        self.hi = self.me // self.low
        self.lo = self.me % self.low

    def size(self, kind):
        return {"all": self.n, "low": self.low, "high": self.high}[kind]

    def mine(self, kind):
        return {"all": self.me, "low": self.lo, "high": self.hi}[kind]

    def peer(self, kind, j):
        at = (self.mine(kind) + j) % self.size(kind)
        if kind == "low":
            return at, {"dp": self.hi * self.low + at}
        if kind == "high":
            return at, {"dp": at * self.low + self.lo}
        return at, {"dp": at}

    def each(self, kind, do):
        size = self.size(kind)
        if size <= 4:
            for j in range(1, size):
                do(j)
        else:

            def body(j, carry):
                do(j)
                return carry

            lax.fori_loop(1, size, body, 0)

    def greet(self, kinds, core=True):
        barrier = pltpu.get_barrier_semaphore()
        for kind in kinds:
            self.each(
                kind,
                lambda j: pl.semaphore_signal(
                    barrier, inc=1, device_id=self.peer(kind, j)[1], device_id_type=MESH
                ),
            )
        if core:
            pl.semaphore_signal(barrier, inc=1, device_id={"mp": 1 - self.core}, device_id_type=MESH)

    def greeted(self, kinds, core=True):
        count = sum(self.size(kind) - 1 for kind in kinds) + (1 if core else 0)
        if count:
            pl.semaphore_wait(pltpu.get_barrier_semaphore(), count)


class Hop:
    def __init__(self, place, kind, piece, slots, send, recv):
        self.place, self.kind, self.piece = place, kind, piece
        self.slots, self.send, self.recv = slots, send, recv

    def copy(self, j, slot):
        at, device = self.place.peer(self.kind, j)
        return pltpu.make_async_remote_copy(
            src_ref=self.piece(at), dst_ref=self.slots.at[slot], send_sem=self.send.at[j],
            recv_sem=self.recv.at[slot], device_id=device, device_id_type=MESH,
        )

    def start(self):
        mine = self.place.mine(self.kind)
        self.place.each(self.kind, lambda j: self.copy(j, mine).start())

    def wait(self):
        self.place.each(self.kind, lambda j: self.copy(j, self.place.peer(self.kind, j)[0]).wait())

    def total(self):
        total = self.piece(self.place.mine(self.kind))[...].astype(f32)
        size = self.place.size(self.kind)
        if size <= 4:
            for j in range(1, size):
                total = total + self.slots[self.place.peer(self.kind, j)[0]].astype(f32)
            return total
        return lax.fori_loop(
            1, size, lambda j, t: t + self.slots[self.place.peer(self.kind, j)[0]].astype(f32), total
        )


def core_copy(place, src, dst, sems):
    return pltpu.make_async_remote_copy(
        src_ref=src, dst_ref=dst, send_sem=sems.at[0], recv_sem=sems.at[1],
        device_id={"mp": 1 - place.core}, device_id_type=MESH,
    )


def slots_of(size, dims, dtype=bf16):
    return [
        pltpu.VMEM((size, *dims), dtype),
        pltpu.SemaphoreType.DMA((size,)),
        pltpu.SemaphoreType.DMA((size,)),
    ]


class View:
    def __init__(self, index, start, stop, order):
        self.index, self.start, self.stop, self.order = index, start, stop, order
        self.width = stop - start

    def kinds(self):
        return ("low", "high") if self.order == "low" else ("high", "low")

    def mid(self, n, rows):
        high, low = split_axis(n)
        return (high if self.order == "low" else low, rows, self.width)

    def first_scratch(self, n, rows):
        high, low = split_axis(n)
        return slots_of(low if self.order == "low" else high, self.mid(n, rows))

    def second_scratch(self, n, rows):
        size, *dims = self.mid(n, rows)
        return slots_of(size, dims)

    def first(self, place, acc, refs):
        cols = slice(self.start, self.stop)
        if self.index is not None:
            acc = acc.at[self.index]
        if self.order == "low":
            piece = lambda p: acc.at[:, p, :, cols]
        else:
            piece = lambda p: acc.at[p, :, :, cols]
        return Hop(place, self.kinds()[0], piece, *refs)

    def whole_first(self, place, acc, refs):
        if self.order == "low":
            return Hop(place, "low", lambda p: acc.at[:, p], *refs)
        return Hop(place, "high", lambda p: acc.at[p], *refs)

    def second(self, place, mid, refs):
        return Hop(place, self.kinds()[1], lambda p: mid.at[p], *refs)


PAIR_VIEWS = (View(0, 0, 1024, "low"), View(1, 0, 384, "low"), View(1, 384, 1024, "high"))
CONV_C = 2 * D + D + 128
CONV_VIEWS = (View(None, 0, 1024, "low"), View(None, 1024, CONV_C, "high"))


def firsts(views, n, rows):
    return [ref for v in views for ref in v.first_scratch(n, rows)]


def seconds(views, n, rows):
    return [ref for v in views for ref in v.second_scratch(n, rows)]


def threes(refs):
    return [refs[i : i + 3] for i in range(0, len(refs), 3)]


def remote(collective_id, mib=60):
    return pltpu.CompilerParams(
        vmem_limit_bytes=mib << 20, collective_id=collective_id, has_side_effects=True,
    )


def slot_sum(slots, n):
    return lax.fori_loop(1, n, lambda j, total: total + slots[j], slots[0])


TR = 128
UP = 512


def row_tiles(rows):
    return [slice(r, r + TR) for r in range(0, rows, TR)]


def tiles(rows, cols, width=256):
    return [(rs, slice(c, c + width)) for rs in row_tiles(rows) for c in range(0, cols, width)]


def transpose_into(dst, src):
    for r in range(0, src.shape[0], 128):
        dst[:, r : r + 128] = src[r : r + 128, :].astype(f32).T.astype(bf16)


class Copies:
    def __init__(self, sems):
        self.sems, self.count = sems, 0

    def start(self, src, dst):
        copy = pltpu.make_async_copy(src, dst, self.sems.at[self.count])
        self.count += 1
        copy.start()
        return copy


ANY = pl.BlockSpec(memory_space=pl.ANY)


def bounds(len_ref, place):
    first = len_ref[place.core, 0]
    return first, first + len_ref[place.core, 1]


def first_kernel(x_in, g1, ga, pin, pout, ck, vec, w1_in, w2_in, wq_in, wk_in, wv_in, v1_in, v2_in, wo_in, rel_in,
                 x1_out, hid_out, na_out, q_out, k_out, v_out,
                 w1_out, w2_out, wq_out, wk_out, wv_out, v1_out, v2_out, wo_out, rel_out, far_out,
                 x_ref, w1, w2, wqkv, n_ref, act_ref, hid_ref, hid16_ref, x1_ref, na_ref, qkv_ref, sems, rsems, piece_ref, far_ref, fsend, frecv):
    place = Place()
    place.greet(("high",))
    copies = Copies(sems)
    cx = copies.start(x_in.at[pl.ds(pl.multiple_of(place.core * SLAB, SLAB), SLAB)], x_ref)
    qkv_in = (wq_in, wk_in, wv_in)
    mine = [copies.start(w1_in, w1.at[1]), copies.start(w2_in, w2.at[1])]
    mine_qkv = [copies.start(a, wqkv.at[1, k]) for k, a in enumerate(qkv_in)]
    piece_ref[:, : 2 * D] = pin[...]
    piece_ref[:, 2 * D : 3 * D] = pout[...]
    piece_ref[:, 3 * D :] = jnp.concatenate([ck[...], vec[...]], 1)
    far = Hop(place, "high", lambda p: piece_ref, far_ref, fsend, frecv)
    pairs = [(w1_in, w1.at[0]), (w2_in, w2.at[0])] + [(a, wqkv.at[0, k]) for k, a in enumerate(qkv_in)]
    pairs += [(v1_in, v1_out), (v2_in, v2_out), (wo_in, wo_out), (rel_in, rel_out)]
    swaps = [core_copy(place, a, b, rsems.at[k]) for k, (a, b) in enumerate(pairs)]
    cx.wait()
    for rs in row_tiles(SLAB):
        xhat, _ = norm_parts(x_ref[rs, :].astype(f32))
        n_ref[rs, :] = (xhat * g1[...]).astype(bf16)
    for copy in mine:
        copy.wait()
    chunks = [(p, c) for p in (1, 0) for c in range(0, w1.shape[2], UP)]
    ends = []

    def up(k):
        p, c = chunks[k]
        hid_ref[k % 2] = dot(n_ref[...], w1[p, :, c : c + UP])

    def down(k):
        p, c = chunks[k]
        part = dot(act_ref[k % 2], w2[p, c : c + UP, :])
        if k == 0:
            x1_ref[...] = part
        else:
            x1_ref[...] += part

    up(0)
    place.greeted(("high",))
    for copy in swaps[:2]:
        copy.start()
    far.start()
    for k, (p, c) in enumerate(chunks):
        for rs, cs in tiles(SLAB, UP):
            hid = hid_ref[k % 2, rs, cs]
            hid16_ref[p, rs, c + cs.start : c + cs.stop] = hid.astype(bf16)
            act_ref[k % 2, rs, cs] = (hid * jax.nn.sigmoid(hid)).astype(bf16)
        if k + 1 < len(chunks):
            if k + 1 == len(chunks) // 2:
                for copy in swaps[:2]:
                    copy.wait()
                for copy in swaps[2:]:
                    copy.start()
                ends.append(copies.start(hid16_ref.at[1], hid_out.at[1]))
                ends += [copies.start(w1.at[0], w1_out), copies.start(w2.at[0], w2_out)]
            up(k + 1)
        if k > 0:
            down(k - 1)
    ends.append(copies.start(hid16_ref.at[0], hid_out.at[0]))
    down(len(chunks) - 1)
    for rs in row_tiles(SLAB):
        x1 = x_ref[rs, :].astype(f32) + 0.5 * x1_ref[rs, :]
        x1_ref[rs, :] = x1
        xhat, _ = norm_parts(x1)
        na_ref[rs, :] = (xhat * ga[...]).astype(bf16)
    ends += [copies.start(x1_ref, x1_out), copies.start(na_ref, na_out)]
    for copy in mine_qkv + swaps[2:5]:
        copy.wait()
    ends += [copies.start(wqkv.at[0, n], out) for n, out in enumerate((wq_out, wk_out, wv_out))]
    w = D // 2
    for n, out in enumerate((q_out, k_out, v_out)):
        for p in (0, 1):
            value = dot(na_ref[...], wqkv[p, n]).astype(bf16)
            if n == 0:
                value = (value.astype(f32) * DH**-0.5).astype(bf16)
            qkv_ref[n, :, (1 - p) * w : (2 - p) * w] = value
        ends.append(copies.start(qkv_ref.at[n], out))
    far.wait()
    far_ref[place.hi] = piece_ref[...]
    far_out[...] = far_ref[...]
    for copy in swaps[5:] + ends:
        copy.wait()


def first_call(frames, g1, ga, pin, pout, ck, vec, w1, w2, wq, wk, wv, v1, v2, wo, rel):
    hid = w1.shape[1]
    moved = (w1, w2, wq, wk, wv, v1, v2, wo, rel)
    high, _ = split_axis(lax.axis_size("dp"))
    piece = (pin.shape[0], CONV_C)
    return pl.pallas_call(
        first_kernel,
        in_specs=[ANY] + [VMEM] * 6 + [ANY] * 9,
        out_specs=[ANY] * 15 + [VMEM],
        out_shape=[shape((SLAB, D), f32), shape((2, SLAB, hid), bf16)]
        + [shape((SLAB, D), bf16)] * 4
        + [shape(a.shape, a.dtype) for a in moved]
        + [shape((high, *piece), bf16)],
        scratch_shapes=[
            pltpu.VMEM((SLAB, D), bf16),
            pltpu.VMEM((2, D, hid), bf16),
            pltpu.VMEM((2, hid, D), bf16),
            pltpu.VMEM((2, 3, D, D // 2), bf16),
            pltpu.VMEM((SLAB, D), bf16),
            pltpu.VMEM((2, SLAB, UP), bf16),
            pltpu.VMEM((2, SLAB, UP), f32),
            pltpu.VMEM((2, SLAB, hid), bf16),
            pltpu.VMEM((SLAB, D), f32),
            pltpu.VMEM((SLAB, D), bf16),
            pltpu.VMEM((3, SLAB, D), bf16),
            pltpu.SemaphoreType.DMA((20,)),
            pltpu.SemaphoreType.DMA((9, 2)),
            pltpu.VMEM(piece, bf16),
        ]
        + slots_of(high, piece),
        compiler_params=remote(5),
        name="ffn1_forward",
    )(frames, g1, ga, pin, pout, ck, vec, *moved)


TI = 384
STAGES = [(h, start) for h in (0, 1) for start in range(0, SLAB, TI)]


def low_lanes(rows, cols=128):
    return lax.broadcasted_iota(jnp.int32, (rows, cols), 1) < 64


def attend_kernel(len_ref, q_ref, k_ref, v_ref, relo_ref, relx_ref, far_ref,
                  o16_ref, li_ref, p_ref, all_ref, o32_ref, qa_ref, ka_ref, va_ref, e_ref, rel_ref, s_ref, near_s, far_s, top_s,
                  near_ref, nsend, nrecv, other_ref, osems):
    step = pl.program_id(0)
    place = Place()
    near = Hop(place, "low", lambda p: far_ref, near_ref, nsend, nrecv)
    across = core_copy(place, near_ref, other_ref, osems)

    @pl.when(step == 0)
    def _():
        place.greet(("low",))

    b1, b2 = bounds(len_ref, place)
    lane = lax.broadcasted_iota(jnp.int32, (SLAB, 128), 1)
    slot = lane & 63
    frame = lax.broadcasted_iota(jnp.int32, (SLAB, 128), 0)
    label = jnp.where(frame < b1, 0, jnp.where(frame < b2, 1, 2))
    mq = jnp.where((slot < 3) & (slot != label), MASKED, 0.0)
    mk = jnp.where(slot == label, 1.0, 0.0)
    rel_ref[: 2 * RW + 1, :] = jnp.where(step < 2, relo_ref[...].astype(f32), relx_ref[...].astype(f32))
    rel_ref[2 * RW + 1 :, :] = jnp.broadcast_to(rel_ref[2 * RW : 2 * RW + 1, :], (255 - 2 * RW, 128))
    q, k, v = (ref[...].astype(f32) for ref in (q_ref, k_ref, v_ref))
    for h in (0, 1):
        mine = (lane < 64) if h == 0 else (lane >= 64)
        qa_ref[h] = jnp.where(mine, q, mq).astype(bf16)
        ka_ref[h] = jnp.where(mine, k, mk).astype(bf16)
        va_ref[h] = jnp.where(mine, v, 1.0).astype(bf16)
        rel_mine = low_lanes(256) if h == 0 else jnp.logical_not(low_lanes(256))
        relz = jnp.where(rel_mine, rel_ref[...], 0.0).astype(bf16)
        e_ref[h] = dot_nt(qa_ref[h], relz)
    subl = lax.broadcasted_iota(jnp.int32, (SUB, 128), 1)
    line = lax.broadcasted_iota(jnp.int32, (SUB, 128), 0)
    left_of = {0: subl < line, 64: subl < line + 64}
    tiles = SLAB // 128

    def scores(t):
        h, start = STAGES[t]
        s_ref[t % 3] = dot_nt(qa_ref[h, start : start + TI, :], ka_ref[h])

    def shift(t):
        h, start = STAGES[t]
        for r in range(0, TI, SUB):
            b = (start + r) // SUB
            off = 64 if b % 2 == 0 else 0
            rows = slice(r, r + SUB)
            eb = e_ref[h, b * SUB : (b + 1) * SUB, :]
            near = pltpu.roll(eb, off, 1, stride=1, stride_axis=0)
            left = jnp.broadcast_to(eb[:, 0:1], (SUB, 128))
            near_s[t % 2, 0, rows, :] = jnp.where(left_of[off], left, near[:, :128])
            near_s[t % 2, 1, rows, :] = near[:, 128:]
            far_s[t % 2, 0, rows, :] = left
            far_s[t % 2, 1, rows, :] = jnp.broadcast_to(eb[:, 128:129], (SUB, 128))

    def groups(t, r):
        b = (STAGES[t][1] + r) // SUB
        first = b // 2 - 1 if b % 2 == 0 else b // 2
        near = [(n, n - first) for n in (first, first + 1) if 0 <= n < tiles]
        return near, list(range(0, max(first, 0))), list(range(first + 2, tiles))

    def find(t, r):
        rows = slice(r, r + SUB)
        near, lefts, rights = groups(t, r)
        s = {n: s_ref[t % 3, rows, n * 128 : (n + 1) * 128] for n in range(tiles)}
        peak = None
        for n, k in near:
            value = s[n] + near_s[t % 2, k, rows, :]
            s_ref[t % 3, rows, n * 128 : (n + 1) * 128] = value
            peak = value if peak is None else jnp.maximum(peak, value)
        far = [far_s[t % 2, k, rows, :] for k in (0, 1)]
        for group, const in ((lefts, far[0]), (rights, far[1])):
            if group:
                top = s[group[0]]
                for n in group[1:]:
                    top = jnp.maximum(top, s[n])
                peak = jnp.maximum(peak, top + const)
        peak = jnp.broadcast_to(jnp.max(peak, -1, keepdims=True), (SUB, 128))
        top_s[t % 2, 0, rows, :] = peak
        top_s[t % 2, 1, rows, :] = peak - far[0]
        top_s[t % 2, 2, rows, :] = peak - far[1]

    def power(t, r):
        h, start = STAGES[t]
        rows = slice(r, r + SUB)
        _, lefts, rights = groups(t, r)
        tops = [top_s[t % 2, k, rows, :] for k in range(3)]
        for n in range(tiles):
            top = tops[1] if n in lefts else tops[2] if n in rights else tops[0]
            s = s_ref[t % 3, rows, n * 128 : (n + 1) * 128]
            p_ref[h, start + r : start + r + SUB, n * 128 : (n + 1) * 128] = jnp.exp(s - top).astype(bf16)

    low = low_lanes(TI)

    def mix(t):
        h, start = STAGES[t]
        rows = slice(start, start + TI)
        pv = dot(p_ref[h, rows, :], va_ref[h])
        li = 1.0 / pltpu.roll(pv, 64, 1)
        o = pv * li
        if h == 1:
            o = jnp.where(low, o32_ref[rows, :], o)
            li = jnp.where(low, li_ref[rows, :], li)
            o16_ref[rows, :] = o.astype(bf16)
        o32_ref[rows, :] = o
        li_ref[rows, :] = li

    count = len(STAGES)
    scores(0)
    shift(0)
    for t in range(count + 2):
        if t + 1 < count:
            shift(t + 1)
        for r in range(0, TI, SUB):
            if t < count:
                find(t, r)
            if 0 < t <= count:
                power(t - 1, r)
        if t + 1 < count:
            scores(t + 1)
        if 2 <= t:
            mix(t - 2)

    @pl.when(step == 0)
    def _():
        place.greeted(("low",))
        near.start()

    @pl.when(step == 2)
    def _():
        near.wait()
        near_ref[place.lo] = far_ref[...]
        across.start()

    @pl.when(step == 3)
    def _():
        across.wait()
        for l in range(place.low):
            all_ref[:, l, place.core] = near_ref[l]
            all_ref[:, l, 1 - place.core] = other_ref[l]


def attend_call(lengths, q, k, v, relo, relx, far):
    n, rows = lax.axis_size("dp"), far.shape[1]
    high, low = split_axis(n)
    pair = pl.BlockSpec((SLAB, 128), lambda h: (0, h))
    table_own = pl.BlockSpec((2 * RW + 1, 128), lambda h: (0, jnp.minimum(h, 1)))
    table_oth = pl.BlockSpec((2 * RW + 1, 128), lambda h: (0, jnp.maximum(h, 2) - 2))
    return pl.pallas_call(
        attend_kernel,
        grid=(D // 128,),
        in_specs=[SMEM, pair, pair, pair, table_own, table_oth, fixed(*far.shape)],
        out_specs=[pair, pair, pl.BlockSpec((2, SLAB, SLAB), lambda h: (h, 0, 0)),
                   fixed(high, low, 2, rows, CONV_C)],
        out_shape=[
            shape((SLAB, D), bf16),
            shape((SLAB, D), f32),
            shape((D // DH, SLAB, SLAB), bf16),
            shape((high, low, 2, rows, CONV_C), bf16),
        ],
        scratch_shapes=[
            pltpu.VMEM((SLAB, 128), f32),
            pltpu.VMEM((2, SLAB, 128), bf16),
            pltpu.VMEM((2, SLAB, 128), bf16),
            pltpu.VMEM((2, SLAB, 128), bf16),
            pltpu.VMEM((2, SLAB, 256), f32),
            pltpu.VMEM((256, 128), f32),
            pltpu.VMEM((3, TI, SLAB), f32),
            pltpu.VMEM((2, 2, TI, 128), f32),
            pltpu.VMEM((2, 2, TI, 128), f32),
            pltpu.VMEM((2, 3, TI, 128), f32),
        ]
        + slots_of(low, (high, rows, CONV_C))
        + [pltpu.VMEM((low, high, rows, CONV_C), bf16), pltpu.SemaphoreType.DMA((2,))],
        compiler_params=remote(6),
        name="attention_forward",
    )(lengths, q, k, v, relo, relx, far)


GAIN_ROW, BN_GAIN_ROW, BN_BIAS_ROW = TAPS, TAPS + 1, TAPS + 2
FLAT = SLAB + 3 * TOP
DEEP = PADDED + 2 * TOP


def spread_out(flat_ref, padded_ref, c, b1, b2):
    zeros = jnp.zeros((TOP, 128), f32)
    flat_ref[c, TOP + SLAB :, :] = jnp.zeros((FLAT - TOP - SLAB, 128), f32)
    padded_ref[c, :TOP, :] = zeros
    padded_ref[c, TOP + PADDED :, :] = zeros
    for t0 in range(0, PADDED, CH):
        t = lax.broadcasted_iota(jnp.int32, (CH, 128), 0) + t0
        at = TOP + t0
        value = jnp.where(t < b1, flat_ref[c, at : at + CH, :], 0.0)
        middle = (t >= b1 + GAP) & (t < b2 + GAP)
        value = jnp.where(middle, flat_ref[c, at - GAP : at - GAP + CH, :], value)
        value = jnp.where(t >= b2 + 2 * GAP, flat_ref[c, at - 2 * GAP : at - 2 * GAP + CH, :], value)
        padded_ref[c, at : at + CH, :] = value


def lane_row(ref, r):
    return jnp.concatenate([ref[c, r : r + 1, :] for c in range(LT)], 1)


def lanes(ref, r):
    return jnp.concatenate([ref[r + c : r + c + 1, :] for c in range(LT)], 1)


def draw_in(padded_ref, c, t0, rows, b1, b2):
    t = lax.broadcasted_iota(jnp.int32, (rows, 128), 0) + t0
    value = jnp.where(t < b1, padded_ref[c, t0 : t0 + rows, :], padded_ref[c, t0 + GAP : t0 + GAP + rows, :])
    return jnp.where(t < b2, value, padded_ref[c, t0 + 2 * GAP : t0 + 2 * GAP + rows, :])


def conv_kernel_fn(len_ref, x1_in, o_in, woo, wox, weights, x2_out, u_out, hd_out, gp_out, st_ref, taps_ref,
                   x2_ref, o_ref, pin, rest, cn_ref, u_ref, u16_ref, hd_ref, gp_ref, flat_ref, out_ref,
                   mine, slots, send, recv, sems):
    place = Place()
    place.greet(("all",), False)
    copies = Copies(sems)
    cx = copies.start(x1_in, x2_ref)
    co = copies.start(o_in, o_ref)
    cr = copies.start(weights.at[:, 3 * D : 3 * D + 128], rest)
    cp = copies.start(weights.at[:, : 2 * D], pin)
    cr.wait()
    across = rest[...].astype(f32).T
    for c in range(LT):
        taps_ref[c] = across[:40, c * 128 : (c + 1) * 128]
    gain = lane_row(taps_ref, GAIN_ROW)
    w = woo.shape[0]
    cx.wait()
    co.wait()
    x2_ref[...] += dot(o_ref[:, :w], woo[...]) + dot(o_ref[:, w:], wox[...])
    for rs in row_tiles(SLAB):
        xhat, _ = norm_parts(x2_ref[rs, :])
        cn_ref[rs, :] = (xhat * gain).astype(bf16)
    ends = [copies.start(x2_ref, x2_out)]
    cp.wait()
    u_ref[...] = dot(cn_ref[...], pin[...])
    for rs in row_tiles(SLAB):
        for c in range(LT):
            cs, gs = slice(c * 128, c * 128 + 128), slice(D + c * 128, D + c * 128 + 128)
            u1, u2 = u_ref[rs, cs], u_ref[rs, gs]
            u16_ref[rs, cs] = u1.astype(bf16)
            u16_ref[rs, gs] = u2.astype(bf16)
            flat_ref[c, TOP + rs.start : TOP + rs.stop, :] = u1 * jax.nn.sigmoid(u2)
    ends.append(copies.start(u16_ref, u_out))
    b1, b2 = bounds(len_ref, place)

    def tile(c, carry):
        spread_out(flat_ref, gp_ref, c, b1, b2)
        for t0 in range(0, PADDED, CH):
            acc = jnp.zeros((CH, 128), f32)
            for b in range(8):
                at = TOP + t0 - TAPS // 2 + b
                x = gp_ref[c, at : at + CH + 24, :]
                for a in range(4):
                    acc = acc + x[8 * a : 8 * a + CH, :] * taps_ref[c, 8 * a + b : 8 * a + b + 1, :]
            out_ref[c, t0 : t0 + CH, :] = acc
        first = jnp.zeros((8, 128), f32)
        second = jnp.zeros((8, 128), f32)
        for t0 in range(0, SLAB, 128):
            hd = draw_in(out_ref, c, t0, 128, b1, b2)
            hd_ref[c, t0 : t0 + 128, :] = hd
            t = lax.broadcasted_iota(jnp.int32, (128, 128), 0) + t0
            hv = jnp.where(t < b2, hd, 0.0)
            first = first + rows_sum(hv)
            second = second + rows_sum(hv * hv)
        mine[pl.ds(c, 1), :] = jnp.sum(first, 0, keepdims=True)
        mine[pl.ds(LT + c, 1), :] = jnp.sum(second, 0, keepdims=True)
        return carry

    lax.fori_loop(0, LT, tile, 0)
    mine[2 * LT :, :] = jnp.full((8, 128), b2.astype(f32))
    slots[place.me] = mine[...]
    place.greeted(("all",), False)
    hop = Hop(place, "all", lambda p: mine, slots, send, recv)
    hop.start()
    ends += [copies.start(hd_ref, hd_out), copies.start(gp_ref, gp_out)]
    hop.wait()
    st_ref[...] = slot_sum(slots, place.n)
    for copy in ends:
        copy.wait()


def conv_call(lengths, x1, o16, woo, wox, gathered):
    n = lax.axis_size("dp")
    st = (2 * LT + 8, 128)
    return pl.pallas_call(
        conv_kernel_fn,
        in_specs=[SMEM, ANY, ANY, VMEM, VMEM, ANY],
        out_specs=[ANY, ANY, ANY, ANY, VMEM, VMEM],
        out_shape=[
            shape((SLAB, D), f32),
            shape((SLAB, 2 * D), bf16),
            shape((LT, SLAB, 128), f32),
            shape((LT, DEEP, 128), f32),
            shape(st, f32),
            shape((LT, 40, 128), f32),
        ],
        scratch_shapes=[
            pltpu.VMEM((SLAB, D), f32),
            pltpu.VMEM((SLAB, D), bf16),
            pltpu.VMEM((D, 2 * D), bf16),
            pltpu.VMEM((D, 128), bf16),
            pltpu.VMEM((SLAB, D), bf16),
            pltpu.VMEM((SLAB, 2 * D), f32),
            pltpu.VMEM((SLAB, 2 * D), bf16),
            pltpu.VMEM((LT, SLAB, 128), f32),
            pltpu.VMEM((LT, DEEP, 128), f32),
            pltpu.VMEM((LT, FLAT, 128), f32),
            pltpu.VMEM((LT, PADDED, 128), f32),
            pltpu.VMEM(st, f32),
        ]
        + slots_of(n, st, f32)
        + [pltpu.SemaphoreType.DMA((8,))],
        compiler_params=remote(0),
        name="conv_forward",
    )(lengths, x1, o16, woo, wox, gathered)


def middle_kernel(len_ref, hd_in, x2_in, ct_in, st, taps_ref, weights, g2, w1o_in, w1x_in, w2o_in, w2x_in, gf,
                  out_out, gx3_out, gz_out, acc, gpw_ref, back_ref, sums_ref,
                  hd_ref, x_ref, ct_ref, pout, w1, w2, wc_ref, n_ref, nt_ref, hid_ref, act_ref, slope_ref,
                  out_ref, out16_ref, gb_ref, gbt_ref, gn_ref, gc_ref, away, back, ssems, mine, slots, send, recv, sems):
    place = Place()
    place.greet(("all",))
    copies = Copies(sems)
    ch = copies.start(hd_in, hd_ref)
    cp = copies.start(weights.at[:, 2 * D : 3 * D], pout)
    cx = copies.start(x2_in, x_ref)
    cw = [copies.start(a, b) for a, b in ((w1x_in, w1.at[0]), (w1o_in, w1.at[1]), (w2x_in, w2.at[0]), (w2o_in, w2.at[1]))]
    start = pl.multiple_of(place.core * SLAB, SLAB)
    cc = copies.start(ct_in.at[pl.ds(start, SLAB)], ct_ref)

    _, b2 = bounds(len_ref, place)
    bng, bnb = lane_row(taps_ref, BN_GAIN_ROW), lane_row(taps_ref, BN_BIAS_ROW)
    count = st[2 * LT : 2 * LT + 1, 0:1]
    centre = lanes(st, 0) / count
    inv_b = lax.rsqrt(lanes(st, LT) / count - centre * centre + BATCH_EPS)

    def normal(rs, c):
        cs = slice(c * 128, c * 128 + 128)
        zh = (hd_ref[c, rs, :] - centre[:, cs]) * inv_b[:, cs]
        z = zh * bng[:, cs] + bnb[:, cs]
        return cs, zh, z, jax.nn.sigmoid(z)

    ch.wait()
    for rs in row_tiles(SLAB):
        for c in range(LT):
            cs, _, z, sg = normal(rs, c)
            wc_ref[rs, cs] = (z * sg).astype(bf16)
    cp.wait()
    cx.wait()
    x_ref[...] += dot(wc_ref[...], pout[...])
    for rs in row_tiles(SLAB):
        xhat, _ = norm_parts(x_ref[rs, :])
        n_ref[rs, :] = (xhat * g2[...]).astype(bf16)
    for copy in cw:
        copy.wait()
    chunks = [(p, c) for p in (0, 1) for c in range(0, w1.shape[2], UP)]

    def up(k):
        p, c = chunks[k]
        hid_ref[k % 2] = dot(n_ref[...], w1[p, :, c : c + UP])

    def down(k):
        p, c = chunks[k]
        part = dot(act_ref[p, :, c : c + UP], w2[p, c : c + UP, :])
        if k == 0:
            out_ref[...] = part
        else:
            out_ref[...] += part

    up(0)
    for k, (p, c) in enumerate(chunks):
        for rs, cs in tiles(SLAB, UP):
            hid = hid_ref[k % 2, rs, cs]
            sg = jax.nn.sigmoid(hid)
            act = hid * sg
            at = slice(c + cs.start, c + cs.stop)
            act_ref[p, rs, at] = act.astype(bf16)
            slope_ref[p, rs, at] = (sg + act * (1.0 - sg)).astype(bf16)
        if k + 1 < len(chunks):
            up(k + 1)
        if k > 0:
            down(k - 1)
    down(len(chunks) - 1)
    transpose_into(nt_ref, n_ref)

    cc.wait()
    final_gain = jnp.zeros((8, D), f32)
    for rs in row_tiles(SLAB):
        t = lax.broadcasted_iota(jnp.int32, (TR, 1), 0) + rs.start
        valid = (t < b2).astype(f32)
        xhat, inv = norm_parts(x_ref[rs, :] + 0.5 * out_ref[rs, :])
        out16_ref[rs, :] = (valid * xhat * gf[...]).astype(bf16)
        g = ct_ref[rs, :].astype(f32) * valid
        gx4 = norm_back(g, gf[...], xhat, inv)
        out_ref[rs, :] = gx4
        gb_ref[rs, :] = (0.5 * gx4).astype(bf16)
        final_gain = final_gain + rows_sum(g * xhat)
    ends = [copies.start(out16_ref, out_out)]
    transpose_into(gbt_ref, gb_ref)

    def gup(k):
        p, c = chunks[k]
        hid_ref[k % 2] = dot_nt(gb_ref[...], w2[p, c : c + UP, :])

    def gdown(k):
        p, c = chunks[k]
        part = dot_nt(slope_ref[p, :, c : c + UP], w1[p, :, c : c + UP])
        if k == 0:
            gn_ref[...] = part
        else:
            gn_ref[...] += part

    gup(0)
    for k, (p, c) in enumerate(chunks):
        for rs, cs in tiles(SLAB, UP):
            at = slice(c + cs.start, c + cs.stop)
            slope_ref[p, rs, at] = (hid_ref[k % 2, rs, cs] * slope_ref[p, rs, at].astype(f32)).astype(bf16)
        if k + 1 < len(chunks):
            gup(k + 1)
        if k > 0:
            gdown(k - 1)
    gdown(len(chunks) - 1)

    ffn_gain = jnp.zeros((8, D), f32)
    for rs in row_tiles(SLAB):
        xhat, inv = norm_parts(x_ref[rs, :])
        gn = gn_ref[rs, :]
        gx3 = out_ref[rs, :] + norm_back(gn, g2[...], xhat, inv)
        x_ref[rs, :] = gx3
        gc_ref[rs, :] = gx3.astype(bf16)
        ffn_gain = ffn_gain + rows_sum(gn * xhat)
    ends.append(copies.start(x_ref, gx3_out))
    gn_ref[...] = dot_nt(gc_ref[...], pout[...])
    parts = [[jnp.zeros((8, 128), f32) for _ in range(4)] for _ in range(LT)]
    for rs in row_tiles(SLAB):
        t = lax.broadcasted_iota(jnp.int32, (TR, 1), 0) + rs.start
        valid = (t < b2).astype(f32)
        for c in range(LT):
            cs, zh, z, sg = normal(rs, c)
            gz = gn_ref[rs, cs] * (sg + z * sg * (1.0 - sg))
            hd_ref[c, rs, :] = gz
            e = gz * bng[:, cs] * valid
            for k, v in enumerate((gz, gz * zh, e, e * zh)):
                parts[c][k] = parts[c][k] + rows_sum(v)
    ends.append(copies.start(hd_ref, gz_out))
    sums_ref[...] = jnp.zeros(sums_ref.shape, f32)
    for c in range(LT):
        cs = slice(c * 128, c * 128 + 128)
        for k in range(4):
            total = jnp.sum(parts[c][k], 0, keepdims=True)
            sums_ref[k : k + 1, cs] = total
            if k >= 2:
                mine[(k - 2) * LT + c : (k - 2) * LT + c + 1, :] = total
    sums_ref[4:5, :] = jnp.sum(final_gain, 0, keepdims=True)
    sums_ref[5:6, :] = jnp.sum(ffn_gain, 0, keepdims=True)
    slots[place.me] = mine[...]
    place.greeted(("all",))
    hop = Hop(place, "all", lambda p: mine, slots, send, recv)
    hop.start()

    dims = acc.shape[1:]
    swaps = [core_copy(place, away.at[k], back.at[k], ssems.at[k]) for k in range(2)]
    lhs, rhs = (nt_ref, gbt_ref), (slope_ref, act_ref)
    for k in range(2):
        away[k] = dot(lhs[k][...], rhs[k][0]).reshape(dims).astype(bf16)
        swaps[k].start()
    gpw_ref[...] = dot_tn(wc_ref[...], gc_ref[...]).astype(bf16)
    for k in range(2):
        own = dot(lhs[k][...], rhs[k][1]).reshape(dims)
        swaps[k].wait()
        acc[k] = (own + back[k].astype(f32)).astype(bf16)
    hop.wait()
    back_ref[...] = slot_sum(slots, place.n)
    for copy in ends:
        copy.wait()


def grad_dims(cols):
    n = lax.axis_size("dp")
    return n, (*split_axis(n), D // n, cols)


def middle_call(lengths, hd, x2, cot, st, taps, gathered, g2, w1o, w1x, w2o, w2x, gf):
    hid = w1o.shape[1]
    n, dims = grad_dims(hid)
    stat = (2 * LT, 128)
    return pl.pallas_call(
        middle_kernel,
        in_specs=[SMEM, ANY, ANY, ANY, VMEM, VMEM, ANY, VMEM, ANY, ANY, ANY, ANY, VMEM],
        out_specs=[ANY, ANY, ANY, VMEM, VMEM, VMEM, VMEM],
        out_shape=[
            shape((SLAB, D), bf16),
            shape((SLAB, D), f32),
            shape((LT, SLAB, 128), f32),
            shape((2, *dims), bf16),
            shape((D, D), bf16),
            shape(stat, f32),
            shape((8, D), f32),
        ],
        scratch_shapes=[
            pltpu.VMEM((LT, SLAB, 128), f32),
            pltpu.VMEM((SLAB, D), f32),
            pltpu.VMEM((SLAB, D), bf16),
            pltpu.VMEM((D, D), bf16),
            pltpu.VMEM((2, D, hid), bf16),
            pltpu.VMEM((2, hid, D), bf16),
            pltpu.VMEM((SLAB, D), bf16),
            pltpu.VMEM((SLAB, D), bf16),
            pltpu.VMEM((D, SLAB), bf16),
            pltpu.VMEM((2, SLAB, UP), f32),
            pltpu.VMEM((2, SLAB, hid), bf16),
            pltpu.VMEM((2, SLAB, hid), bf16),
            pltpu.VMEM((SLAB, D), f32),
            pltpu.VMEM((SLAB, D), bf16),
            pltpu.VMEM((SLAB, D), bf16),
            pltpu.VMEM((D, SLAB), bf16),
            pltpu.VMEM((SLAB, D), f32),
            pltpu.VMEM((SLAB, D), bf16),
            pltpu.VMEM((2, *dims), bf16),
            pltpu.VMEM((2, *dims), bf16),
            pltpu.SemaphoreType.DMA((2, 2)),
            pltpu.VMEM(stat, f32),
        ]
        + slots_of(n, stat, f32)
        + [pltpu.SemaphoreType.DMA((12,))],
        compiler_params=remote(1),
        name="ffn2_forward_backward",
    )(lengths, hd, x2, cot, st, taps, gathered, g2, w1o, w1x, w2o, w2x, gf)


def conv_back_kernel(len_ref, acc_in, gz_in, hd_in, gp_in, st, back, taps_ref, u_in, x2_in, gx3_in, weights, woo, wox,
                     gpw, sums, gx2_out, ga_out, go_out, cg_ref, mid0, mid1, mid2,
                     gz_ref, hd_ref, gp_ref, u_ref, x2_ref, gx_ref, pin, flat_ref, pad_ref, out_ref, acc_ref, gtap_ref,
                     gu_ref, gn_ref, cn_ref, ga_ref, go_ref, sems, tsems, *scr):
    place = Place()
    place.greet(("low", "high"), False)
    copies = Copies(sems)
    def tile_copies(c):
        pairs = ((gz_in, gz_ref), (hd_in, hd_ref), (gp_in, gp_ref))
        return [pltpu.make_async_copy(a.at[c], b.at[c], tsems.at[k, c]) for k, (a, b) in enumerate(pairs)]

    for c in range(LT):
        for copy in tile_copies(c):
            copy.start()
    rest = [copies.start(a, b) for a, b in (
        (u_in, u_ref), (weights.at[:, : 2 * D], pin), (x2_in, x2_ref), (gx3_in, gx_ref))]
    b1, b2 = bounds(len_ref, place)
    gain = lane_row(taps_ref, GAIN_ROW)
    hops = [v.first(place, acc_in, refs) for v, refs in zip(PAIR_VIEWS, threes(scr))]
    place.greeted(("low", "high"), False)
    for hop in hops:
        hop.start()

    def tile(c, carry):
        for copy in tile_copies(c):
            copy.wait()
        count = st[2 * LT : 2 * LT + 1, :]
        centre = st[pl.ds(c, 1), :] / count
        inv_b = lax.rsqrt(st[pl.ds(LT + c, 1), :] / count - centre * centre + BATCH_EPS)
        a1 = back[pl.ds(c, 1), :] / count
        a2 = back[pl.ds(LT + c, 1), :] / count
        bn_gain = taps_ref[c, BN_GAIN_ROW : BN_GAIN_ROW + 1, :]
        for t0 in range(0, SLAB, 128):
            t = lax.broadcasted_iota(jnp.int32, (128, 128), 0) + t0
            zh = (hd_ref[c, t0 : t0 + 128, :] - centre) * inv_b
            away = jnp.where(t < b2, a1 + zh * a2, 0.0)
            flat_ref[c, TOP + t0 : TOP + t0 + 128, :] = inv_b * (gz_ref[c, t0 : t0 + 128, :] * bn_gain - away)
        spread_out(flat_ref, pad_ref, c, b1, b2)
        acc_ref[...] = jnp.zeros(acc_ref.shape, f32)
        for t0 in range(0, PADDED, CH):
            acc = jnp.zeros((CH, 128), f32)
            gl = gp_ref[c, TOP + t0 : TOP + t0 + CH, :]
            for b in range(8):
                at = TOP + t0 + TAPS // 2 - TAPS + 1 + b
                x = pad_ref[c, at : at + CH + 24, :]
                for a in range(4):
                    k = TAPS - 1 - (8 * a + b)
                    part = x[8 * a : 8 * a + CH, :]
                    acc = acc + part * taps_ref[c, k : k + 1, :]
                    acc_ref[8 * k : 8 * k + 8, :] += rows_sum(part * gl)
            out_ref[c, t0 : t0 + CH, :] = acc
        gtap_ref[c] = jnp.sum(acc_ref[...].reshape(TAPS, 8, 128), 1)
        for t0 in range(0, SLAB, 128):
            flat_ref[c, t0 : t0 + 128, :] = draw_in(out_ref, c, t0, 128, b1, b2)
        return carry

    lax.fori_loop(0, LT, tile, 0)
    for copy in rest:
        copy.wait()
    for rs in row_tiles(SLAB):
        for c in range(LT):
            cs, gs = slice(c * 128, c * 128 + 128), slice(D + c * 128, D + c * 128 + 128)
            sg = jax.nn.sigmoid(u_ref[rs, gs].astype(f32))
            g = flat_ref[c, rs, :] * sg
            gu_ref[rs, cs] = g.astype(bf16)
            gu_ref[rs, gs] = (g * u_ref[rs, cs].astype(f32) * (1.0 - sg)).astype(bf16)
    gn_ref[...] = dot_nt(gu_ref[...], pin[...])
    gain_sum = jnp.zeros((8, D), f32)
    for rs in row_tiles(SLAB):
        xhat, inv = norm_parts(x2_ref[rs, :])
        gn = gn_ref[rs, :]
        gx2 = gx_ref[rs, :] + norm_back(gn, gain, xhat, inv)
        gx_ref[rs, :] = gx2
        ga_ref[rs, :] = gx2.astype(bf16)
        cn_ref[rs, :] = (xhat * gain).astype(bf16)
        gain_sum = gain_sum + rows_sum(gn * xhat)
    ends = [copies.start(gx_ref, gx2_out), copies.start(ga_ref, ga_out)]
    w = woo.shape[0]
    go_ref[:, :w] = dot_nt(ga_ref[...], woo[...]).astype(bf16)
    go_ref[:, w:] = dot_nt(ga_ref[...], wox[...]).astype(bf16)
    ends.append(copies.start(go_ref, go_out))
    cg_ref[:, : 2 * D] = dot_tn(cn_ref[...], gu_ref[...]).astype(bf16)
    cg_ref[:, 2 * D : 3 * D] = gpw[...]
    gain_sum = jnp.sum(gain_sum, 0, keepdims=True)
    for c in range(LT):
        cols = slice(c * 128, (c + 1) * 128)
        rows = [gtap_ref[c], gain_sum[:, cols], sums[1:2, cols], sums[0:1, cols]]
        block = jnp.concatenate(rows + [jnp.zeros((128 - TAPS - 3, 128), f32)], 0)
        cg_ref[c * 128 : (c + 1) * 128, 3 * D :] = block.T.astype(bf16)
    for hop, mid in zip(hops, (mid0, mid1, mid2)):
        hop.wait()
        mid[...] = hop.total().astype(bf16)
    for copy in ends:
        copy.wait()


def conv_back_call(lengths, acc, gz, hd, gp, st, back, taps, u, x2, gx3, gathered, woo, wox, gpw, sums):
    n, rows = lax.axis_size("dp"), acc.shape[3]
    return pl.pallas_call(
        conv_back_kernel,
        in_specs=[SMEM, VMEM, ANY, ANY, ANY, VMEM, VMEM, VMEM, ANY, ANY, ANY, ANY, VMEM, VMEM, VMEM, VMEM],
        out_specs=[ANY, ANY, ANY, VMEM, VMEM, VMEM, VMEM],
        out_shape=[
            shape((SLAB, D), f32),
            shape((SLAB, D), bf16),
            shape((SLAB, D), bf16),
            shape((D, CONV_C), bf16),
        ]
        + [shape(v.mid(n, rows), bf16) for v in PAIR_VIEWS],
        scratch_shapes=[
            pltpu.VMEM((LT, SLAB, 128), f32),
            pltpu.VMEM((LT, SLAB, 128), f32),
            pltpu.VMEM((LT, DEEP, 128), f32),
            pltpu.VMEM((SLAB, 2 * D), bf16),
            pltpu.VMEM((SLAB, D), f32),
            pltpu.VMEM((SLAB, D), f32),
            pltpu.VMEM((D, 2 * D), bf16),
            pltpu.VMEM((LT, FLAT, 128), f32),
            pltpu.VMEM((LT, DEEP, 128), f32),
            pltpu.VMEM((LT, PADDED, 128), f32),
            pltpu.VMEM((TAPS * 8, 128), f32),
            pltpu.VMEM((LT, TAPS, 128), f32),
            pltpu.VMEM((SLAB, 2 * D), bf16),
            pltpu.VMEM((SLAB, D), f32),
            pltpu.VMEM((SLAB, D), bf16),
            pltpu.VMEM((SLAB, D), bf16),
            pltpu.VMEM((SLAB, D), bf16),
            pltpu.SemaphoreType.DMA((10,)),
            pltpu.SemaphoreType.DMA((3, LT)),
        ]
        + firsts(PAIR_VIEWS, n, rows),
        compiler_params=remote(2),
        name="conv_backward",
    )(lengths, acc, gz, hd, gp, st, back, taps, u, x2, gx3, gathered, woo, wox, gpw, sums)


HEAD_VIEWS = (View(None, 0, 384, "low"), View(None, 384, 512, "high"))


def attend_back_kernel(q_ref, k_ref, v_ref, g_ref, o_ref, li_ref, p_ref, relo_ref, relx_ref,
                       wqo, wko, wvo, wqx, wkx, wvx, o16_ref, na_in, gatt_in, x1_in, gx2_in, gain,
                       mid0, mid1, mid2, cg_ref,
                       gt_ref, gx1_out, agains_ref, f2a_ref, f2b_ref, cpi_ref, cpo_ref, crest_ref, h0_ref, acc1_ref,
                       ga_ref, va_ref, kt_ref, qt_ref, got_ref, gs_ref, gp_ref, w_ref, fl_ref, n_ref, all_ref, other_ref,
                       relt_ref, far_s, flip_ref, rel_ref, relf_ref, wide_ref, gn_ref, x1_ref, gx_ref,
                       pg_ref, away, hback, hsems, acc0_ref, sems, cback, csems, cacc, *scr):
    step = pl.program_id(0)
    place = Place()
    loads = [pltpu.make_async_copy(a, b, sems.at[k]) for k, (a, b) in enumerate((
        (na_in, wide_ref.at[0]), (gatt_in, wide_ref.at[1]), (x1_in, x1_ref), (gx2_in, gx_ref)))]
    gx1_copy = pltpu.make_async_copy(gx_ref, gx1_out, sems.at[4])
    scr = threes(scr)
    nv = len(PAIR_VIEWS)
    last = [v.second(place, mid, refs) for v, mid, refs in zip(PAIR_VIEWS, (mid0, mid1, mid2), scr[:nv])]
    cfirst = [v.first(place, cacc, refs) for v, refs in zip(CONV_VIEWS, scr[nv:])]
    nc = len(CONV_VIEWS)
    cmids = scr[nv + 2 * nc][:nc]
    csecond = [v.second(place, mid, refs) for v, mid, refs in zip(CONV_VIEWS, cmids, scr[nv + nc :])]
    cswap = core_copy(place, cg_ref.at[:, :, 1 - place.core], cback, csems)
    hswaps = [core_copy(place, away.at[k], hback.at[k], hsems.at[k]) for k in range(2)]
    at = nv + 2 * nc + 1
    hfirst = [v.first(place, acc0_ref, refs) for v, refs in zip(HEAD_VIEWS, scr[at:])]
    nh = len(HEAD_VIEWS)
    hmids = scr[at + 2 * nh][:nh]
    hsecond = [v.second(place, mid, refs) for v, mid, refs in zip(HEAD_VIEWS, hmids, scr[at + nh :])]
    kinds = ("low", "high")

    @pl.when(step == 0)
    def _():
        place.greet(kinds)
        for copy in loads:
            copy.start()
        line = lax.broadcasted_iota(jnp.int32, (256, 256), 0)
        flip_ref[...] = jnp.where(line + lax.broadcasted_iota(jnp.int32, (256, 256), 1) == 255, 1.0, 0.0).astype(bf16)
        line = lax.broadcasted_iota(jnp.int32, (128, 128), 0)
        other = (line < 64) != (lax.broadcasted_iota(jnp.int32, (128, 128), 1) < 64)
        other_ref[...] = jnp.where(other, 1.0, 0.0).astype(bf16)

    lane = lax.broadcasted_iota(jnp.int32, (SLAB, 128), 1)
    go = g_ref[...].astype(f32) * li_ref[...]
    got_ref[...] = go.T.astype(bf16)
    qt_ref[...] = q_ref[...].astype(f32).T.astype(bf16)
    kt_ref[...] = k_ref[...].astype(f32).T.astype(bf16)
    go = go.astype(bf16).astype(f32)
    product = go * o_ref[...].astype(f32)
    product_hi = product.astype(bf16)
    product_lo = (product - product_hi.astype(f32)).astype(bf16)
    inner = dot(product_hi, other_ref[...]) + dot(product_lo, other_ref[...])
    inner_hi = inner.astype(bf16).astype(f32)
    inner_lo = inner - inner_hi
    own_pair = step >= 2
    rel_ref[: 2 * RW + 1, :] = jnp.where(own_pair, relo_ref[...].astype(f32), relx_ref[...].astype(f32))
    relf_ref[:128, :] = dot(flip_ref[128:, :128], rel_ref[:128, :].astype(bf16))
    line = lax.broadcasted_iota(jnp.int32, (128, 128), 0)
    relf_ref[128:, :] = jnp.where(
        line < 2, rel_ref[0:1, :], jnp.where(line < 4, rel_ref[2 * RW : 2 * RW + 1, :], 0.0)
    )
    relt_ref[...] = relf_ref[...].T.astype(bf16)
    for h in (0, 1):
        mine = (lane < 64) if h == 0 else (lane >= 64)
        base = 64 - 64 * h
        extra = jnp.where(lane == base, -inner_hi, jnp.where(lane == base + 1, -inner_lo, 0.0))
        ga_ref[h] = jnp.where(mine, go, extra).astype(bf16)
        ones = jnp.where((lane == base) | (lane == base + 1), 1.0, 0.0)
        va_ref[h] = jnp.where(mine, v_ref[...].astype(f32), ones).astype(bf16)

    subl = lax.broadcasted_iota(jnp.int32, (SUB, 128), 1)
    line = lax.broadcasted_iota(jnp.int32, (SUB, 128), 0)
    left_of = {0: subl < line, 64: subl < line + 64}
    tiles = SLAB // 128
    zero16 = jnp.zeros((SUB, 128), bf16)

    def grow(t):
        h, start = STAGES[t]
        gp_ref[t % 2] = dot_nt(ga_ref[h, start : start + TI, :], va_ref[h])

    def weigh(t):
        h, start = STAGES[t]
        for r in range(0, TI, SUB):
            b = (start + r) // SUB
            off = 64 if b % 2 == 0 else 0
            first = b // 2 - 1 if b % 2 == 0 else b // 2
            rows = slice(start + r, start + r + SUB)
            near = slice(r, r + SUB)
            sums = [jnp.zeros((SUB, 128), f32), jnp.zeros((SUB, 128), f32)]
            for n in range(tiles):
                cols = slice(n * 128, (n + 1) * 128)
                gs = p_ref[h, rows, cols].astype(f32) * gp_ref[t % 2, near, cols]
                gs16 = gs.astype(bf16)
                gs_ref[h, rows, cols] = gs16
                if n < first:
                    sums[0] = sums[0] + gs
                elif n > first + 1:
                    sums[1] = sums[1] + gs
                elif n == first:
                    w_ref[t % 2, near, :128] = gs16
                    sums[0] = sums[0] + jnp.where(left_of[off], gs, 0.0)
                else:
                    w_ref[t % 2, near, 128:] = gs16
                    sums[1] = sums[1] + jnp.where(left_of[off], 0.0, gs)
            if first < 0:
                w_ref[t % 2, near, :128] = zero16
            if first + 1 >= tiles:
                w_ref[t % 2, near, 128:] = zero16
            far_s[t % 2, 0, near, :] = sums[0]
            far_s[t % 2, 1, near, :] = sums[1]

    def flip(t):
        fl_ref[t % 2] = dot(w_ref[t % 2], flip_ref[...])

    def unroll(t):
        h, start = STAGES[t]
        for r in range(0, TI, SUB):
            off = 64 if ((start + r) // SUB) % 2 == 0 else 0
            near = pltpu.roll(fl_ref[t % 2, r : r + SUB, :], (off + 128) % 256, 1, stride=1, stride_axis=0)
            n_ref[h, start + r : start + r + SUB, :128] = near[:, :128].astype(bf16)
            far_left = jnp.sum(far_s[t % 2, 0, r : r + SUB, :], -1, keepdims=True)
            far_right = jnp.sum(far_s[t % 2, 1, r : r + SUB, :], -1, keepdims=True)
            left_hi = far_left.astype(bf16).astype(f32)
            right_hi = far_right.astype(bf16).astype(f32)
            far = jnp.where(subl == 0, left_hi, 0.0)
            far = jnp.where(subl == 1, far_left - left_hi, far)
            far = jnp.where(subl == 2, right_hi, far)
            far = jnp.where(subl == 3, far_right - right_hi, far)
            n_ref[h, start + r : start + r + SUB, 128:] = far.astype(bf16)

    def query(t):
        h, start = STAGES[t]
        rows = slice(start, start + TI)
        half = slice(64 * h, 64 * h + 64)
        part = dot_nt(kt_ref[half, :], gs_ref[h, rows, :]) + dot_nt(relt_ref[half, :], n_ref[h, rows, :])
        all_ref[half, rows] = (part * DH**-0.5).astype(bf16)

    def key(h):
        half = slice(64 * h, 64 * h + 64)
        all_ref[128 + 64 * h : 192 + 64 * h, :] = dot(qt_ref[half, :], gs_ref[h]).astype(bf16)
        gt_ref[half, :] = dot(qt_ref[half, :], n_ref[h])

    def value(h):
        half = slice(64 * h, 64 * h + 64)
        all_ref[256 + 64 * h : 320 + 64 * h, :] = dot(got_ref[half, :], p_ref[h]).astype(bf16)

    grow(0)
    for t in range(len(STAGES)):
        weigh(t)
        if t > 0:
            unroll(t - 1)
        if t + 1 < len(STAGES):
            grow(t + 1)
        flip(t)
        if t > 0:
            query(t - 1)
        if t == 1:
            value(0)
        if t == 2:
            value(1)
        if t == 3:
            key(0)
        if t == 4:
            all_ref[384:, :] = o16_ref[...].astype(f32).T.astype(bf16)
    unroll(len(STAGES) - 1)
    query(len(STAGES) - 1)
    key(1)

    @pl.when(step == 0)
    def _():
        loads[0].wait()
        loads[1].wait()

    def choose(own, oth):
        return jnp.where(own_pair, own[...].astype(f32), oth[...].astype(f32)).astype(bf16)

    weights = jnp.concatenate([choose(wqo, wqx), choose(wko, wkx), choose(wvo, wvx)], 1)
    gn_ref[...] = jnp.where(step == 0, 0.0, gn_ref[...]) + dot(weights, all_ref[:384, :])
    pg_ref[:384, :] = dot(all_ref[:384, :], wide_ref[0])
    pg_ref[384:, :] = dot(all_ref[384:, :], wide_ref[1])
    pg_ref[...] = pg_ref[...].T
    dims = acc1_ref.shape

    @pl.when(step == 0)
    def _():
        place.greeted(kinds)
        for hop in last:
            hop.start()
        cswap.start()
        away[0] = pg_ref[...].reshape(dims).astype(bf16)
        hswaps[0].start()

    @pl.when(step == 1)
    def _():
        away[1] = pg_ref[...].reshape(dims).astype(bf16)
        hswaps[1].start()
        cswap.wait()
        cacc[...] = (cg_ref[:, :, place.core].astype(f32) + cback[...].astype(f32)).astype(bf16)
        for hop in cfirst:
            hop.start()
        for hop, v in zip(last, PAIR_VIEWS):
            hop.wait()
            if v.index == 0:
                f2a_ref[:, v.start : v.stop] = hop.total()
            else:
                f2b_ref[:, v.start : v.stop] = hop.total()

    @pl.when(step == 2)
    def _():
        hswaps[0].wait()
        acc0_ref[...] = (pg_ref[...].reshape(dims) + hback[0].astype(f32)).astype(bf16)
        for hop in hfirst:
            hop.start()
        for hop, mid, on in zip(cfirst, cmids, csecond):
            hop.wait()
            mid[...] = hop.total().astype(bf16)
            on.start()

    @pl.when(step == 3)
    def _():
        hswaps[1].wait()
        acc1_ref[...] = (pg_ref[...].reshape(dims) + hback[1].astype(f32)).astype(bf16)
        csecond[0].wait()
        cpi_ref[...] = csecond[0].total()
        csecond[1].wait()
        total = csecond[1].total()
        cpo_ref[...] = total[:, :D]
        crest_ref[...] = total[:, D:]
        for hop, mid, on in zip(hfirst, hmids, hsecond):
            hop.wait()
            mid[...] = hop.total().astype(bf16)
            on.start()
        loads[2].wait()
        loads[3].wait()
        total = jnp.zeros((8, D), f32)
        for rs in row_tiles(SLAB):
            xhat, inv = norm_parts(x1_ref[rs, :])
            gn = gn_ref[:, rs].T
            gx_ref[rs, :] = gx_ref[rs, :] + norm_back(gn, gain[...], xhat, inv)
            total = total + rows_sum(gn * xhat)
        gx1_copy.start()
        agains_ref[...] = total
        for hop, v in zip(hsecond, HEAD_VIEWS):
            hop.wait()
            h0_ref[:, v.start : v.stop] = hop.total()
        gx1_copy.wait()


def pair_of(s):
    return (s + 2) % 4


def attend_back_call(q, k, v, go, o32, li, p, relo, relx, weights, o16, na, gatt, x1, gx2, gain, mids, cg):
    n, rows, crows = lax.axis_size("dp"), mids[0].shape[1], cg.shape[3]
    high, low = split_axis(n)
    cdims = (high, low, crows, CONV_C)
    hdims = (high, low, rows, 512)
    pair = pl.BlockSpec((SLAB, 128), lambda s: (0, pair_of(s)))
    head_map = pl.BlockSpec((2, SLAB, SLAB), lambda s: (pair_of(s), 0, 0))
    own = lambda s: (0, jnp.maximum(s, 2) - 2)
    oth = lambda s: (0, jnp.minimum(s, 1))
    table_own, table_oth = pl.BlockSpec((2 * RW + 1, 128), own), pl.BlockSpec((2 * RW + 1, 128), oth)
    w_own, w_oth = pl.BlockSpec((D, 128), own), pl.BlockSpec((D, 128), oth)
    return pl.pallas_call(
        attend_back_kernel,
        grid=(D // 128,),
        in_specs=[pair] * 6 + [head_map, table_own, table_oth] + [w_own] * 3 + [w_oth] * 3 + [pair]
        + [ANY] * 4 + [fixed(1, D)] + [fixed(*a.shape) for a in (*mids, cg)],
        out_specs=[pl.BlockSpec((128, 256), lambda s: (pair_of(s), 0)), ANY, fixed(8, D), fixed(rows, 1024),
                   fixed(rows, 1024), fixed(crows, 2 * D), fixed(crows, D), fixed(crows, 128),
                   fixed(rows, 512), fixed(*hdims)],
        out_shape=[
            shape((D, 256), f32),
            shape((SLAB, D), f32),
            shape((8, D), f32),
            shape((rows, 1024), f32),
            shape((rows, 1024), f32),
            shape((crows, 2 * D), f32),
            shape((crows, D), f32),
            shape((crows, 128), f32),
            shape((rows, 512), f32),
            shape(hdims, bf16),
        ],
        scratch_shapes=[
            pltpu.VMEM((2, SLAB, 128), bf16),
            pltpu.VMEM((2, SLAB, 128), bf16),
            pltpu.VMEM((128, SLAB), bf16),
            pltpu.VMEM((128, SLAB), bf16),
            pltpu.VMEM((128, SLAB), bf16),
            pltpu.VMEM((2, SLAB, SLAB), bf16),
            pltpu.VMEM((2, TI, SLAB), f32),
            pltpu.VMEM((2, TI, 256), bf16),
            pltpu.VMEM((2, TI, 256), f32),
            pltpu.VMEM((2, SLAB, 256), bf16),
            pltpu.VMEM((512, SLAB), bf16),
            pltpu.VMEM((128, 128), bf16),
            pltpu.VMEM((128, 256), bf16),
            pltpu.VMEM((2, 2, TI, 128), f32),
            pltpu.VMEM((256, 256), bf16),
            pltpu.VMEM((136, 128), f32),
            pltpu.VMEM((256, 128), f32),
            pltpu.VMEM((2, SLAB, D), bf16),
            pltpu.VMEM((D, SLAB), f32),
            pltpu.VMEM((SLAB, D), f32),
            pltpu.VMEM((SLAB, D), f32),
            pltpu.VMEM((D, 512), f32),
            pltpu.VMEM((2, *hdims), bf16),
            pltpu.VMEM((2, *hdims), bf16),
            pltpu.SemaphoreType.DMA((2, 2)),
            pltpu.VMEM(hdims, bf16),
            pltpu.SemaphoreType.DMA((5,)),
            pltpu.VMEM(cdims, bf16),
            pltpu.SemaphoreType.DMA((2,)),
            pltpu.VMEM(cdims, bf16),
        ]
        + seconds(PAIR_VIEWS, n, rows)
        + firsts(CONV_VIEWS, n, crows)
        + seconds(CONV_VIEWS, n, crows)
        + padded_three([pltpu.VMEM(v.mid(n, crows), bf16) for v in CONV_VIEWS])
        + firsts(HEAD_VIEWS, n, rows)
        + seconds(HEAD_VIEWS, n, rows)
        + padded_three([pltpu.VMEM(v.mid(n, rows), bf16) for v in HEAD_VIEWS]),
        compiler_params=remote(3),
        name="attention_backward",
    )(q, k, v, go, o32, li, p, relo, relx, *weights, o16, na, gatt, x1, gx2, gain, *mids, cg)


PART = 256
PARTS = 4


def last_kernel(gx1_in, x_in, hid_in, w1o_in, w1x_in, w2o_in, w2x_in, g1, sums, agains, acc1, table_ref,
                gx_out, gxx_out, fa_ref, fb_ref, gain0, gain1, gain2, gain3, h1_ref, to_ref,
                gx_ref, x_ref, hid_ref, w1, w2, gb_ref, gbt_ref, nt_ref, n_ref, gact_ref, act_ref, ghid_ref, gn_ref,
                gx16_ref, both_ref, away, back, ssems, gsems, xmine, xback, xsum, xsems, xmid, x1s, x1a, x1b, x2s, x2a, x2b,
                tnear, tback, tsems, tsum, t1, t2, t1s, t1a, t1b, t2s, t2a, t2b, t3s, t3a, t3b, t4s, t4a, t4b, sems, *scr):
    place = Place()
    place.greet(("low", "high"))
    copies = Copies(sems)
    cx = copies.start(x_in.at[pl.ds(pl.multiple_of(place.core * SLAB, SLAB), SLAB)], x_ref)
    cg = copies.start(gx1_in, gx_ref)
    cw = [copies.start(a, b) for a, b in (
        (w2x_in, w2.at[0]), (hid_in.at[0], hid_ref.at[0]), (w1x_in, w1.at[0]),
        (w2o_in, w2.at[1]), (hid_in.at[1], hid_ref.at[1]), (w1o_in, w1.at[1]))]
    refs = threes(scr)
    nh = len(HEAD_VIEWS)

    def chain(acc):
        nonlocal refs
        first = [v.first(place, acc, r) for v, r in zip(HEAD_VIEWS, refs)]
        mids = refs[2 * nh][:nh]
        second = [v.second(place, mid, r) for v, mid, r in zip(HEAD_VIEWS, mids, refs[nh:])]
        refs = refs[2 * nh + 1 :]
        return first, mids, second

    def chain_split(accs):
        nonlocal refs
        first = [v.whole_first(place, a, r) for v, a, r in zip(HEAD_VIEWS, accs, refs)]
        mids = refs[2 * nh][:nh]
        second = [v.second(place, mid, r) for v, mid, r in zip(HEAD_VIEWS, mids, refs[nh:])]
        refs = refs[2 * nh + 1 :]
        return first, mids, second

    heads = chain(acc1)
    accs, chains = [], []
    for k in range(PARTS):
        accs.append(refs[0][:nh])
        refs = refs[1:]
        chains.append(chain_split(accs[k]))

    def begin(chain):
        for hop in chain[0]:
            hop.start()

    def turn(chain):
        for hop, mid, on in zip(*chain):
            hop.wait()
            mid[...] = hop.total().astype(bf16)
            on.start()

    tswap = core_copy(place, tnear.at[1], tback, tsems)
    scatter1 = Hop(place, "low", lambda p: tsum.at[:, p], t1s, t1a, t1b)
    scatter2 = Hop(place, "high", lambda p: t1.at[p], t2s, t2a, t2b)
    gather1 = Hop(place, "high", lambda p: t2, t3s, t3a, t3b)
    gather2 = Hop(place, "low", lambda p: t3s, t4s, t4a, t4b)
    xswap = core_copy(place, xmine, xback, xsems)
    xhop1 = Hop(place, "low", lambda p: xsum, x1s, x1a, x1b)
    xhop2 = Hop(place, "high", lambda p: xmid, x2s, x2a, x2b)
    swaps = [core_copy(place, away.at[k], back.at[k], ssems.at[k]) for k in range(PARTS)]

    slot = lax.broadcasted_iota(jnp.int32, (256, 128), 1)
    diagonal = (lax.broadcasted_iota(jnp.int32, (256, 128), 0) & 127) == slot
    for half in (0, 1):
        block = table_ref[half].reshape(256, 256)
        far = block[:, 128:]
        left = far[:, 0:1] + far[:, 1:2]
        right = far[:, 2:3] + far[:, 3:4]
        tnear[half] = (block[:, :128] + jnp.where(slot == 127, left, 0.0)).reshape(tnear.shape[1:])
        spread = jnp.where(diagonal, right, 0.0)
        for r in (0, 1):
            at = 4 * LT + 2 * half + r
            xmine[at : at + 1, :] = jnp.sum(spread[r * 128 : (r + 1) * 128], 0, keepdims=True)
    cx.wait()
    for rs in row_tiles(SLAB):
        xhat, _ = norm_parts(x_ref[rs, :].astype(f32))
        n_ref[rs, :] = (xhat * g1[...]).astype(bf16)
    transpose_into(nt_ref, n_ref)
    cg.wait()
    for rs in row_tiles(SLAB):
        gb_ref[rs, :] = (0.5 * gx_ref[rs, :]).astype(bf16)
    transpose_into(gbt_ref, gb_ref)
    place.greeted(("low", "high"))
    tswap.start()
    begin(heads)
    for copy in cw:
        copy.wait()
    dims = away.shape[1:]
    half_dims = (*dims[:3], PART)

    order = [(0, 0), (1, 0), (0, 1), (0, 2), (1, 1), (0, 3), (1, 2), (1, 3)]

    def up(i):
        p, k = order[i]
        gact_ref[i % 2] = dot_nt(gb_ref[...], w2[p, k * PART : (k + 1) * PART, :])

    def weigh(i):
        p, k = order[i]
        for rs in row_tiles(SLAB):
            hid = hid_ref[p, rs, k * PART : (k + 1) * PART].astype(f32)
            sg = jax.nn.sigmoid(hid)
            act = hid * sg
            act_ref[rs, :] = act.astype(bf16)
            ghid_ref[rs, :] = (gact_ref[i % 2, rs, :] * (sg + act * (1.0 - sg))).astype(bf16)

    def down(i):
        p, k = order[i]
        part = dot_nt(ghid_ref[...], w1[p, :, k * PART : (k + 1) * PART])
        if i == 0:
            gn_ref[...] = part
        else:
            gn_ref[...] += part
        return dot(nt_ref[...], ghid_ref[...]), dot(gbt_ref[...], act_ref[...])

    up(0)
    for i, (p, k) in enumerate(order):
        weigh(i)
        if i + 1 < len(order):
            up(i + 1)
        left, right = down(i)
        if p == 0:
            away[k, :, :, :, :PART] = left.reshape(half_dims).astype(bf16)
            away[k, :, :, :, PART:] = right.reshape(half_dims).astype(bf16)
            swaps[k].start()
        else:
            swaps[k].wait()
            left = left.reshape(half_dims) + back[k, :, :, :, :PART].astype(f32)
            right = right.reshape(half_dims) + back[k, :, :, :, PART:].astype(f32)
            accs[k][0][:, :, :, :PART] = left.astype(bf16)
            accs[k][0][:, :, :, PART:] = right[:, :, :, : 384 - PART].astype(bf16)
            accs[k][1][...] = right[:, :, :, 384 - PART :].astype(bf16)
            begin(chains[k])
        if i == 0:
            tswap.wait()
            tsum[...] = tnear[0] + tback[...]
            scatter1.start()
        elif i == 2:
            scatter1.wait()
            t1[...] = scatter1.total()
            scatter2.start()
            turn(heads)
        elif i == 4:
            scatter2.wait()
            t2[...] = scatter2.total()
            t3s[place.hi] = t2[...]
            gather1.start()
        elif i == 5:
            turn(chains[0])
        elif i == 6:
            gather1.wait()
            t4s[place.lo] = t3s[...]
            gather2.start()
        elif i == 7:
            turn(chains[1])

    ffn_gain = jnp.zeros((8, D), f32)
    for rs in row_tiles(SLAB):
        xhat, inv = norm_parts(x_ref[rs, :].astype(f32))
        gn = gn_ref[rs, :]
        gx16_ref[rs, :] = (gx_ref[rs, :] + norm_back(gn, g1[...], xhat, inv)).astype(bf16)
        ffn_gain = ffn_gain + rows_sum(gn * xhat)
    gains = (
        jnp.sum(ffn_gain, 0, keepdims=True),
        jnp.sum(agains[...], 0, keepdims=True),
        sums[5:6, :],
        sums[4:5, :],
    )
    for r, g in enumerate(gains):
        for c in range(LT):
            xmine[r * LT + c : r * LT + c + 1, :] = g[:, c * 128 : (c + 1) * 128]
    xmine[4 * LT + 4 :, :] = jnp.zeros((4, 128), f32)
    xswap.start()
    out_copy = copies.start(gx16_ref, gx_out)
    gxswap = core_copy(place, gx16_ref, gxx_out, gsems)
    gxswap.start()
    xswap.wait()
    xsum[...] = xmine[...] + xback[...]
    at = 4 * LT
    xsum[at : at + 2, :] = xmine[at : at + 2, :] + xback[at + 2 : at + 4, :]
    x1s[place.lo] = xsum[...]
    xhop1.start()
    turn(chains[PARTS - 2])
    xhop1.wait()
    xmid[...] = slot_sum(x1s, place.low)
    x2s[place.hi] = xmid[...]
    xhop2.start()
    turn(chains[PARTS - 1])
    for hop, v in zip(heads[2], HEAD_VIEWS):
        hop.wait()
        h1_ref[:, v.start : v.stop] = hop.total()
    gather2.wait()
    xhop2.wait()
    total = slot_sum(x2s, place.high)
    for r, ref in enumerate((gain0, gain1, gain2, gain3)):
        for c in range(LT):
            ref[:, c * 128 : (c + 1) * 128] = total[r * LT + c : r * LT + c + 1, :]
    line = lax.broadcasted_iota(jnp.int32, (128, 128), 0)
    choice = jnp.where(line + lax.broadcasted_iota(jnp.int32, (128, 128), 1) == 127, 1.0, 0.0)
    tall = jnp.stack([t4s[l, h] for h in range(place.high) for l in range(place.low)]).reshape(256, 128)
    to_ref[: 2 * RW, :] = lax.dot_general(
        choice, tall, (((1,), (1,)), ((), ())), preferred_element_type=f32, precision=lax.Precision.HIGHEST
    )
    for r in (0, 1):
        to_ref[2 * RW : 2 * RW + 1, r * 128 : (r + 1) * 128] = total[at + r : at + r + 1, :]
    for k in range(PARTS):
        for hop, v in zip(chains[k][2], HEAD_VIEWS):
            hop.wait()
            both_ref[:, v.start : v.stop] = hop.total()
        fa_ref[:, k * PART : (k + 1) * PART] = both_ref[:, :PART]
        fb_ref[:, k * PART : (k + 1) * PART] = both_ref[:, PART:]
    out_copy.wait()
    gxswap.wait()


def padded_three(refs):
    return refs + [pltpu.SemaphoreType.DMA((1,))] * (-len(refs) % 3)


def last_call(gx1, frames, hid, w1o, w1x, w2o, w2x, g1, sums, agains, acc1, table):
    width = w1o.shape[1]
    n, dims = grad_dims(2 * PART)
    rows = dims[2]
    high, low = split_axis(n)
    trows = table.shape[3]
    gains = (4 * LT + 8, 128)
    link = firsts(HEAD_VIEWS, n, rows) + seconds(HEAD_VIEWS, n, rows)
    link = link + padded_three([pltpu.VMEM(v.mid(n, rows), bf16) for v in HEAD_VIEWS])
    part = padded_three([pltpu.VMEM((*dims[:3], v.width), bf16) for v in HEAD_VIEWS]) + link
    return pl.pallas_call(
        last_kernel,
        in_specs=[ANY] * 7 + [VMEM] * 5,
        out_specs=[ANY] * 2 + [VMEM] * 8,
        out_shape=[
            shape((SLAB, D), bf16),
            shape((SLAB, D), bf16),
            shape((rows, width), f32),
            shape((rows, width), f32),
        ]
        + [shape((1, D), f32)] * 4
        + [shape((rows, 512), f32), shape((2 * RW + 1, 256), f32)],
        scratch_shapes=[
            pltpu.VMEM((SLAB, D), f32),
            pltpu.VMEM((SLAB, D), bf16),
            pltpu.VMEM((2, SLAB, width), bf16),
            pltpu.VMEM((2, D, width), bf16),
            pltpu.VMEM((2, width, D), bf16),
            pltpu.VMEM((SLAB, D), bf16),
            pltpu.VMEM((D, SLAB), bf16),
            pltpu.VMEM((D, SLAB), bf16),
            pltpu.VMEM((SLAB, D), bf16),
            pltpu.VMEM((2, SLAB, PART), f32),
            pltpu.VMEM((SLAB, PART), bf16),
            pltpu.VMEM((SLAB, PART), bf16),
            pltpu.VMEM((SLAB, D), f32),
            pltpu.VMEM((SLAB, D), bf16),
            pltpu.VMEM((rows, 2 * PART), f32),
            pltpu.VMEM((PARTS, *dims), bf16),
            pltpu.VMEM((PARTS, *dims), bf16),
            pltpu.SemaphoreType.DMA((PARTS, 2)),
            pltpu.SemaphoreType.DMA((2,)),
            pltpu.VMEM(gains, f32),
            pltpu.VMEM(gains, f32),
            pltpu.VMEM(gains, f32),
            pltpu.SemaphoreType.DMA((2,)),
            pltpu.VMEM(gains, f32),
        ]
        + slots_of(low, gains, f32)
        + slots_of(high, gains, f32)
        + [
            pltpu.VMEM((2, high, low, trows, 128), f32),
            pltpu.VMEM((high, low, trows, 128), f32),
            pltpu.SemaphoreType.DMA((2,)),
            pltpu.VMEM((high, low, trows, 128), f32),
            pltpu.VMEM((high, trows, 128), f32),
            pltpu.VMEM((trows, 128), f32),
        ]
        + slots_of(low, (high, trows, 128), f32)
        + slots_of(high, (trows, 128), f32)
        + slots_of(high, (trows, 128), f32)
        + slots_of(low, (high, trows, 128), f32)
        + [pltpu.SemaphoreType.DMA((10,))]
        + link
        + part * PARTS,
        compiler_params=remote(4),
        name="ffn1_backward",
    )(gx1, frames, hid, w1o, w1x, w2o, w2x, g1, sums, agains, acc1, table)


def results_kernel(out_own, out_oth, gx_own, gx_oth, *refs):
    count = len(SMALL)
    smalls, (out_ref, gx_out), outs, (load_ref, gx_ref, sems) = (
        refs[:count], refs[count : count + 2], refs[count + 2 : -3], refs[-3:]
    )
    core = lax.axis_index("mp")
    own = pl.ds(pl.multiple_of(core * SLAB, SLAB), SLAB)
    oth = pl.ds(pl.multiple_of((1 - core) * SLAB, SLAB), SLAB)
    copies = Copies(sems)
    loads = [copies.start(gx_own, load_ref.at[0]), copies.start(gx_oth, load_ref.at[1])]
    loads += [copies.start(out_own, load_ref.at[2]), copies.start(out_oth, load_ref.at[3])]
    ends = []
    for k, rows in ((0, own), (1, oth)):
        loads[k].wait()
        for rs in row_tiles(SLAB):
            gx_ref[k, rs, :] = load_ref[k, rs, :].astype(f32)
        ends.append(copies.start(gx_ref.at[k], gx_out.at[rows]))
    for k, rows in ((2, own), (3, oth)):
        loads[k].wait()
        ends.append(copies.start(load_ref.at[k], out_ref.at[rows]))
    (f1a, f1b, f2a, f2b, h0, h1, cpi, cpo, crest, table, gain0, gain1, gain2, gain3) = smalls
    (of1a, of1b, of2a, of2b, oq, ok, ov, oo, ocpi, ocpo, ock, ov0, ov1, ov2, otable, og0, og1, og2, og3) = outs
    for dst, src in ((of1a, f1a), (of1b, f1b), (of2a, f2a), (of2b, f2b), (ocpi, cpi), (ocpo, cpo), (otable, table),
                     (og0, gain0), (og1, gain1), (og2, gain2), (og3, gain3)):
        dst[...] = src[...]
    for n, dst in enumerate((oq, ok, ov, oo)):
        dst[:, :128] = h0[:, n * 128 : (n + 1) * 128]
        dst[:, 128:] = h1[:, n * 128 : (n + 1) * 128]
    ock[...] = crest[:, :TAPS]
    across = crest[...].T
    for n, dst in enumerate((ov0, ov1, ov2)):
        dst[...] = across[TAPS + n : TAPS + n + 1, :]
    for copy in ends:
        copy.wait()


SMALL = range(14)


def results(out, out_oth, gx, gx_oth, smalls):
    rows, crows = smalls[0].shape[0], smalls[6].shape[0]
    outs = [shape(a.shape, f32) for a in smalls[:4]]
    outs += [shape((rows, D // 2), f32)] * 4
    outs += [shape((crows, 2 * D), f32), shape((crows, D), f32), shape((crows, TAPS), f32)]
    outs += [shape((1, crows), f32)] * 3 + [shape(a.shape, f32) for a in smalls[9:]]
    return pl.pallas_call(
        results_kernel,
        in_specs=[ANY] * 4 + [VMEM] * len(smalls),
        out_specs=[ANY] * 2 + [VMEM] * len(outs),
        out_shape=[shape((2 * SLAB, D), bf16), shape((2 * SLAB, D), f32)] + outs,
        scratch_shapes=[
            pltpu.VMEM((4, SLAB, D), bf16),
            pltpu.VMEM((2, SLAB, D), f32),
            pltpu.SemaphoreType.DMA((8,)),
        ],
        compiler_params=pltpu.CompilerParams(vmem_limit_bytes=60 << 20),
        name="results",
    )(out, out_oth, gx, gx_oth, *smalls)


def shards(
    frames, lengths, cotangent, ffn1_gain, ffn1_in, ffn1_out, attn_gain, query_weight, key_weight,
    value_weight, out_weight, rel_table, conv_gain, pointwise_in, conv_kernel, bn_gain, bn_bias,
    pointwise_out, ffn2_gain, ffn2_in, ffn2_out, final_gain,
):
    n = lax.axis_size("dp")
    high, low = split_axis(n)
    column = jnp.arange(128 - TAPS)[None, :]
    vectors = sum(
        jnp.where(column == k, v[:, None], 0) for k, v in enumerate((conv_gain, bn_gain, bn_bias))
    ).astype(bf16)
    g1, ga, g2, gf = (g[None, :] for g in (ffn1_gain, attn_gain, ffn2_gain, final_gain))
    qkvo = (query_weight, key_weight, value_weight)

    x1, hid1, na, q, k, v, w1x, w2x, wqx, wkx, wvx, v1x, v2x, wox, relx, far = first_call(
        frames, g1, ga, pointwise_in, pointwise_out, conv_kernel, vectors, ffn1_in, ffn1_out, *qkvo, ffn2_in, ffn2_out, out_weight, rel_table
    )
    o16, li, p, gathered = attend_call(lengths, q, k, v, rel_table, relx, far)
    gathered = gathered.reshape(D, CONV_C)
    x2, u, hd, gp, st, taps = conv_call(lengths, x1, o16, out_weight, wox, gathered)
    out, gx3, gz, acc2, gpw, back, sums = middle_call(
        lengths, hd, x2, cotangent, st, taps, gathered, g2, ffn2_in, v1x, ffn2_out, v2x, gf
    )
    gx2, gatt, go, conv_g, *mids = conv_back_call(
        lengths, acc2, gz, hd, gp, st, back, taps, u, x2, gx3, gathered, out_weight, wox, gpw, sums
    )
    conv_g = conv_g.reshape(high, low, 2, D // n // 2, CONV_C)
    gtab, gx1, agains, f2a, f2b, cpi, cpo, crest, h0, acc1 = attend_back_call(
        q, k, v, go, o16, li, p, rel_table, relx, (*qkvo, wqx, wkx, wvx), o16, na, gatt, x1, gx2, ga, mids, conv_g
    )
    gx, gx_oth, f1a, f1b, gain0, gain1, gain2, gain3, h1, table = last_call(
        gx1, frames, hid1, ffn1_in, w1x, ffn1_out, w2x, g1, sums, agains, acc1,
        gtab.reshape(2, high, low, D // 2 // n, 256),
    )
    (block_output, frames_grad, f1a, f1b, f2a, f2b, q_grad, k_grad, v_grad, o_grad, cpi, cpo, ck, cg, bg, bb,
     table, gain0, gain1, gain2, gain3) = results(
        out, lax.ppermute(out, "mp", [(0, 1), (1, 0)]), gx, gx_oth,
        (f1a, f1b, f2a, f2b, h0, h1, cpi, cpo, crest, table, gain0, gain1, gain2, gain3),
    )
    return (
        block_output, frames_grad, gain0[0], f1a, f1b.T, gain1[0], q_grad, k_grad, v_grad, o_grad.T, table, cg[0],
        cpi, ck, bg[0], bb[0], cpo, gain2[0], f2a, f2b.T, gain3[0],
    )


def solution(mesh):
    return jax.shard_map(
        shards,
        mesh=mesh,
        in_specs=(
            P("dp", None), P("dp", None), P("dp", None), P(), P(None, "mp"), P("mp", None), P(),
            P(None, "mp"), P(None, "mp"), P(None, "mp"), P("mp", None), P(None, "mp"),
            P(("dp", "mp")), P(("dp", "mp"), None), P(("dp", "mp"), None), P(("dp", "mp")),
            P(("dp", "mp")), P(("dp", "mp"), None), P(), P(None, "mp"), P("mp", None), P(),
        ),
        out_specs=(
            P("dp", None), P("dp", None), P(), P("dp", "mp"), P("mp", "dp"), P(), P("dp", "mp"),
            P("dp", "mp"), P("dp", "mp"), P("mp", "dp"), P(None, "mp"), P(("dp", "mp")),
            P(("dp", "mp"), None), P(("dp", "mp"), None), P(("dp", "mp")), P(("dp", "mp")),
            P(("dp", "mp"), None), P(), P("dp", "mp"), P("mp", "dp"), P(),
        ),
        check_vma=False,
    )
```
